32 devices in a mesh: wide: 8 (over z, core), narrow: 4 (over y, x).
Axes of the slice: x: 2, y: 2, z: 4, core: 2. Of those that a mesh axis runs over, the one named last changes fastest.
Arguments:
- tokens: bfloat16 [32768, 768], P(('wide', 'narrow')), may hold values from -6 to 6
- cotangent: bfloat16 [32768, 768], P(('wide', 'narrow')), may hold values from -6 to 6
- bucket_counts: int32 [32, 3], P(('wide', 'narrow')), may hold values from 0 to 2, as said below
- attn_gain: bfloat16 [768], P(('wide', 'narrow')), may hold values from 0.5 to 1.5
- attn_shift: bfloat16 [768], P(('wide', 'narrow')), may hold values from -4 to 4
- dense_weight: bfloat16 [12, 768, 768], P(None, ('wide', 'narrow')), may hold values from -0.21875 to 0.21875
- dense_bias: bfloat16 [9216], P(('wide', 'narrow')), may hold values from -6 to 6
- logit_weight: bfloat16 [12, 768, 512], P(None, ('wide', 'narrow')), may hold values from -0.5 to 0.5
- logit_bias: bfloat16 [6144], P(('wide', 'narrow')), may hold values from -6 to 6
- value_weight: bfloat16 [768, 768], P(('wide', 'narrow')), may hold values from -0.21875 to 0.21875
- value_bias: bfloat16 [768], P(('wide', 'narrow')), may hold values from -4 to 4
- output_weight: bfloat16 [768, 768], P(('wide', 'narrow')), may hold values from -0.625 to 0.625
- output_bias: bfloat16 [768], P(('wide', 'narrow')), may hold values from -4 to 4
- feed_gain: bfloat16 [768], P(('wide', 'narrow')), may hold values from 0.5 to 1.5
- feed_shift: bfloat16 [768], P(('wide', 'narrow')), may hold values from -4 to 4
- expand_weight: bfloat16 [768, 3072], P(('wide', 'narrow')), may hold values from -0.21875 to 0.21875
- expand_bias: bfloat16 [3072], P(('wide', 'narrow')), may hold values from -6 to 6
- reduce_weight: bfloat16 [3072, 768], P(('wide', 'narrow')), may hold values from -0.15625 to 0.15625
- reduce_bias: bfloat16 [768], P(('wide', 'narrow')), may hold values from -6 to 6
Outputs:
- layer_out: float32 [32768, 768], P(('wide', 'narrow'))
- tokens_grad: float32 [32768, 768], P(('wide', 'narrow'))
- attn_gain_grad: float32 [768], P(('wide', 'narrow'))
- attn_shift_grad: float32 [768], P(('wide', 'narrow'))
- dense_weight_grad: float32 [12, 768, 768], P(None, ('wide', 'narrow'))
- dense_bias_grad: float32 [9216], P(('wide', 'narrow'))
- logit_weight_grad: float32 [12, 768, 512], P(None, ('wide', 'narrow'))
- logit_bias_grad: float32 [6144], P(('wide', 'narrow'))
- value_weight_grad: float32 [768, 768], P(('wide', 'narrow'))
- value_bias_grad: float32 [768], P(('wide', 'narrow'))
- output_weight_grad: float32 [768, 768], P(('wide', 'narrow'))
- output_bias_grad: float32 [768], P(('wide', 'narrow'))
- feed_gain_grad: float32 [768], P(('wide', 'narrow'))
- feed_shift_grad: float32 [768], P(('wide', 'narrow'))
- expand_weight_grad: float32 [768, 3072], P(('wide', 'narrow'))
- expand_bias_grad: float32 [3072], P(('wide', 'narrow'))
- reduce_weight_grad: float32 [3072, 768], P(('wide', 'narrow'))
- reduce_bias_grad: float32 [768], P(('wide', 'narrow'))
The draws below stay inside these ranges and needn't reach their ends.
Inputs may be any that keep to these rules, and one draw needn't show every extreme that they name: bucket_counts[d, k] is at most 2, 1 and 1 for k = 0, 1, 2; a device's live slots are its first ones in each bucket; in every draw one device has all its slots live and another has none.
All inputs are finite; a program needn't handle non-finite values.
Results may differ from the reference program's by a relative error of at most 0.012.
Values may be sent and summed in bfloat16 or wider, within the bound.
A program may use at most 384 MiB of HBM per device.

```python
import jax
import jax.numpy as jnp
from jax import lax

D = 768
HEADS = 12
HEAD_DIM = 64
HIDDEN_SIZE = 768
FF = 3072
L3 = 512
L1 = 128
L2 = 256
S1 = 2
S2 = 1
S3 = 1
ROWS_DEV = 1024
ROWS = 32768
N_WIDE = 8
N_NARROW = 4


def draw_bucket_counts(key, part):
    device_count = ROWS // ROWS_DEV
    key_one, key_two, key_three, key_full = jax.random.split(key, 4)
    columns = []
    for key_slot, slot_count in ((key_one, S1), (key_two, S2), (key_three, S3)):
        coins = jax.random.randint(key_slot, (device_count, slot_count), 0, 4)
        columns.append(jnp.sum(jnp.where(coins > 0, 1, 0), axis=1).astype(jnp.int32))
    counts = jnp.stack(columns, axis=1)
    full_device = jax.random.randint(key_full, (), 0, device_count).astype(jnp.int32)
    empty_device = (full_device + device_count // 2) % device_count
    device_ids = jnp.arange(device_count, dtype=jnp.int32)[:, None]
    limits = jnp.array([S1, S2, S3], dtype=jnp.int32)[None, :]
    counts = jnp.where(device_ids == full_device, limits, counts)
    counts = jnp.where(device_ids == empty_device, 0, counts)
    return counts.astype(jnp.int32)


def shard_levels(key, dims, shards, least, largest):
    def one(position, shards_of):
        steps = jax.random.uniform(jax.random.fold_in(jax.random.fold_in(key, 6), position), (shards_of,), jnp.float32, least / len(shards), largest / len(shards))
        return jnp.repeat(jnp.exp(steps), dims[position] // shards_of).reshape((-1,) + (1,) * (len(dims) - position - 1))

    level = one(*shards[0])
    for cut in shards[1:]:
        level = level * one(*cut)
    return level


def noise(rng, extent, deviation, most, cuts=(), kind=jnp.bfloat16):
    result = deviation * jax.random.normal(rng, extent, jnp.float32)
    if cuts:
        result = result * shard_levels(rng, extent, cuts, -0.22, 0.18)
    return jnp.clip(result, -most, most).astype(kind)


def setup_inputs(seed: int = 0) -> dict:
    arg_keys = jax.random.split(jax.random.key(seed), 20)
    return {
        "tokens": noise(arg_keys[0], (ROWS, D), 1.0, 6.0, ((0, 32),)),
        "cotangent": noise(arg_keys[1], (ROWS, D), 1.0, 6.0, ((0, 32),)),
        "bucket_counts": draw_bucket_counts(jax.random.fold_in(arg_keys[19], 71), 0),
        "attn_gain": jnp.clip(1.0 + 0.1 * jax.random.normal(arg_keys[3], (D,), jnp.float32), 0.5, 1.5).astype(jnp.bfloat16),
        "attn_shift": noise(arg_keys[4], (D,), 0.3, 4.0, ((0, 32),)),
        "dense_weight": noise(arg_keys[5], (HEADS, D, HIDDEN_SIZE), D ** -0.5, 0.21875, ((1, 32),)),
        "dense_bias": noise(arg_keys[6], (HEADS * HIDDEN_SIZE,), 0.5, 6.0, ((0, 32),)),
        "logit_weight": noise(arg_keys[7], (HEADS, HIDDEN_SIZE, L3), (HIDDEN_SIZE // 6) ** -0.5, 0.5, ((1, 32),)),
        "logit_bias": noise(arg_keys[8], (HEADS * L3,), 1.0, 6.0, ((0, 32),)),
        "value_weight": noise(arg_keys[9], (D, D), D ** -0.5, 0.21875, ((0, 32),)),
        "value_bias": noise(arg_keys[10], (D,), 0.3, 4.0, ((0, 32),)),
        "output_weight": noise(arg_keys[11], (D, D), (D // 8) ** -0.5, 0.625, ((0, 32),)),
        "output_bias": noise(arg_keys[12], (D,), 0.3, 4.0, ((0, 32),)),
        "feed_gain": jnp.clip(1.0 + 0.1 * jax.random.normal(arg_keys[13], (D,), jnp.float32), 0.5, 1.5).astype(jnp.bfloat16),
        "feed_shift": noise(arg_keys[14], (D,), 0.3, 4.0, ((0, 32),)),
        "expand_weight": noise(arg_keys[15], (D, FF), D ** -0.5, 0.21875, ((0, 32),)),
        "expand_bias": noise(arg_keys[16], (FF,), 0.5, 6.0, ((0, 32),)),
        "reduce_weight": noise(arg_keys[17], (FF, D), (FF // 2) ** -0.5, 0.15625, ((0, 32),)),
        "reduce_bias": noise(arg_keys[18], (D,), 0.6, 6.0, ((0, 32),)),
    }


norm_eps = 1e-05
highest = lax.Precision.HIGHEST
gelu_root = 0.7978845608028654
gelu_cube = 0.044715

@jax.custom_vjp
def low(v):
    return lax.optimization_barrier(v.astype(jnp.bfloat16)).astype(jnp.float32)

@jax.custom_vjp
def low_back(v):
    return v

def low_keep(v):
    return (low(v), None)

def low_pass(kept, grad):
    return (grad,)

def back_keep(v):
    return (v, None)

def back_low(kept, grad):
    return (low(grad),)
low.defvjp(low_keep, low_pass)
low_back.defvjp(back_keep, back_low)

def smooth_gate(values_in):
    return 0.5 * values_in * (1.0 + jnp.tanh(gelu_root * (values_in + gelu_cube * values_in * values_in * values_in)))

def bucket_layout():
    return ((S1, L1), (S2, L2), (S3, L3))

def live_rows(counts):
    pieces = []
    for bucket_index, (slot_count, seq_length) in enumerate(bucket_layout()):
        slot_of_row = jnp.arange(slot_count * seq_length, dtype=jnp.int32) // seq_length
        pieces.append(jnp.where(slot_of_row < counts[bucket_index], 1.0, 0.0).astype(jnp.float32))
    return jnp.concatenate(pieces)

def layer_norm(values_in, norm_gain, norm_shift):
    row_mean = lax.optimization_barrier(jnp.mean(values_in, axis=-1, keepdims=True))
    centred = values_in - row_mean
    variance = lax.optimization_barrier(jnp.mean(centred * centred, axis=-1, keepdims=True))
    return centred * lax.rsqrt(variance + norm_eps) * norm_gain + norm_shift

def matmul(left_side, right_side):
    return jnp.dot(left_side, right_side, precision=highest, preferred_element_type=jnp.float32)

def device_rows(inputs_float, live_mask, weights):
    attn_gain, attn_shift, dense_weight, dense_bias, logit_weight, logit_bias, value_weight, value_bias, output_weight, output_bias, feed_gain, feed_shift, expand_weight, expand_bias, reduce_weight, reduce_bias = weights
    normed = low(layer_norm(inputs_float, attn_gain, attn_shift))
    values = low(low_back(matmul(normed, value_weight) + value_bias))
    dense_heads = dense_bias.reshape(HEADS, 1, HIDDEN_SIZE)
    logit_heads = logit_bias.reshape(HEADS, 1, L3)
    mixed_list = []
    start_row = 0
    for slot_count, seq_length in bucket_layout():
        stop_row = start_row + slot_count * seq_length
        block_rows = normed[start_row:stop_row]
        pre_act = jnp.einsum('rd,hde->hre', block_rows, dense_weight, precision=highest) + dense_heads
        hidden = low(smooth_gate(low_back(pre_act)))
        scores = jnp.einsum('hre,hel->hrl', hidden, logit_weight[:, :, :seq_length], precision=highest)
        scores = low_back(scores + logit_heads[:, :, :seq_length])
        attention = low(jax.nn.softmax(scores, axis=-1))
        attention = attention.reshape(HEADS, slot_count, seq_length, seq_length)
        block_values = values[start_row:stop_row].reshape(slot_count, seq_length, HEADS, HEAD_DIM)
        mixed_heads = jnp.einsum('hsql,slhc->sqhc', attention, block_values, precision=highest)
        mixed_list.append(mixed_heads.reshape(slot_count * seq_length, D))
        start_row = stop_row
    mixed_all = low(low_back(jnp.concatenate(mixed_list, axis=0)))
    attended = low_back(matmul(mixed_all, output_weight) + output_bias)
    residual = inputs_float + attended
    normed_two = low(layer_norm(residual, feed_gain, feed_shift))
    inner_act = low(smooth_gate(low_back(matmul(normed_two, expand_weight) + expand_bias)))
    feed_out = low_back(matmul(inner_act, reduce_weight) + reduce_bias)
    return live_mask[:, None] * (residual + feed_out)

def reference(tokens, cotangent, bucket_counts, attn_gain, attn_shift, dense_weight, dense_bias, logit_weight, logit_bias, value_weight, value_bias, output_weight, output_bias, feed_gain, feed_shift, expand_weight, expand_bias, reduce_weight, reduce_bias):
    device_count = N_WIDE * N_NARROW
    params = tuple((weight_arg.astype(jnp.float32) for weight_arg in (attn_gain, attn_shift, dense_weight, dense_bias, logit_weight, logit_bias, value_weight, value_bias, output_weight, output_bias, feed_gain, feed_shift, expand_weight, expand_bias, reduce_weight, reduce_bias)))
    inputs_all = tokens.astype(jnp.float32).reshape(device_count, -1, D)
    grads_in = cotangent.astype(jnp.float32).reshape(device_count, -1, D)
    live_all = jax.vmap(live_rows)(bucket_counts)
    step_fn = jax.checkpoint(device_rows)

    def forward(inputs_every, weights):

        def scan_body(carry, item):
            return (carry, step_fn(item[0], item[1], weights))
        _, outputs = lax.scan(scan_body, None, (inputs_every, live_all))
        return outputs
    outputs, pullback = jax.vjp(forward, inputs_all, params)
    grad_inputs, grad_params = pullback(grads_in)
    g_attn_gain, g_attn_shift, g_dense_weight, g_dense_bias, g_logit_weight, g_logit_bias, g_value_weight, g_value_bias, g_output_weight, g_output_bias, g_feed_gain, g_feed_shift, g_expand_weight, g_expand_bias, g_reduce_weight, g_reduce_bias = grad_params
    return (outputs.reshape(-1, D), grad_inputs.reshape(-1, D), g_attn_gain, g_attn_shift, g_dense_weight, g_dense_bias, g_logit_weight, g_logit_bias, g_value_weight, g_value_bias, g_output_weight, g_output_bias, g_feed_gain, g_feed_shift, g_expand_weight, g_expand_bias, g_reduce_weight, g_reduce_bias)
```

```python
import functools

import jax
import jax.numpy as jnp
import numpy as np
from jax import lax
from jax.experimental import pallas as pl
from jax.experimental.pallas import tpu as pltpu
from jax.sharding import PartitionSpec as P

D = 768
HEADS = 12
HEAD_DIM = 64
HIDDEN_SIZE = 768
L3 = 512
AXES = ("wide", "narrow")
L1 = 128
L2 = 256
S1 = 2
S2 = 1
S3 = 1

norm_eps = 1e-05
gelu_root = 0.7978845608028654
gelu_cube = 0.044715

MESH = pl.DeviceIdType.MESH
HBM = pl.BlockSpec(memory_space=pltpu.HBM)
VMEM = pl.BlockSpec(memory_space=pltpu.VMEM)
VMEM_LIMIT = 63 * 1024 * 1024
f32 = jnp.float32
bf16 = jnp.bfloat16

ROWS_DEV = 1024
CHIP_ROWS = 2048
HALF = 384
NN = (((1,), (0,)), ((), ()))
NT = (((1,), (1,)), ((), ()))
TN = (((0,), (0,)), ((), ()))


def dot(a, b, dims=NN):
    return lax.dot_general(a, b, dims, preferred_element_type=f32)


def gelu_both(v):
    sq = v * v
    t = jnp.tanh(v * (gelu_root + gelu_root * gelu_cube * sq))
    up = 0.5 + 0.5 * t
    slope = up + 0.5 * v * (1.0 - t * t) * (gelu_root + 3.0 * gelu_root * gelu_cube * sq)
    return v * up, slope


def norm_rows(x):
    mean = jnp.mean(x, axis=-1, keepdims=True)
    cen = x - mean
    inv = lax.rsqrt(jnp.mean(cen * cen, axis=-1, keepdims=True) + norm_eps)
    return cen * inv, inv


class Place:
    def __init__(self):
        w = lax.axis_index(AXES[0])
        n = lax.axis_index(AXES[1])
        self.w, self.n = w, n
        self.z, self.c = w // 2, w % 2
        self.nx = n + 1 - 2 * (n % 2)
        self.ny = (n + 2) % 4
        self.nd = 3 - n
        self.xdev = (w, self.nx)
        self.ydev = (w, self.ny)
        self.sib = (self.z * 2 + 1 - self.c, n)

    def zpos(self, i):
        return (self.z + i) % 4

    def zdev(self, zz):
        return (zz * 2 + self.c, self.n)

    def near(self):
        return [self.xdev, self.ydev, self.sib] + [self.zdev(self.zpos(i)) for i in (1, 2, 3)]


def greet(devs):
    bar = pltpu.get_barrier_semaphore()
    for dev in devs:
        pl.semaphore_signal(bar, inc=1, device_id=dev, device_id_type=MESH)
    pl.semaphore_wait(bar, len(devs))


def remote(src, dst, ssem, rsem, dev):
    return pltpu.make_async_remote_copy(
        src_ref=src, dst_ref=dst, send_sem=ssem, recv_sem=rsem, device_id=dev, device_id_type=MESH
    )


def k0_kernel(s_in, tok_in, dense, logit, vo, ff, s_all, tok, md, ml, mvo, mf, ss, sr, es, er):
    pc = Place()
    c = pc.c
    me = pc.w * 4 + pc.n
    bar = pltpu.get_barrier_semaphore()

    @pl.loop(1, 32)
    def _(j):
        t = (me + j) % 32
        pl.semaphore_signal(bar, inc=1, device_id=(t // 4, t % 4), device_id_type=MESH)

    pl.semaphore_wait(bar, 31)
    o = 1 - c

    @pl.loop(1, 32)
    def _(j):
        t = (me + j) % 32
        remote(s_in, s_all.at[me], ss.at[t], sr.at[me], (t // 4, t % 4)).start()

    pairs = [
        (dense.at[pl.ds(3 * o, 3)], md.at[:, c]),
        (logit.at[pl.ds(3 * o, 3)], ml.at[:, c]),
        (vo.at[o], mvo.at[c]),
        (ff.at[o], mf.at[:, c]),
        (tok_in, tok),
    ]
    rems = [remote(give, slot, es.at[i], er.at[i], pc.sib) for i, (give, slot) in enumerate(pairs)]
    for cp in rems:
        cp.start()
    s_all[me] = s_in[...]
    md[:, c] = dense[pl.ds(3 * c, 3)]
    ml[:, c] = logit[pl.ds(3 * c, 3)]
    mvo[c] = vo[c]
    mf[:, c] = ff[c]
    for cp in rems:
        cp.wait()

    @pl.loop(1, 32)
    def _(j):
        t = (me + j) % 32
        f = (me + 32 - j) % 32
        cp = remote(s_in, s_all.at[f], ss.at[t], sr.at[f], (t // 4, t % 4))
        cp.wait_send()
        cp.wait_recv()


def k0_call(s_in, tok, dense, logit, vo, ff):
    sds = jax.ShapeDtypeStruct
    return pl.pallas_call(
        k0_kernel,
        out_shape=(
            sds((32, 16, 128), bf16),
            sds((ROWS_DEV, D), bf16),
            sds((3, 2, 48, D), bf16),
            sds((3, 2, 48, L3), bf16),
            sds((2, 48, HALF), bf16),
            sds((2, 2, 48, D), bf16),
        ),
        in_specs=[VMEM, HBM, VMEM, VMEM, VMEM, VMEM],
        out_specs=(VMEM, HBM, VMEM, VMEM, VMEM, VMEM),
        scratch_shapes=[
            pltpu.SemaphoreType.DMA((32,)),
            pltpu.SemaphoreType.DMA((32,)),
            pltpu.SemaphoreType.DMA((5,)),
            pltpu.SemaphoreType.DMA((5,)),
        ],
        compiler_params=pltpu.CompilerParams(collective_id=0, has_side_effects=True),
        name="k0_exchange",
    )(s_in, tok, dense, logit, vo, ff)


class Gather:
    def __init__(self, pc, sems):
        self.pc = pc
        self.zs, self.zr, self.xs, self.xr, self.ys, self.yr, self.ds, self.dr, self.ls = sems

    def zcopy(self, k, src, buf, i, sender=None):
        pc = self.pc
        zz = pc.z if sender is None else sender
        return remote(src, buf.at[zz, :, pc.n], self.zs.at[k, i], self.zr.at[k, zz], pc.zdev(pc.zpos(i)))

    def zsend(self, k, src, buf):
        for i in (1, 2, 3):
            self.zcopy(k, src, buf, i).start()
        self.own(k, src, buf).start()

    def own(self, k, src, buf):
        return pltpu.make_async_copy(src, buf.at[self.pc.z, :, self.pc.n], self.ls.at[k])

    def xcopy(self, k, buf, zz, src=None, col=None):
        pc = self.pc
        col = pc.n if col is None else col
        slot = buf.at[zz, :, col]
        return remote(slot if src is None else src, slot, self.xs.at[k, zz], self.xr.at[k, zz], pc.xdev)

    def ycopy(self, k, buf, zz, src=None, col=None):
        pc = self.pc
        col = pc.n if col is None else col
        slot = buf.at[zz, :, col]
        return remote(slot if src is None else src, slot, self.ys.at[k, zz], self.yr.at[k, zz], pc.ydev)

    def col(self, k, src, buf, i):
        pc = self.pc
        zz = pc.zpos(i)
        if i:
            self.zcopy(k, src, buf, i, sender=zz).wait_recv()
        s = None if i else src
        self.xcopy(k, buf, zz, s).start()
        self.ycopy(k, buf, zz, s).start()

    def dcopy(self, k, buf, zz):
        pc = self.pc
        if zz < 2:
            slot, dev = buf.at[zz, :, pc.nx], pc.ydev
        else:
            slot, dev = buf.at[zz, :, pc.ny], pc.xdev
        return remote(slot, slot, self.ds.at[k, zz], self.dr.at[k, zz], dev)

    def diag(self, k, buf, zz):
        pc = self.pc
        self.xcopy(k, buf, zz, col=pc.nx).wait_recv()
        self.ycopy(k, buf, zz, col=pc.ny).wait_recv()
        self.dcopy(k, buf, zz).start()

    def fin(self, k, src, buf):
        for zz in range(4):
            remote(
                buf.at[zz, :, self.pc.nd],
                buf.at[zz, :, self.pc.nd],
                self.ds.at[k, zz],
                self.dr.at[k, zz],
                self.pc.xdev,
            ).wait_recv()
        self.own(k, src, buf).wait()

    def sent(self, k, src, buf):
        for i in (1, 2, 3):
            self.zcopy(k, src, buf, i).wait_send()
        for zz in range(4):
            self.xcopy(k, buf, zz).wait_send()
            self.ycopy(k, buf, zz).wait_send()
            self.dcopy(k, buf, zz).wait_send()


def gather_sems(k):
    dma = pltpu.SemaphoreType.DMA
    return [dma((k, 4))] * 8 + [dma((k,))]


def join_pair(stage, dst_of, rows_of):
    @pl.loop(0, 4)
    def _(zz):
        for cc in range(2):
            for nn in (0, 2):
                one = stage[zz, cc, nn].astype(f32)
                two = stage[zz, cc, nn + 1].astype(f32)
                row = pl.multiple_of(zz * 192 + cc * 96 + nn * 24, 16)
                for e in rows_of:
                    both = jnp.concatenate(
                        [one[24 * e : 24 * e + 24], two[24 * e : 24 * e + 24]], axis=0
                    )
                    dst_of(e, pl.ds(row, 48), both.astype(bf16))


def k1_kernel(
    tok, tok2, vec, db, lb, vb, mvo, md, ml, mf,
    ovo, gd, gl, ef, nrm_o, val_o, hid_o, slo_o, atl_o, atm_o, ats_o, wa_o, la_o, mix_o, vv_o,
    tokv, nrm, val, vst, vv, wst, lst, wv, lv, hidv, slov, atlv, atmv, atsv, mixv,
    zs, zr, xs, xr, ys, yr, ds, dr, ls, tsem, osem, wsem, lsem, ssem, rsem, msem,
):
    pc = Place()
    c = pc.c
    g = Gather(pc, (zs, zr, xs, xr, ys, yr, ds, dr, ls))
    tcopies = []
    for i, (ref, d) in enumerate(((tok, c), (tok2, 1 - c))):
        for j, (at, to) in enumerate(((512, d * 512), (0, 1024 + d * 512))):
            rows = pl.ds(pl.multiple_of(to, 512), 512)
            tcopies.append(pltpu.make_async_copy(ref.at[pl.ds(at, 512)], tokv.at[rows], tsem.at[2 * i + j]))
    for cp in tcopies:
        cp.start()
    greet(pc.near())

    vo_args = (0, mvo, ovo.at[c])
    dd = lambda p: (1 + 2 * p, md.at[p], gd.at[p])
    ll = lambda p: (2 + 2 * p, ml.at[p], gl.at[p])
    fa = (7, mf.at[0], ef.at[c, 0])
    fb = (8, mf.at[1], ef.at[c, 1])

    g.zsend(*vo_args)
    g.zsend(*dd(0))
    for i in range(4):
        g.col(*vo_args, i)
    g.zsend(*ll(0))
    for i in range(4):
        g.col(*dd(0), i)
    for zz in range(4):
        g.diag(vo_args[0], vo_args[2], zz)

    for cp in tcopies:
        cp.wait()

    @pl.loop(0, 8)
    def _(b):
        rows = pl.ds(pl.multiple_of(b * 256, 256), 256)
        unit, _ = norm_rows(tokv[rows].astype(f32))
        nrm[rows] = (unit * vec[0:1] + vec[1:2]).astype(bf16)

    nrm_copy = pltpu.make_async_copy(nrm, nrm_o, tsem.at[4])
    nrm_copy.start()
    g.zsend(*dd(1))
    for i in range(4):
        g.col(*ll(0), i)
    g.fin(*vo_args)
    vo_load = pltpu.make_async_copy(ovo.at[c], vst, tsem.at[5])
    vo_load.start()
    vo_swap = remote(ovo.at[c], ovo.at[c], ssem.at[0], rsem.at[0], pc.sib)
    vo_swap.start()
    vo_load.wait()

    def put_v(e, rows, x):
        vv[rows] = x

    join_pair(vst, put_v, (0,))

    @pl.loop(0, 4)
    def _(b):
        rows = pl.ds(pl.multiple_of(b * 512, 512), 512)
        val[rows] = (dot(nrm[rows], vv[...]) + vb[...]).astype(bf16)

    val_copy = pltpu.make_async_copy(val, val_o, tsem.at[6])
    val_copy.start()
    vv_copy = pltpu.make_async_copy(vv, vv_o, tsem.at[5])
    vv_copy.start()
    for zz in range(4):
        g.diag(dd(0)[0], dd(0)[2], zz)
    g.zsend(*ll(1))
    for i in range(2):
        g.col(*dd(1), i)
    for zz in range(4):
        g.diag(ll(0)[0], ll(0)[2], zz)
    g.fin(*dd(0))
    g.fin(*ll(0))

    lane = lax.broadcasted_iota(jnp.int32, (1, 128), 1)
    keeps = [(lane < HEAD_DIM).astype(bf16), (lane >= HEAD_DIM).astype(bf16)]

    def softmax(s):
        m = jnp.max(s, axis=-1, keepdims=True)
        ex = jnp.exp(s - m)
        return (ex / jnp.sum(ex, axis=-1, keepdims=True)).astype(bf16)

    @pl.loop(0, 3)
    def _(p):
        q = p + 1
        more = p < 2
        ka, kb = 1 + 2 * q, 2 + 2 * q

        def on_a(fn):
            @pl.when(more)
            def _():
                fn(ka, md.at[q % 3], gd.at[q % 3])

            @pl.when(jnp.logical_not(more))
            def _():
                fn(*fa)

        def on_b(fn):
            @pl.when(more)
            def _():
                fn(kb, ml.at[q % 3], gl.at[q % 3])

            @pl.when(jnp.logical_not(more))
            def _():
                fn(*fb)

        def on_next(fn):
            @pl.when(p == 0)
            def _():
                fn(5, md.at[2], gd.at[2])

            @pl.when(p == 1)
            def _():
                fn(*fa)

        def on_next_b(fn):
            @pl.when(p == 0)
            def _():
                fn(6, ml.at[2], gl.at[2])

            @pl.when(p == 1)
            def _():
                fn(*fb)

        def tick(pos):
            if pos == 0:
                on_a(lambda k, s, b: g.col(k, s, b, 2))
                on_a(lambda k, s, b: g.col(k, s, b, 3))
                on_next(g.zsend)
            elif pos == 1:
                on_b(lambda k, s, b: g.col(k, s, b, 0))
                on_b(lambda k, s, b: g.col(k, s, b, 1))
            elif pos == 2:
                on_a(lambda k, s, b: g.diag(k, b, 0))
                on_a(lambda k, s, b: g.diag(k, b, 2))
            elif pos == 3:
                on_b(lambda k, s, b: g.col(k, s, b, 2))
                on_b(lambda k, s, b: g.col(k, s, b, 3))
            elif pos == 4:
                on_a(lambda k, s, b: g.diag(k, b, 1))
                on_a(lambda k, s, b: g.diag(k, b, 3))
                on_next_b(g.zsend)
            elif pos == 5:
                on_next(lambda k, s, b: g.col(k, s, b, 0))
                on_b(lambda k, s, b: g.diag(k, b, 0))
            elif pos == 6:
                on_b(lambda k, s, b: g.diag(k, b, 2))
                on_next(lambda k, s, b: g.col(k, s, b, 1))
            elif pos == 7:
                on_b(lambda k, s, b: g.diag(k, b, 1))
                on_b(lambda k, s, b: g.diag(k, b, 3))

        wload = pltpu.make_async_copy(gd.at[p], wst, tsem.at[7])
        lload = pltpu.make_async_copy(gl.at[p], lst, tsem.at[8])
        wload.start()
        lload.start()
        wcopy = lambda r: pltpu.make_async_copy(wv, wa_o.at[pl.ds(2 * r, 2)], wsem)
        lcopy = lambda r: pltpu.make_async_copy(lv, la_o.at[pl.ds(2 * r, 2)], lsem)

        @pl.when(p > 0)
        def _():
            wcopy(p - 1).wait()
            lcopy(p - 1).wait()

        wload.wait()

        def put_w(e, rows, x):
            wv[e, rows] = x

        def put_l(e, rows, x):
            lv[e, rows] = x

        join_pair(wst, put_w, (0, 1))
        lload.wait()
        join_pair(lst, put_l, (0, 1))
        wcopy(p).start()
        lcopy(p).start()
        lanes = pl.ds(pl.multiple_of(p * 128, 128), 128)

        def out_copies(e, d, long, h):
            row = d * 512 if long else 1024 + d * 512
            rows = pl.ds(row, 512)
            cps = [
                pltpu.make_async_copy(hidv.at[e], hid_o.at[h, rows], osem.at[e, 0]),
                pltpu.make_async_copy(slov.at[e], slo_o.at[h, rows], osem.at[e, 1]),
            ]
            if long:
                cps.append(pltpu.make_async_copy(atlv.at[e], atl_o.at[h, pl.ds(d * 512, 512)], osem.at[e, 2]))
            else:
                part = pl.ds(d * 256, 256)
                cps.append(pltpu.make_async_copy(atmv.at[e], atm_o.at[h, part], osem.at[e, 3]))
                cps.append(pltpu.make_async_copy(atsv.at[e], ats_o.at[h, part], osem.at[e, 4]))
            return cps

        pos = 0
        for d in range(2):
            for long in (True, False):
                row = d * 512 if long else 1024 + d * 512
                rows = slice(row, row + 512)
                mixed = None
                for e in range(2):
                    h = 2 * p + e
                    pre = dot(nrm[rows], wv[e]) + db[pl.ds(h, 1)]
                    hid, slo = gelu_both(pre)
                    if d == 0 and long:

                        @pl.when(p > 0)
                        def _():
                            for cp in out_copies(e, 1, False, h):
                                cp.wait()
                    else:
                        for cp in out_copies(e, d if not long else d - 1, not long, h):
                            cp.wait()
                    hidv[e] = hid.astype(bf16)
                    slov[e] = slo.astype(bf16)
                    lbias = lb[pl.ds(h, 1)]
                    vpair = val[rows, lanes] * keeps[e]
                    if long:
                        att = softmax(dot(hidv[e], lv[e]) + lbias)
                        atlv[e] = att
                        m = dot(att, vpair)
                    else:
                        short = softmax(dot(hidv[e, 0:256], lv[e, :, 0:128]) + lbias[:, 0:128])
                        mid = softmax(dot(hidv[e, 256:512], lv[e, :, 0:256]) + lbias[:, 0:256])
                        atsv[e] = short
                        atmv[e] = mid
                        m = jnp.concatenate(
                            [
                                dot(short[0:128], vpair[0:128]),
                                dot(short[128:256], vpair[128:256]),
                                dot(mid, vpair[256:512]),
                            ],
                            axis=0,
                        )
                    mixed = m if mixed is None else mixed + m
                    for cp in out_copies(e, d, long, h):
                        cp.start()
                    tick(pos)
                    pos += 1
                mixv[rows, lanes] = mixed.astype(bf16)
        on_a(g.fin)
        on_b(g.fin)

        @pl.when(p == 2)
        def _():
            for e in range(2):
                for cp in out_copies(e, 1, False, 2 * p + e):
                    cp.wait()
            wcopy(p).wait()
            lcopy(p).wait()

    swaps = [remote(ef.at[c], ef.at[c], ssem.at[1], rsem.at[1], pc.sib), vo_swap]
    swaps[0].start()
    o = 1 - c
    for i, (start, to) in enumerate(((0, 512), (1024, 0))):
        mine = pltpu.make_async_copy(
            mixv.at[pl.ds(start + c * 512, 512)], mix_o.at[c, pl.ds(to, 512)], msem.at[i]
        )
        mine.start()
        other = remote(
            mixv.at[pl.ds(start + o * 512, 512)], mix_o.at[c, pl.ds(to, 512)], ssem.at[2 + i], rsem.at[2 + i], pc.sib
        )
        other.start()
        swaps += [mine, other]
    for cp in swaps + [nrm_copy, val_copy, vv_copy]:
        cp.wait()
    g.sent(*vo_args)
    for p in range(3):
        g.sent(*dd(p))
        g.sent(*ll(p))
    g.sent(*fa)
    g.sent(*fb)


def k1_call(tok, tok2, vec, db, lb, vb, mvo, md, ml, mf):
    sds = jax.ShapeDtypeStruct
    dma = pltpu.SemaphoreType.DMA
    return pl.pallas_call(
        k1_kernel,
        out_shape=(
            sds((2, 4, 2, 4, 48, HALF), bf16),
            sds((3, 4, 2, 4, 48, D), bf16),
            sds((3, 4, 2, 4, 48, L3), bf16),
            sds((2, 2, 4, 2, 4, 48, D), bf16),
            sds((CHIP_ROWS, D), bf16),
            sds((CHIP_ROWS, HALF), bf16),
            sds((6, CHIP_ROWS, HIDDEN_SIZE), bf16),
            sds((6, CHIP_ROWS, HIDDEN_SIZE), bf16),
            sds((6, 1024, L3), bf16),
            sds((6, 512, L2), bf16),
            sds((6, 512, L1), bf16),
            sds((6, D, HIDDEN_SIZE), bf16),
            sds((6, HIDDEN_SIZE, L3), bf16),
            sds((2, ROWS_DEV, HALF), bf16),
            sds((D, HALF), bf16),
        ),
        in_specs=[HBM] * 2 + [VMEM] * 8,
        out_specs=(HBM,) * 15,
        scratch_shapes=[
            pltpu.VMEM((CHIP_ROWS, D), bf16),
            pltpu.VMEM((CHIP_ROWS, D), bf16),
            pltpu.VMEM((CHIP_ROWS, HALF), bf16),
            pltpu.VMEM((4, 2, 4, 48, HALF), bf16),
            pltpu.VMEM((D, HALF), bf16),
            pltpu.VMEM((4, 2, 4, 48, D), bf16),
            pltpu.VMEM((4, 2, 4, 48, L3), bf16),
            pltpu.VMEM((2, D, HIDDEN_SIZE), bf16),
            pltpu.VMEM((2, HIDDEN_SIZE, L3), bf16),
            pltpu.VMEM((2, 512, HIDDEN_SIZE), bf16),
            pltpu.VMEM((2, 512, HIDDEN_SIZE), bf16),
            pltpu.VMEM((2, 512, L3), bf16),
            pltpu.VMEM((2, 256, L2), bf16),
            pltpu.VMEM((2, 256, L1), bf16),
            pltpu.VMEM((CHIP_ROWS, HALF), bf16),
        ]
        + gather_sems(9)
        + [dma((9,)), dma((2, 5)), dma, dma, dma((4,)), dma((4,)), dma((2,))],
        compiler_params=pltpu.CompilerParams(
            collective_id=1, has_side_effects=True, vmem_limit_bytes=VMEM_LIMIT
        ),
        name="k1_attention",
    )(tok, tok2, vec, db, lb, vb, mvo, md, ml, mf)


def prepare(tokens, attn_gain, attn_shift, dense_weight, dense_bias, logit_weight, logit_bias, value_weight,
            value_bias, output_weight, output_bias, feed_gain, feed_shift, expand_weight, expand_bias,
            reduce_weight, reduce_bias):
    core = lax.axis_index(AXES[0]) % 2
    small = jnp.concatenate(
        [attn_gain, attn_shift, value_bias, output_bias, feed_gain, feed_shift, reduce_bias,
         expand_bias, logit_bias, dense_bias, jnp.zeros((2048 - 744,), bf16)]
    ).reshape(16, 128)
    dense = dense_weight.reshape(6, 48, D)
    logit = logit_weight.reshape(6, 48, L3)
    vo = jnp.stack([value_weight.reshape(24, 2, HALF), output_weight.reshape(24, 2, HALF)]).transpose(2, 0, 1, 3)
    vo = vo.reshape(2, 48, HALF)
    ff = jnp.stack(
        [expand_weight.reshape(24, 4, D).transpose(1, 0, 2).reshape(2, 48, D), reduce_weight.reshape(2, 48, D)]
    )
    s_all, tok2, md, ml, mvo, mf = k0_call(small, tokens, dense, logit, vo, ff)
    flat = s_all.reshape(32, 2048)[:, :744].astype(f32)
    vec = flat[:, :168].reshape(32, 7, 24).transpose(1, 0, 2).reshape(7, D)
    eb = flat[:, 168:264].reshape(4, D)
    lb = lax.dynamic_slice(flat[:, 264:456].reshape(HEADS, L3), (6 * core, 0), (6, L3))
    db = lax.dynamic_slice(flat[:, 456:744].reshape(HEADS, HIDDEN_SIZE), (6 * core, 0), (6, HIDDEN_SIZE))
    vb = lax.dynamic_slice(vec[2:3], (0, HALF * core), (1, HALF))
    return tok2, vec, eb, lb, db, vb, md, ml, mvo, mf


def k2_kernel(
    x, cot, counts, mix, ovo, ef, vec, eb,
    lay_o, gres_o, gmix_o, def_o, do_o, sums_o,
    ev, rv, ow, inner, ge, n2, gf, ga, acc, dst, rsem, dsem, osem,
):
    oloads = []
    for half in range(2):
        lanes = pl.ds(half * HALF, HALF)
        oloads.append(pltpu.make_async_copy(ovo.at[half], dst.at[0, :, :, :, :, lanes], osem.at[half]))
    loads = [pltpu.make_async_copy(ef.at[0, f], dst.at[1 - f], dsem.at[1 - f]) for f in range(2)]
    for cp in oloads:
        cp.start()
    loads[0].start()
    rloads = []
    for f in range(2):
        for j in range(4):
            rloads.append(
                pltpu.make_async_copy(ef.at[1, f, j], rv.at[j, :, :, pl.ds(48 * f, 48)], rsem.at[f, j])
            )
    for cp in rloads:
        cp.start()

    def put_o(e, rows, v):
        ow[rows] = v

    for cp in oloads:
        cp.wait()
    join_pair(dst.at[0], put_o, (1,))
    loads[1].start()
    for f in range(2):

        def put_e(e, rows, v):
            ev[2 * f + e, rows] = v

        loads[f].wait()
        join_pair(dst.at[1 - f], put_e, (0, 1))
    for cp in rloads:
        cp.wait()
    fg, fs = vec[4:5], vec[5:6]
    sums_o[...] = jnp.zeros_like(sums_o)

    @pl.loop(0, 4)
    def _(b):
        rows = pl.ds(pl.multiple_of(b * 256, 256), 256)
        mixed = jnp.concatenate([mix[0, rows], mix[1, rows]], axis=1)
        res = x[rows].astype(f32) + (dot(mixed, ow[...]) + vec[3:4])
        unit, inv = norm_rows(res)
        n2v = (unit * fg + fs).astype(bf16)
        n2[rows] = n2v
        later = jnp.where(b == 1, counts[0, 1], counts[0, 2])
        low = jnp.where(b == 0, counts[0, 0], later) >= 1
        high = jnp.where(b == 0, counts[0, 0] - 1, later) >= 1
        top = lax.broadcasted_iota(jnp.int32, (256, 1), 0) < L1
        alive = jnp.where(top, jnp.where(low, 1.0, 0.0), jnp.where(high, 1.0, 0.0))
        gout = cot[rows].astype(f32) * alive
        gfb = gout.astype(bf16)
        gf[rows] = gfb
        feed = None
        gn2 = None
        for j in range(4):
            cols = slice(j * D, j * D + D)
            rj = rv[j].reshape(D, D)
            hid, slo = gelu_both(dot(n2v, ev[j]) + eb[j : j + 1])
            hb = hid.astype(bf16)
            inner[rows, cols] = hb
            f_j = dot(hb, rj)
            feed = f_j if feed is None else feed + f_j
            geb = (dot(gfb, rj, NT) * slo).astype(bf16)
            ge[rows, cols] = geb
            g_j = dot(geb, ev[j], NT)
            gn2 = g_j if gn2 is None else gn2 + g_j
        lay_o[rows] = alive * (res + (feed + vec[6:7]))
        q = gn2 * fg
        gres = gout + inv * (
            q - jnp.mean(q, axis=-1, keepdims=True) - unit * jnp.mean(q * unit, axis=-1, keepdims=True)
        )
        gres_o[rows] = gres
        gab = gres.astype(bf16)
        ga[rows] = gab
        gm = dot(gab, ow[...], NT).astype(bf16)
        gmix_o[0, rows] = gm[:, :HALF]
        gmix_o[1, rows] = gm[:, HALF:]
        sums_o[0:1] += jnp.sum(gn2 * unit, axis=0, keepdims=True)
        sums_o[1:2] += jnp.sum(gn2, axis=0, keepdims=True)

    ones = jnp.ones((8, ROWS_DEV), bf16)
    sums_o[2:3] = dot(ones, gf[...])[0:1]
    sums_o[3:4] = dot(ones, ga[...])[0:1]

    def out_copy(t, f):
        return pltpu.make_async_copy(dst.at[f], def_o.at[t, f], dsem.at[f])

    for f in range(2):
        for e in range(2):
            j = 2 * f + e
            sums_o[4 + j : 5 + j] = dot(ones, ge[:, j * D : j * D + D])[0:1]
            acc[e] = dot(n2[...], ge[:, j * D : j * D + D], TN)

        @pl.loop(0, 4)
        def _(zz):
            for i in range(8):
                row = pl.ds(pl.multiple_of(zz * 192 + i * 24, 8), 24)
                both = jnp.concatenate([acc[0, row], acc[1, row]], axis=0)
                dst[f, zz, i // 4, i % 4] = both.astype(bf16)

        out_copy(0, f).start()
    for j in range(4):
        acc[j % 2] = dot(inner[:, j * D : j * D + D], gf[...], TN)
        if j == 0:
            out_copy(0, 0).wait()
            out_copy(0, 1).wait()
        for i in range(8):
            for f in range(2):
                at = i * 96 + f * 48
                dst[f, j, i // 4, i % 4] = acc[j % 2, at : at + 48].astype(bf16)
    for f in range(2):
        out_copy(1, f).start()
    zero = jnp.zeros((24, HALF), f32)
    for hh in range(2):
        acc[0, 0:HALF] = dot(mix[hh], ga[...], TN)
        for i in range(16):
            for half in range(2):
                part = acc[0, i * 24 : i * 24 + 24, half * HALF : half * HALF + HALF]
                do_o[half, 2 * hh + i // 8, (i // 4) % 2, i % 4] = jnp.concatenate([zero, part], axis=0).astype(bf16)
    for f in range(2):
        out_copy(1, f).wait()


def k2_call(x, cot, counts, mix, ovo, ef, vec, eb):
    sds = jax.ShapeDtypeStruct
    dma = pltpu.SemaphoreType.DMA
    return pl.pallas_call(
        k2_kernel,
        out_shape=(
            sds((ROWS_DEV, D), f32),
            sds((ROWS_DEV, D), f32),
            sds((2, ROWS_DEV, HALF), bf16),
            sds((2, 2, 4, 2, 4, 48, D), bf16),
            sds((2, 4, 2, 4, 48, HALF), bf16),
            sds((8, D), f32),
        ),
        in_specs=[VMEM, VMEM, pl.BlockSpec(memory_space=pltpu.SMEM), VMEM] + [HBM] * 2 + [VMEM] * 2,
        out_specs=(VMEM, VMEM, VMEM, HBM, VMEM, VMEM),
        scratch_shapes=[
            pltpu.VMEM((4, D, D), bf16),
            pltpu.VMEM((4, 2, 4, 96, D), bf16),
            pltpu.VMEM((D, D), bf16),
            pltpu.VMEM((ROWS_DEV, 4 * D), bf16),
            pltpu.VMEM((ROWS_DEV, 4 * D), bf16),
            pltpu.VMEM((ROWS_DEV, D), bf16),
            pltpu.VMEM((ROWS_DEV, D), bf16),
            pltpu.VMEM((ROWS_DEV, D), bf16),
            pltpu.VMEM((2, D, D), f32),
            pltpu.VMEM((2, 4, 2, 4, 48, D), bf16),
            dma((2, 4)),
            dma((2,)),
            dma((2,)),
        ],
        compiler_params=pltpu.CompilerParams(vmem_limit_bytes=VMEM_LIMIT),
        name="k2_feed",
    )(x, cot, counts, mix, ovo, ef, vec, eb)


class Scatter:
    def __init__(self, pc, sems):
        self.pc = pc
        self.as_, self.ar, self.xs, self.xr, self.ys, self.yr, self.zs, self.zr, self.os, self.or_ = sems

    def acopy(self, k, p5, bufs, zz):
        dev = self.pc.xdev if zz < 2 else self.pc.ydev
        return remote(p5.at[zz, :, self.pc.nd], bufs[0].at[zz], self.as_.at[k, zz], self.ar.at[k, zz], dev)

    def xcopy(self, k, p5, bufs, zz):
        return remote(p5.at[zz, :, self.pc.nx], bufs[1].at[zz], self.xs.at[k, zz], self.xr.at[k, zz], self.pc.xdev)

    def ycopy(self, k, p5, bufs, zz):
        return remote(p5.at[zz, :, self.pc.ny], bufs[2].at[zz], self.ys.at[k, zz], self.yr.at[k, zz], self.pc.ydev)

    def zcopy(self, k, p5, bufs, i):
        zz = self.pc.zpos(i)
        return remote(
            p5.at[zz, :, self.pc.n], bufs[3].at[i - 1], self.zs.at[k, i], self.zr.at[k, i], self.pc.zdev(zz)
        )

    def one(self, k, p5, bufs):
        for zz in range(4):
            self.acopy(k, p5, bufs, zz).start()
        for zz in range(4):
            (self.xcopy if zz < 2 else self.ycopy)(k, p5, bufs, zz).start()

    def two(self, k, p5, bufs, zz):
        col = self.pc.ny if zz < 2 else self.pc.nx
        self.acopy(k, p5, bufs, zz).wait_recv()
        p5[zz, :, col] = (p5[zz, :, col].astype(f32) + bufs[0][zz].astype(f32)).astype(bf16)
        (self.ycopy if zz < 2 else self.xcopy)(k, p5, bufs, zz).start()

    def column(self, k, p5, bufs, zz):
        self.xcopy(k, p5, bufs, zz).wait_recv()
        self.ycopy(k, p5, bufs, zz).wait_recv()
        return p5[zz, :, self.pc.n].astype(f32) + bufs[1][zz].astype(f32) + bufs[2][zz].astype(f32)

    def three(self, k, p5, bufs, i):
        zz = self.pc.zpos(i)
        p5[zz, :, self.pc.n] = self.column(k, p5, bufs, zz).astype(bf16)
        self.zcopy(k, p5, bufs, i).start()

    def outs(self, k, st, out):
        c = self.pc.c
        return (
            pltpu.make_async_copy(st.at[c], out, self.os.at[k, 1]),
            remote(st.at[1 - c], out, self.os.at[k, 0], self.or_.at[k], self.pc.sib),
        )

    def four(self, k, p5, bufs, st, out):
        total = self.column(k, p5, bufs, self.pc.z)
        for i in (1, 2, 3):
            self.zcopy(k, p5, bufs, i).wait_recv()
            total = total + bufs[3][i - 1].astype(f32)
        st[...] = total
        for cp in self.outs(k, st, out):
            cp.start()

    def sent(self, k, p5, bufs):
        for zz in range(4):
            self.acopy(k, p5, bufs, zz).wait_send()
            self.xcopy(k, p5, bufs, zz).wait_send()
            self.ycopy(k, p5, bufs, zz).wait_send()
        for i in (1, 2, 3):
            self.zcopy(k, p5, bufs, i).wait_send()


def k3_kernel(
    def_in, do_in, nrm_i, val_i, gmix, hid_i, slo_i, atl_i, atm_i, ats_i, wa_i, la_i, vv_i, tok, gres, vec,
    tg_o, od, ol, ofe, ovo, db_o, lb_o, vb_o, ag_o,
    nrm, val, gm, gn, hid, slo, atl, atm, ats, gsl, gsm, gd, wv, lv, dwf, vsb, vv, own,
    pd, pll, pv, ad, xd, yd, zd, al, xl, yl, zl, av, xv, yv, zv, std, stl, stv,
    as_, ar, xs, xr, ys, yr, zs, zr, os_, or_, lsem, ssem, rsem, gs_, gr_, free, hsem, fsem, dsem,
):
    pc = Place()
    c = pc.c
    o = 1 - c
    s = Scatter(pc, (as_, ar, xs, xr, ys, yr, zs, zr, os_, or_))
    copy = pltpu.make_async_copy
    first = [copy(nrm_i, nrm, lsem.at[0]), copy(val_i, val, lsem.at[1]), copy(vv_i, vv, lsem.at[2])]
    for i, (at, to) in enumerate(((512, 0), (0, 1024))):
        first.append(copy(gmix.at[c, pl.ds(at, 512)], gm.at[pl.ds(pl.multiple_of(to + c * 512, 512), 512)], lsem.at[4 + i]))
    for cp in first:
        cp.start()

    def att_loads(h):
        return [copy(atl_i.at[h], atl, hsem.at[0]), copy(atm_i.at[h], atm, hsem.at[1]), copy(ats_i.at[h], ats, hsem.at[2])]

    hid_load = lambda h: copy(hid_i.at[h], hid, hsem.at[3])
    w_load = lambda h: copy(wa_i.at[h], wv, hsem.at[4])
    l_load = lambda h: copy(la_i.at[h], lv, hsem.at[5])
    slo_load = lambda h, b: copy(slo_i.at[h, pl.ds(b * 512, 512)], slo.at[b % 2], hsem.at[6 + b % 2])
    for cp in att_loads(0) + [hid_load(0), l_load(0), slo_load(0, 0), slo_load(0, 1), w_load(0)]:
        cp.start()
    own_load = lambda f, zz: copy(def_in.at[c, f, zz], own.at[zz % 2], fsem.at[zz % 2])
    own_load(0, 0).start()
    own_load(0, 1).start()

    greet(pc.near())
    swaps = []
    for f in range(2):
        swaps.append(remote(def_in.at[o, f], pd.at[f], ssem.at[f], rsem.at[f], pc.sib))
    swaps.append(remote(do_in.at[o], pv, ssem.at[2], rsem.at[2], pc.sib))
    for i, (at, to) in enumerate(((512, 0), (0, 1024))):
        swaps.append(
            remote(
                gmix.at[o, pl.ds(at, 512)],
                gm.at[pl.ds(pl.multiple_of(to + c * 512, 512), 512)],
                ssem.at[3 + i],
                rsem.at[3 + i],
                pc.sib,
            )
        )
    for i in (3, 4, 0, 1, 2):
        swaps[i].start()

    def d_args(k):
        slot = k % 3
        return pd.at[slot], (ad.at[k], xd.at[k], yd.at[k], zd.at[k])

    def l_args(p):
        return pll.at[p % 2], (al.at[p], xl.at[p], yl.at[p], zl.at[p])

    v_args = (pv, (av, xv, yv, zv))
    gn[...] = jnp.zeros_like(gn)
    gsm[...] = jnp.zeros_like(gsm)

    for f in range(2):
        swaps[f].wait()
        for zz in range(4):
            own_load(f, zz).wait()
            pd[f, zz] = (pd[f, zz].astype(f32) + own[zz % 2].astype(f32)).astype(bf16)
            if zz < 2:
                own_load(f, zz + 2).start()
            elif f == 0:
                own_load(1, zz - 2).start()
        s.one(f, *d_args(f))
    dloads = []
    for zz in range(4):
        lanes = pl.ds(HALF * (zz % 2), HALF)
        dloads.append(copy(do_in.at[c, zz], own.at[zz // 2, :, :, :, lanes], dsem.at[zz]))
    for cp in dloads:
        cp.start()
    swaps[3].wait()
    swaps[4].wait()
    for cp in first:
        cp.wait()

    lane = lax.broadcasted_iota(jnp.int32, (1, 128), 1)
    keeps = [(lane < HEAD_DIM).astype(bf16), (lane >= HEAD_DIM).astype(bf16)]
    ones = jnp.ones((8, 1024), bf16)

    def score_grad(att, g):
        a = att.astype(f32)
        t = a * g
        return (t - a * jnp.sum(t, axis=-1, keepdims=True)).astype(bf16)

    def put_pair(p5, half, e, width):
        @pl.loop(0, 2)
        def _(zi):
            for i in range(8):
                row = pl.ds(pl.multiple_of(zi * 192 + i * 24, 8), 24)
                part = dwf[row, 0:width]
                if e == 0:
                    both = jnp.concatenate([part, part], axis=0)
                else:
                    old = p5[2 * half + zi, i // 4, i % 4].astype(f32)
                    both = jnp.concatenate([old[0:24], part], axis=0)
                p5[2 * half + zi, i // 4, i % 4] = both.astype(bf16)

    @pl.loop(0, 3)
    def _(p):
        lanes = pl.ds(pl.multiple_of(p * 128, 128), 128)
        begin = p == 0
        later = p > 0
        kd = p + 2
        dslot = kd % 3

        def on_a(fn):
            @pl.when(begin)
            def _():
                fn(0, *d_args(0))

            @pl.when(later)
            def _():
                fn(kd - 1, *d_args(kd - 1))

        def on_b(fn):
            @pl.when(begin)
            def _():
                fn(1, *d_args(1))

            @pl.when(later)
            def _():
                fn(5 + (p + 2) % 3, *l_args((p + 2) % 3))

        def four_a():
            @pl.when(begin)
            def _():
                s.four(0, *d_args(0), std.at[0], ofe.at[c, 0])

            @pl.when(p == 2)
            def _():
                for cp in s.outs(0, std.at[0], ofe.at[c, 0]):
                    cp.wait()

            @pl.when(later)
            def _():
                s.four(kd - 1, *d_args(kd - 1), std.at[(kd - 1) % 3], od.at[3 * c + (p + 2) % 3])

        def four_b():
            @pl.when(begin)
            def _():
                s.four(1, *d_args(1), std.at[1], ofe.at[c, 1])

            @pl.when(later)
            def _():
                r = (p + 2) % 3
                s.four(5 + r, *l_args(r), stl.at[r], ol.at[3 * c + r])

        for e in range(2):
            h = 2 * p + e
            more = h < 5

            def ahead(*cps):
                @pl.when(more)
                def _():
                    for cp in cps:
                        cp.start()

            for cp in att_loads(h):
                cp.wait()
            for b in range(4):
                at = b * 512
                rows = slice(at, at + 512)
                gpair = gm[rows, lanes]
                vpair = val[rows, lanes] * keeps[e]
                gkeep = gpair * keeps[e]
                if b < 2:
                    att = atl[rows]
                    gsl[rows] = score_grad(att, dot(gpair, vpair, NT))
                    vs = dot(att, gkeep, TN)
                else:
                    part = slice((b - 2) * 256, (b - 2) * 256 + 256)
                    sh, mi = ats[part], atm[part]
                    g_sh = jnp.concatenate(
                        [dot(gpair[0:128], vpair[0:128], NT), dot(gpair[128:256], vpair[128:256], NT)], axis=0
                    )
                    at2 = (b - 2) * 512
                    gsm[at2 : at2 + 256, 0:128] = score_grad(sh, g_sh)
                    gsm[at2 + 256 : at2 + 512] = score_grad(mi, dot(gpair[256:512], vpair[256:512], NT))
                    vs = jnp.concatenate(
                        [
                            dot(sh[0:128], gkeep[0:128], TN),
                            dot(sh[128:256], gkeep[128:256], TN),
                            dot(mi, gkeep[256:512], TN),
                        ],
                        axis=0,
                    )
                if e == 0:
                    vsb[rows] = vs.astype(bf16)
                else:
                    gm[rows, lanes] = vsb[rows] + vs.astype(bf16)
            ahead(*att_loads(h + 1))
            lsum = dot(ones, gsl[...])
            lb_o[pl.ds(h, 1)] = lsum[0:1]
            lb_o[pl.ds(h, 1), 0:256] += dot(ones, gsm[...])[0:1]
            if e == 0:
                on_a(lambda k, p5, bufs: s.two(k, p5, bufs, 0))
                on_a(lambda k, p5, bufs: s.two(k, p5, bufs, 2))
            else:
                for i in (1, 2, 3):
                    on_a(lambda k, p5, bufs, i=i: s.three(k, p5, bufs, i))
            if e == 0:

                @pl.when(p == 2)
                def _():
                    s.sent(5, *l_args(0))

            hid_load(h).wait()
            for half in range(2):
                cols = slice(half * HALF, half * HALF + HALF)
                dwf[:, 0:512] = dot(hid[0:1024, cols], gsl[...], TN)
                dwf[:, 0:256] += dot(hid[1024:2048, cols], gsm[...], TN)
                put_pair(pll.at[p % 2], half, e, 512)
            ahead(hid_load(h + 1))
            if e == 1:
                s.one(5 + p, *l_args(p))
            else:
                on_a(lambda k, p5, bufs: s.two(k, p5, bufs, 1))
                on_a(lambda k, p5, bufs: s.two(k, p5, bufs, 3))
            l_load(h).wait()
            for b in range(4):
                rows = slice(b * 512, b * 512 + 512)
                slo_load(h, b).wait()
                if b < 2:
                    gh = dot(gsl[rows], lv[...], NT)
                else:
                    gh = dot(gsm[(b - 2) * 512 : (b - 2) * 512 + 512], lv[:, 0:256], NT)
                gd[rows] = (gh * slo[b % 2].astype(f32)).astype(bf16)
                if b < 2:
                    slo_load(h, b + 2).start()
                else:
                    ahead(slo_load(h + 1, b - 2))
            ahead(l_load(h + 1))
            db_o[pl.ds(h, 1)] = (dot(ones, gd[0:1024]) + dot(ones, gd[1024:2048]))[0:1]
            if e == 0:
                on_b(lambda k, p5, bufs: s.two(k, p5, bufs, 0))
                on_b(lambda k, p5, bufs: s.two(k, p5, bufs, 2))
            else:
                for i in (1, 2, 3):
                    on_b(lambda k, p5, bufs, i=i: s.three(k, p5, bufs, i))
            if e == 0:

                @pl.when(later)
                def _():
                    s.sent(kd - 3, *d_args(kd - 3))

            for half in range(2):
                cols = slice(half * HALF, half * HALF + HALF)
                dwf[...] = dot(nrm[:, cols], gd[...], TN)
                put_pair(pd.at[dslot], half, e, D)
            if e == 1:
                s.one(kd, *d_args(kd))
                four_a()
            else:
                on_b(lambda k, p5, bufs: s.two(k, p5, bufs, 1))
                on_b(lambda k, p5, bufs: s.two(k, p5, bufs, 3))
            w_load(h).wait()

            @pl.loop(0, 4)
            def _(b):
                rows = pl.ds(pl.multiple_of(b * 512, 512), 512)
                gn[rows] += dot(gd[rows], wv[...], NT)

            ahead(w_load(h + 1))
            if e == 1:
                four_b()

    vb_o[...] = dot(ones, gm[0:1024]) + dot(ones, gm[1024:2048])
    swaps[2].wait()
    for cp in dloads:
        cp.wait()
    for half in range(2):
        cols = slice(half * HALF, half * HALF + HALF)
        dwf[:, 0:HALF] = dot(nrm[:, cols], gm[...], TN)

        for zi in range(2):

            @pl.loop(0, 8)
            def _(i):
                row = pl.ds(pl.multiple_of(zi * 192 + i * 24, 8), 24)
                part = dwf[row, 0:HALF]
                at = (2 * half + zi, i // 4, i % 4)
                mine = own[half, i // 4, i % 4, :, HALF * zi : HALF * zi + HALF]
                both = pv[at].astype(f32) + mine.astype(f32)
                pv[at] = jnp.concatenate([part, both[24:48]], axis=0).astype(bf16)

    s.one(8, *v_args)
    for zz in (0, 2):
        s.two(4, *d_args(4), zz)
    for zz in (0, 2):
        s.two(7, *l_args(2), zz)
    pl.semaphore_signal(free, inc=1, device_id=pc.sib, device_id_type=MESH)

    @pl.loop(0, 4)
    def _(b):
        rows = pl.ds(pl.multiple_of(b * 512, 512), 512)
        gn[rows] += dot(gm[rows], vv[...], NT)

    for zz in (1, 3):
        s.two(4, *d_args(4), zz)
    for zz in (1, 3):
        s.two(7, *l_args(2), zz)
    for zz in (0, 2, 1, 3):
        s.two(8, *v_args, zz)
    other = lambda to: pl.ds(pl.multiple_of(to + o * 512, 512), 512)
    mine = lambda to: pl.ds(pl.multiple_of(to + c * 512, 512), 512)
    hid[0:512] = gn[other(1024)].astype(bf16)
    hid[512:1024] = gn[other(0)].astype(bf16)
    pl.semaphore_wait(free, 1)
    gswap = remote(hid.at[pl.ds(0, 1024)], gd.at[pl.ds(0, 1024)], gs_, gr_, pc.sib)
    gswap.start()
    tloads = [copy(tok.at[pl.ds(i * 512, 512)], slo.at[i], hsem.at[6 + i]) for i in range(2)]
    for cp in tloads:
        cp.start()
    for i in (1, 2, 3):
        s.three(4, *d_args(4), i)
    for i in (1, 2, 3):
        s.three(7, *l_args(2), i)
    for cp in tloads:
        cp.wait()
    gswap.wait()
    ag_o[...] = jnp.zeros_like(ag_o)

    @pl.loop(0, 4)
    def _(b):
        nat = pl.ds(pl.multiple_of(b * 256, 256), 256)
        trow = pl.ds(pl.multiple_of(jnp.where(b < 2, 1024 + b * 256, b * 256 - 512) + c * 512, 256), 256)
        load = copy(gres.at[nat], dwf.at[pl.ds(0, 256)], lsem.at[6])
        load.start()
        unit, inv = norm_rows(slo[b // 2, pl.ds(pl.multiple_of((b % 2) * 256, 256), 256)].astype(f32))
        g = gn[trow] + gd[nat].astype(f32)
        q = g * vec[0:1]
        back = inv * (q - jnp.mean(q, axis=-1, keepdims=True) - unit * jnp.mean(q * unit, axis=-1, keepdims=True))
        load.wait()
        dwf[0:256] = dwf[0:256] + back
        ag_o[0:1] += jnp.sum(g * unit, axis=0, keepdims=True)
        ag_o[1:2] += jnp.sum(g, axis=0, keepdims=True)
        store = copy(dwf.at[pl.ds(0, 256)], tg_o.at[nat], lsem.at[7])
        store.start()
        store.wait()

    for i in (1, 2, 3):
        s.three(8, *v_args, i)
    for cp in s.outs(1, std.at[1], ofe.at[c, 1]):
        cp.wait()
    s.four(4, *d_args(4), std.at[1], od.at[3 * c + 2])
    s.four(7, *l_args(2), stl.at[2], ol.at[3 * c + 2])
    s.four(8, *v_args, stv, ovo.at[c])
    ends = []
    for p in range(3):
        ends.append(s.outs(2 + p, std.at[(2 + p) % 3], od.at[3 * c + p]))
        ends.append(s.outs(5 + p, stl.at[p], ol.at[3 * c + p]))
    ends.append(s.outs(8, stv, ovo.at[c]))
    for pair in ends:
        for cp in pair:
            cp.wait()
    for k in (2, 3, 4):
        s.sent(k, *d_args(k))
    for p in (1, 2):
        s.sent(5 + p, *l_args(p))
    s.sent(8, *v_args)


def k3_call(*args):
    sds = jax.ShapeDtypeStruct
    dma = pltpu.SemaphoreType.DMA
    V = pltpu.VMEM

    def bufs(shape, width):
        return [V(shape + (4, 2, 48, width), bf16)] * 3 + [V(shape + (3, 2, 48, width), bf16)]

    return pl.pallas_call(
        k3_kernel,
        out_shape=(
            sds((ROWS_DEV, D), f32),
            sds((6, 48, D), f32),
            sds((6, 48, L3), f32),
            sds((2, 2, 48, D), f32),
            sds((2, 48, HALF), f32),
            sds((8, D), f32),
            sds((8, L3), f32),
            sds((8, HALF), f32),
            sds((8, D), f32),
        ),
        in_specs=[HBM] * 15 + [VMEM],
        out_specs=(HBM,) * 5 + (VMEM,) * 4,
        scratch_shapes=[
            V((CHIP_ROWS, D), bf16),
            V((CHIP_ROWS, HALF), bf16),
            V((CHIP_ROWS, HALF), bf16),
            V((CHIP_ROWS, D), f32),
            V((CHIP_ROWS, HIDDEN_SIZE), bf16),
            V((2, 512, HIDDEN_SIZE), bf16),
            V((1024, L3), bf16),
            V((512, L2), bf16),
            V((512, L1), bf16),
            V((1024, L3), bf16),
            V((1024, L2), bf16),
            V((CHIP_ROWS, HIDDEN_SIZE), bf16),
            V((D, HIDDEN_SIZE), bf16),
            V((HIDDEN_SIZE, L3), bf16),
            V((HALF, D), f32),
            V((CHIP_ROWS, 128), bf16),
            V((D, HALF), bf16),
            V((2, 2, 4, 48, D), bf16),
            V((3, 4, 2, 4, 48, D), bf16),
            V((2, 4, 2, 4, 48, L3), bf16),
            V((4, 2, 4, 48, HALF), bf16),
        ]
        + bufs((5,), D)
        + bufs((3,), L3)
        + bufs((), HALF)
        + [V((3, 2, 48, D), f32), V((3, 2, 48, L3), f32), V((2, 48, HALF), f32)]
        + [dma((9, 4))] * 8
        + [dma((9, 2)), dma((9,)), dma((8,)), dma((5,)), dma((5,)), dma, dma, pltpu.SemaphoreType.REGULAR]
        + [dma((8,)), dma((2,)), dma((4,))],
        compiler_params=pltpu.CompilerParams(
            collective_id=2, has_side_effects=True, vmem_limit_bytes=VMEM_LIMIT
        ),
        name="k3_backward",
    )(*args)


def k4_kernel(g, out, slots, ss, sr):
    pc = Place()
    me = pc.w * 4 + pc.n
    bar = pltpu.get_barrier_semaphore()

    @pl.loop(1, 32)
    def _(j):
        t = (me + j) % 32
        pl.semaphore_signal(bar, inc=1, device_id=(t // 4, t % 4), device_id_type=MESH)

    pl.semaphore_wait(bar, 31)

    @pl.loop(1, 32)
    def _(j):
        t = (me + j) % 32
        remote(g.at[t], slots.at[me], ss.at[t], sr.at[me], (t // 4, t % 4)).start()

    slots[me] = g[me]

    @pl.loop(1, 32)
    def _(j):
        t = (me + j) % 32
        f = (me + 32 - j) % 32
        cp = remote(g.at[t], slots.at[f], ss.at[t], sr.at[f], (t // 4, t % 4))
        cp.wait_send()
        cp.wait_recv()

    out[...] = jnp.sum(slots[...], axis=0)


def k4_call(g):
    return pl.pallas_call(
        k4_kernel,
        out_shape=jax.ShapeDtypeStruct((8, 128), f32),
        in_specs=[VMEM],
        out_specs=VMEM,
        scratch_shapes=[
            pltpu.VMEM((32, 8, 128), f32),
            pltpu.SemaphoreType.DMA((32,)),
            pltpu.SemaphoreType.DMA((32,)),
        ],
        compiler_params=pltpu.CompilerParams(collective_id=3, has_side_effects=True),
        name="k4_vectors",
    )(g)


def chip_body(tokens, cotangent, bucket_counts, *params):
    core = lax.axis_index(AXES[0]) % 2
    tok2, vec, eb, lb, db, vb, md, ml, mvo, mf = prepare(tokens, *params)
    vec = jnp.pad(vec, ((0, 1), (0, 0)))
    ovo, _, _, ef, nrm, val, hid, slo, atl, atm, ats, wa, la, mix, vv = k1_call(
        tokens, tok2, vec, db, lb, vb, mvo, md, ml, mf
    )
    lay, gres, gmix, dff, dout, sums = k2_call(tokens, cotangent, bucket_counts, mix, ovo, ef, vec, eb)
    tg, od, ol, ofe, dvo, dbs, lbs, vbs, ags = k3_call(
        dff, dout, nrm, val, gmix, hid, slo, atl, atm, ats, wa, la, vv, tokens, gres, vec
    )
    vb_all = lax.dynamic_update_slice(jnp.zeros((1, D), f32), vbs[0:1], (0, HALF * core))
    lb_all = lax.dynamic_update_slice(jnp.zeros((HEADS, L3), f32), lbs[0:6], (6 * core, 0))
    db_all = lax.dynamic_update_slice(jnp.zeros((HEADS, HIDDEN_SIZE), f32), dbs[0:6], (6 * core, 0))
    v7 = jnp.concatenate([ags[0:2], vb_all, sums[3:4], sums[0:2], sums[2:3]])
    pack = jnp.concatenate(
        [
            v7.reshape(7, 32, 24).transpose(1, 0, 2).reshape(32, 168),
            sums[4:8].reshape(32, 96),
            lb_all.reshape(32, 192),
            db_all.reshape(32, 288),
            jnp.zeros((32, 1024 - 744), f32),
        ],
        axis=1,
    )
    red = k4_call(pack.reshape(32, 8, 128)).reshape(1024)
    small = lambda i: red[24 * i : 24 * i + 24]
    return (
        lay,
        tg,
        small(0),
        small(1),
        od.reshape(HEADS, 24, HIDDEN_SIZE),
        red[456:744],
        ol.reshape(HEADS, 24, L3),
        red[264:456],
        dvo[:, 0:24].transpose(1, 0, 2).reshape(24, D),
        small(2),
        dvo[:, 24:48].transpose(1, 0, 2).reshape(24, D),
        small(3),
        small(4),
        small(5),
        ofe[0].reshape(4, 24, D).transpose(1, 0, 2).reshape(24, 4 * D),
        red[168:264],
        ofe[1].reshape(96, D),
        small(6),
    )


def smooth_gate(values_in):
    return (
        0.5
        * values_in
        * (1.0 + jnp.tanh(gelu_root * (values_in + gelu_cube * values_in * values_in * values_in)))
    )


def gate_slope(values_in):
    squared = values_in * values_in
    tangent = jnp.tanh(gelu_root * (values_in + gelu_cube * squared * values_in))
    return 0.5 * (1.0 + tangent) + 0.5 * values_in * (1.0 - tangent * tangent) * gelu_root * (
        1.0 + 3.0 * gelu_cube * squared
    )


def bucket_layout():
    return ((S1, L1), (S2, L2), (S3, L3))


def live_rows(counts):
    pieces = []
    for bucket_index, (slot_count, seq_length) in enumerate(bucket_layout()):
        slot_of_row = jnp.arange(slot_count * seq_length, dtype=jnp.int32) // seq_length
        pieces.append(jnp.where(slot_of_row < counts[bucket_index], 1.0, 0.0).astype(jnp.float32))
    return jnp.concatenate(pieces)


def product(left_side, right_side):
    return jnp.dot(left_side, right_side, preferred_element_type=jnp.float32)


def column_sums(matrix_rows):
    return jnp.sum(matrix_rows.astype(jnp.float32), axis=0)


def norm_forward(inputs_float, norm_gain, norm_shift):
    row_mean = jnp.mean(inputs_float, axis=-1, keepdims=True)
    centred = inputs_float - row_mean
    inverse_scale = lax.rsqrt(jnp.mean(centred * centred, axis=-1, keepdims=True) + norm_eps)
    unit_rows = centred * inverse_scale
    return (unit_rows * norm_gain + norm_shift, unit_rows, inverse_scale)


def norm_backward(grad_normed, unit_rows, inverse_scale, norm_gain):
    grad_unit = grad_normed * norm_gain
    grad_inputs = inverse_scale * (
        grad_unit
        - jnp.mean(grad_unit, axis=-1, keepdims=True)
        - unit_rows * jnp.mean(grad_unit * unit_rows, axis=-1, keepdims=True)
    )
    return (grad_inputs, jnp.sum(grad_normed * unit_rows, axis=0), jnp.sum(grad_normed, axis=0))


def forward_pass(tokens, live_mask, gathered):
    (
        attn_gain,
        attn_shift,
        dense_weight,
        dense_bias,
        logit_weight,
        logit_bias,
        value_weight,
        value_bias,
        output_weight,
        output_bias,
        feed_gain,
        feed_shift,
        expand_weight,
        expand_bias,
        reduce_weight,
        reduce_bias,
    ) = gathered
    inputs_float = tokens.astype(jnp.float32)
    normed_float, unit_one, scale_one = norm_forward(
        inputs_float, attn_gain.astype(jnp.float32), attn_shift.astype(jnp.float32)
    )
    normed = normed_float.astype(jnp.bfloat16)
    values = (product(normed, value_weight) + value_bias.astype(jnp.float32)).astype(jnp.bfloat16)
    dense_heads = dense_bias.astype(jnp.float32).reshape(HEADS, 1, HIDDEN_SIZE)
    logit_heads = logit_bias.astype(jnp.float32).reshape(HEADS, 1, L3)
    pre_list, hidden_list, attention_list, mixed_list = ([], [], [], [])
    start_row = 0
    for slot_count, seq_length in bucket_layout():
        stop_row = start_row + slot_count * seq_length
        pre_act = (
            jnp.einsum(
                "rd,hde->hre",
                normed[start_row:stop_row],
                dense_weight,
                preferred_element_type=jnp.float32,
            )
            + dense_heads
        )
        hidden = smooth_gate(pre_act).astype(jnp.bfloat16)
        scores = (
            jnp.einsum(
                "hre,hel->hrl",
                hidden,
                logit_weight[:, :, :seq_length],
                preferred_element_type=jnp.float32,
            )
            + logit_heads[:, :, :seq_length]
        )
        attention = jax.nn.softmax(scores, axis=-1)
        attention_low = attention.astype(jnp.bfloat16).reshape(
            HEADS, slot_count, seq_length, seq_length
        )
        block_values = values[start_row:stop_row].reshape(slot_count, seq_length, HEADS, HEAD_DIM)
        mixed_heads = jnp.einsum(
            "hsql,slhc->sqhc", attention_low, block_values, preferred_element_type=jnp.float32
        )
        mixed_list.append(mixed_heads.reshape(slot_count * seq_length, D))
        pre_list.append(pre_act)
        hidden_list.append(hidden)
        attention_list.append(attention)
        start_row = stop_row
    mixed_all = jnp.concatenate(mixed_list, axis=0).astype(jnp.bfloat16)
    attended = product(mixed_all, output_weight) + output_bias.astype(jnp.float32)
    residual = inputs_float + attended
    normed_two_float, unit_two, scale_two = norm_forward(
        residual, feed_gain.astype(jnp.float32), feed_shift.astype(jnp.float32)
    )
    normed_two = normed_two_float.astype(jnp.bfloat16)
    expand_pre = product(normed_two, expand_weight) + expand_bias.astype(jnp.float32)
    inner_act = smooth_gate(expand_pre).astype(jnp.bfloat16)
    feed_out = product(inner_act, reduce_weight) + reduce_bias.astype(jnp.float32)
    layer_out = live_mask[:, None] * (residual + feed_out)
    stored = (
        normed,
        unit_one,
        scale_one,
        values,
        pre_list,
        hidden_list,
        attention_list,
        mixed_all,
        unit_two,
        scale_two,
        normed_two,
        expand_pre,
        inner_act,
    )
    return (layer_out, stored)


def backward_pass(cotangent, live_mask, gathered, stored):
    (
        attn_gain,
        attn_shift,
        dense_weight,
        dense_bias,
        logit_weight,
        logit_bias,
        value_weight,
        value_bias,
        output_weight,
        output_bias,
        feed_gain,
        feed_shift,
        expand_weight,
        expand_bias,
        reduce_weight,
        reduce_bias,
    ) = gathered
    (
        normed,
        unit_one,
        scale_one,
        values,
        pre_list,
        hidden_list,
        attention_list,
        mixed_all,
        unit_two,
        scale_two,
        normed_two,
        expand_pre,
        inner_act,
    ) = stored
    grad_out = cotangent.astype(jnp.float32) * live_mask[:, None]
    grad_feed = grad_out.astype(jnp.bfloat16)
    reduce_weight_grad = jnp.einsum(
        "rf,rd->fd", inner_act, grad_feed, preferred_element_type=jnp.float32
    )
    reduce_bias_grad = column_sums(grad_feed)
    grad_inner = jnp.einsum(
        "rd,fd->rf", grad_feed, reduce_weight, preferred_element_type=jnp.float32
    )
    grad_expand = (grad_inner * gate_slope(expand_pre)).astype(jnp.bfloat16)
    expand_weight_grad = jnp.einsum(
        "rd,rf->df", normed_two, grad_expand, preferred_element_type=jnp.float32
    )
    expand_bias_grad = column_sums(grad_expand)
    grad_normed_two = jnp.einsum(
        "rf,df->rd", grad_expand, expand_weight, preferred_element_type=jnp.float32
    )
    grad_residual_norm, feed_gain_grad, feed_shift_grad = norm_backward(
        grad_normed_two, unit_two, scale_two, feed_gain.astype(jnp.float32)
    )
    grad_residual = grad_out + grad_residual_norm
    grad_attended = grad_residual.astype(jnp.bfloat16)
    output_weight_grad = jnp.einsum(
        "rd,re->de", mixed_all, grad_attended, preferred_element_type=jnp.float32
    )
    output_bias_grad = column_sums(grad_attended)
    grad_mixed = jnp.einsum(
        "re,de->rd", grad_attended, output_weight, preferred_element_type=jnp.float32
    ).astype(jnp.bfloat16)
    dense_weight_grad = jnp.zeros((HEADS, D, HIDDEN_SIZE), jnp.float32)
    dense_bias_grad = jnp.zeros((HEADS, HIDDEN_SIZE), jnp.float32)
    logit_weight_grad = jnp.zeros((HEADS, HIDDEN_SIZE, L3), jnp.float32)
    logit_bias_grad = jnp.zeros((HEADS, L3), jnp.float32)
    grad_normed_list, value_sum_list = ([], [])
    start_row = 0
    for bucket_index, (slot_count, seq_length) in enumerate(bucket_layout()):
        row_count = slot_count * seq_length
        stop_row = start_row + row_count
        attention = attention_list[bucket_index]
        hidden = hidden_list[bucket_index]
        pre_act = pre_list[bucket_index]
        attention_low = attention.astype(jnp.bfloat16).reshape(
            HEADS, slot_count, seq_length, seq_length
        )
        block_values = values[start_row:stop_row].reshape(slot_count, seq_length, HEADS, HEAD_DIM)
        block_grad = grad_mixed[start_row:stop_row].reshape(slot_count, seq_length, HEADS, HEAD_DIM)
        grad_attention = jnp.einsum(
            "sqhc,slhc->hsql", block_grad, block_values, preferred_element_type=jnp.float32
        ).reshape(HEADS, row_count, seq_length)
        value_sum_list.append(
            jnp.einsum(
                "hsql,sqhc->slhc", attention_low, block_grad, preferred_element_type=jnp.float32
            ).reshape(row_count, D)
        )
        grad_scores = (
            attention
            * (grad_attention - jnp.sum(attention * grad_attention, axis=-1, keepdims=True))
        ).astype(jnp.bfloat16)
        logit_weight_grad = logit_weight_grad.at[:, :, :seq_length].add(
            jnp.einsum("hre,hrl->hel", hidden, grad_scores, preferred_element_type=jnp.float32)
        )
        logit_bias_grad = logit_bias_grad.at[:, :seq_length].add(
            jnp.sum(grad_scores.astype(jnp.float32), axis=1)
        )
        grad_hidden = jnp.einsum(
            "hrl,hel->hre",
            grad_scores,
            logit_weight[:, :, :seq_length],
            preferred_element_type=jnp.float32,
        )
        grad_dense = (grad_hidden * gate_slope(pre_act)).astype(jnp.bfloat16)
        dense_weight_grad = dense_weight_grad + jnp.einsum(
            "rd,hre->hde",
            normed[start_row:stop_row],
            grad_dense,
            preferred_element_type=jnp.float32,
        )
        dense_bias_grad = dense_bias_grad + jnp.sum(grad_dense.astype(jnp.float32), axis=1)
        grad_normed_list.append(
            jnp.einsum("hre,hde->rd", grad_dense, dense_weight, preferred_element_type=jnp.float32)
        )
        start_row = stop_row
    grad_values = jnp.concatenate(value_sum_list, axis=0).astype(jnp.bfloat16)
    value_weight_grad = jnp.einsum(
        "rd,re->de", normed, grad_values, preferred_element_type=jnp.float32
    )
    value_bias_grad = column_sums(grad_values)
    grad_normed = jnp.concatenate(grad_normed_list, axis=0) + jnp.einsum(
        "re,de->rd", grad_values, value_weight, preferred_element_type=jnp.float32
    )
    grad_inputs_norm, attn_gain_grad, attn_shift_grad = norm_backward(
        grad_normed, unit_one, scale_one, attn_gain.astype(jnp.float32)
    )
    tokens_grad = grad_residual + grad_inputs_norm
    return (
        tokens_grad,
        (
            attn_gain_grad,
            attn_shift_grad,
            dense_weight_grad,
            dense_bias_grad.reshape(-1),
            logit_weight_grad,
            logit_bias_grad.reshape(-1),
            value_weight_grad,
            value_bias_grad,
            output_weight_grad,
            output_bias_grad,
            feed_gain_grad,
            feed_shift_grad,
            expand_weight_grad,
            expand_bias_grad,
            reduce_weight_grad,
            reduce_bias_grad,
        ),
    )


def body(
    tokens,
    cotangent,
    bucket_counts,
    attn_gain,
    attn_shift,
    dense_weight,
    dense_bias,
    logit_weight,
    logit_bias,
    value_weight,
    value_bias,
    output_weight,
    output_bias,
    feed_gain,
    feed_shift,
    expand_weight,
    expand_bias,
    reduce_weight,
    reduce_bias,
):
    gathered = (
        lax.all_gather(attn_gain, AXES, axis=0, tiled=True),
        lax.all_gather(attn_shift, AXES, axis=0, tiled=True),
        lax.all_gather(dense_weight, AXES, axis=1, tiled=True),
        lax.all_gather(dense_bias, AXES, axis=0, tiled=True),
        lax.all_gather(logit_weight, AXES, axis=1, tiled=True),
        lax.all_gather(logit_bias, AXES, axis=0, tiled=True),
        lax.all_gather(value_weight, AXES, axis=0, tiled=True),
        lax.all_gather(value_bias, AXES, axis=0, tiled=True),
        lax.all_gather(output_weight, AXES, axis=0, tiled=True),
        lax.all_gather(output_bias, AXES, axis=0, tiled=True),
        lax.all_gather(feed_gain, AXES, axis=0, tiled=True),
        lax.all_gather(feed_shift, AXES, axis=0, tiled=True),
        lax.all_gather(expand_weight, AXES, axis=0, tiled=True),
        lax.all_gather(expand_bias, AXES, axis=0, tiled=True),
        lax.all_gather(reduce_weight, AXES, axis=0, tiled=True),
        lax.all_gather(reduce_bias, AXES, axis=0, tiled=True),
    )
    live_mask = live_rows(bucket_counts[0])
    layer_out, stored = forward_pass(tokens, live_mask, gathered)
    gathered = (
        lax.all_gather(attn_gain, AXES, axis=0, tiled=True),
        lax.all_gather(attn_shift, AXES, axis=0, tiled=True),
        lax.all_gather(dense_weight, AXES, axis=1, tiled=True),
        lax.all_gather(dense_bias, AXES, axis=0, tiled=True),
        lax.all_gather(logit_weight, AXES, axis=1, tiled=True),
        lax.all_gather(logit_bias, AXES, axis=0, tiled=True),
        lax.all_gather(value_weight, AXES, axis=0, tiled=True),
        lax.all_gather(value_bias, AXES, axis=0, tiled=True),
        lax.all_gather(output_weight, AXES, axis=0, tiled=True),
        lax.all_gather(output_bias, AXES, axis=0, tiled=True),
        lax.all_gather(feed_gain, AXES, axis=0, tiled=True),
        lax.all_gather(feed_shift, AXES, axis=0, tiled=True),
        lax.all_gather(expand_weight, AXES, axis=0, tiled=True),
        lax.all_gather(expand_bias, AXES, axis=0, tiled=True),
        lax.all_gather(reduce_weight, AXES, axis=0, tiled=True),
        lax.all_gather(reduce_bias, AXES, axis=0, tiled=True),
    )
    tokens_grad, grads = backward_pass(cotangent, live_mask, gathered, stored)
    shards = (
        lax.psum_scatter(grads[0], AXES, scatter_dimension=0, tiled=True),
        lax.psum_scatter(grads[1], AXES, scatter_dimension=0, tiled=True),
        lax.psum_scatter(grads[2], AXES, scatter_dimension=1, tiled=True),
        lax.psum_scatter(grads[3], AXES, scatter_dimension=0, tiled=True),
        lax.psum_scatter(grads[4], AXES, scatter_dimension=1, tiled=True),
        lax.psum_scatter(grads[5], AXES, scatter_dimension=0, tiled=True),
        lax.psum_scatter(grads[6], AXES, scatter_dimension=0, tiled=True),
        lax.psum_scatter(grads[7], AXES, scatter_dimension=0, tiled=True),
        lax.psum_scatter(grads[8], AXES, scatter_dimension=0, tiled=True),
        lax.psum_scatter(grads[9], AXES, scatter_dimension=0, tiled=True),
        lax.psum_scatter(grads[10], AXES, scatter_dimension=0, tiled=True),
        lax.psum_scatter(grads[11], AXES, scatter_dimension=0, tiled=True),
        lax.psum_scatter(grads[12], AXES, scatter_dimension=0, tiled=True),
        lax.psum_scatter(grads[13], AXES, scatter_dimension=0, tiled=True),
        lax.psum_scatter(grads[14], AXES, scatter_dimension=0, tiled=True),
        lax.psum_scatter(grads[15], AXES, scatter_dimension=0, tiled=True),
    )
    return (layer_out, tokens_grad) + tuple(shards)


def solution(mesh):
    in_specs = (
        P(AXES, None),
        P(AXES, None),
        P(AXES, None),
        P(AXES),
        P(AXES),
        P(None, AXES, None),
        P(AXES),
        P(None, AXES, None),
        P(AXES),
        P(AXES, None),
        P(AXES),
        P(AXES, None),
        P(AXES),
        P(AXES),
        P(AXES),
        P(AXES, None),
        P(AXES),
        P(AXES, None),
        P(AXES),
    )
    out_specs = (
        P(AXES, None),
        P(AXES, None),
        P(AXES),
        P(AXES),
        P(None, AXES, None),
        P(AXES),
        P(None, AXES, None),
        P(AXES),
        P(AXES, None),
        P(AXES),
        P(AXES, None),
        P(AXES),
        P(AXES),
        P(AXES),
        P(AXES, None),
        P(AXES),
        P(AXES, None),
        P(AXES),
    )
    shape = tuple(mesh.shape[a] for a in AXES)
    chosen = chip_body if shape == (8, 4) else body
    return jax.shard_map(chosen, mesh=mesh, in_specs=in_specs, out_specs=out_specs, check_vma=False)
```

```python
import functools

import jax
import jax.numpy as jnp
import numpy as np
from jax import lax
from jax.experimental import pallas as pl
from jax.experimental.pallas import tpu as pltpu
from jax.sharding import PartitionSpec as P

D = 768
HEADS = 12
HEAD_DIM = 64
HIDDEN_SIZE = 768
L3 = 512
AXES = ("wide", "narrow")
L1 = 128
L2 = 256
S1 = 2
S2 = 1
S3 = 1

norm_eps = 1e-05
gelu_root = 0.7978845608028654
gelu_cube = 0.044715

MESH = pl.DeviceIdType.MESH
HBM = pl.BlockSpec(memory_space=pltpu.HBM)
VMEM = pl.BlockSpec(memory_space=pltpu.VMEM)
VMEM_LIMIT = 63 * 1024 * 1024
f32 = jnp.float32
bf16 = jnp.bfloat16

ROWS_DEV = 1024
CHIP_ROWS = 2048
HALF = 384
NN = (((1,), (0,)), ((), ()))
NT = (((1,), (1,)), ((), ()))
TN = (((0,), (0,)), ((), ()))


def dot(a, b, dims=NN):
    return lax.dot_general(a, b, dims, preferred_element_type=f32)


def gelu_both(v):
    sq = v * v
    t = jnp.tanh(v * (gelu_root + gelu_root * gelu_cube * sq))
    up = 0.5 + 0.5 * t
    slope = up + 0.5 * v * (1.0 - t * t) * (gelu_root + 3.0 * gelu_root * gelu_cube * sq)
    return v * up, slope


def norm_rows(x):
    mean = jnp.mean(x, axis=-1, keepdims=True)
    cen = x - mean
    inv = lax.rsqrt(jnp.mean(cen * cen, axis=-1, keepdims=True) + norm_eps)
    return cen * inv, inv


class Place:
    def __init__(self):
        w = lax.axis_index(AXES[0])
        n = lax.axis_index(AXES[1])
        self.w, self.n = w, n
        self.z, self.c = w // 2, w % 2
        self.nx = n + 1 - 2 * (n % 2)
        self.ny = (n + 2) % 4
        self.nd = 3 - n
        self.xdev = (w, self.nx)
        self.ydev = (w, self.ny)
        self.sib = (self.z * 2 + 1 - self.c, n)

    def zpos(self, i):
        return (self.z + i) % 4

    def zdev(self, zz):
        return (zz * 2 + self.c, self.n)

    def near(self):
        return [self.xdev, self.ydev, self.sib] + [self.zdev(self.zpos(i)) for i in (1, 2, 3)]


def greet(devs):
    bar = pltpu.get_barrier_semaphore()
    for dev in devs:
        pl.semaphore_signal(bar, inc=1, device_id=dev, device_id_type=MESH)
    pl.semaphore_wait(bar, len(devs))


def remote(src, dst, ssem, rsem, dev):
    return pltpu.make_async_remote_copy(
        src_ref=src, dst_ref=dst, send_sem=ssem, recv_sem=rsem, device_id=dev, device_id_type=MESH
    )


def k0_kernel(s_in, tok_in, dense, logit, vo, ff, s_all, tok, md, ml, mvo, mf, ss, sr, es, er):
    pc = Place()
    c = pc.c
    me = pc.w * 4 + pc.n
    bar = pltpu.get_barrier_semaphore()

    @pl.loop(1, 32)
    def _(j):
        t = (me + j) % 32
        pl.semaphore_signal(bar, inc=1, device_id=(t // 4, t % 4), device_id_type=MESH)

    pl.semaphore_wait(bar, 31)
    o = 1 - c

    @pl.loop(1, 32)
    def _(j):
        t = (me + j) % 32
        remote(s_in, s_all.at[me], ss.at[t], sr.at[me], (t // 4, t % 4)).start()

    pairs = [
        (dense.at[pl.ds(3 * o, 3)], md.at[:, c]),
        (logit.at[pl.ds(3 * o, 3)], ml.at[:, c]),
        (vo.at[o], mvo.at[c]),
        (ff.at[o], mf.at[:, c]),
        (tok_in, tok),
    ]
    rems = [remote(give, slot, es.at[i], er.at[i], pc.sib) for i, (give, slot) in enumerate(pairs)]
    for cp in rems:
        cp.start()
    s_all[me] = s_in[...]
    md[:, c] = dense[pl.ds(3 * c, 3)]
    ml[:, c] = logit[pl.ds(3 * c, 3)]
    mvo[c] = vo[c]
    mf[:, c] = ff[c]
    for cp in rems:
        cp.wait()

    @pl.loop(1, 32)
    def _(j):
        t = (me + j) % 32
        f = (me + 32 - j) % 32
        cp = remote(s_in, s_all.at[f], ss.at[t], sr.at[f], (t // 4, t % 4))
        cp.wait_send()
        cp.wait_recv()


def k0_call(s_in, tok, dense, logit, vo, ff):
    sds = jax.ShapeDtypeStruct
    return pl.pallas_call(
        k0_kernel,
        out_shape=(
            sds((32, 16, 128), bf16),
            sds((ROWS_DEV, D), bf16),
            sds((3, 2, 48, D), bf16),
            sds((3, 2, 48, L3), bf16),
            sds((2, 48, HALF), bf16),
            sds((2, 2, 48, D), bf16),
        ),
        in_specs=[VMEM, HBM, VMEM, VMEM, VMEM, VMEM],
        out_specs=(VMEM, HBM, VMEM, VMEM, VMEM, VMEM),
        scratch_shapes=[
            pltpu.SemaphoreType.DMA((32,)),
            pltpu.SemaphoreType.DMA((32,)),
            pltpu.SemaphoreType.DMA((5,)),
            pltpu.SemaphoreType.DMA((5,)),
        ],
        compiler_params=pltpu.CompilerParams(collective_id=0, has_side_effects=True),
        name="k0_exchange",
    )(s_in, tok, dense, logit, vo, ff)


class Gather:
    def __init__(self, pc, sems):
        self.pc = pc
        self.zs, self.zr, self.xs, self.xr, self.ys, self.yr, self.ds, self.dr, self.ls = sems

    def zcopy(self, k, src, buf, i, sender=None):
        pc = self.pc
        zz = pc.z if sender is None else sender
        return remote(src, buf.at[zz, :, pc.n], self.zs.at[k, i], self.zr.at[k, zz], pc.zdev(pc.zpos(i)))

    def zsend(self, k, src, buf):
        for i in (1, 2, 3):
            self.zcopy(k, src, buf, i).start()
        self.own(k, src, buf).start()

    def own(self, k, src, buf):
        return pltpu.make_async_copy(src, buf.at[self.pc.z, :, self.pc.n], self.ls.at[k])

    def xcopy(self, k, buf, zz, src=None, col=None):
        pc = self.pc
        col = pc.n if col is None else col
        slot = buf.at[zz, :, col]
        return remote(slot if src is None else src, slot, self.xs.at[k, zz], self.xr.at[k, zz], pc.xdev)

    def ycopy(self, k, buf, zz, src=None, col=None):
        pc = self.pc
        col = pc.n if col is None else col
        slot = buf.at[zz, :, col]
        return remote(slot if src is None else src, slot, self.ys.at[k, zz], self.yr.at[k, zz], pc.ydev)

    def col(self, k, src, buf, i):
        pc = self.pc
        zz = pc.zpos(i)
        if i:
            self.zcopy(k, src, buf, i, sender=zz).wait_recv()
        s = None if i else src
        self.xcopy(k, buf, zz, s).start()
        self.ycopy(k, buf, zz, s).start()

    def dcopy(self, k, buf, zz):
        pc = self.pc
        if zz < 2:
            slot, dev = buf.at[zz, :, pc.nx], pc.ydev
        else:
            slot, dev = buf.at[zz, :, pc.ny], pc.xdev
        return remote(slot, slot, self.ds.at[k, zz], self.dr.at[k, zz], dev)

    def diag(self, k, buf, zz):
        pc = self.pc
        self.xcopy(k, buf, zz, col=pc.nx).wait_recv()
        self.ycopy(k, buf, zz, col=pc.ny).wait_recv()
        self.dcopy(k, buf, zz).start()

    def fin(self, k, src, buf, each=None):
        self.own(k, src, buf).wait()
        for zz in range(4):
            remote(
                buf.at[zz, :, self.pc.nd],
                buf.at[zz, :, self.pc.nd],
                self.ds.at[k, zz],
                self.dr.at[k, zz],
                self.pc.xdev,
            ).wait_recv()
            if each is not None:
                each(zz)

    def sent(self, k, src, buf):
        for i in (1, 2, 3):
            self.zcopy(k, src, buf, i).wait_send()
        for zz in range(4):
            self.xcopy(k, buf, zz).wait_send()
            self.ycopy(k, buf, zz).wait_send()
            self.dcopy(k, buf, zz).wait_send()


class LayerFirst:
    def __init__(self, pc, src, buf, cs, cr, us, ur, vs, vr, ls, ps, pr):
        self.pc, self.src, self.buf = pc, src, buf
        self.cs, self.cr, self.us, self.ur, self.vs, self.vr, self.ls = cs, cr, us, ur, vs, vr, ls
        self.ps, self.pr = ps, pr

    def side(self, i, src, slot):
        dev = self.pc.xdev if i in (0, 3) else self.pc.ydev
        return remote(src, slot, self.cs.at[i], self.cr.at[i], dev)

    def local(self):
        return pltpu.make_async_copy(self.src, self.buf.at[self.pc.z, :, self.pc.n], self.ls)

    def first(self):
        pc = self.pc
        self.local().start()
        for i in (0, 1):
            self.side(i, self.src, self.buf.at[pc.z, :, pc.n]).start()

    def halves(self):
        pc = self.pc
        a, b = self.buf.at[pc.z, 0, pc.nx], self.buf.at[pc.z, 1, pc.ny]
        return self.side(2, a, a), self.side(3, b, b)

    def second(self):
        for i in (0, 1):
            self.side(i, self.src, self.buf.at[self.pc.z, :, self.pc.n]).wait_recv()
        for cp in self.halves():
            cp.start()

    def up(self, r):
        return remote(self.buf.at[r], self.buf.at[r], self.us.at[r], self.ur.at[r], self.pc.zdev((self.pc.z + 1) % 4))

    def down(self, r):
        return remote(self.buf.at[r], self.buf.at[r], self.vs.at[r], self.vr.at[r], self.pc.zdev((self.pc.z + 3) % 4))

    def swap(self, r):
        return remote(self.buf.at[r], self.buf.at[r], self.ps.at[r], self.pr.at[r], self.pc.sib)

    def third(self):
        z = self.pc.z
        for cp in self.halves():
            cp.wait_recv()
        self.local().wait()

        @pl.when(z < 3)
        def _():
            self.up(z).start()

        @pl.when(z > 0)
        def _():
            self.down(z).start()

        self.swap(z).start()

    def level(self, k):
        z = self.pc.z

        @pl.when(z >= k)
        def _():
            self.up(z - k).wait_recv()

            @pl.when(z < 3)
            def _():
                self.up(z - k).start()

            self.swap(z - k).start()

        @pl.when(z + k <= 3)
        def _():
            self.down(z + k).wait_recv()

            @pl.when(z > 0)
            def _():
                self.down(z + k).start()

            self.swap(z + k).start()

    def finish(self):
        z = self.pc.z
        for i in (0, 1):
            self.side(i, self.src, self.buf.at[self.pc.z, :, self.pc.n]).wait_send()
        for cp in self.halves():
            cp.wait_send()
        for r in range(4):

            @pl.when((z < 3) & (z >= r))
            def _():
                self.up(r).wait_send()

            @pl.when((z > 0) & (z <= r))
            def _():
                self.down(r).wait_send()

            self.swap(r).wait()


def gather_sems(k):
    dma = pltpu.SemaphoreType.DMA
    return [dma((k, 4))] * 8 + [dma((k,))]


def join_pair(stage, dst_of, rows_of):
    @pl.loop(0, 4)
    def _(zz):
        for cc in range(2):
            for nn in (0, 2):
                one = stage[zz, cc, nn].astype(f32)
                two = stage[zz, cc, nn + 1].astype(f32)
                row = pl.multiple_of(zz * 192 + cc * 96 + nn * 24, 16)
                for e in rows_of:
                    both = jnp.concatenate(
                        [one[24 * e : 24 * e + 24], two[24 * e : 24 * e + 24]], axis=0
                    )
                    dst_of(e, pl.ds(row, 48), both.astype(bf16))


def k1_kernel(
    tok, tok2, vec, db, lb, vb, mvo, md, ml, mf,
    ovo, gd, gl, ef, nrm_o, val_o, hid_o, slo_o, atl_o, atm_o, ats_o, wa_o, la_o, mix_o, vv_o,
    tokv, nrm, val, vst, vv, wst, lst, wv, lv, hidv, slov, atlv, atmv, atsv, mixv,
    zs, zr, xs, xr, ys, yr, ds, dr, ls, tsem, osem, wsem, lsem, ssem, rsem, msem,
    cs, cr, us, ur, vs, vr, cls, ps, pr,
):
    pc = Place()
    c = pc.c
    g = Gather(pc, (zs, zr, xs, xr, ys, yr, ds, dr, ls))
    tcopies = []
    for i, (ref, d) in enumerate(((tok, c), (tok2, 1 - c))):
        for j, (at, to) in enumerate(((512, d * 512), (0, 1024 + d * 512))):
            rows = pl.ds(pl.multiple_of(to, 512), 512)
            tcopies.append(pltpu.make_async_copy(ref.at[pl.ds(at, 512)], tokv.at[rows], tsem.at[2 * i + j]))
    for cp in tcopies:
        cp.start()
    greet(pc.near())

    vo_args = (0, mvo, ovo.at[c])
    dd = lambda p: (1 + 2 * p, md.at[p], gd.at[p])
    ll = lambda p: (2 + 2 * p, ml.at[p], gl.at[p])
    fb = (7, mf.at[1], ef.at[c, 1])
    fa = LayerFirst(pc, mf.at[0], ef.at[c, 0], cs, cr, us, ur, vs, vr, cls, ps, pr)

    g.zsend(*vo_args)
    g.zsend(*dd(0))
    g.col(*vo_args, 0)
    g.col(*dd(0), 0)
    fa.first()
    g.col(*ll(0), 0)

    for cp in tcopies:
        cp.wait()

    @pl.loop(0, 8)
    def _(b):
        rows = pl.ds(pl.multiple_of(b * 256, 256), 256)
        unit, _ = norm_rows(tokv[rows].astype(f32))
        nrm[rows] = (unit * vec[0:1] + vec[1:2]).astype(bf16)

    nrm_copy = pltpu.make_async_copy(nrm, nrm_o, tsem.at[4])
    nrm_copy.start()
    for i in (1, 2, 3):
        g.col(*vo_args, i)
    g.zsend(*ll(0))
    fa.second()
    g.col(*dd(1), 0)
    for i in (1, 2, 3):
        g.col(*dd(0), i)
    g.zsend(*dd(1))
    fa.third()
    for zz in range(4):
        g.diag(vo_args[0], vo_args[2], zz)
    g.col(*ll(1), 0)
    for i in (1, 2, 3):
        g.col(*ll(0), i)
    g.zsend(*ll(1))
    for zz in (0, 2, 1, 3):
        g.diag(dd(0)[0], dd(0)[2], zz)
    g.fin(*vo_args)
    vo_load = pltpu.make_async_copy(ovo.at[c], vst, tsem.at[5])
    vo_load.start()
    vo_swap = remote(ovo.at[c], ovo.at[c], ssem.at[0], rsem.at[0], pc.sib)
    vo_swap.start()
    vo_load.wait()

    def put_v(e, rows, x):
        vv[rows] = x

    join_pair(vst, put_v, (0,))

    @pl.loop(0, 4)
    def _(b):
        rows = pl.ds(pl.multiple_of(b * 512, 512), 512)
        val[rows] = (dot(nrm[rows], vv[...]) + vb[...]).astype(bf16)

    val_copy = pltpu.make_async_copy(val, val_o, tsem.at[6])
    val_copy.start()
    vv_copy = pltpu.make_async_copy(vv, vv_o, tsem.at[5])
    vv_copy.start()
    g.col(*dd(1), 1)
    for zz in (0, 2, 1, 3):
        g.diag(ll(0)[0], ll(0)[2], zz)
    g.fin(*dd(0))
    g.fin(*ll(0))

    lane = lax.broadcasted_iota(jnp.int32, (1, 128), 1)
    keeps = [(lane < HEAD_DIM).astype(bf16), (lane >= HEAD_DIM).astype(bf16)]

    def softmax(s):
        m = jnp.max(s, axis=-1, keepdims=True)
        ex = jnp.exp(s - m)
        return (ex / jnp.sum(ex, axis=-1, keepdims=True)).astype(bf16)

    @pl.loop(0, 3)
    def _(p):
        q = p + 1
        more = p < 2
        ka, kb = 1 + 2 * q, 2 + 2 * q

        def on_a(fn):
            @pl.when(more)
            def _():
                fn(ka, md.at[q % 3], gd.at[q % 3])

            @pl.when(jnp.logical_not(more))
            def _():
                fn(*fb)

        def on_b(fn):
            @pl.when(more)
            def _():
                fn(kb, ml.at[q % 3], gl.at[q % 3])

        def on_next(fn):
            @pl.when(p == 0)
            def _():
                fn(5, md.at[2], gd.at[2])

            @pl.when(p == 1)
            def _():
                fn(*fb)

        def on_next_b(fn):
            @pl.when(p == 0)
            def _():
                fn(6, ml.at[2], gl.at[2])

        def tick(pos):
            if pos == 0:
                on_next(lambda k, s, b: g.col(k, s, b, 0))
                on_a(lambda k, s, b: g.col(k, s, b, 2))
                on_a(lambda k, s, b: g.col(k, s, b, 3))
                on_next(g.zsend)
            elif pos == 1:
                on_b(lambda k, s, b: g.col(k, s, b, 1))
                on_b(lambda k, s, b: g.col(k, s, b, 2))
            elif pos == 2:
                on_b(lambda k, s, b: g.col(k, s, b, 3))
                on_next_b(lambda k, s, b: g.col(k, s, b, 0))
            elif pos == 3:
                on_a(lambda k, s, b: g.diag(k, b, 0))
                on_a(lambda k, s, b: g.diag(k, b, 2))
                for r in range(3):

                    @pl.when(p == r)
                    def _():
                        fa.level(r + 1)
            elif pos == 4:
                on_a(lambda k, s, b: g.diag(k, b, 1))
                on_a(lambda k, s, b: g.diag(k, b, 3))
                on_next_b(g.zsend)
            elif pos == 5:
                on_next(lambda k, s, b: g.col(k, s, b, 1))
                on_b(lambda k, s, b: g.diag(k, b, 0))
            elif pos == 6:
                on_b(lambda k, s, b: g.diag(k, b, 2))
            elif pos == 7:
                on_b(lambda k, s, b: g.diag(k, b, 1))
                on_b(lambda k, s, b: g.diag(k, b, 3))

        wload = pltpu.make_async_copy(gd.at[p], wst, tsem.at[7])
        lload = pltpu.make_async_copy(gl.at[p], lst, tsem.at[8])
        wload.start()
        lload.start()
        wcopy = lambda r: pltpu.make_async_copy(wv, wa_o.at[pl.ds(2 * r, 2)], wsem)
        lcopy = lambda r: pltpu.make_async_copy(lv, la_o.at[pl.ds(2 * r, 2)], lsem)

        @pl.when(p > 0)
        def _():
            wcopy(p - 1).wait()
            lcopy(p - 1).wait()

        wload.wait()

        def put_w(e, rows, x):
            wv[e, rows] = x

        def put_l(e, rows, x):
            lv[e, rows] = x

        join_pair(wst, put_w, (0, 1))
        lload.wait()
        join_pair(lst, put_l, (0, 1))
        wcopy(p).start()
        lcopy(p).start()
        lanes = pl.ds(pl.multiple_of(p * 128, 128), 128)

        def out_copies(e, d, long, h):
            row = d * 512 if long else 1024 + d * 512
            rows = pl.ds(row, 512)
            cps = [
                pltpu.make_async_copy(hidv.at[e], hid_o.at[h, rows], osem.at[e, 0]),
                pltpu.make_async_copy(slov.at[e], slo_o.at[h, rows], osem.at[e, 1]),
            ]
            if long:
                cps.append(pltpu.make_async_copy(atlv.at[e], atl_o.at[h, pl.ds(d * 512, 512)], osem.at[e, 2]))
            else:
                part = pl.ds(d * 256, 256)
                cps.append(pltpu.make_async_copy(atmv.at[e], atm_o.at[h, part], osem.at[e, 3]))
                cps.append(pltpu.make_async_copy(atsv.at[e], ats_o.at[h, part], osem.at[e, 4]))
            return cps

        pos = 0
        for d in range(2):
            for long in (True, False):
                row = d * 512 if long else 1024 + d * 512
                rows = slice(row, row + 512)
                mixed = None
                for e in range(2):
                    h = 2 * p + e
                    pre = dot(nrm[rows], wv[e]) + db[pl.ds(h, 1)]
                    hid, slo = gelu_both(pre)
                    if d == 0 and long:

                        @pl.when(p > 0)
                        def _():
                            for cp in out_copies(e, 1, False, h):
                                cp.wait()
                    else:
                        for cp in out_copies(e, d if not long else d - 1, not long, h):
                            cp.wait()
                    hidv[e] = hid.astype(bf16)
                    slov[e] = slo.astype(bf16)
                    lbias = lb[pl.ds(h, 1)]
                    vpair = val[rows, lanes] * keeps[e]
                    if long:
                        att = softmax(dot(hidv[e], lv[e]) + lbias)
                        atlv[e] = att
                        m = dot(att, vpair)
                    else:
                        short = softmax(dot(hidv[e, 0:256], lv[e, :, 0:128]) + lbias[:, 0:128])
                        mid = softmax(dot(hidv[e, 256:512], lv[e, :, 0:256]) + lbias[:, 0:256])
                        atsv[e] = short
                        atmv[e] = mid
                        m = jnp.concatenate(
                            [
                                dot(short[0:128], vpair[0:128]),
                                dot(short[128:256], vpair[128:256]),
                                dot(mid, vpair[256:512]),
                            ],
                            axis=0,
                        )
                    mixed = m if mixed is None else mixed + m
                    for cp in out_copies(e, d, long, h):
                        cp.start()
                    tick(pos)
                    pos += 1
                mixv[rows, lanes] = mixed.astype(bf16)

        @pl.when(more)
        def _():
            g.fin(ka, md.at[q % 3], gd.at[q % 3])

        on_b(g.fin)

        @pl.when(p == 2)
        def _():
            for e in range(2):
                for cp in out_copies(e, 1, False, 2 * p + e):
                    cp.wait()
            wcopy(p).wait()
            lcopy(p).wait()

    fb_swap = lambda r: remote(ef.at[c, 1, r], ef.at[c, 1, r], ssem.at[4 + r], rsem.at[4 + r], pc.sib)
    swaps = [vo_swap]
    o = 1 - c
    for i, (start, to) in enumerate(((0, 512), (1024, 0))):
        mine = pltpu.make_async_copy(
            mixv.at[pl.ds(start + c * 512, 512)], mix_o.at[c, pl.ds(to, 512)], msem.at[i]
        )
        mine.start()
        other = remote(
            mixv.at[pl.ds(start + o * 512, 512)], mix_o.at[c, pl.ds(to, 512)], ssem.at[2 + i], rsem.at[2 + i], pc.sib
        )
        other.start()
        swaps += [mine, other]
    g.fin(*fb, each=lambda r: fb_swap(r).start())
    for cp in swaps + [nrm_copy, val_copy, vv_copy] + [fb_swap(r) for r in range(4)]:
        cp.wait()
    fa.finish()
    g.sent(*vo_args)
    for p in range(3):
        g.sent(*dd(p))
        g.sent(*ll(p))
    g.sent(*fb)


def k1_call(tok, tok2, vec, db, lb, vb, mvo, md, ml, mf):
    sds = jax.ShapeDtypeStruct
    dma = pltpu.SemaphoreType.DMA
    return pl.pallas_call(
        k1_kernel,
        out_shape=(
            sds((2, 4, 2, 4, 48, HALF), bf16),
            sds((3, 4, 2, 4, 48, D), bf16),
            sds((3, 4, 2, 4, 48, L3), bf16),
            sds((2, 2, 4, 2, 4, 48, D), bf16),
            sds((CHIP_ROWS, D), bf16),
            sds((CHIP_ROWS, HALF), bf16),
            sds((6, CHIP_ROWS, HIDDEN_SIZE), bf16),
            sds((6, CHIP_ROWS, HIDDEN_SIZE), bf16),
            sds((6, 1024, L3), bf16),
            sds((6, 512, L2), bf16),
            sds((6, 512, L1), bf16),
            sds((6, D, HIDDEN_SIZE), bf16),
            sds((6, HIDDEN_SIZE, L3), bf16),
            sds((2, ROWS_DEV, HALF), bf16),
            sds((D, HALF), bf16),
        ),
        in_specs=[HBM] * 2 + [VMEM] * 8,
        out_specs=(HBM,) * 15,
        scratch_shapes=[
            pltpu.VMEM((CHIP_ROWS, D), bf16),
            pltpu.VMEM((CHIP_ROWS, D), bf16),
            pltpu.VMEM((CHIP_ROWS, HALF), bf16),
            pltpu.VMEM((4, 2, 4, 48, HALF), bf16),
            pltpu.VMEM((D, HALF), bf16),
            pltpu.VMEM((4, 2, 4, 48, D), bf16),
            pltpu.VMEM((4, 2, 4, 48, L3), bf16),
            pltpu.VMEM((2, D, HIDDEN_SIZE), bf16),
            pltpu.VMEM((2, HIDDEN_SIZE, L3), bf16),
            pltpu.VMEM((2, 512, HIDDEN_SIZE), bf16),
            pltpu.VMEM((2, 512, HIDDEN_SIZE), bf16),
            pltpu.VMEM((2, 512, L3), bf16),
            pltpu.VMEM((2, 256, L2), bf16),
            pltpu.VMEM((2, 256, L1), bf16),
            pltpu.VMEM((CHIP_ROWS, HALF), bf16),
        ]
        + gather_sems(8)
        + [dma((9,)), dma((2, 5)), dma, dma, dma((8,)), dma((8,)), dma((2,))]
        + [dma((4,))] * 6
        + [dma, dma((4,)), dma((4,))],
        compiler_params=pltpu.CompilerParams(
            collective_id=1, has_side_effects=True, vmem_limit_bytes=VMEM_LIMIT
        ),
        name="k1_attention",
    )(tok, tok2, vec, db, lb, vb, mvo, md, ml, mf)


def prepare(tokens, attn_gain, attn_shift, dense_weight, dense_bias, logit_weight, logit_bias, value_weight,
            value_bias, output_weight, output_bias, feed_gain, feed_shift, expand_weight, expand_bias,
            reduce_weight, reduce_bias):
    core = lax.axis_index(AXES[0]) % 2
    narrow_rows = jnp.stack([attn_gain, attn_shift, value_bias, output_bias, feed_gain, feed_shift, reduce_bias])
    wide_rows = [expand_bias.reshape(1, 96), logit_bias.reshape(2, 96), dense_bias.reshape(3, 96)]
    small = jnp.concatenate(
        [jnp.pad(narrow_rows, ((0, 0), (0, 104)))] + [jnp.pad(v, ((0, 0), (0, 32))) for v in wide_rows]
    )
    small = jnp.pad(small, ((0, 3), (0, 0)))
    dense = dense_weight.reshape(6, 48, D)
    logit = logit_weight.reshape(6, 48, L3)
    vo = jnp.stack([value_weight.reshape(24, 2, HALF), output_weight.reshape(24, 2, HALF)]).transpose(2, 0, 1, 3)
    vo = vo.reshape(2, 48, HALF)
    ff = jnp.stack(
        [expand_weight.reshape(24, 4, D).transpose(1, 0, 2).reshape(2, 48, D), reduce_weight.reshape(2, 48, D)]
    )
    s_all, tok2, md, ml, mvo, mf = k0_call(small, tokens, dense, logit, vo, ff)
    every = s_all.astype(f32)
    vec = every[:, 0:7, :24].transpose(1, 0, 2).reshape(7, D)
    eb = every[:, 7, :96].reshape(4, D)
    lb = lax.dynamic_slice(every[:, 8:10, :96].reshape(HEADS, L3), (6 * core, 0), (6, L3))
    db = lax.dynamic_slice(every[:, 10:13, :96].reshape(HEADS, HIDDEN_SIZE), (6 * core, 0), (6, HIDDEN_SIZE))
    vb = lax.dynamic_slice(vec[2:3], (0, HALF * core), (1, HALF))
    return tok2, vec, eb, lb, db, vb, md, ml, mvo, mf


def k2_kernel(
    x, cot, counts, mix, ovo, ef, vec, eb,
    lay_o, gres_o, gmix_o, def_o, do_o, sums_o,
    ev, rv, ow, inner, ge, n2, gf, ga, acc, dst, rsem, dsem, osem,
):
    oloads = []
    for half in range(2):
        lanes = pl.ds(half * HALF, HALF)
        oloads.append(pltpu.make_async_copy(ovo.at[half], dst.at[0, :, :, :, :, lanes], osem.at[half]))
    loads = [pltpu.make_async_copy(ef.at[0, f], dst.at[1 - f], dsem.at[1 - f]) for f in range(2)]
    for cp in oloads:
        cp.start()
    loads[0].start()
    rloads = []
    for f in range(2):
        for j in range(4):
            rloads.append(
                pltpu.make_async_copy(ef.at[1, f, j], rv.at[j, :, :, pl.ds(48 * f, 48)], rsem.at[f, j])
            )
    for cp in rloads:
        cp.start()

    def put_o(e, rows, v):
        ow[rows] = v

    for cp in oloads:
        cp.wait()
    join_pair(dst.at[0], put_o, (1,))
    loads[1].start()
    for f in range(2):

        def put_e(e, rows, v):
            ev[2 * f + e, rows] = v

        loads[f].wait()
        join_pair(dst.at[1 - f], put_e, (0, 1))
    for cp in rloads:
        cp.wait()
    fg, fs = vec[4:5], vec[5:6]
    sums_o[...] = jnp.zeros_like(sums_o)

    @pl.loop(0, 4)
    def _(b):
        rows = pl.ds(pl.multiple_of(b * 256, 256), 256)
        mixed = jnp.concatenate([mix[0, rows], mix[1, rows]], axis=1)
        res = x[rows].astype(f32) + (dot(mixed, ow[...]) + vec[3:4])
        unit, inv = norm_rows(res)
        n2v = (unit * fg + fs).astype(bf16)
        n2[rows] = n2v
        later = jnp.where(b == 1, counts[0, 1], counts[0, 2])
        low = jnp.where(b == 0, counts[0, 0], later) >= 1
        high = jnp.where(b == 0, counts[0, 0] - 1, later) >= 1
        top = lax.broadcasted_iota(jnp.int32, (256, 1), 0) < L1
        alive = jnp.where(top, jnp.where(low, 1.0, 0.0), jnp.where(high, 1.0, 0.0))
        gout = cot[rows].astype(f32) * alive
        gfb = gout.astype(bf16)
        gf[rows] = gfb
        feed = None
        gn2 = None
        for j in range(4):
            cols = slice(j * D, j * D + D)
            rj = rv[j].reshape(D, D)
            hid, slo = gelu_both(dot(n2v, ev[j]) + eb[j : j + 1])
            hb = hid.astype(bf16)
            inner[rows, cols] = hb
            f_j = dot(hb, rj)
            feed = f_j if feed is None else feed + f_j
            geb = (dot(gfb, rj, NT) * slo).astype(bf16)
            ge[rows, cols] = geb
            g_j = dot(geb, ev[j], NT)
            gn2 = g_j if gn2 is None else gn2 + g_j
        lay_o[rows] = alive * (res + (feed + vec[6:7]))
        q = gn2 * fg
        gres = gout + inv * (
            q - jnp.mean(q, axis=-1, keepdims=True) - unit * jnp.mean(q * unit, axis=-1, keepdims=True)
        )
        gres_o[rows] = gres
        gab = gres.astype(bf16)
        ga[rows] = gab
        gm = dot(gab, ow[...], NT).astype(bf16)
        gmix_o[0, rows] = gm[:, :HALF]
        gmix_o[1, rows] = gm[:, HALF:]
        sums_o[0:1] += jnp.sum(gn2 * unit, axis=0, keepdims=True)
        sums_o[1:2] += jnp.sum(gn2, axis=0, keepdims=True)

    ones = jnp.ones((8, ROWS_DEV), bf16)
    sums_o[2:3] = dot(ones, gf[...])[0:1]
    sums_o[3:4] = dot(ones, ga[...])[0:1]

    def out_copy(t, f):
        return pltpu.make_async_copy(dst.at[f], def_o.at[t, f], dsem.at[f])

    for f in range(2):
        for e in range(2):
            j = 2 * f + e
            sums_o[4 + j : 5 + j] = dot(ones, ge[:, j * D : j * D + D])[0:1]
            acc[e] = dot(n2[...], ge[:, j * D : j * D + D], TN)

        @pl.loop(0, 4)
        def _(zz):
            for i in range(8):
                row = pl.ds(pl.multiple_of(zz * 192 + i * 24, 8), 24)
                both = jnp.concatenate([acc[0, row], acc[1, row]], axis=0)
                dst[f, zz, i // 4, i % 4] = both.astype(bf16)

        out_copy(0, f).start()
    for j in range(4):
        acc[j % 2] = dot(inner[:, j * D : j * D + D], gf[...], TN)
        if j == 0:
            out_copy(0, 0).wait()
            out_copy(0, 1).wait()
        for i in range(8):
            for f in range(2):
                at = i * 96 + f * 48
                dst[f, j, i // 4, i % 4] = acc[j % 2, at : at + 48].astype(bf16)
    for f in range(2):
        out_copy(1, f).start()
    zero = jnp.zeros((24, 128), f32)
    for hh in range(2):
        acc[0, 0:HALF] = dot(mix[hh], ga[...], TN)
        for i in range(16):
            for half in range(2):
                for r in range(3):
                    at = half * HALF + r * 128
                    part = acc[0, i * 24 : i * 24 + 24, at : at + 128]
                    both = jnp.concatenate([zero, part], axis=0).astype(bf16)
                    do_o[half, r, 2 * hh + i // 8, (i // 4) % 2, i % 4] = both
    for f in range(2):
        out_copy(1, f).wait()


def k2_call(x, cot, counts, mix, ovo, ef, vec, eb):
    sds = jax.ShapeDtypeStruct
    dma = pltpu.SemaphoreType.DMA
    return pl.pallas_call(
        k2_kernel,
        out_shape=(
            sds((ROWS_DEV, D), f32),
            sds((ROWS_DEV, D), f32),
            sds((2, ROWS_DEV, HALF), bf16),
            sds((2, 2, 4, 2, 4, 48, D), bf16),
            sds((2, 3, 4, 2, 4, 48, 128), bf16),
            sds((8, D), f32),
        ),
        in_specs=[VMEM, VMEM, pl.BlockSpec(memory_space=pltpu.SMEM), VMEM] + [HBM] * 2 + [VMEM] * 2,
        out_specs=(VMEM, VMEM, VMEM, HBM, VMEM, VMEM),
        scratch_shapes=[
            pltpu.VMEM((4, D, D), bf16),
            pltpu.VMEM((4, 2, 4, 96, D), bf16),
            pltpu.VMEM((D, D), bf16),
            pltpu.VMEM((ROWS_DEV, 4 * D), bf16),
            pltpu.VMEM((ROWS_DEV, 4 * D), bf16),
            pltpu.VMEM((ROWS_DEV, D), bf16),
            pltpu.VMEM((ROWS_DEV, D), bf16),
            pltpu.VMEM((ROWS_DEV, D), bf16),
            pltpu.VMEM((2, D, D), f32),
            pltpu.VMEM((2, 4, 2, 4, 48, D), bf16),
            dma((2, 4)),
            dma((2,)),
            dma((2,)),
        ],
        compiler_params=pltpu.CompilerParams(vmem_limit_bytes=VMEM_LIMIT),
        name="k2_feed",
    )(x, cot, counts, mix, ovo, ef, vec, eb)


class Scatter:
    def __init__(self, pc, sems):
        self.pc = pc
        self.as_, self.ar, self.xs, self.xr, self.ys, self.yr, self.zs, self.zr, self.os, self.or_ = sems

    def acopy(self, k, p5, bufs, zz):
        dev = self.pc.xdev if zz < 2 else self.pc.ydev
        return remote(p5.at[zz, :, self.pc.nd], bufs[0].at[zz], self.as_.at[k, zz], self.ar.at[k, zz], dev)

    def xcopy(self, k, p5, bufs, zz):
        return remote(p5.at[zz, :, self.pc.nx], bufs[1].at[zz], self.xs.at[k, zz], self.xr.at[k, zz], self.pc.xdev)

    def ycopy(self, k, p5, bufs, zz):
        return remote(p5.at[zz, :, self.pc.ny], bufs[2].at[zz], self.ys.at[k, zz], self.yr.at[k, zz], self.pc.ydev)

    def zcopy(self, k, p5, bufs, i):
        zz = self.pc.zpos(i)
        return remote(
            p5.at[zz, :, self.pc.n], bufs[3].at[i - 1], self.zs.at[k, i], self.zr.at[k, i], self.pc.zdev(zz)
        )

    def row(self, k, p5, bufs, zz):
        self.acopy(k, p5, bufs, zz).start()
        (self.xcopy if zz < 2 else self.ycopy)(k, p5, bufs, zz).start()

    def one(self, k, p5, bufs):
        for zz in (0, 2, 1, 3):
            self.acopy(k, p5, bufs, zz).start()
        for zz in (0, 2, 1, 3):
            (self.xcopy if zz < 2 else self.ycopy)(k, p5, bufs, zz).start()

    def twos(self, k, p5, bufs):
        for zz in (0, 2, 1, 3):
            self.two(k, p5, bufs, zz)

    def threes(self, k, p5, bufs):
        for i in (1, 2, 3):
            self.three(k, p5, bufs, i)

    def two(self, k, p5, bufs, zz):
        col = self.pc.ny if zz < 2 else self.pc.nx
        self.acopy(k, p5, bufs, zz).wait_recv()
        p5[zz, :, col] = (p5[zz, :, col].astype(f32) + bufs[0][zz].astype(f32)).astype(bf16)
        (self.ycopy if zz < 2 else self.xcopy)(k, p5, bufs, zz).start()

    def column(self, k, p5, bufs, zz):
        self.xcopy(k, p5, bufs, zz).wait_recv()
        self.ycopy(k, p5, bufs, zz).wait_recv()
        return p5[zz, :, self.pc.n].astype(f32) + bufs[1][zz].astype(f32) + bufs[2][zz].astype(f32)

    def three(self, k, p5, bufs, i):
        zz = self.pc.zpos(i)
        p5[zz, :, self.pc.n] = self.column(k, p5, bufs, zz).astype(bf16)
        self.zcopy(k, p5, bufs, i).start()

    def outs(self, k, st, out):
        c = self.pc.c
        return (
            pltpu.make_async_copy(st.at[c], out, self.os.at[k, 1]),
            remote(st.at[1 - c], out, self.os.at[k, 0], self.or_.at[k], self.pc.sib),
        )

    def four(self, k, p5, bufs, st, out):
        total = self.column(k, p5, bufs, self.pc.z)
        for i in (1, 2, 3):
            self.zcopy(k, p5, bufs, i).wait_recv()
            total = total + bufs[3][i - 1].astype(f32)
        st[...] = total
        for cp in self.outs(k, st, out):
            cp.start()

    def sent(self, k, p5, bufs):
        for zz in range(4):
            self.acopy(k, p5, bufs, zz).wait_send()
            self.xcopy(k, p5, bufs, zz).wait_send()
            self.ycopy(k, p5, bufs, zz).wait_send()
        for i in (1, 2, 3):
            self.zcopy(k, p5, bufs, i).wait_send()


def k3_kernel(
    def_in, do_in, nrm_i, val_i, gmix, hid_i, slo_i, atl_i, atm_i, ats_i, wa_i, la_i, vv_i, tok, gres, vec,
    tg_o, od, ol, ofe, ovo, db_o, lb_o, vb_o, ag_o,
    nrm, val, gm, gn, hid, slo, atl, atm, ats, gsl, gsm, gd, wv, lv, dwf, vsb, vv, own,
    pd, pll, pv, ad, xd, yd, zd, al, xl, yl, zl, av, xv, yv, zv, std, stl, stv,
    as_, ar, xs, xr, ys, yr, zs, zr, os_, or_, lsem, ssem, rsem, gs_, gr_, free, hsem, fsem, dsem,
    fss, fsr,
):
    pc = Place()
    c = pc.c
    o = 1 - c
    s = Scatter(pc, (as_, ar, xs, xr, ys, yr, zs, zr, os_, or_))
    copy = pltpu.make_async_copy
    first = [copy(nrm_i, nrm, lsem.at[0]), copy(val_i, val, lsem.at[1]), copy(vv_i, vv, lsem.at[2])]
    for i, (at, to) in enumerate(((512, 0), (0, 1024))):
        first.append(copy(gmix.at[c, pl.ds(at, 512)], gm.at[pl.ds(pl.multiple_of(to + c * 512, 512), 512)], lsem.at[4 + i]))
    for cp in first:
        cp.start()

    def att_loads(h):
        return [copy(atl_i.at[h], atl, hsem.at[0]), copy(atm_i.at[h], atm, hsem.at[1]), copy(ats_i.at[h], ats, hsem.at[2])]

    hid_load = lambda h: copy(hid_i.at[h], hid, hsem.at[3])
    w_load = lambda h: copy(wa_i.at[h], wv, hsem.at[4])
    l_load = lambda h: copy(la_i.at[h], lv, hsem.at[5])
    slo_load = lambda h, b: copy(slo_i.at[h, pl.ds(b * 512, 512)], slo.at[b % 2], hsem.at[6 + b % 2])
    for cp in att_loads(0) + [hid_load(0), l_load(0), slo_load(0, 0), slo_load(0, 1), w_load(0)]:
        cp.start()
    order = [(f, zz) for f in (1, 0) for zz in (0, 2, 1, 3)]
    own_load = lambda i: copy(def_in.at[(c,) + order[i]], own.at[i % 2], fsem.at[i % 2])
    own_load(0).start()
    own_load(1).start()

    greet(pc.near())
    fswaps = []
    for i, (f, zz) in enumerate(order):
        fswaps.append(remote(def_in.at[o, f, zz], pd.at[f, zz], fss.at[i], fsr.at[i], pc.sib))
    swaps = [None, None]
    swaps.append(remote(do_in.at[o], pv, ssem.at[2], rsem.at[2], pc.sib))
    for i, (at, to) in enumerate(((512, 0), (0, 1024))):
        swaps.append(
            remote(
                gmix.at[o, pl.ds(at, 512)],
                gm.at[pl.ds(pl.multiple_of(to + c * 512, 512), 512)],
                ssem.at[3 + i],
                rsem.at[3 + i],
                pc.sib,
            )
        )
    for cp in fswaps[0:4] + swaps[3:5] + fswaps[4:8] + swaps[2:3]:
        cp.start()

    def d_args(k):
        slot = k % 3
        return pd.at[slot], (ad.at[k], xd.at[k], yd.at[k], zd.at[k])

    def l_args(p):
        return pll.at[p % 2], (al.at[p], xl.at[p], yl.at[p], zl.at[p])

    def v_args(p):
        return pv.at[p], (av.at[p], xv.at[p], yv.at[p], zv.at[p])

    gn[...] = jnp.zeros_like(gn)
    gsm[...] = jnp.zeros_like(gsm)


    def core_sum(i):
        f, zz = order[i]
        fswaps[i].wait()
        own_load(i).wait()
        pd[f, zz] = (pd[f, zz].astype(f32) + own[i % 2].astype(f32)).astype(bf16)
        if i < 6:
            own_load(i + 2).start()
        s.row(f, *d_args(f), zz)

    dloads = []
    for r in range(3):
        for zz in range(4):
            to = pl.ds(HALF * (zz % 2) + 128 * r, 128)
            dloads.append(copy(do_in.at[c, r, zz], own.at[zz // 2, :, :, :, to], dsem.at[r, zz]))

    def other_half():
        for i in range(4, 8):
            core_sum(i)
        for cp in dloads:
            cp.start()

    def dloads_done():
        for cp in swaps[2:3] + dloads:
            cp.wait()

    for i in range(4):
        core_sum(i)
    swaps[3].wait()
    swaps[4].wait()
    for cp in first:
        cp.wait()

    lane = lax.broadcasted_iota(jnp.int32, (1, 128), 1)
    keeps = [(lane < HEAD_DIM).astype(bf16), (lane >= HEAD_DIM).astype(bf16)]
    ones = jnp.ones((8, 1024), bf16)

    def score_grad(att, g):
        a = att.astype(f32)
        t = a * g
        return (t - a * jnp.sum(t, axis=-1, keepdims=True)).astype(bf16)

    def put_pair(p5, half, e, width):
        @pl.loop(0, 2)
        def _(zi):
            for i in range(8):
                row = pl.ds(pl.multiple_of(zi * 192 + i * 24, 8), 24)
                part = dwf[row, 0:width]
                if e == 0:
                    both = jnp.concatenate([part, part], axis=0)
                else:
                    old = p5[2 * half + zi, i // 4, i % 4].astype(f32)
                    both = jnp.concatenate([old[0:24], part], axis=0)
                p5[2 * half + zi, i // 4, i % 4] = both.astype(bf16)

    @pl.loop(0, 3)
    def _(p):
        lanes = pl.ds(pl.multiple_of(p * 128, 128), 128)
        begin = p == 0
        later = p > 0
        kd = p + 2
        dslot = kd % 3

        def on_a(fn):
            fn(kd - 1, *d_args(kd - 1))

        def on_b(fn):
            @pl.when(begin)
            def _():
                fn(0, *d_args(0))

            @pl.when(later)
            def _():
                fn(5 + (p + 2) % 3, *l_args((p + 2) % 3))

        def on_first(*fns):
            for r, fn in enumerate(fns):
                if fn is not None:
                    pl.when(p == r)(fn)

        def on_v(fn):
            @pl.when(later)
            def _():
                fn(8 + (p + 2) % 3, *v_args((p + 2) % 3))

        def four_a():
            @pl.when(begin)
            def _():
                s.four(1, *d_args(1), std.at[1], ofe.at[c, 1])

            @pl.when(p == 2)
            def _():
                for cp in s.outs(0, std.at[0], ofe.at[c, 0]):
                    cp.wait()

            @pl.when(later)
            def _():
                s.four(kd - 1, *d_args(kd - 1), std.at[(kd - 1) % 3], od.at[3 * c + (p + 2) % 3])

        def four_b():
            @pl.when(begin)
            def _():
                s.four(0, *d_args(0), std.at[0], ofe.at[c, 0])

            @pl.when(later)
            def _():
                r = (p + 2) % 3
                s.four(5 + r, *l_args(r), stl.at[r], ol.at[3 * c + r])

        def four_v():
            @pl.when(later)
            def _():
                r = (p + 2) % 3
                s.four(8 + r, *v_args(r), stv.at[r], ovo.at[r, c])

        def value_part():
            for half in range(2):
                cols = slice(half * HALF, half * HALF + HALF)
                dwf[:, 0:128] = dot(nrm[:, cols], gm[:, lanes], TN)

                @pl.loop(0, 8)
                def _(i):
                    for zi in range(2):
                        row = pl.ds(pl.multiple_of(zi * 192 + i * 24, 8), 24)
                        at = (2 * half + zi, i // 4, i % 4)
                        to = pl.ds(pl.multiple_of(HALF * zi + 128 * p, 128), 128)
                        both = pv[(p,) + at].astype(f32) + own[half, i // 4, i % 4, :, to].astype(f32)
                        pv[(p,) + at] = jnp.concatenate([dwf[row, 0:128], both[24:48]], axis=0).astype(bf16)

        def tick(e, what):
            if what == "gs" and e == 0:
                on_first(lambda: s.twos(1, *d_args(1)))
                on_v(s.threes)
            elif what == "gd" and e == 0:
                on_first(other_half)
                four_v()
            elif what == "dw" and e == 0:
                on_b(s.twos)
            elif what == "gs":
                on_first(dloads_done)
                value_part()
                s.one(8 + p, *v_args(p))
                on_a(s.threes)
            elif what == "gd":
                on_b(s.threes)
            elif what == "dw":
                s.twos(8 + p, *v_args(p))
                s.one(kd, *d_args(kd))
            elif what == "dl" and e == 1:
                s.one(5 + p, *l_args(p))
                four_a()
            elif what == "gn" and e == 1:
                s.twos(kd, *d_args(kd))
                four_b()

        def logit_part(e):
            h = 2 * p + e
            if e == 0:

                @pl.when(p == 2)
                def _():
                    s.sent(5, *l_args(0))

            hid_load(h).wait()
            for half in range(2):
                cols = slice(half * HALF, half * HALF + HALF)
                dwf[:, 0:512] = dot(hid[0:1024, cols], gsl[e], TN)
                dwf[:, 0:256] += dot(hid[1024:2048, cols], gsm[e], TN)
                put_pair(pll.at[p % 2], half, e, 512)

            @pl.when(h < 5)
            def _():
                hid_load(h + 1).start()

            tick(e, "dl")

        for e in range(2):
            h = 2 * p + e
            more = h < 5

            def ahead(*cps):
                @pl.when(more)
                def _():
                    for cp in cps:
                        cp.start()

            for cp in att_loads(h):
                cp.wait()
            for b in range(4):
                at = b * 512
                rows = slice(at, at + 512)
                gpair = gm[rows, lanes]
                vpair = val[rows, lanes] * keeps[e]
                gkeep = gpair * keeps[e]
                if b < 2:
                    att = atl[rows]
                    gsl[e, rows] = score_grad(att, dot(gpair, vpair, NT))
                    vs = dot(att, gkeep, TN)
                else:
                    part = slice((b - 2) * 256, (b - 2) * 256 + 256)
                    sh, mi = ats[part], atm[part]
                    g_sh = jnp.concatenate(
                        [dot(gpair[0:128], vpair[0:128], NT), dot(gpair[128:256], vpair[128:256], NT)], axis=0
                    )
                    at2 = (b - 2) * 512
                    gsm[e, at2 : at2 + 256, 0:128] = score_grad(sh, g_sh)
                    gsm[e, at2 + 256 : at2 + 512] = score_grad(mi, dot(gpair[256:512], vpair[256:512], NT))
                    vs = jnp.concatenate(
                        [
                            dot(sh[0:128], gkeep[0:128], TN),
                            dot(sh[128:256], gkeep[128:256], TN),
                            dot(mi, gkeep[256:512], TN),
                        ],
                        axis=0,
                    )
                if e == 0:
                    vsb[rows] = vs.astype(bf16)
                else:
                    gm[rows, lanes] = vsb[rows] + vs.astype(bf16)
            ahead(*att_loads(h + 1))
            lsum = dot(ones, gsl[e])
            lb_o[pl.ds(h, 1)] = lsum[0:1]
            lb_o[pl.ds(h, 1), 0:256] += dot(ones, gsm[e])[0:1]
            tick(e, "gs")
            l_load(h).wait()
            for b in range(4):
                rows = slice(b * 512, b * 512 + 512)
                slo_load(h, b).wait()
                if b < 2:
                    gh = dot(gsl[e, rows], lv[...], NT)
                else:
                    gh = dot(gsm[e, (b - 2) * 512 : (b - 2) * 512 + 512], lv[:, 0:256], NT)
                gd[rows] = (gh * slo[b % 2].astype(f32)).astype(bf16)
                if b < 2:
                    slo_load(h, b + 2).start()
                else:
                    ahead(slo_load(h + 1, b - 2))
            ahead(l_load(h + 1))
            db_o[pl.ds(h, 1)] = (dot(ones, gd[0:1024]) + dot(ones, gd[1024:2048]))[0:1]
            tick(e, "gd")
            if e == 0:

                @pl.when(later)
                def _():
                    s.sent(kd - 3, *d_args(kd - 3))

            for half in range(2):
                cols = slice(half * HALF, half * HALF + HALF)
                dwf[...] = dot(nrm[:, cols], gd[...], TN)
                put_pair(pd.at[dslot], half, e, D)
            tick(e, "dw")
            if e == 1:
                logit_part(0)
                logit_part(1)
            w_load(h).wait()

            @pl.loop(0, 4)
            def _(b):
                rows = pl.ds(pl.multiple_of(b * 512, 512), 512)
                gn[rows] += dot(gd[rows], wv[...], NT)

            ahead(w_load(h + 1))
            tick(e, "gn")

    pl.semaphore_signal(free, inc=1, device_id=pc.sib, device_id_type=MESH)
    vb_o[...] = dot(ones, gm[0:1024]) + dot(ones, gm[1024:2048])

    @pl.loop(0, 4)
    def _(b):
        rows = pl.ds(pl.multiple_of(b * 512, 512), 512)
        gn[rows] += dot(gm[rows], vv[...], NT)

    s.threes(10, *v_args(2))
    other = lambda to: pl.ds(pl.multiple_of(to + o * 512, 512), 512)
    mine = lambda to: pl.ds(pl.multiple_of(to + c * 512, 512), 512)
    hid[0:512] = gn[other(1024)].astype(bf16)
    hid[512:1024] = gn[other(0)].astype(bf16)
    pl.semaphore_wait(free, 1)
    gswap = remote(hid.at[pl.ds(0, 1024)], gd.at[pl.ds(0, 1024)], gs_, gr_, pc.sib)
    gswap.start()
    tloads = [copy(tok.at[pl.ds(i * 512, 512)], slo.at[i], hsem.at[6 + i]) for i in range(2)]
    for cp in tloads:
        cp.start()
    s.twos(7, *l_args(2))
    for cp in tloads:
        cp.wait()
    gswap.wait()
    ag_o[...] = jnp.zeros_like(ag_o)

    @pl.loop(0, 4)
    def _(b):
        nat = pl.ds(pl.multiple_of(b * 256, 256), 256)
        trow = pl.ds(pl.multiple_of(jnp.where(b < 2, 1024 + b * 256, b * 256 - 512) + c * 512, 256), 256)
        load = copy(gres.at[nat], dwf.at[pl.ds(0, 256)], lsem.at[6])
        load.start()
        unit, inv = norm_rows(slo[b // 2, pl.ds(pl.multiple_of((b % 2) * 256, 256), 256)].astype(f32))
        g = gn[trow] + gd[nat].astype(f32)
        q = g * vec[0:1]
        back = inv * (q - jnp.mean(q, axis=-1, keepdims=True) - unit * jnp.mean(q * unit, axis=-1, keepdims=True))
        load.wait()
        dwf[0:256] = dwf[0:256] + back
        ag_o[0:1] += jnp.sum(g * unit, axis=0, keepdims=True)
        ag_o[1:2] += jnp.sum(g, axis=0, keepdims=True)
        store = copy(dwf.at[pl.ds(0, 256)], tg_o.at[nat], lsem.at[7])
        store.start()
        store.wait()

    s.threes(4, *d_args(4))
    s.threes(7, *l_args(2))
    s.four(10, *v_args(2), stv.at[2], ovo.at[2, c])
    for cp in s.outs(1, std.at[1], ofe.at[c, 1]):
        cp.wait()
    s.four(4, *d_args(4), std.at[1], od.at[3 * c + 2])
    s.four(7, *l_args(2), stl.at[2], ol.at[3 * c + 2])
    ends = []
    for p in range(3):
        ends.append(s.outs(2 + p, std.at[(2 + p) % 3], od.at[3 * c + p]))
        ends.append(s.outs(5 + p, stl.at[p], ol.at[3 * c + p]))
        ends.append(s.outs(8 + p, stv.at[p], ovo.at[p, c]))
    for pair in ends:
        for cp in pair:
            cp.wait()
    for k in (2, 3, 4):
        s.sent(k, *d_args(k))
    for p in (1, 2):
        s.sent(5 + p, *l_args(p))
    for p in range(3):
        s.sent(8 + p, *v_args(p))


def k3_call(*args):
    sds = jax.ShapeDtypeStruct
    dma = pltpu.SemaphoreType.DMA
    V = pltpu.VMEM

    def bufs(shape, width):
        return [V(shape + (4, 2, 48, width), bf16)] * 3 + [V(shape + (3, 2, 48, width), bf16)]

    return pl.pallas_call(
        k3_kernel,
        out_shape=(
            sds((ROWS_DEV, D), f32),
            sds((6, 48, D), f32),
            sds((6, 48, L3), f32),
            sds((2, 2, 48, D), f32),
            sds((3, 2, 48, 128), f32),
            sds((8, D), f32),
            sds((8, L3), f32),
            sds((8, HALF), f32),
            sds((8, D), f32),
        ),
        in_specs=[HBM] * 15 + [VMEM],
        out_specs=(HBM,) * 5 + (VMEM,) * 4,
        scratch_shapes=[
            V((CHIP_ROWS, D), bf16),
            V((CHIP_ROWS, HALF), bf16),
            V((CHIP_ROWS, HALF), bf16),
            V((CHIP_ROWS, D), f32),
            V((CHIP_ROWS, HIDDEN_SIZE), bf16),
            V((2, 512, HIDDEN_SIZE), bf16),
            V((1024, L3), bf16),
            V((512, L2), bf16),
            V((512, L1), bf16),
            V((2, 1024, L3), bf16),
            V((2, 1024, L2), bf16),
            V((CHIP_ROWS, HIDDEN_SIZE), bf16),
            V((D, HIDDEN_SIZE), bf16),
            V((HIDDEN_SIZE, L3), bf16),
            V((HALF, D), f32),
            V((CHIP_ROWS, 128), bf16),
            V((D, HALF), bf16),
            V((2, 2, 4, 48, D), bf16),
            V((3, 4, 2, 4, 48, D), bf16),
            V((2, 4, 2, 4, 48, L3), bf16),
            V((3, 4, 2, 4, 48, 128), bf16),
        ]
        + bufs((5,), D)
        + bufs((3,), L3)
        + bufs((3,), 128)
        + [V((3, 2, 48, D), f32), V((3, 2, 48, L3), f32), V((3, 2, 48, 128), f32)]
        + [dma((11, 4))] * 8
        + [dma((11, 2)), dma((11,)), dma((8,)), dma((5,)), dma((5,)), dma, dma, pltpu.SemaphoreType.REGULAR]
        + [dma((8,)), dma((2,)), dma((3, 4))]
        + [dma((8,))] * 2,
        compiler_params=pltpu.CompilerParams(
            collective_id=2, has_side_effects=True, vmem_limit_bytes=VMEM_LIMIT
        ),
        name="k3_backward",
    )(*args)


def k4_kernel(g, out, slots, ss, sr):
    pc = Place()
    me = pc.w * 4 + pc.n
    bar = pltpu.get_barrier_semaphore()

    @pl.loop(1, 32)
    def _(j):
        t = (me + j) % 32
        pl.semaphore_signal(bar, inc=1, device_id=(t // 4, t % 4), device_id_type=MESH)

    pl.semaphore_wait(bar, 31)

    @pl.loop(1, 32)
    def _(j):
        t = (me + j) % 32
        remote(g.at[t], slots.at[me], ss.at[t], sr.at[me], (t // 4, t % 4)).start()

    slots[me] = g[me]

    @pl.loop(1, 32)
    def _(j):
        t = (me + j) % 32
        f = (me + 32 - j) % 32
        cp = remote(g.at[t], slots.at[f], ss.at[t], sr.at[f], (t // 4, t % 4))
        cp.wait_send()
        cp.wait_recv()

    out[...] = jnp.sum(slots[...], axis=0)


def k4_call(g):
    return pl.pallas_call(
        k4_kernel,
        out_shape=jax.ShapeDtypeStruct((16, 128), f32),
        in_specs=[VMEM],
        out_specs=VMEM,
        scratch_shapes=[
            pltpu.VMEM((32, 16, 128), f32),
            pltpu.SemaphoreType.DMA((32,)),
            pltpu.SemaphoreType.DMA((32,)),
        ],
        compiler_params=pltpu.CompilerParams(collective_id=3, has_side_effects=True),
        name="k4_vectors",
    )(g)


def chip_body(tokens, cotangent, bucket_counts, *params):
    core = lax.axis_index(AXES[0]) % 2
    tok2, vec, eb, lb, db, vb, md, ml, mvo, mf = prepare(tokens, *params)
    vec = jnp.pad(vec, ((0, 1), (0, 0)))
    ovo, _, _, ef, nrm, val, hid, slo, atl, atm, ats, wa, la, mix, vv = k1_call(
        tokens, tok2, vec, db, lb, vb, mvo, md, ml, mf
    )
    lay, gres, gmix, dff, dout, sums = k2_call(tokens, cotangent, bucket_counts, mix, ovo, ef, vec, eb)
    tg, od, ol, ofe, dvo, dbs, lbs, vbs, ags = k3_call(
        dff, dout, nrm, val, gmix, hid, slo, atl, atm, ats, wa, la, vv, tokens, gres, vec
    )
    vb_all = lax.dynamic_update_slice(jnp.zeros((1, D), f32), vbs[0:1], (0, HALF * core))
    lb_all = lax.dynamic_update_slice(jnp.zeros((HEADS, L3), f32), lbs[0:6], (6 * core, 0))
    db_all = lax.dynamic_update_slice(jnp.zeros((HEADS, HIDDEN_SIZE), f32), dbs[0:6], (6 * core, 0))
    v7 = jnp.concatenate([ags[0:2], vb_all, sums[3:4], sums[0:2], sums[2:3]])
    narrow_rows = v7.reshape(7, 32, 24).transpose(1, 0, 2)
    wide_rows = jnp.concatenate(
        [sums[4:8].reshape(32, 1, 96), lb_all.reshape(32, 2, 96), db_all.reshape(32, 3, 96)], axis=1
    )
    pack = jnp.concatenate(
        [jnp.pad(narrow_rows, ((0, 0), (0, 0), (0, 104))), jnp.pad(wide_rows, ((0, 0), (0, 3), (0, 32)))], axis=1
    )
    red = k4_call(pack)
    vo_shard = lambda r: dvo[:, :, r : r + 24].transpose(2, 1, 0, 3).reshape(24, D)
    small = lambda i: red[i, :24]
    return (
        lay,
        tg,
        small(0),
        small(1),
        od.reshape(HEADS, 24, HIDDEN_SIZE),
        red[10:13, :96].reshape(288),
        ol.reshape(HEADS, 24, L3),
        red[8:10, :96].reshape(192),
        vo_shard(0),
        small(2),
        vo_shard(24),
        small(3),
        small(4),
        small(5),
        ofe[0].reshape(4, 24, D).transpose(1, 0, 2).reshape(24, 4 * D),
        red[7, :96],
        ofe[1].reshape(96, D),
        small(6),
    )


def smooth_gate(values_in):
    return (
        0.5
        * values_in
        * (1.0 + jnp.tanh(gelu_root * (values_in + gelu_cube * values_in * values_in * values_in)))
    )


def gate_slope(values_in):
    squared = values_in * values_in
    tangent = jnp.tanh(gelu_root * (values_in + gelu_cube * squared * values_in))
    return 0.5 * (1.0 + tangent) + 0.5 * values_in * (1.0 - tangent * tangent) * gelu_root * (
        1.0 + 3.0 * gelu_cube * squared
    )


def bucket_layout():
    return ((S1, L1), (S2, L2), (S3, L3))


def live_rows(counts):
    pieces = []
    for bucket_index, (slot_count, seq_length) in enumerate(bucket_layout()):
        slot_of_row = jnp.arange(slot_count * seq_length, dtype=jnp.int32) // seq_length
        pieces.append(jnp.where(slot_of_row < counts[bucket_index], 1.0, 0.0).astype(jnp.float32))
    return jnp.concatenate(pieces)


def product(left_side, right_side):
    return jnp.dot(left_side, right_side, preferred_element_type=jnp.float32)


def column_sums(matrix_rows):
    return jnp.sum(matrix_rows.astype(jnp.float32), axis=0)


def norm_forward(inputs_float, norm_gain, norm_shift):
    row_mean = jnp.mean(inputs_float, axis=-1, keepdims=True)
    centred = inputs_float - row_mean
    inverse_scale = lax.rsqrt(jnp.mean(centred * centred, axis=-1, keepdims=True) + norm_eps)
    unit_rows = centred * inverse_scale
    return (unit_rows * norm_gain + norm_shift, unit_rows, inverse_scale)


def norm_backward(grad_normed, unit_rows, inverse_scale, norm_gain):
    grad_unit = grad_normed * norm_gain
    grad_inputs = inverse_scale * (
        grad_unit
        - jnp.mean(grad_unit, axis=-1, keepdims=True)
        - unit_rows * jnp.mean(grad_unit * unit_rows, axis=-1, keepdims=True)
    )
    return (grad_inputs, jnp.sum(grad_normed * unit_rows, axis=0), jnp.sum(grad_normed, axis=0))


def forward_pass(tokens, live_mask, gathered):
    (
        attn_gain,
        attn_shift,
        dense_weight,
        dense_bias,
        logit_weight,
        logit_bias,
        value_weight,
        value_bias,
        output_weight,
        output_bias,
        feed_gain,
        feed_shift,
        expand_weight,
        expand_bias,
        reduce_weight,
        reduce_bias,
    ) = gathered
    inputs_float = tokens.astype(jnp.float32)
    normed_float, unit_one, scale_one = norm_forward(
        inputs_float, attn_gain.astype(jnp.float32), attn_shift.astype(jnp.float32)
    )
    normed = normed_float.astype(jnp.bfloat16)
    values = (product(normed, value_weight) + value_bias.astype(jnp.float32)).astype(jnp.bfloat16)
    dense_heads = dense_bias.astype(jnp.float32).reshape(HEADS, 1, HIDDEN_SIZE)
    logit_heads = logit_bias.astype(jnp.float32).reshape(HEADS, 1, L3)
    pre_list, hidden_list, attention_list, mixed_list = ([], [], [], [])
    start_row = 0
    for slot_count, seq_length in bucket_layout():
        stop_row = start_row + slot_count * seq_length
        pre_act = (
            jnp.einsum(
                "rd,hde->hre",
                normed[start_row:stop_row],
                dense_weight,
                preferred_element_type=jnp.float32,
            )
            + dense_heads
        )
        hidden = smooth_gate(pre_act).astype(jnp.bfloat16)
        scores = (
            jnp.einsum(
                "hre,hel->hrl",
                hidden,
                logit_weight[:, :, :seq_length],
                preferred_element_type=jnp.float32,
            )
            + logit_heads[:, :, :seq_length]
        )
        attention = jax.nn.softmax(scores, axis=-1)
        attention_low = attention.astype(jnp.bfloat16).reshape(
            HEADS, slot_count, seq_length, seq_length
        )
        block_values = values[start_row:stop_row].reshape(slot_count, seq_length, HEADS, HEAD_DIM)
        mixed_heads = jnp.einsum(
            "hsql,slhc->sqhc", attention_low, block_values, preferred_element_type=jnp.float32
        )
        mixed_list.append(mixed_heads.reshape(slot_count * seq_length, D))
        pre_list.append(pre_act)
        hidden_list.append(hidden)
        attention_list.append(attention)
        start_row = stop_row
    mixed_all = jnp.concatenate(mixed_list, axis=0).astype(jnp.bfloat16)
    attended = product(mixed_all, output_weight) + output_bias.astype(jnp.float32)
    residual = inputs_float + attended
    normed_two_float, unit_two, scale_two = norm_forward(
        residual, feed_gain.astype(jnp.float32), feed_shift.astype(jnp.float32)
    )
    normed_two = normed_two_float.astype(jnp.bfloat16)
    expand_pre = product(normed_two, expand_weight) + expand_bias.astype(jnp.float32)
    inner_act = smooth_gate(expand_pre).astype(jnp.bfloat16)
    feed_out = product(inner_act, reduce_weight) + reduce_bias.astype(jnp.float32)
    layer_out = live_mask[:, None] * (residual + feed_out)
    stored = (
        normed,
        unit_one,
        scale_one,
        values,
        pre_list,
        hidden_list,
        attention_list,
        mixed_all,
        unit_two,
        scale_two,
        normed_two,
        expand_pre,
        inner_act,
    )
    return (layer_out, stored)


def backward_pass(cotangent, live_mask, gathered, stored):
    (
        attn_gain,
        attn_shift,
        dense_weight,
        dense_bias,
        logit_weight,
        logit_bias,
        value_weight,
        value_bias,
        output_weight,
        output_bias,
        feed_gain,
        feed_shift,
        expand_weight,
        expand_bias,
        reduce_weight,
        reduce_bias,
    ) = gathered
    (
        normed,
        unit_one,
        scale_one,
        values,
        pre_list,
        hidden_list,
        attention_list,
        mixed_all,
        unit_two,
        scale_two,
        normed_two,
        expand_pre,
        inner_act,
    ) = stored
    grad_out = cotangent.astype(jnp.float32) * live_mask[:, None]
    grad_feed = grad_out.astype(jnp.bfloat16)
    reduce_weight_grad = jnp.einsum(
        "rf,rd->fd", inner_act, grad_feed, preferred_element_type=jnp.float32
    )
    reduce_bias_grad = column_sums(grad_feed)
    grad_inner = jnp.einsum(
        "rd,fd->rf", grad_feed, reduce_weight, preferred_element_type=jnp.float32
    )
    grad_expand = (grad_inner * gate_slope(expand_pre)).astype(jnp.bfloat16)
    expand_weight_grad = jnp.einsum(
        "rd,rf->df", normed_two, grad_expand, preferred_element_type=jnp.float32
    )
    expand_bias_grad = column_sums(grad_expand)
    grad_normed_two = jnp.einsum(
        "rf,df->rd", grad_expand, expand_weight, preferred_element_type=jnp.float32
    )
    grad_residual_norm, feed_gain_grad, feed_shift_grad = norm_backward(
        grad_normed_two, unit_two, scale_two, feed_gain.astype(jnp.float32)
    )
    grad_residual = grad_out + grad_residual_norm
    grad_attended = grad_residual.astype(jnp.bfloat16)
    output_weight_grad = jnp.einsum(
        "rd,re->de", mixed_all, grad_attended, preferred_element_type=jnp.float32
    )
    output_bias_grad = column_sums(grad_attended)
    grad_mixed = jnp.einsum(
        "re,de->rd", grad_attended, output_weight, preferred_element_type=jnp.float32
    ).astype(jnp.bfloat16)
    dense_weight_grad = jnp.zeros((HEADS, D, HIDDEN_SIZE), jnp.float32)
    dense_bias_grad = jnp.zeros((HEADS, HIDDEN_SIZE), jnp.float32)
    logit_weight_grad = jnp.zeros((HEADS, HIDDEN_SIZE, L3), jnp.float32)
    logit_bias_grad = jnp.zeros((HEADS, L3), jnp.float32)
    grad_normed_list, value_sum_list = ([], [])
    start_row = 0
    for bucket_index, (slot_count, seq_length) in enumerate(bucket_layout()):
        row_count = slot_count * seq_length
        stop_row = start_row + row_count
        attention = attention_list[bucket_index]
        hidden = hidden_list[bucket_index]
        pre_act = pre_list[bucket_index]
        attention_low = attention.astype(jnp.bfloat16).reshape(
            HEADS, slot_count, seq_length, seq_length
        )
        block_values = values[start_row:stop_row].reshape(slot_count, seq_length, HEADS, HEAD_DIM)
        block_grad = grad_mixed[start_row:stop_row].reshape(slot_count, seq_length, HEADS, HEAD_DIM)
        grad_attention = jnp.einsum(
            "sqhc,slhc->hsql", block_grad, block_values, preferred_element_type=jnp.float32
        ).reshape(HEADS, row_count, seq_length)
        value_sum_list.append(
            jnp.einsum(
                "hsql,sqhc->slhc", attention_low, block_grad, preferred_element_type=jnp.float32
            ).reshape(row_count, D)
        )
        grad_scores = (
            attention
            * (grad_attention - jnp.sum(attention * grad_attention, axis=-1, keepdims=True))
        ).astype(jnp.bfloat16)
        logit_weight_grad = logit_weight_grad.at[:, :, :seq_length].add(
            jnp.einsum("hre,hrl->hel", hidden, grad_scores, preferred_element_type=jnp.float32)
        )
        logit_bias_grad = logit_bias_grad.at[:, :seq_length].add(
            jnp.sum(grad_scores.astype(jnp.float32), axis=1)
        )
        grad_hidden = jnp.einsum(
            "hrl,hel->hre",
            grad_scores,
            logit_weight[:, :, :seq_length],
            preferred_element_type=jnp.float32,
        )
        grad_dense = (grad_hidden * gate_slope(pre_act)).astype(jnp.bfloat16)
        dense_weight_grad = dense_weight_grad + jnp.einsum(
            "rd,hre->hde",
            normed[start_row:stop_row],
            grad_dense,
            preferred_element_type=jnp.float32,
        )
        dense_bias_grad = dense_bias_grad + jnp.sum(grad_dense.astype(jnp.float32), axis=1)
        grad_normed_list.append(
            jnp.einsum("hre,hde->rd", grad_dense, dense_weight, preferred_element_type=jnp.float32)
        )
        start_row = stop_row
    grad_values = jnp.concatenate(value_sum_list, axis=0).astype(jnp.bfloat16)
    value_weight_grad = jnp.einsum(
        "rd,re->de", normed, grad_values, preferred_element_type=jnp.float32
    )
    value_bias_grad = column_sums(grad_values)
    grad_normed = jnp.concatenate(grad_normed_list, axis=0) + jnp.einsum(
        "re,de->rd", grad_values, value_weight, preferred_element_type=jnp.float32
    )
    grad_inputs_norm, attn_gain_grad, attn_shift_grad = norm_backward(
        grad_normed, unit_one, scale_one, attn_gain.astype(jnp.float32)
    )
    tokens_grad = grad_residual + grad_inputs_norm
    return (
        tokens_grad,
        (
            attn_gain_grad,
            attn_shift_grad,
            dense_weight_grad,
            dense_bias_grad.reshape(-1),
            logit_weight_grad,
            logit_bias_grad.reshape(-1),
            value_weight_grad,
            value_bias_grad,
            output_weight_grad,
            output_bias_grad,
            feed_gain_grad,
            feed_shift_grad,
            expand_weight_grad,
            expand_bias_grad,
            reduce_weight_grad,
            reduce_bias_grad,
        ),
    )


def body(
    tokens,
    cotangent,
    bucket_counts,
    attn_gain,
    attn_shift,
    dense_weight,
    dense_bias,
    logit_weight,
    logit_bias,
    value_weight,
    value_bias,
    output_weight,
    output_bias,
    feed_gain,
    feed_shift,
    expand_weight,
    expand_bias,
    reduce_weight,
    reduce_bias,
):
    gathered = (
        lax.all_gather(attn_gain, AXES, axis=0, tiled=True),
        lax.all_gather(attn_shift, AXES, axis=0, tiled=True),
        lax.all_gather(dense_weight, AXES, axis=1, tiled=True),
        lax.all_gather(dense_bias, AXES, axis=0, tiled=True),
        lax.all_gather(logit_weight, AXES, axis=1, tiled=True),
        lax.all_gather(logit_bias, AXES, axis=0, tiled=True),
        lax.all_gather(value_weight, AXES, axis=0, tiled=True),
        lax.all_gather(value_bias, AXES, axis=0, tiled=True),
        lax.all_gather(output_weight, AXES, axis=0, tiled=True),
        lax.all_gather(output_bias, AXES, axis=0, tiled=True),
        lax.all_gather(feed_gain, AXES, axis=0, tiled=True),
        lax.all_gather(feed_shift, AXES, axis=0, tiled=True),
        lax.all_gather(expand_weight, AXES, axis=0, tiled=True),
        lax.all_gather(expand_bias, AXES, axis=0, tiled=True),
        lax.all_gather(reduce_weight, AXES, axis=0, tiled=True),
        lax.all_gather(reduce_bias, AXES, axis=0, tiled=True),
    )
    live_mask = live_rows(bucket_counts[0])
    layer_out, stored = forward_pass(tokens, live_mask, gathered)
    gathered = (
        lax.all_gather(attn_gain, AXES, axis=0, tiled=True),
        lax.all_gather(attn_shift, AXES, axis=0, tiled=True),
        lax.all_gather(dense_weight, AXES, axis=1, tiled=True),
        lax.all_gather(dense_bias, AXES, axis=0, tiled=True),
        lax.all_gather(logit_weight, AXES, axis=1, tiled=True),
        lax.all_gather(logit_bias, AXES, axis=0, tiled=True),
        lax.all_gather(value_weight, AXES, axis=0, tiled=True),
        lax.all_gather(value_bias, AXES, axis=0, tiled=True),
        lax.all_gather(output_weight, AXES, axis=0, tiled=True),
        lax.all_gather(output_bias, AXES, axis=0, tiled=True),
        lax.all_gather(feed_gain, AXES, axis=0, tiled=True),
        lax.all_gather(feed_shift, AXES, axis=0, tiled=True),
        lax.all_gather(expand_weight, AXES, axis=0, tiled=True),
        lax.all_gather(expand_bias, AXES, axis=0, tiled=True),
        lax.all_gather(reduce_weight, AXES, axis=0, tiled=True),
        lax.all_gather(reduce_bias, AXES, axis=0, tiled=True),
    )
    tokens_grad, grads = backward_pass(cotangent, live_mask, gathered, stored)
    shards = (
        lax.psum_scatter(grads[0], AXES, scatter_dimension=0, tiled=True),
        lax.psum_scatter(grads[1], AXES, scatter_dimension=0, tiled=True),
        lax.psum_scatter(grads[2], AXES, scatter_dimension=1, tiled=True),
        lax.psum_scatter(grads[3], AXES, scatter_dimension=0, tiled=True),
        lax.psum_scatter(grads[4], AXES, scatter_dimension=1, tiled=True),
        lax.psum_scatter(grads[5], AXES, scatter_dimension=0, tiled=True),
        lax.psum_scatter(grads[6], AXES, scatter_dimension=0, tiled=True),
        lax.psum_scatter(grads[7], AXES, scatter_dimension=0, tiled=True),
        lax.psum_scatter(grads[8], AXES, scatter_dimension=0, tiled=True),
        lax.psum_scatter(grads[9], AXES, scatter_dimension=0, tiled=True),
        lax.psum_scatter(grads[10], AXES, scatter_dimension=0, tiled=True),
        lax.psum_scatter(grads[11], AXES, scatter_dimension=0, tiled=True),
        lax.psum_scatter(grads[12], AXES, scatter_dimension=0, tiled=True),
        lax.psum_scatter(grads[13], AXES, scatter_dimension=0, tiled=True),
        lax.psum_scatter(grads[14], AXES, scatter_dimension=0, tiled=True),
        lax.psum_scatter(grads[15], AXES, scatter_dimension=0, tiled=True),
    )
    return (layer_out, tokens_grad) + tuple(shards)


def solution(mesh):
    in_specs = (
        P(AXES, None),
        P(AXES, None),
        P(AXES, None),
        P(AXES),
        P(AXES),
        P(None, AXES, None),
        P(AXES),
        P(None, AXES, None),
        P(AXES),
        P(AXES, None),
        P(AXES),
        P(AXES, None),
        P(AXES),
        P(AXES),
        P(AXES),
        P(AXES, None),
        P(AXES),
        P(AXES, None),
        P(AXES),
    )
    out_specs = (
        P(AXES, None),
        P(AXES, None),
        P(AXES),
        P(AXES),
        P(None, AXES, None),
        P(AXES),
        P(None, AXES, None),
        P(AXES),
        P(AXES, None),
        P(AXES),
        P(AXES, None),
        P(AXES),
        P(AXES),
        P(AXES),
        P(AXES, None),
        P(AXES),
        P(AXES, None),
        P(AXES),
    )
    shape = tuple(mesh.shape[a] for a in AXES)
    chosen = chip_body if shape == (8, 4) else body
    return jax.shard_map(chosen, mesh=mesh, in_specs=in_specs, out_specs=out_specs, check_vma=False)
```

```python
import functools

import jax
import jax.numpy as jnp
import numpy as np
from jax import lax
from jax.experimental import pallas as pl
from jax.experimental.pallas import tpu as pltpu
from jax.sharding import PartitionSpec as P

D = 768
HEADS = 12
HEAD_DIM = 64
HIDDEN_SIZE = 768
L3 = 512
AXES = ("wide", "narrow")
L1 = 128
L2 = 256
S1 = 2
S2 = 1
S3 = 1

norm_eps = 1e-05
gelu_root = 0.7978845608028654
gelu_cube = 0.044715

MESH = pl.DeviceIdType.MESH
HBM = pl.BlockSpec(memory_space=pltpu.HBM)
VMEM = pl.BlockSpec(memory_space=pltpu.VMEM)
VMEM_LIMIT = 63 * 1024 * 1024
f32 = jnp.float32
bf16 = jnp.bfloat16

ROWS_DEV = 1024
CHIP_ROWS = 2048
HALF = 384
NN = (((1,), (0,)), ((), ()))
NT = (((1,), (1,)), ((), ()))
TN = (((0,), (0,)), ((), ()))


def dot(a, b, dims=NN):
    return lax.dot_general(a, b, dims, preferred_element_type=f32)


def gelu_both(v):
    sq = v * v
    t = jnp.tanh(v * (gelu_root + gelu_root * gelu_cube * sq))
    up = 0.5 + 0.5 * t
    slope = up + 0.5 * v * (1.0 - t * t) * (gelu_root + 3.0 * gelu_root * gelu_cube * sq)
    return v * up, slope


def norm_rows(x):
    mean = jnp.mean(x, axis=-1, keepdims=True)
    cen = x - mean
    inv = lax.rsqrt(jnp.mean(cen * cen, axis=-1, keepdims=True) + norm_eps)
    return cen * inv, inv


class Place:
    def __init__(self):
        w = lax.axis_index(AXES[0])
        n = lax.axis_index(AXES[1])
        self.w, self.n = w, n
        self.z, self.c = w // 2, w % 2
        self.nx = n + 1 - 2 * (n % 2)
        self.ny = (n + 2) % 4
        self.nd = 3 - n
        self.xdev = (w, self.nx)
        self.ydev = (w, self.ny)
        self.sib = (self.z * 2 + 1 - self.c, n)

    def zpos(self, i):
        return (self.z + i) % 4

    def zdev(self, zz):
        return (zz * 2 + self.c, self.n)

    def near(self):
        return [self.xdev, self.ydev, self.sib] + [self.zdev(self.zpos(i)) for i in (1, 2, 3)]


def greet(devs):
    bar = pltpu.get_barrier_semaphore()
    for dev in devs:
        pl.semaphore_signal(bar, inc=1, device_id=dev, device_id_type=MESH)
    pl.semaphore_wait(bar, len(devs))


def remote(src, dst, ssem, rsem, dev):
    return pltpu.make_async_remote_copy(
        src_ref=src, dst_ref=dst, send_sem=ssem, recv_sem=rsem, device_id=dev, device_id_type=MESH
    )


def everyone(me, fn):
    @pl.loop(1, 32)
    def _(j):
        t = (me + j) % 32
        fn(t, (me + 32 - j) % 32, (t // 4, t % 4))


def spread(s_all, rows, width, count, base):
    n = len(rows)
    parts = jnp.concatenate([s_all[:, r, :] for r in rows], axis=0).astype(bf16)
    q = lax.broadcasted_iota(jnp.int32, (8, 32 * n), 1)
    h = lax.broadcasted_iota(jnp.int32, (8, 32 * n), 0) + base
    piece = n * (q & 31) + (q >> 5)
    lane = lax.broadcasted_iota(jnp.int32, (128, 8 * width), 0)
    to = lax.broadcasted_iota(jnp.int32, (128, 8 * width), 1)
    out = jnp.zeros((8, 8 * width), f32)
    for pos in range(8):
        pick = jnp.where(piece == 8 * h + pos, 1.0, 0.0).astype(bf16)
        move = jnp.where((to == width * pos + lane) & (lane < width), 1.0, 0.0).astype(bf16)
        out = out + dot(dot(pick, parts).astype(bf16), move)
    return out[0:count]


def spread_narrow(s_all, vec):
    dev = lax.broadcasted_iota(jnp.int32, (32, D), 0)
    owner = (lax.broadcasted_iota(jnp.int32, (32, D), 1) * 2731) >> 16
    lane = lax.broadcasted_iota(jnp.int32, (128, D), 0)
    to = lax.broadcasted_iota(jnp.int32, (128, D), 1)
    move = jnp.where(to - 24 * ((to * 2731) >> 16) == lane, 1.0, 0.0).astype(bf16)
    for i in range(7):
        wide = dot(s_all[:, i, :].astype(bf16), move)
        vec[i : i + 1] = jnp.sum(jnp.where(owner == dev, wide, 0.0), axis=0, keepdims=True)
    vec[7:8] = jnp.zeros((1, D), f32)


class Gather:
    def __init__(self, pc, sems):
        self.pc = pc
        self.zs, self.zr, self.xs, self.xr, self.ys, self.yr, self.ds, self.dr, self.ls = sems

    def zcopy(self, k, src, buf, i, sender=None):
        pc = self.pc
        zz = pc.z if sender is None else sender
        return remote(src, buf.at[zz, :, pc.n], self.zs.at[k, i], self.zr.at[k, zz], pc.zdev(pc.zpos(i)))

    def zsend(self, k, src, buf):
        for i in (1, 2, 3):
            self.zcopy(k, src, buf, i).start()
        self.own(k, src, buf).start()

    def own(self, k, src, buf):
        return pltpu.make_async_copy(src, buf.at[self.pc.z, :, self.pc.n], self.ls.at[k])

    def xcopy(self, k, buf, zz, src=None, col=None):
        pc = self.pc
        col = pc.n if col is None else col
        slot = buf.at[zz, :, col]
        return remote(slot if src is None else src, slot, self.xs.at[k, zz], self.xr.at[k, zz], pc.xdev)

    def ycopy(self, k, buf, zz, src=None, col=None):
        pc = self.pc
        col = pc.n if col is None else col
        slot = buf.at[zz, :, col]
        return remote(slot if src is None else src, slot, self.ys.at[k, zz], self.yr.at[k, zz], pc.ydev)

    def col(self, k, src, buf, i):
        pc = self.pc
        zz = pc.zpos(i)
        if i:
            self.zcopy(k, src, buf, i, sender=zz).wait_recv()
        s = None if i else src
        self.xcopy(k, buf, zz, s).start()
        self.ycopy(k, buf, zz, s).start()

    def dcopy(self, k, buf, zz):
        pc = self.pc
        if zz < 2:
            slot, dev = buf.at[zz, :, pc.nx], pc.ydev
        else:
            slot, dev = buf.at[zz, :, pc.ny], pc.xdev
        return remote(slot, slot, self.ds.at[k, zz], self.dr.at[k, zz], dev)

    def diag(self, k, buf, zz):
        pc = self.pc
        self.xcopy(k, buf, zz, col=pc.nx).wait_recv()
        self.ycopy(k, buf, zz, col=pc.ny).wait_recv()
        self.dcopy(k, buf, zz).start()

    def fin(self, k, src, buf, each=None):
        self.own(k, src, buf).wait()
        for zz in range(4):
            remote(
                buf.at[zz, :, self.pc.nd],
                buf.at[zz, :, self.pc.nd],
                self.ds.at[k, zz],
                self.dr.at[k, zz],
                self.pc.xdev,
            ).wait_recv()
            if each is not None:
                each(zz)

    def sent(self, k, src, buf):
        for i in (1, 2, 3):
            self.zcopy(k, src, buf, i).wait_send()
        for zz in range(4):
            self.xcopy(k, buf, zz).wait_send()
            self.ycopy(k, buf, zz).wait_send()
            self.dcopy(k, buf, zz).wait_send()


class LayerFirst:
    def __init__(self, pc, src, buf, cs, cr, us, ur, vs, vr, ls, ps, pr):
        self.pc, self.src, self.buf = pc, src, buf
        self.cs, self.cr, self.us, self.ur, self.vs, self.vr, self.ls = cs, cr, us, ur, vs, vr, ls
        self.ps, self.pr = ps, pr

    def side(self, i, src, slot):
        dev = self.pc.xdev if i in (0, 3) else self.pc.ydev
        return remote(src, slot, self.cs.at[i], self.cr.at[i], dev)

    def local(self):
        return pltpu.make_async_copy(self.src, self.buf.at[self.pc.z, :, self.pc.n], self.ls)

    def first(self):
        pc = self.pc
        self.local().start()
        for i in (0, 1):
            self.side(i, self.src, self.buf.at[pc.z, :, pc.n]).start()

    def halves(self):
        pc = self.pc
        a, b = self.buf.at[pc.z, 0, pc.nx], self.buf.at[pc.z, 1, pc.ny]
        return self.side(2, a, a), self.side(3, b, b)

    def second(self):
        for i in (0, 1):
            self.side(i, self.src, self.buf.at[self.pc.z, :, self.pc.n]).wait_recv()
        for cp in self.halves():
            cp.start()

    def up(self, r):
        return remote(self.buf.at[r], self.buf.at[r], self.us.at[r], self.ur.at[r], self.pc.zdev((self.pc.z + 1) % 4))

    def down(self, r):
        return remote(self.buf.at[r], self.buf.at[r], self.vs.at[r], self.vr.at[r], self.pc.zdev((self.pc.z + 3) % 4))

    def swap(self, r):
        return remote(self.buf.at[r], self.buf.at[r], self.ps.at[r], self.pr.at[r], self.pc.sib)

    def third(self):
        z = self.pc.z
        for cp in self.halves():
            cp.wait_recv()
        self.local().wait()

        @pl.when(z < 3)
        def _():
            self.up(z).start()

        @pl.when(z > 0)
        def _():
            self.down(z).start()

        self.swap(z).start()

    def level(self, k):
        z = self.pc.z

        @pl.when(z >= k)
        def _():
            self.up(z - k).wait_recv()

            @pl.when(z < 3)
            def _():
                self.up(z - k).start()

            self.swap(z - k).start()

        @pl.when(z + k <= 3)
        def _():
            self.down(z + k).wait_recv()

            @pl.when(z > 0)
            def _():
                self.down(z + k).start()

            self.swap(z + k).start()

    def finish(self):
        z = self.pc.z
        for i in (0, 1):
            self.side(i, self.src, self.buf.at[self.pc.z, :, self.pc.n]).wait_send()
        for cp in self.halves():
            cp.wait_send()
        for r in range(4):

            @pl.when((z < 3) & (z >= r))
            def _():
                self.up(r).wait_send()

            @pl.when((z > 0) & (z <= r))
            def _():
                self.down(r).wait_send()

            self.swap(r).wait()


def gather_sems(k):
    dma = pltpu.SemaphoreType.DMA
    return [dma((k, 4))] * 8 + [dma((k,))]


def join_pair(stage, dst_of, rows_of):
    @pl.loop(0, 4)
    def _(zz):
        for cc in range(2):
            for nn in (0, 2):
                one = stage[zz, cc, nn].astype(f32)
                two = stage[zz, cc, nn + 1].astype(f32)
                row = pl.multiple_of(zz * 192 + cc * 96 + nn * 24, 16)
                for e in rows_of:
                    both = jnp.concatenate(
                        [one[24 * e : 24 * e + 24], two[24 * e : 24 * e + 24]], axis=0
                    )
                    dst_of(e, pl.ds(row, 48), both.astype(bf16))


def k1_kernel(
    s_in, tok, dense, logit, vo, ff,
    ovo, gd, gl, ef, nrm_o, val_o, hid_o, slo_o, atl_o, atm_o, ats_o, wa_o, la_o, mix_o, vv_o, vec, eb,
    s_all, db, lb, vb, mvo, md, ml, mf, tokv, nrm, val, vst, vv, wst, lst, wv, lv, hidv, slov, atlv, atmv, atsv, mixv,
    zs, zr, xs, xr, ys, yr, ds, dr, ls, tsem, osem, wsem, lsem, ssem, rsem, msem,
    cs, cr, us, ur, vs, vr, cls, ps, pr, vss, vsr, es, er,
):
    pc = Place()
    c = pc.c
    g = Gather(pc, (zs, zr, xs, xr, ys, yr, ds, dr, ls))
    o = 1 - c
    me = pc.w * 4 + pc.n
    tcopies = []
    trows = [pl.ds(pl.multiple_of(to + c * 512, 512), 512) for to in (0, 1024)]
    for i, at in enumerate((512, 0)):
        tcopies.append(pltpu.make_async_copy(tok.at[pl.ds(at, 512)], tokv.at[trows[i]], tsem.at[i]))
    for cp in tcopies:
        cp.start()
    bar = pltpu.get_barrier_semaphore()
    everyone(me, lambda t, f, dev: pl.semaphore_signal(bar, inc=1, device_id=dev, device_id_type=MESH))
    pl.semaphore_wait(bar, 31)
    gives = [
        (vo.at[o], mvo.at[c]),
        (dense.at[pl.ds(3 * o, 3)], md.at[:, c]),
        (ff.at[o], mf.at[:, c]),
        (logit.at[pl.ds(3 * o, 3)], ml.at[:, c]),
    ]
    for i, at in enumerate((512, 0)):
        gives.append((tok.at[pl.ds(at, 512)], tokv.at[trows[i]]))
    rems = [remote(give, slot, es.at[i], er.at[i], pc.sib) for i, (give, slot) in enumerate(gives)]
    for cp in rems[0:4]:
        cp.start()
    everyone(me, lambda t, f, dev: remote(s_in, s_all.at[me], vss.at[t], vsr.at[me], dev).start())
    mvo[c] = vo[c]
    md[:, c] = dense[pl.ds(3 * c, 3)]
    mf[:, c] = ff[c]
    ml[:, c] = logit[pl.ds(3 * c, 3)]
    small = lambda t, f, dev: remote(s_in, s_all.at[f], vss.at[t], vsr.at[f], dev)
    for cp in rems[4:6]:
        cp.start()
    for cp in rems[0:4]:
        cp.wait()

    vo_args = (0, mvo, ovo.at[c])
    dd = lambda p: (1 + 2 * p, md.at[p], gd.at[p])
    ll = lambda p: (2 + 2 * p, ml.at[p], gl.at[p])
    fb = (7, mf.at[1], ef.at[c, 1])
    fa = LayerFirst(pc, mf.at[0], ef.at[c, 0], cs, cr, us, ur, vs, vr, cls, ps, pr)

    g.zsend(*vo_args)
    g.zsend(*dd(0))
    g.col(*vo_args, 0)
    g.col(*dd(0), 0)
    fa.first()
    g.col(*ll(0), 0)
    s_all[me] = s_in[...]

    for i in (1, 2, 3):
        g.col(*vo_args, i)
    g.zsend(*ll(0))
    fa.second()
    g.col(*dd(1), 0)

    def arrived(t, f, dev):
        small(t, f, dev).wait_send()
        small(t, f, dev).wait_recv()

    everyone(me, arrived)
    spread_narrow(s_all, vec)
    db[0:6] = spread(s_all, (11, 12, 13), 96, 6, 6 * c)
    lb[0:6] = spread(s_all, (8, 9, 10), 64, 6, 6 * c)
    eb[...] = spread(s_all, (7,), 96, 4, 0)
    vb[0:1] = jnp.where(c == 0, vec[2:3, 0:HALF], vec[2:3, HALF:D])

    for cp in tcopies + rems[4:6]:
        cp.wait()

    @pl.loop(0, 8)
    def _(b):
        rows = pl.ds(pl.multiple_of(b * 256, 256), 256)
        unit, _ = norm_rows(tokv[rows].astype(f32))
        nrm[rows] = (unit * vec[0:1] + vec[1:2]).astype(bf16)

    nrm_copy = pltpu.make_async_copy(nrm, nrm_o, tsem.at[4])
    nrm_copy.start()
    for i in (1, 2, 3):
        g.col(*dd(0), i)
    g.zsend(*dd(1))
    fa.third()
    for zz in range(4):
        g.diag(vo_args[0], vo_args[2], zz)
    g.col(*ll(1), 0)
    for i in (1, 2, 3):
        g.col(*ll(0), i)
    g.zsend(*ll(1))
    for zz in (0, 2, 1, 3):
        g.diag(dd(0)[0], dd(0)[2], zz)
    g.fin(*vo_args)
    vo_load = pltpu.make_async_copy(ovo.at[c], vst, tsem.at[5])
    vo_load.start()
    vo_swap = remote(ovo.at[c], ovo.at[c], ssem.at[0], rsem.at[0], pc.sib)
    vo_swap.start()
    vo_load.wait()

    def put_v(e, rows, x):
        vv[rows] = x

    join_pair(vst, put_v, (0,))

    @pl.loop(0, 4)
    def _(b):
        rows = pl.ds(pl.multiple_of(b * 512, 512), 512)
        val[rows] = (dot(nrm[rows], vv[...]) + vb[0:1]).astype(bf16)

    val_copy = pltpu.make_async_copy(val, val_o, tsem.at[6])
    val_copy.start()
    vv_copy = pltpu.make_async_copy(vv, vv_o, tsem.at[5])
    vv_copy.start()
    g.col(*dd(1), 1)
    for zz in (0, 2, 1, 3):
        g.diag(ll(0)[0], ll(0)[2], zz)
    g.fin(*dd(0))
    g.fin(*ll(0))

    lane = lax.broadcasted_iota(jnp.int32, (1, 128), 1)
    keeps = [(lane < HEAD_DIM).astype(bf16), (lane >= HEAD_DIM).astype(bf16)]

    def softmax(s):
        m = jnp.max(s, axis=-1, keepdims=True)
        ex = jnp.exp(s - m)
        return (ex / jnp.sum(ex, axis=-1, keepdims=True)).astype(bf16)

    @pl.loop(0, 3)
    def _(p):
        q = p + 1
        more = p < 2
        ka, kb = 1 + 2 * q, 2 + 2 * q

        def on_a(fn):
            @pl.when(more)
            def _():
                fn(ka, md.at[q % 3], gd.at[q % 3])

            @pl.when(jnp.logical_not(more))
            def _():
                fn(*fb)

        def on_b(fn):
            @pl.when(more)
            def _():
                fn(kb, ml.at[q % 3], gl.at[q % 3])

        def on_next(fn):
            @pl.when(p == 0)
            def _():
                fn(5, md.at[2], gd.at[2])

            @pl.when(p == 1)
            def _():
                fn(*fb)

        def on_next_b(fn):
            @pl.when(p == 0)
            def _():
                fn(6, ml.at[2], gl.at[2])

        def tick(pos):
            if pos == 0:
                on_next(lambda k, s, b: g.col(k, s, b, 0))
                on_a(lambda k, s, b: g.col(k, s, b, 2))
                on_a(lambda k, s, b: g.col(k, s, b, 3))
                on_next(g.zsend)
            elif pos == 1:
                on_b(lambda k, s, b: g.col(k, s, b, 1))
                on_b(lambda k, s, b: g.col(k, s, b, 2))
            elif pos == 2:
                on_b(lambda k, s, b: g.col(k, s, b, 3))
                on_next_b(lambda k, s, b: g.col(k, s, b, 0))
            elif pos == 3:
                on_a(lambda k, s, b: g.diag(k, b, 0))
                on_a(lambda k, s, b: g.diag(k, b, 2))
                for r in range(3):

                    @pl.when(p == r)
                    def _():
                        fa.level(r + 1)
            elif pos == 4:
                on_a(lambda k, s, b: g.diag(k, b, 1))
                on_a(lambda k, s, b: g.diag(k, b, 3))
                on_next_b(g.zsend)
            elif pos == 5:
                on_next(lambda k, s, b: g.col(k, s, b, 1))
                on_b(lambda k, s, b: g.diag(k, b, 0))
            elif pos == 6:
                on_b(lambda k, s, b: g.diag(k, b, 2))
            elif pos == 7:
                on_b(lambda k, s, b: g.diag(k, b, 1))
                on_b(lambda k, s, b: g.diag(k, b, 3))

        wload = pltpu.make_async_copy(gd.at[p], wst, tsem.at[7])
        lload = pltpu.make_async_copy(gl.at[p], lst, tsem.at[8])
        wload.start()
        lload.start()
        wcopy = lambda r: pltpu.make_async_copy(wv, wa_o.at[pl.ds(2 * r, 2)], wsem)
        lcopy = lambda r: pltpu.make_async_copy(lv, la_o.at[pl.ds(2 * r, 2)], lsem)

        @pl.when(p > 0)
        def _():
            wcopy(p - 1).wait()
            lcopy(p - 1).wait()

        wload.wait()

        def put_w(e, rows, x):
            wv[e, rows] = x

        def put_l(e, rows, x):
            lv[e, rows] = x

        join_pair(wst, put_w, (0, 1))
        lload.wait()
        join_pair(lst, put_l, (0, 1))
        wcopy(p).start()
        lcopy(p).start()
        lanes = pl.ds(pl.multiple_of(p * 128, 128), 128)

        def out_copies(e, d, long, h):
            row = d * 512 if long else 1024 + d * 512
            rows = pl.ds(row, 512)
            cps = [
                pltpu.make_async_copy(hidv.at[e], hid_o.at[h, rows], osem.at[e, 0]),
                pltpu.make_async_copy(slov.at[e], slo_o.at[h, rows], osem.at[e, 1]),
            ]
            if long:
                cps.append(pltpu.make_async_copy(atlv.at[e], atl_o.at[h, pl.ds(d * 512, 512)], osem.at[e, 2]))
            else:
                part = pl.ds(d * 256, 256)
                cps.append(pltpu.make_async_copy(atmv.at[e], atm_o.at[h, part], osem.at[e, 3]))
                cps.append(pltpu.make_async_copy(atsv.at[e], ats_o.at[h, part], osem.at[e, 4]))
            return cps

        pos = 0
        for d in range(2):
            for long in (True, False):
                row = d * 512 if long else 1024 + d * 512
                rows = slice(row, row + 512)
                mixed = None
                for e in range(2):
                    h = 2 * p + e
                    pre = dot(nrm[rows], wv[e]) + db[pl.ds(h, 1)]
                    hid, slo = gelu_both(pre)
                    if d == 0 and long:

                        @pl.when(p > 0)
                        def _():
                            for cp in out_copies(e, 1, False, h):
                                cp.wait()
                    else:
                        for cp in out_copies(e, d if not long else d - 1, not long, h):
                            cp.wait()
                    hidv[e] = hid.astype(bf16)
                    slov[e] = slo.astype(bf16)
                    lbias = lb[pl.ds(h, 1)]
                    vpair = val[rows, lanes] * keeps[e]
                    if long:
                        att = softmax(dot(hidv[e], lv[e]) + lbias)
                        atlv[e] = att
                        m = dot(att, vpair)
                    else:
                        short = softmax(dot(hidv[e, 0:256], lv[e, :, 0:128]) + lbias[:, 0:128])
                        mid = softmax(dot(hidv[e, 256:512], lv[e, :, 0:256]) + lbias[:, 0:256])
                        atsv[e] = short
                        atmv[e] = mid
                        m = jnp.concatenate(
                            [
                                dot(short[0:128], vpair[0:128]),
                                dot(short[128:256], vpair[128:256]),
                                dot(mid, vpair[256:512]),
                            ],
                            axis=0,
                        )
                    mixed = m if mixed is None else mixed + m
                    for cp in out_copies(e, d, long, h):
                        cp.start()
                    tick(pos)
                    pos += 1
                mixv[rows, lanes] = mixed.astype(bf16)

        @pl.when(more)
        def _():
            g.fin(ka, md.at[q % 3], gd.at[q % 3])

        on_b(g.fin)

        @pl.when(p == 2)
        def _():
            for e in range(2):
                for cp in out_copies(e, 1, False, 2 * p + e):
                    cp.wait()
            wcopy(p).wait()
            lcopy(p).wait()

    fb_swap = lambda r: remote(ef.at[c, 1, r], ef.at[c, 1, r], ssem.at[4 + r], rsem.at[4 + r], pc.sib)
    swaps = [vo_swap]
    for i, (start, to) in enumerate(((0, 512), (1024, 0))):
        mine = pltpu.make_async_copy(
            mixv.at[pl.ds(start + c * 512, 512)], mix_o.at[c, pl.ds(to, 512)], msem.at[i]
        )
        mine.start()
        other = remote(
            mixv.at[pl.ds(start + o * 512, 512)], mix_o.at[c, pl.ds(to, 512)], ssem.at[2 + i], rsem.at[2 + i], pc.sib
        )
        other.start()
        swaps += [mine, other]
    g.fin(*fb, each=lambda r: fb_swap(r).start())
    for cp in swaps + [nrm_copy, val_copy, vv_copy] + [fb_swap(r) for r in range(4)]:
        cp.wait()
    fa.finish()
    g.sent(*vo_args)
    for p in range(3):
        g.sent(*dd(p))
        g.sent(*ll(p))
    g.sent(*fb)


def k1_call(s_in, tok, dense, logit, vo, ff):
    sds = jax.ShapeDtypeStruct
    dma = pltpu.SemaphoreType.DMA
    return pl.pallas_call(
        k1_kernel,
        out_shape=(
            sds((2, 4, 2, 4, 48, HALF), bf16),
            sds((3, 4, 2, 4, 48, D), bf16),
            sds((3, 4, 2, 4, 48, L3), bf16),
            sds((2, 2, 4, 2, 4, 48, D), bf16),
            sds((CHIP_ROWS, D), bf16),
            sds((CHIP_ROWS, HALF), bf16),
            sds((6, CHIP_ROWS, HIDDEN_SIZE), bf16),
            sds((6, CHIP_ROWS, HIDDEN_SIZE), bf16),
            sds((6, 1024, L3), bf16),
            sds((6, 512, L2), bf16),
            sds((6, 512, L1), bf16),
            sds((6, D, HIDDEN_SIZE), bf16),
            sds((6, HIDDEN_SIZE, L3), bf16),
            sds((2, ROWS_DEV, HALF), bf16),
            sds((D, HALF), bf16),
            sds((8, D), f32),
            sds((4, D), f32),
        ),
        in_specs=[VMEM, HBM] + [VMEM] * 4,
        out_specs=(HBM,) * 15 + (VMEM,) * 2,
        scratch_shapes=[
            pltpu.VMEM((32, 16, 128), f32),
            pltpu.VMEM((8, HIDDEN_SIZE), f32),
            pltpu.VMEM((8, L3), f32),
            pltpu.VMEM((8, HALF), f32),
            pltpu.VMEM((2, 48, HALF), bf16),
            pltpu.VMEM((3, 2, 48, D), bf16),
            pltpu.VMEM((3, 2, 48, L3), bf16),
            pltpu.VMEM((2, 2, 48, D), bf16),
            pltpu.VMEM((CHIP_ROWS, D), bf16),
            pltpu.VMEM((CHIP_ROWS, D), bf16),
            pltpu.VMEM((CHIP_ROWS, HALF), bf16),
            pltpu.VMEM((4, 2, 4, 48, HALF), bf16),
            pltpu.VMEM((D, HALF), bf16),
            pltpu.VMEM((4, 2, 4, 48, D), bf16),
            pltpu.VMEM((4, 2, 4, 48, L3), bf16),
            pltpu.VMEM((2, D, HIDDEN_SIZE), bf16),
            pltpu.VMEM((2, HIDDEN_SIZE, L3), bf16),
            pltpu.VMEM((2, 512, HIDDEN_SIZE), bf16),
            pltpu.VMEM((2, 512, HIDDEN_SIZE), bf16),
            pltpu.VMEM((2, 512, L3), bf16),
            pltpu.VMEM((2, 256, L2), bf16),
            pltpu.VMEM((2, 256, L1), bf16),
            pltpu.VMEM((CHIP_ROWS, HALF), bf16),
        ]
        + gather_sems(8)
        + [dma((9,)), dma((2, 5)), dma, dma, dma((8,)), dma((8,)), dma((2,))]
        + [dma((4,))] * 6
        + [dma, dma((4,)), dma((4,)), dma((32,)), dma((32,)), dma((6,)), dma((6,))],
        compiler_params=pltpu.CompilerParams(
            collective_id=1, has_side_effects=True, vmem_limit_bytes=VMEM_LIMIT
        ),
        name="k1_attention",
    )(s_in, tok, dense, logit, vo, ff)


def prepare(tokens, attn_gain, attn_shift, dense_weight, dense_bias, logit_weight, logit_bias, value_weight,
            value_bias, output_weight, output_bias, feed_gain, feed_shift, expand_weight, expand_bias,
            reduce_weight, reduce_bias):
    narrow_rows = jnp.stack([attn_gain, attn_shift, value_bias, output_bias, feed_gain, feed_shift, reduce_bias])
    wide_rows = [(expand_bias.reshape(1, 96), 32), (logit_bias.reshape(3, 64), 64), (dense_bias.reshape(3, 96), 32)]
    small = jnp.concatenate(
        [jnp.pad(narrow_rows, ((0, 0), (0, 104)))] + [jnp.pad(v, ((0, 0), (0, pad))) for v, pad in wide_rows]
    )
    small = jnp.pad(small, ((0, 2), (0, 0))).astype(f32)
    dense = dense_weight.reshape(6, 48, D)
    logit = logit_weight.reshape(6, 48, L3)
    vo = jnp.stack([value_weight.reshape(24, 2, HALF), output_weight.reshape(24, 2, HALF)]).transpose(2, 0, 1, 3)
    vo = vo.reshape(2, 48, HALF)
    ff = jnp.stack(
        [expand_weight.reshape(24, 4, D).transpose(1, 0, 2).reshape(2, 48, D), reduce_weight.reshape(2, 48, D)]
    )
    return small, tokens, dense, logit, vo, ff


def k2_kernel(
    x, cot, counts, mix, ovo, ef, vec, eb,
    lay_o, gres_o, gmix_o, def_o, do_o, sums_o,
    ev, rv, ow, inner, ge, n2, gf, ga, acc, dst, rsem, dsem, osem,
):
    oloads = []
    for half in range(2):
        lanes = pl.ds(half * HALF, HALF)
        oloads.append(pltpu.make_async_copy(ovo.at[half], dst.at[0, :, :, :, :, lanes], osem.at[half]))
    loads = [pltpu.make_async_copy(ef.at[0, f], dst.at[1 - f], dsem.at[1 - f]) for f in range(2)]
    for cp in oloads:
        cp.start()
    loads[0].start()
    rloads = []
    for f in range(2):
        for j in range(4):
            rloads.append(
                pltpu.make_async_copy(ef.at[1, f, j], rv.at[j, :, :, pl.ds(48 * f, 48)], rsem.at[f, j])
            )
    for cp in rloads:
        cp.start()

    def put_o(e, rows, v):
        ow[rows] = v

    for cp in oloads:
        cp.wait()
    join_pair(dst.at[0], put_o, (1,))
    loads[1].start()
    for f in range(2):

        def put_e(e, rows, v):
            ev[2 * f + e, rows] = v

        loads[f].wait()
        join_pair(dst.at[1 - f], put_e, (0, 1))
    for cp in rloads:
        cp.wait()
    fg, fs = vec[4:5], vec[5:6]
    sums_o[...] = jnp.zeros_like(sums_o)

    @pl.loop(0, 4)
    def _(b):
        rows = pl.ds(pl.multiple_of(b * 256, 256), 256)
        mixed = jnp.concatenate([mix[0, rows], mix[1, rows]], axis=1)
        res = x[rows].astype(f32) + (dot(mixed, ow[...]) + vec[3:4])
        unit, inv = norm_rows(res)
        n2v = (unit * fg + fs).astype(bf16)
        n2[rows] = n2v
        later = jnp.where(b == 1, counts[0, 1], counts[0, 2])
        low = jnp.where(b == 0, counts[0, 0], later) >= 1
        high = jnp.where(b == 0, counts[0, 0] - 1, later) >= 1
        top = lax.broadcasted_iota(jnp.int32, (256, 1), 0) < L1
        alive = jnp.where(top, jnp.where(low, 1.0, 0.0), jnp.where(high, 1.0, 0.0))
        gout = cot[rows].astype(f32) * alive
        gfb = gout.astype(bf16)
        gf[rows] = gfb
        feed = None
        gn2 = None
        for j in range(4):
            cols = slice(j * D, j * D + D)
            rj = rv[j].reshape(D, D)
            hid, slo = gelu_both(dot(n2v, ev[j]) + eb[j : j + 1])
            hb = hid.astype(bf16)
            inner[rows, cols] = hb
            f_j = dot(hb, rj)
            feed = f_j if feed is None else feed + f_j
            geb = (dot(gfb, rj, NT) * slo).astype(bf16)
            ge[rows, cols] = geb
            g_j = dot(geb, ev[j], NT)
            gn2 = g_j if gn2 is None else gn2 + g_j
        lay_o[rows] = alive * (res + (feed + vec[6:7]))
        q = gn2 * fg
        gres = gout + inv * (
            q - jnp.mean(q, axis=-1, keepdims=True) - unit * jnp.mean(q * unit, axis=-1, keepdims=True)
        )
        gres_o[rows] = gres
        gab = gres.astype(bf16)
        ga[rows] = gab
        gm = dot(gab, ow[...], NT).astype(bf16)
        gmix_o[0, rows] = gm[:, :HALF]
        gmix_o[1, rows] = gm[:, HALF:]
        sums_o[0:1] += jnp.sum(gn2 * unit, axis=0, keepdims=True)
        sums_o[1:2] += jnp.sum(gn2, axis=0, keepdims=True)

    ones = jnp.ones((8, ROWS_DEV), bf16)
    sums_o[2:3] = dot(ones, gf[...])[0:1]
    sums_o[3:4] = dot(ones, ga[...])[0:1]

    def out_copy(t, f):
        return pltpu.make_async_copy(dst.at[f], def_o.at[t, f], dsem.at[f])

    for f in range(2):
        for e in range(2):
            j = 2 * f + e
            sums_o[4 + j : 5 + j] = dot(ones, ge[:, j * D : j * D + D])[0:1]
            acc[e] = dot(n2[...], ge[:, j * D : j * D + D], TN)

        @pl.loop(0, 4)
        def _(zz):
            for i in range(8):
                row = pl.ds(pl.multiple_of(zz * 192 + i * 24, 8), 24)
                both = jnp.concatenate([acc[0, row], acc[1, row]], axis=0)
                dst[f, zz, i // 4, i % 4] = both.astype(bf16)

        out_copy(0, f).start()
    for j in range(4):
        acc[j % 2] = dot(inner[:, j * D : j * D + D], gf[...], TN)
        if j == 0:
            out_copy(0, 0).wait()
            out_copy(0, 1).wait()
        for i in range(8):
            for f in range(2):
                at = i * 96 + f * 48
                dst[f, j, i // 4, i % 4] = acc[j % 2, at : at + 48].astype(bf16)
    for f in range(2):
        out_copy(1, f).start()
    zero = jnp.zeros((24, 128), f32)
    for hh in range(2):
        acc[0, 0:HALF] = dot(mix[hh], ga[...], TN)
        for i in range(16):
            for half in range(2):
                for r in range(3):
                    at = half * HALF + r * 128
                    part = acc[0, i * 24 : i * 24 + 24, at : at + 128]
                    both = jnp.concatenate([zero, part], axis=0).astype(bf16)
                    do_o[half, r, 2 * hh + i // 8, (i // 4) % 2, i % 4] = both
    for f in range(2):
        out_copy(1, f).wait()


def k2_call(x, cot, counts, mix, ovo, ef, vec, eb):
    sds = jax.ShapeDtypeStruct
    dma = pltpu.SemaphoreType.DMA
    return pl.pallas_call(
        k2_kernel,
        out_shape=(
            sds((ROWS_DEV, D), f32),
            sds((ROWS_DEV, D), f32),
            sds((2, ROWS_DEV, HALF), bf16),
            sds((2, 2, 4, 2, 4, 48, D), bf16),
            sds((2, 3, 4, 2, 4, 48, 128), bf16),
            sds((8, D), f32),
        ),
        in_specs=[VMEM, VMEM, pl.BlockSpec(memory_space=pltpu.SMEM), VMEM] + [HBM] * 2 + [VMEM] * 2,
        out_specs=(VMEM, VMEM, VMEM, HBM, VMEM, VMEM),
        scratch_shapes=[
            pltpu.VMEM((4, D, D), bf16),
            pltpu.VMEM((4, 2, 4, 96, D), bf16),
            pltpu.VMEM((D, D), bf16),
            pltpu.VMEM((ROWS_DEV, 4 * D), bf16),
            pltpu.VMEM((ROWS_DEV, 4 * D), bf16),
            pltpu.VMEM((ROWS_DEV, D), bf16),
            pltpu.VMEM((ROWS_DEV, D), bf16),
            pltpu.VMEM((ROWS_DEV, D), bf16),
            pltpu.VMEM((2, D, D), f32),
            pltpu.VMEM((2, 4, 2, 4, 48, D), bf16),
            dma((2, 4)),
            dma((2,)),
            dma((2,)),
        ],
        compiler_params=pltpu.CompilerParams(vmem_limit_bytes=VMEM_LIMIT),
        name="k2_feed",
    )(x, cot, counts, mix, ovo, ef, vec, eb)


class Scatter:
    def __init__(self, pc, sems):
        self.pc = pc
        self.as_, self.ar, self.xs, self.xr, self.ys, self.yr, self.zs, self.zr, self.os, self.or_ = sems

    def acopy(self, k, p5, bufs, zz):
        dev = self.pc.xdev if zz < 2 else self.pc.ydev
        return remote(p5.at[zz, :, self.pc.nd], bufs[0].at[zz], self.as_.at[k, zz], self.ar.at[k, zz], dev)

    def xcopy(self, k, p5, bufs, zz):
        return remote(p5.at[zz, :, self.pc.nx], bufs[1].at[zz], self.xs.at[k, zz], self.xr.at[k, zz], self.pc.xdev)

    def ycopy(self, k, p5, bufs, zz):
        return remote(p5.at[zz, :, self.pc.ny], bufs[2].at[zz], self.ys.at[k, zz], self.yr.at[k, zz], self.pc.ydev)

    def zcopy(self, k, p5, bufs, i):
        zz = self.pc.zpos(i)
        return remote(
            p5.at[zz, :, self.pc.n], bufs[3].at[i - 1], self.zs.at[k, i], self.zr.at[k, i], self.pc.zdev(zz)
        )

    def row(self, k, p5, bufs, zz):
        self.acopy(k, p5, bufs, zz).start()
        (self.xcopy if zz < 2 else self.ycopy)(k, p5, bufs, zz).start()

    def one(self, k, p5, bufs):
        for zz in (0, 2, 1, 3):
            self.acopy(k, p5, bufs, zz).start()
        for zz in (0, 2, 1, 3):
            (self.xcopy if zz < 2 else self.ycopy)(k, p5, bufs, zz).start()

    def twos(self, k, p5, bufs):
        for zz in (0, 2, 1, 3):
            self.two(k, p5, bufs, zz)

    def threes(self, k, p5, bufs):
        for i in (1, 2, 3):
            self.three(k, p5, bufs, i)

    def two(self, k, p5, bufs, zz):
        col = self.pc.ny if zz < 2 else self.pc.nx
        self.acopy(k, p5, bufs, zz).wait_recv()
        p5[zz, :, col] = (p5[zz, :, col].astype(f32) + bufs[0][zz].astype(f32)).astype(bf16)
        (self.ycopy if zz < 2 else self.xcopy)(k, p5, bufs, zz).start()

    def column(self, k, p5, bufs, zz):
        self.xcopy(k, p5, bufs, zz).wait_recv()
        self.ycopy(k, p5, bufs, zz).wait_recv()
        return p5[zz, :, self.pc.n].astype(f32) + bufs[1][zz].astype(f32) + bufs[2][zz].astype(f32)

    def three(self, k, p5, bufs, i):
        zz = self.pc.zpos(i)
        p5[zz, :, self.pc.n] = self.column(k, p5, bufs, zz).astype(bf16)
        self.zcopy(k, p5, bufs, i).start()

    def outs(self, k, st, out):
        c = self.pc.c
        return (
            pltpu.make_async_copy(st.at[c], out, self.os.at[k, 1]),
            remote(st.at[1 - c], out, self.os.at[k, 0], self.or_.at[k], self.pc.sib),
        )

    def four(self, k, p5, bufs, st, out):
        total = self.column(k, p5, bufs, self.pc.z)
        for i in (1, 2, 3):
            self.zcopy(k, p5, bufs, i).wait_recv()
            total = total + bufs[3][i - 1].astype(f32)
        st[...] = total
        for cp in self.outs(k, st, out):
            cp.start()

    def sent(self, k, p5, bufs):
        for zz in range(4):
            self.acopy(k, p5, bufs, zz).wait_send()
            self.xcopy(k, p5, bufs, zz).wait_send()
            self.ycopy(k, p5, bufs, zz).wait_send()
        for i in (1, 2, 3):
            self.zcopy(k, p5, bufs, i).wait_send()


def k3_kernel(
    def_in, do_in, nrm_i, val_i, gmix, hid_i, slo_i, atl_i, atm_i, ats_i, wa_i, la_i, vv_i, tok, gres, vec,
    tg_o, od, ol, ofe, ovo, db_o, lb_o, vb_o, ag_o,
    nrm, val, gm, gn, hid, slo, atl, atm, ats, gsl, gsm, gd, wv, lv, dwf, vsb, vv, own,
    pd, pll, pv, ad, xd, yd, zd, al, xl, yl, zl, av, xv, yv, zv, std, stl, stv,
    as_, ar, xs, xr, ys, yr, zs, zr, os_, or_, lsem, ssem, rsem, gs_, gr_, free, hsem, fsem, dsem,
    fss, fsr,
):
    pc = Place()
    c = pc.c
    o = 1 - c
    s = Scatter(pc, (as_, ar, xs, xr, ys, yr, zs, zr, os_, or_))
    copy = pltpu.make_async_copy
    first = [copy(nrm_i, nrm, lsem.at[0]), copy(val_i, val, lsem.at[1]), copy(vv_i, vv, lsem.at[2])]
    for i, (at, to) in enumerate(((512, 0), (0, 1024))):
        first.append(copy(gmix.at[c, pl.ds(at, 512)], gm.at[pl.ds(pl.multiple_of(to + c * 512, 512), 512)], lsem.at[4 + i]))
    for cp in first:
        cp.start()

    def att_loads(h):
        return [copy(atl_i.at[h], atl, hsem.at[0]), copy(atm_i.at[h], atm, hsem.at[1]), copy(ats_i.at[h], ats, hsem.at[2])]

    hid_load = lambda h: copy(hid_i.at[h], hid, hsem.at[3])
    w_load = lambda h: copy(wa_i.at[h], wv, hsem.at[4])
    l_load = lambda h: copy(la_i.at[h], lv, hsem.at[5])
    slo_load = lambda h, b: copy(slo_i.at[h, pl.ds(b * 512, 512)], slo.at[b % 2], hsem.at[6 + b % 2])
    for cp in att_loads(0) + [hid_load(0), l_load(0), slo_load(0, 0), slo_load(0, 1), w_load(0)]:
        cp.start()
    order = [(f, zz) for f in (1, 0) for zz in (0, 2, 1, 3)]
    own_load = lambda i: copy(def_in.at[(c,) + order[i]], own.at[i % 2], fsem.at[i % 2])
    own_load(0).start()
    own_load(1).start()

    greet(pc.near())
    fswaps = []
    for i, (f, zz) in enumerate(order):
        fswaps.append(remote(def_in.at[o, f, zz], pd.at[f, zz], fss.at[i], fsr.at[i], pc.sib))
    swaps = [None, None]
    swaps.append(remote(do_in.at[o], pv, ssem.at[2], rsem.at[2], pc.sib))
    for i, (at, to) in enumerate(((512, 0), (0, 1024))):
        swaps.append(
            remote(
                gmix.at[o, pl.ds(at, 512)],
                gm.at[pl.ds(pl.multiple_of(to + c * 512, 512), 512)],
                ssem.at[3 + i],
                rsem.at[3 + i],
                pc.sib,
            )
        )
    for cp in fswaps[0:4] + swaps[3:5] + fswaps[4:8] + swaps[2:3]:
        cp.start()

    def d_args(k):
        slot = k % 3
        return pd.at[slot], (ad.at[k], xd.at[k], yd.at[k], zd.at[k])

    def l_args(p):
        return pll.at[p % 2], (al.at[p], xl.at[p], yl.at[p], zl.at[p])

    def v_args(p):
        return pv.at[p], (av.at[p], xv.at[p], yv.at[p], zv.at[p])

    gn[...] = jnp.zeros_like(gn)
    gsm[...] = jnp.zeros_like(gsm)


    def core_sum(i):
        f, zz = order[i]
        fswaps[i].wait()
        own_load(i).wait()
        pd[f, zz] = (pd[f, zz].astype(f32) + own[i % 2].astype(f32)).astype(bf16)
        if i < 6:
            own_load(i + 2).start()
        s.row(f, *d_args(f), zz)

    dloads = []
    for r in range(3):
        for zz in range(4):
            to = pl.ds(HALF * (zz % 2) + 128 * r, 128)
            dloads.append(copy(do_in.at[c, r, zz], own.at[zz // 2, :, :, :, to], dsem.at[r, zz]))

    def other_half():
        for i in range(4, 8):
            core_sum(i)
        for cp in dloads:
            cp.start()

    def dloads_done():
        for cp in swaps[2:3] + dloads:
            cp.wait()

    for i in range(4):
        core_sum(i)
    swaps[3].wait()
    swaps[4].wait()
    for cp in first:
        cp.wait()

    lane = lax.broadcasted_iota(jnp.int32, (1, 128), 1)
    keeps = [(lane < HEAD_DIM).astype(bf16), (lane >= HEAD_DIM).astype(bf16)]
    ones = jnp.ones((8, 1024), bf16)

    def score_grad(att, g):
        a = att.astype(f32)
        t = a * g
        return (t - a * jnp.sum(t, axis=-1, keepdims=True)).astype(bf16)

    def put_pair(p5, half, e, width):
        @pl.loop(0, 2)
        def _(zi):
            for i in range(8):
                row = pl.ds(pl.multiple_of(zi * 192 + i * 24, 8), 24)
                part = dwf[row, 0:width]
                if e == 0:
                    both = jnp.concatenate([part, part], axis=0)
                else:
                    old = p5[2 * half + zi, i // 4, i % 4].astype(f32)
                    both = jnp.concatenate([old[0:24], part], axis=0)
                p5[2 * half + zi, i // 4, i % 4] = both.astype(bf16)

    @pl.loop(0, 3)
    def _(p):
        lanes = pl.ds(pl.multiple_of(p * 128, 128), 128)
        begin = p == 0
        later = p > 0
        kd = p + 2
        dslot = kd % 3

        def on_a(fn):
            fn(kd - 1, *d_args(kd - 1))

        def on_b(fn):
            @pl.when(begin)
            def _():
                fn(0, *d_args(0))

            @pl.when(later)
            def _():
                fn(5 + (p + 2) % 3, *l_args((p + 2) % 3))

        def on_first(*fns):
            for r, fn in enumerate(fns):
                if fn is not None:
                    pl.when(p == r)(fn)

        def on_v(fn):
            @pl.when(later)
            def _():
                fn(8 + (p + 2) % 3, *v_args((p + 2) % 3))

        def four_a():
            @pl.when(begin)
            def _():
                s.four(1, *d_args(1), std.at[1], ofe.at[c, 1])

            @pl.when(p == 2)
            def _():
                for cp in s.outs(0, std.at[0], ofe.at[c, 0]):
                    cp.wait()

            @pl.when(later)
            def _():
                s.four(kd - 1, *d_args(kd - 1), std.at[(kd - 1) % 3], od.at[3 * c + (p + 2) % 3])

        def four_b():
            @pl.when(begin)
            def _():
                s.four(0, *d_args(0), std.at[0], ofe.at[c, 0])

            @pl.when(later)
            def _():
                r = (p + 2) % 3
                s.four(5 + r, *l_args(r), stl.at[r], ol.at[3 * c + r])

        def four_v():
            @pl.when(later)
            def _():
                r = (p + 2) % 3
                s.four(8 + r, *v_args(r), stv.at[r], ovo.at[r, c])

        def value_part():
            for half in range(2):
                cols = slice(half * HALF, half * HALF + HALF)
                dwf[:, 0:128] = dot(nrm[:, cols], gm[:, lanes], TN)

                @pl.loop(0, 8)
                def _(i):
                    for zi in range(2):
                        row = pl.ds(pl.multiple_of(zi * 192 + i * 24, 8), 24)
                        at = (2 * half + zi, i // 4, i % 4)
                        to = pl.ds(pl.multiple_of(HALF * zi + 128 * p, 128), 128)
                        both = pv[(p,) + at].astype(f32) + own[half, i // 4, i % 4, :, to].astype(f32)
                        pv[(p,) + at] = jnp.concatenate([dwf[row, 0:128], both[24:48]], axis=0).astype(bf16)

        def tick(e, what):
            if what == "gs" and e == 0:
                on_first(lambda: s.twos(1, *d_args(1)))
                on_v(s.threes)
            elif what == "gd" and e == 0:
                on_first(other_half)
                four_v()
            elif what == "dw" and e == 0:
                on_b(s.twos)
            elif what == "gs":
                on_first(dloads_done)
                value_part()
                s.one(8 + p, *v_args(p))
                on_a(s.threes)
            elif what == "gd":
                on_b(s.threes)
            elif what == "dw":
                s.twos(8 + p, *v_args(p))
                s.one(kd, *d_args(kd))
            elif what == "dl" and e == 1:
                s.one(5 + p, *l_args(p))
                four_a()
            elif what == "gn" and e == 1:
                s.twos(kd, *d_args(kd))
                four_b()

        def logit_part(e):
            h = 2 * p + e
            if e == 0:

                @pl.when(p == 2)
                def _():
                    s.sent(5, *l_args(0))

            hid_load(h).wait()
            for half in range(2):
                cols = slice(half * HALF, half * HALF + HALF)
                dwf[:, 0:512] = dot(hid[0:1024, cols], gsl[e], TN)
                dwf[:, 0:256] += dot(hid[1024:2048, cols], gsm[e], TN)
                put_pair(pll.at[p % 2], half, e, 512)

            @pl.when(h < 5)
            def _():
                hid_load(h + 1).start()

            tick(e, "dl")

        for e in range(2):
            h = 2 * p + e
            more = h < 5

            def ahead(*cps):
                @pl.when(more)
                def _():
                    for cp in cps:
                        cp.start()

            for cp in att_loads(h):
                cp.wait()
            for b in range(4):
                at = b * 512
                rows = slice(at, at + 512)
                gpair = gm[rows, lanes]
                vpair = val[rows, lanes] * keeps[e]
                gkeep = gpair * keeps[e]
                if b < 2:
                    att = atl[rows]
                    gsl[e, rows] = score_grad(att, dot(gpair, vpair, NT))
                    vs = dot(att, gkeep, TN)
                else:
                    part = slice((b - 2) * 256, (b - 2) * 256 + 256)
                    sh, mi = ats[part], atm[part]
                    g_sh = jnp.concatenate(
                        [dot(gpair[0:128], vpair[0:128], NT), dot(gpair[128:256], vpair[128:256], NT)], axis=0
                    )
                    at2 = (b - 2) * 512
                    gsm[e, at2 : at2 + 256, 0:128] = score_grad(sh, g_sh)
                    gsm[e, at2 + 256 : at2 + 512] = score_grad(mi, dot(gpair[256:512], vpair[256:512], NT))
                    vs = jnp.concatenate(
                        [
                            dot(sh[0:128], gkeep[0:128], TN),
                            dot(sh[128:256], gkeep[128:256], TN),
                            dot(mi, gkeep[256:512], TN),
                        ],
                        axis=0,
                    )
                if e == 0:
                    vsb[rows] = vs.astype(bf16)
                else:
                    gm[rows, lanes] = vsb[rows] + vs.astype(bf16)
            ahead(*att_loads(h + 1))
            lsum = dot(ones, gsl[e])
            lb_o[pl.ds(h, 1)] = lsum[0:1]
            lb_o[pl.ds(h, 1), 0:256] += dot(ones, gsm[e])[0:1]
            tick(e, "gs")
            l_load(h).wait()
            for b in range(4):
                rows = slice(b * 512, b * 512 + 512)
                slo_load(h, b).wait()
                if b < 2:
                    gh = dot(gsl[e, rows], lv[...], NT)
                else:
                    gh = dot(gsm[e, (b - 2) * 512 : (b - 2) * 512 + 512], lv[:, 0:256], NT)
                gd[rows] = (gh * slo[b % 2].astype(f32)).astype(bf16)
                if b < 2:
                    slo_load(h, b + 2).start()
                else:
                    ahead(slo_load(h + 1, b - 2))
            ahead(l_load(h + 1))
            db_o[pl.ds(h, 1)] = (dot(ones, gd[0:1024]) + dot(ones, gd[1024:2048]))[0:1]
            tick(e, "gd")
            if e == 0:

                @pl.when(later)
                def _():
                    s.sent(kd - 3, *d_args(kd - 3))

            for half in range(2):
                cols = slice(half * HALF, half * HALF + HALF)
                dwf[...] = dot(nrm[:, cols], gd[...], TN)
                put_pair(pd.at[dslot], half, e, D)
            tick(e, "dw")
            if e == 1:
                logit_part(0)
                logit_part(1)
            w_load(h).wait()

            @pl.loop(0, 4)
            def _(b):
                rows = pl.ds(pl.multiple_of(b * 512, 512), 512)
                gn[rows] += dot(gd[rows], wv[...], NT)

            ahead(w_load(h + 1))
            tick(e, "gn")

    pl.semaphore_signal(free, inc=1, device_id=pc.sib, device_id_type=MESH)
    vb_o[...] = dot(ones, gm[0:1024]) + dot(ones, gm[1024:2048])

    @pl.loop(0, 4)
    def _(b):
        rows = pl.ds(pl.multiple_of(b * 512, 512), 512)
        gn[rows] += dot(gm[rows], vv[...], NT)

    s.threes(10, *v_args(2))
    other = lambda to: pl.ds(pl.multiple_of(to + o * 512, 512), 512)
    mine = lambda to: pl.ds(pl.multiple_of(to + c * 512, 512), 512)
    hid[0:512] = gn[other(1024)].astype(bf16)
    hid[512:1024] = gn[other(0)].astype(bf16)
    pl.semaphore_wait(free, 1)
    gswap = remote(hid.at[pl.ds(0, 1024)], gd.at[pl.ds(0, 1024)], gs_, gr_, pc.sib)
    gswap.start()
    tloads = [copy(tok.at[pl.ds(i * 512, 512)], slo.at[i], hsem.at[6 + i]) for i in range(2)]
    for cp in tloads:
        cp.start()
    s.twos(7, *l_args(2))
    for cp in tloads:
        cp.wait()
    gswap.wait()
    ag_o[...] = jnp.zeros_like(ag_o)

    @pl.loop(0, 4)
    def _(b):
        nat = pl.ds(pl.multiple_of(b * 256, 256), 256)
        trow = pl.ds(pl.multiple_of(jnp.where(b < 2, 1024 + b * 256, b * 256 - 512) + c * 512, 256), 256)
        load = copy(gres.at[nat], dwf.at[pl.ds(0, 256)], lsem.at[6])
        load.start()
        unit, inv = norm_rows(slo[b // 2, pl.ds(pl.multiple_of((b % 2) * 256, 256), 256)].astype(f32))
        g = gn[trow] + gd[nat].astype(f32)
        q = g * vec[0:1]
        back = inv * (q - jnp.mean(q, axis=-1, keepdims=True) - unit * jnp.mean(q * unit, axis=-1, keepdims=True))
        load.wait()
        dwf[0:256] = dwf[0:256] + back
        ag_o[0:1] += jnp.sum(g * unit, axis=0, keepdims=True)
        ag_o[1:2] += jnp.sum(g, axis=0, keepdims=True)
        store = copy(dwf.at[pl.ds(0, 256)], tg_o.at[nat], lsem.at[7])
        store.start()
        store.wait()

    s.threes(4, *d_args(4))
    s.threes(7, *l_args(2))
    s.four(10, *v_args(2), stv.at[2], ovo.at[2, c])
    for cp in s.outs(1, std.at[1], ofe.at[c, 1]):
        cp.wait()
    s.four(4, *d_args(4), std.at[1], od.at[3 * c + 2])
    s.four(7, *l_args(2), stl.at[2], ol.at[3 * c + 2])
    ends = []
    for p in range(3):
        ends.append(s.outs(2 + p, std.at[(2 + p) % 3], od.at[3 * c + p]))
        ends.append(s.outs(5 + p, stl.at[p], ol.at[3 * c + p]))
        ends.append(s.outs(8 + p, stv.at[p], ovo.at[p, c]))
    for pair in ends:
        for cp in pair:
            cp.wait()
    for k in (2, 3, 4):
        s.sent(k, *d_args(k))
    for p in (1, 2):
        s.sent(5 + p, *l_args(p))
    for p in range(3):
        s.sent(8 + p, *v_args(p))


def k3_call(*args):
    sds = jax.ShapeDtypeStruct
    dma = pltpu.SemaphoreType.DMA
    V = pltpu.VMEM

    def bufs(shape, width):
        return [V(shape + (4, 2, 48, width), bf16)] * 3 + [V(shape + (3, 2, 48, width), bf16)]

    return pl.pallas_call(
        k3_kernel,
        out_shape=(
            sds((ROWS_DEV, D), f32),
            sds((6, 48, D), f32),
            sds((6, 48, L3), f32),
            sds((2, 2, 48, D), f32),
            sds((3, 2, 48, 128), f32),
            sds((8, D), f32),
            sds((8, L3), f32),
            sds((8, HALF), f32),
            sds((8, D), f32),
        ),
        in_specs=[HBM] * 15 + [VMEM],
        out_specs=(HBM,) * 5 + (VMEM,) * 4,
        scratch_shapes=[
            V((CHIP_ROWS, D), bf16),
            V((CHIP_ROWS, HALF), bf16),
            V((CHIP_ROWS, HALF), bf16),
            V((CHIP_ROWS, D), f32),
            V((CHIP_ROWS, HIDDEN_SIZE), bf16),
            V((2, 512, HIDDEN_SIZE), bf16),
            V((1024, L3), bf16),
            V((512, L2), bf16),
            V((512, L1), bf16),
            V((2, 1024, L3), bf16),
            V((2, 1024, L2), bf16),
            V((CHIP_ROWS, HIDDEN_SIZE), bf16),
            V((D, HIDDEN_SIZE), bf16),
            V((HIDDEN_SIZE, L3), bf16),
            V((HALF, D), f32),
            V((CHIP_ROWS, 128), bf16),
            V((D, HALF), bf16),
            V((2, 2, 4, 48, D), bf16),
            V((3, 4, 2, 4, 48, D), bf16),
            V((2, 4, 2, 4, 48, L3), bf16),
            V((3, 4, 2, 4, 48, 128), bf16),
        ]
        + bufs((5,), D)
        + bufs((3,), L3)
        + bufs((3,), 128)
        + [V((3, 2, 48, D), f32), V((3, 2, 48, L3), f32), V((3, 2, 48, 128), f32)]
        + [dma((11, 4))] * 8
        + [dma((11, 2)), dma((11,)), dma((8,)), dma((5,)), dma((5,)), dma, dma, pltpu.SemaphoreType.REGULAR]
        + [dma((8,)), dma((2,)), dma((3, 4))]
        + [dma((8,))] * 2,
        compiler_params=pltpu.CompilerParams(
            collective_id=2, has_side_effects=True, vmem_limit_bytes=VMEM_LIMIT
        ),
        name="k3_backward",
    )(*args)


def k4_kernel(g, out, slots, ss, sr):
    pc = Place()
    me = pc.w * 4 + pc.n
    bar = pltpu.get_barrier_semaphore()

    @pl.loop(1, 32)
    def _(j):
        t = (me + j) % 32
        pl.semaphore_signal(bar, inc=1, device_id=(t // 4, t % 4), device_id_type=MESH)

    pl.semaphore_wait(bar, 31)

    @pl.loop(1, 32)
    def _(j):
        t = (me + j) % 32
        remote(g.at[t], slots.at[me], ss.at[t], sr.at[me], (t // 4, t % 4)).start()

    slots[me] = g[me]

    @pl.loop(1, 32)
    def _(j):
        t = (me + j) % 32
        f = (me + 32 - j) % 32
        cp = remote(g.at[t], slots.at[f], ss.at[t], sr.at[f], (t // 4, t % 4))
        cp.wait_send()
        cp.wait_recv()

    out[...] = jnp.sum(slots[...], axis=0)


def k4_call(g):
    return pl.pallas_call(
        k4_kernel,
        out_shape=jax.ShapeDtypeStruct((16, 128), f32),
        in_specs=[VMEM],
        out_specs=VMEM,
        scratch_shapes=[
            pltpu.VMEM((32, 16, 128), f32),
            pltpu.SemaphoreType.DMA((32,)),
            pltpu.SemaphoreType.DMA((32,)),
        ],
        compiler_params=pltpu.CompilerParams(collective_id=3, has_side_effects=True),
        name="k4_vectors",
    )(g)


def chip_body(tokens, cotangent, bucket_counts, *params):
    core = lax.axis_index(AXES[0]) % 2
    ovo, _, _, ef, nrm, val, hid, slo, atl, atm, ats, wa, la, mix, vv, vec, eb = k1_call(*prepare(tokens, *params))
    lay, gres, gmix, dff, dout, sums = k2_call(tokens, cotangent, bucket_counts, mix, ovo, ef, vec, eb)
    tg, od, ol, ofe, dvo, dbs, lbs, vbs, ags = k3_call(
        dff, dout, nrm, val, gmix, hid, slo, atl, atm, ats, wa, la, vv, tokens, gres, vec
    )
    vb_all = lax.dynamic_update_slice(jnp.zeros((1, D), f32), vbs[0:1], (0, HALF * core))
    lb_all = lax.dynamic_update_slice(jnp.zeros((HEADS, L3), f32), lbs[0:6], (6 * core, 0))
    db_all = lax.dynamic_update_slice(jnp.zeros((HEADS, HIDDEN_SIZE), f32), dbs[0:6], (6 * core, 0))
    v7 = jnp.concatenate([ags[0:2], vb_all, sums[3:4], sums[0:2], sums[2:3]])
    narrow_rows = v7.reshape(7, 32, 24).transpose(1, 0, 2)
    wide_rows = jnp.concatenate(
        [sums[4:8].reshape(32, 1, 96), lb_all.reshape(32, 2, 96), db_all.reshape(32, 3, 96)], axis=1
    )
    pack = jnp.concatenate(
        [jnp.pad(narrow_rows, ((0, 0), (0, 0), (0, 104))), jnp.pad(wide_rows, ((0, 0), (0, 3), (0, 32)))], axis=1
    )
    red = k4_call(pack)
    vo_shard = lambda r: dvo[:, :, r : r + 24].transpose(2, 1, 0, 3).reshape(24, D)
    small = lambda i: red[i, :24]
    return (
        lay,
        tg,
        small(0),
        small(1),
        od.reshape(HEADS, 24, HIDDEN_SIZE),
        red[10:13, :96].reshape(288),
        ol.reshape(HEADS, 24, L3),
        red[8:10, :96].reshape(192),
        vo_shard(0),
        small(2),
        vo_shard(24),
        small(3),
        small(4),
        small(5),
        ofe[0].reshape(4, 24, D).transpose(1, 0, 2).reshape(24, 4 * D),
        red[7, :96],
        ofe[1].reshape(96, D),
        small(6),
    )


def smooth_gate(values_in):
    return (
        0.5
        * values_in
        * (1.0 + jnp.tanh(gelu_root * (values_in + gelu_cube * values_in * values_in * values_in)))
    )


def gate_slope(values_in):
    squared = values_in * values_in
    tangent = jnp.tanh(gelu_root * (values_in + gelu_cube * squared * values_in))
    return 0.5 * (1.0 + tangent) + 0.5 * values_in * (1.0 - tangent * tangent) * gelu_root * (
        1.0 + 3.0 * gelu_cube * squared
    )


def bucket_layout():
    return ((S1, L1), (S2, L2), (S3, L3))


def live_rows(counts):
    pieces = []
    for bucket_index, (slot_count, seq_length) in enumerate(bucket_layout()):
        slot_of_row = jnp.arange(slot_count * seq_length, dtype=jnp.int32) // seq_length
        pieces.append(jnp.where(slot_of_row < counts[bucket_index], 1.0, 0.0).astype(jnp.float32))
    return jnp.concatenate(pieces)


def product(left_side, right_side):
    return jnp.dot(left_side, right_side, preferred_element_type=jnp.float32)


def column_sums(matrix_rows):
    return jnp.sum(matrix_rows.astype(jnp.float32), axis=0)


def norm_forward(inputs_float, norm_gain, norm_shift):
    row_mean = jnp.mean(inputs_float, axis=-1, keepdims=True)
    centred = inputs_float - row_mean
    inverse_scale = lax.rsqrt(jnp.mean(centred * centred, axis=-1, keepdims=True) + norm_eps)
    unit_rows = centred * inverse_scale
    return (unit_rows * norm_gain + norm_shift, unit_rows, inverse_scale)


def norm_backward(grad_normed, unit_rows, inverse_scale, norm_gain):
    grad_unit = grad_normed * norm_gain
    grad_inputs = inverse_scale * (
        grad_unit
        - jnp.mean(grad_unit, axis=-1, keepdims=True)
        - unit_rows * jnp.mean(grad_unit * unit_rows, axis=-1, keepdims=True)
    )
    return (grad_inputs, jnp.sum(grad_normed * unit_rows, axis=0), jnp.sum(grad_normed, axis=0))


def forward_pass(tokens, live_mask, gathered):
    (
        attn_gain,
        attn_shift,
        dense_weight,
        dense_bias,
        logit_weight,
        logit_bias,
        value_weight,
        value_bias,
        output_weight,
        output_bias,
        feed_gain,
        feed_shift,
        expand_weight,
        expand_bias,
        reduce_weight,
        reduce_bias,
    ) = gathered
    inputs_float = tokens.astype(jnp.float32)
    normed_float, unit_one, scale_one = norm_forward(
        inputs_float, attn_gain.astype(jnp.float32), attn_shift.astype(jnp.float32)
    )
    normed = normed_float.astype(jnp.bfloat16)
    values = (product(normed, value_weight) + value_bias.astype(jnp.float32)).astype(jnp.bfloat16)
    dense_heads = dense_bias.astype(jnp.float32).reshape(HEADS, 1, HIDDEN_SIZE)
    logit_heads = logit_bias.astype(jnp.float32).reshape(HEADS, 1, L3)
    pre_list, hidden_list, attention_list, mixed_list = ([], [], [], [])
    start_row = 0
    for slot_count, seq_length in bucket_layout():
        stop_row = start_row + slot_count * seq_length
        pre_act = (
            jnp.einsum(
                "rd,hde->hre",
                normed[start_row:stop_row],
                dense_weight,
                preferred_element_type=jnp.float32,
            )
            + dense_heads
        )
        hidden = smooth_gate(pre_act).astype(jnp.bfloat16)
        scores = (
            jnp.einsum(
                "hre,hel->hrl",
                hidden,
                logit_weight[:, :, :seq_length],
                preferred_element_type=jnp.float32,
            )
            + logit_heads[:, :, :seq_length]
        )
        attention = jax.nn.softmax(scores, axis=-1)
        attention_low = attention.astype(jnp.bfloat16).reshape(
            HEADS, slot_count, seq_length, seq_length
        )
        block_values = values[start_row:stop_row].reshape(slot_count, seq_length, HEADS, HEAD_DIM)
        mixed_heads = jnp.einsum(
            "hsql,slhc->sqhc", attention_low, block_values, preferred_element_type=jnp.float32
        )
        mixed_list.append(mixed_heads.reshape(slot_count * seq_length, D))
        pre_list.append(pre_act)
        hidden_list.append(hidden)
        attention_list.append(attention)
        start_row = stop_row
    mixed_all = jnp.concatenate(mixed_list, axis=0).astype(jnp.bfloat16)
    attended = product(mixed_all, output_weight) + output_bias.astype(jnp.float32)
    residual = inputs_float + attended
    normed_two_float, unit_two, scale_two = norm_forward(
        residual, feed_gain.astype(jnp.float32), feed_shift.astype(jnp.float32)
    )
    normed_two = normed_two_float.astype(jnp.bfloat16)
    expand_pre = product(normed_two, expand_weight) + expand_bias.astype(jnp.float32)
    inner_act = smooth_gate(expand_pre).astype(jnp.bfloat16)
    feed_out = product(inner_act, reduce_weight) + reduce_bias.astype(jnp.float32)
    layer_out = live_mask[:, None] * (residual + feed_out)
    stored = (
        normed,
        unit_one,
        scale_one,
        values,
        pre_list,
        hidden_list,
        attention_list,
        mixed_all,
        unit_two,
        scale_two,
        normed_two,
        expand_pre,
        inner_act,
    )
    return (layer_out, stored)


def backward_pass(cotangent, live_mask, gathered, stored):
    (
        attn_gain,
        attn_shift,
        dense_weight,
        dense_bias,
        logit_weight,
        logit_bias,
        value_weight,
        value_bias,
        output_weight,
        output_bias,
        feed_gain,
        feed_shift,
        expand_weight,
        expand_bias,
        reduce_weight,
        reduce_bias,
    ) = gathered
    (
        normed,
        unit_one,
        scale_one,
        values,
        pre_list,
        hidden_list,
        attention_list,
        mixed_all,
        unit_two,
        scale_two,
        normed_two,
        expand_pre,
        inner_act,
    ) = stored
    grad_out = cotangent.astype(jnp.float32) * live_mask[:, None]
    grad_feed = grad_out.astype(jnp.bfloat16)
    reduce_weight_grad = jnp.einsum(
        "rf,rd->fd", inner_act, grad_feed, preferred_element_type=jnp.float32
    )
    reduce_bias_grad = column_sums(grad_feed)
    grad_inner = jnp.einsum(
        "rd,fd->rf", grad_feed, reduce_weight, preferred_element_type=jnp.float32
    )
    grad_expand = (grad_inner * gate_slope(expand_pre)).astype(jnp.bfloat16)
    expand_weight_grad = jnp.einsum(
        "rd,rf->df", normed_two, grad_expand, preferred_element_type=jnp.float32
    )
    expand_bias_grad = column_sums(grad_expand)
    grad_normed_two = jnp.einsum(
        "rf,df->rd", grad_expand, expand_weight, preferred_element_type=jnp.float32
    )
    grad_residual_norm, feed_gain_grad, feed_shift_grad = norm_backward(
        grad_normed_two, unit_two, scale_two, feed_gain.astype(jnp.float32)
    )
    grad_residual = grad_out + grad_residual_norm
    grad_attended = grad_residual.astype(jnp.bfloat16)
    output_weight_grad = jnp.einsum(
        "rd,re->de", mixed_all, grad_attended, preferred_element_type=jnp.float32
    )
    output_bias_grad = column_sums(grad_attended)
    grad_mixed = jnp.einsum(
        "re,de->rd", grad_attended, output_weight, preferred_element_type=jnp.float32
    ).astype(jnp.bfloat16)
    dense_weight_grad = jnp.zeros((HEADS, D, HIDDEN_SIZE), jnp.float32)
    dense_bias_grad = jnp.zeros((HEADS, HIDDEN_SIZE), jnp.float32)
    logit_weight_grad = jnp.zeros((HEADS, HIDDEN_SIZE, L3), jnp.float32)
    logit_bias_grad = jnp.zeros((HEADS, L3), jnp.float32)
    grad_normed_list, value_sum_list = ([], [])
    start_row = 0
    for bucket_index, (slot_count, seq_length) in enumerate(bucket_layout()):
        row_count = slot_count * seq_length
        stop_row = start_row + row_count
        attention = attention_list[bucket_index]
        hidden = hidden_list[bucket_index]
        pre_act = pre_list[bucket_index]
        attention_low = attention.astype(jnp.bfloat16).reshape(
            HEADS, slot_count, seq_length, seq_length
        )
        block_values = values[start_row:stop_row].reshape(slot_count, seq_length, HEADS, HEAD_DIM)
        block_grad = grad_mixed[start_row:stop_row].reshape(slot_count, seq_length, HEADS, HEAD_DIM)
        grad_attention = jnp.einsum(
            "sqhc,slhc->hsql", block_grad, block_values, preferred_element_type=jnp.float32
        ).reshape(HEADS, row_count, seq_length)
        value_sum_list.append(
            jnp.einsum(
                "hsql,sqhc->slhc", attention_low, block_grad, preferred_element_type=jnp.float32
            ).reshape(row_count, D)
        )
        grad_scores = (
            attention
            * (grad_attention - jnp.sum(attention * grad_attention, axis=-1, keepdims=True))
        ).astype(jnp.bfloat16)
        logit_weight_grad = logit_weight_grad.at[:, :, :seq_length].add(
            jnp.einsum("hre,hrl->hel", hidden, grad_scores, preferred_element_type=jnp.float32)
        )
        logit_bias_grad = logit_bias_grad.at[:, :seq_length].add(
            jnp.sum(grad_scores.astype(jnp.float32), axis=1)
        )
        grad_hidden = jnp.einsum(
            "hrl,hel->hre",
            grad_scores,
            logit_weight[:, :, :seq_length],
            preferred_element_type=jnp.float32,
        )
        grad_dense = (grad_hidden * gate_slope(pre_act)).astype(jnp.bfloat16)
        dense_weight_grad = dense_weight_grad + jnp.einsum(
            "rd,hre->hde",
            normed[start_row:stop_row],
            grad_dense,
            preferred_element_type=jnp.float32,
        )
        dense_bias_grad = dense_bias_grad + jnp.sum(grad_dense.astype(jnp.float32), axis=1)
        grad_normed_list.append(
            jnp.einsum("hre,hde->rd", grad_dense, dense_weight, preferred_element_type=jnp.float32)
        )
        start_row = stop_row
    grad_values = jnp.concatenate(value_sum_list, axis=0).astype(jnp.bfloat16)
    value_weight_grad = jnp.einsum(
        "rd,re->de", normed, grad_values, preferred_element_type=jnp.float32
    )
    value_bias_grad = column_sums(grad_values)
    grad_normed = jnp.concatenate(grad_normed_list, axis=0) + jnp.einsum(
        "re,de->rd", grad_values, value_weight, preferred_element_type=jnp.float32
    )
    grad_inputs_norm, attn_gain_grad, attn_shift_grad = norm_backward(
        grad_normed, unit_one, scale_one, attn_gain.astype(jnp.float32)
    )
    tokens_grad = grad_residual + grad_inputs_norm
    return (
        tokens_grad,
        (
            attn_gain_grad,
            attn_shift_grad,
            dense_weight_grad,
            dense_bias_grad.reshape(-1),
            logit_weight_grad,
            logit_bias_grad.reshape(-1),
            value_weight_grad,
            value_bias_grad,
            output_weight_grad,
            output_bias_grad,
            feed_gain_grad,
            feed_shift_grad,
            expand_weight_grad,
            expand_bias_grad,
            reduce_weight_grad,
            reduce_bias_grad,
        ),
    )


def body(
    tokens,
    cotangent,
    bucket_counts,
    attn_gain,
    attn_shift,
    dense_weight,
    dense_bias,
    logit_weight,
    logit_bias,
    value_weight,
    value_bias,
    output_weight,
    output_bias,
    feed_gain,
    feed_shift,
    expand_weight,
    expand_bias,
    reduce_weight,
    reduce_bias,
):
    gathered = (
        lax.all_gather(attn_gain, AXES, axis=0, tiled=True),
        lax.all_gather(attn_shift, AXES, axis=0, tiled=True),
        lax.all_gather(dense_weight, AXES, axis=1, tiled=True),
        lax.all_gather(dense_bias, AXES, axis=0, tiled=True),
        lax.all_gather(logit_weight, AXES, axis=1, tiled=True),
        lax.all_gather(logit_bias, AXES, axis=0, tiled=True),
        lax.all_gather(value_weight, AXES, axis=0, tiled=True),
        lax.all_gather(value_bias, AXES, axis=0, tiled=True),
        lax.all_gather(output_weight, AXES, axis=0, tiled=True),
        lax.all_gather(output_bias, AXES, axis=0, tiled=True),
        lax.all_gather(feed_gain, AXES, axis=0, tiled=True),
        lax.all_gather(feed_shift, AXES, axis=0, tiled=True),
        lax.all_gather(expand_weight, AXES, axis=0, tiled=True),
        lax.all_gather(expand_bias, AXES, axis=0, tiled=True),
        lax.all_gather(reduce_weight, AXES, axis=0, tiled=True),
        lax.all_gather(reduce_bias, AXES, axis=0, tiled=True),
    )
    live_mask = live_rows(bucket_counts[0])
    layer_out, stored = forward_pass(tokens, live_mask, gathered)
    gathered = (
        lax.all_gather(attn_gain, AXES, axis=0, tiled=True),
        lax.all_gather(attn_shift, AXES, axis=0, tiled=True),
        lax.all_gather(dense_weight, AXES, axis=1, tiled=True),
        lax.all_gather(dense_bias, AXES, axis=0, tiled=True),
        lax.all_gather(logit_weight, AXES, axis=1, tiled=True),
        lax.all_gather(logit_bias, AXES, axis=0, tiled=True),
        lax.all_gather(value_weight, AXES, axis=0, tiled=True),
        lax.all_gather(value_bias, AXES, axis=0, tiled=True),
        lax.all_gather(output_weight, AXES, axis=0, tiled=True),
        lax.all_gather(output_bias, AXES, axis=0, tiled=True),
        lax.all_gather(feed_gain, AXES, axis=0, tiled=True),
        lax.all_gather(feed_shift, AXES, axis=0, tiled=True),
        lax.all_gather(expand_weight, AXES, axis=0, tiled=True),
        lax.all_gather(expand_bias, AXES, axis=0, tiled=True),
        lax.all_gather(reduce_weight, AXES, axis=0, tiled=True),
        lax.all_gather(reduce_bias, AXES, axis=0, tiled=True),
    )
    tokens_grad, grads = backward_pass(cotangent, live_mask, gathered, stored)
    shards = (
        lax.psum_scatter(grads[0], AXES, scatter_dimension=0, tiled=True),
        lax.psum_scatter(grads[1], AXES, scatter_dimension=0, tiled=True),
        lax.psum_scatter(grads[2], AXES, scatter_dimension=1, tiled=True),
        lax.psum_scatter(grads[3], AXES, scatter_dimension=0, tiled=True),
        lax.psum_scatter(grads[4], AXES, scatter_dimension=1, tiled=True),
        lax.psum_scatter(grads[5], AXES, scatter_dimension=0, tiled=True),
        lax.psum_scatter(grads[6], AXES, scatter_dimension=0, tiled=True),
        lax.psum_scatter(grads[7], AXES, scatter_dimension=0, tiled=True),
        lax.psum_scatter(grads[8], AXES, scatter_dimension=0, tiled=True),
        lax.psum_scatter(grads[9], AXES, scatter_dimension=0, tiled=True),
        lax.psum_scatter(grads[10], AXES, scatter_dimension=0, tiled=True),
        lax.psum_scatter(grads[11], AXES, scatter_dimension=0, tiled=True),
        lax.psum_scatter(grads[12], AXES, scatter_dimension=0, tiled=True),
        lax.psum_scatter(grads[13], AXES, scatter_dimension=0, tiled=True),
        lax.psum_scatter(grads[14], AXES, scatter_dimension=0, tiled=True),
        lax.psum_scatter(grads[15], AXES, scatter_dimension=0, tiled=True),
    )
    return (layer_out, tokens_grad) + tuple(shards)


def solution(mesh):
    in_specs = (
        P(AXES, None),
        P(AXES, None),
        P(AXES, None),
        P(AXES),
        P(AXES),
        P(None, AXES, None),
        P(AXES),
        P(None, AXES, None),
        P(AXES),
        P(AXES, None),
        P(AXES),
        P(AXES, None),
        P(AXES),
        P(AXES),
        P(AXES),
        P(AXES, None),
        P(AXES),
        P(AXES, None),
        P(AXES),
    )
    out_specs = (
        P(AXES, None),
        P(AXES, None),
        P(AXES),
        P(AXES),
        P(None, AXES, None),
        P(AXES),
        P(None, AXES, None),
        P(AXES),
        P(AXES, None),
        P(AXES),
        P(AXES, None),
        P(AXES),
        P(AXES),
        P(AXES),
        P(AXES, None),
        P(AXES),
        P(AXES, None),
        P(AXES),
    )
    shape = tuple(mesh.shape[a] for a in AXES)
    chosen = chip_body if shape == (8, 4) else body
    return jax.shard_map(chosen, mesh=mesh, in_specs=in_specs, out_specs=out_specs, check_vma=False)
```

```python
import functools

import jax
import jax.numpy as jnp
import numpy as np
from jax import lax
from jax.experimental import pallas as pl
from jax.experimental.pallas import tpu as pltpu
from jax.sharding import PartitionSpec as P

D = 768
HEADS = 12
HEAD_DIM = 64
HIDDEN_SIZE = 768
L3 = 512
AXES = ("wide", "narrow")
L1 = 128
L2 = 256
S1 = 2
S2 = 1
S3 = 1

norm_eps = 1e-05
gelu_root = 0.7978845608028654
gelu_cube = 0.044715

MESH = pl.DeviceIdType.MESH
HBM = pl.BlockSpec(memory_space=pltpu.HBM)
VMEM = pl.BlockSpec(memory_space=pltpu.VMEM)
VMEM_LIMIT = 63 * 1024 * 1024
f32 = jnp.float32
bf16 = jnp.bfloat16

ROWS_DEV = 1024
CHIP_ROWS = 2048
HALF = 384
NN = (((1,), (0,)), ((), ()))
NT = (((1,), (1,)), ((), ()))
TN = (((0,), (0,)), ((), ()))


def dot(a, b, dims=NN):
    return lax.dot_general(a, b, dims, preferred_element_type=f32)


def gelu_both(v):
    sq = v * v
    t = jnp.tanh(v * (gelu_root + gelu_root * gelu_cube * sq))
    up = 0.5 + 0.5 * t
    slope = up + 0.5 * v * (1.0 - t * t) * (gelu_root + 3.0 * gelu_root * gelu_cube * sq)
    return v * up, slope


def norm_rows(x):
    mean = jnp.mean(x, axis=-1, keepdims=True)
    cen = x - mean
    inv = lax.rsqrt(jnp.mean(cen * cen, axis=-1, keepdims=True) + norm_eps)
    return cen * inv, inv


class Place:
    def __init__(self):
        w = lax.axis_index(AXES[0])
        n = lax.axis_index(AXES[1])
        self.w, self.n = w, n
        self.z, self.c = w // 2, w % 2
        self.nx = n + 1 - 2 * (n % 2)
        self.ny = (n + 2) % 4
        self.nd = 3 - n
        self.xdev = (w, self.nx)
        self.ydev = (w, self.ny)
        self.sib = (self.z * 2 + 1 - self.c, n)

    def zpos(self, i):
        return (self.z + i) % 4

    def zdev(self, zz):
        return (zz * 2 + self.c, self.n)

    def near(self):
        return [self.xdev, self.ydev, self.sib] + [self.zdev(self.zpos(i)) for i in (1, 2, 3)]


def greet(devs):
    bar = pltpu.get_barrier_semaphore()
    for dev in devs:
        pl.semaphore_signal(bar, inc=1, device_id=dev, device_id_type=MESH)
    pl.semaphore_wait(bar, len(devs))


def remote(src, dst, ssem, rsem, dev):
    return pltpu.make_async_remote_copy(
        src_ref=src, dst_ref=dst, send_sem=ssem, recv_sem=rsem, device_id=dev, device_id_type=MESH
    )


def everyone(me, fn):
    @pl.loop(1, 32)
    def _(j):
        t = (me + j) % 32
        fn(t, (me + 32 - j) % 32, (t // 4, t % 4))


def spread(s_all, rows, width, count, base):
    n = len(rows)
    parts = jnp.concatenate([s_all[:, r, :] for r in rows], axis=0).astype(bf16)
    q = lax.broadcasted_iota(jnp.int32, (8, 32 * n), 1)
    h = lax.broadcasted_iota(jnp.int32, (8, 32 * n), 0) + base
    piece = n * (q & 31) + (q >> 5)
    lane = lax.broadcasted_iota(jnp.int32, (128, 8 * width), 0)
    to = lax.broadcasted_iota(jnp.int32, (128, 8 * width), 1)
    out = jnp.zeros((8, 8 * width), f32)
    for pos in range(8):
        pick = jnp.where(piece == 8 * h + pos, 1.0, 0.0).astype(bf16)
        move = jnp.where((to == width * pos + lane) & (lane < width), 1.0, 0.0).astype(bf16)
        out = out + dot(dot(pick, parts).astype(bf16), move)
    return out[0:count]


def spread_narrow(s_all, vec):
    dev = lax.broadcasted_iota(jnp.int32, (32, D), 0)
    owner = (lax.broadcasted_iota(jnp.int32, (32, D), 1) * 2731) >> 16
    lane = lax.broadcasted_iota(jnp.int32, (128, D), 0)
    to = lax.broadcasted_iota(jnp.int32, (128, D), 1)
    move = jnp.where(to - 24 * ((to * 2731) >> 16) == lane, 1.0, 0.0).astype(bf16)
    for i in range(7):
        wide = dot(s_all[:, i, :].astype(bf16), move)
        vec[i : i + 1] = jnp.sum(jnp.where(owner == dev, wide, 0.0), axis=0, keepdims=True)
    vec[7:8] = jnp.zeros((1, D), f32)


class Gather:
    def __init__(self, pc, sems):
        self.pc = pc
        self.zs, self.zr, self.xs, self.xr, self.ys, self.yr, self.ds, self.dr, self.ls = sems

    def zcopy(self, k, src, buf, i, sender=None):
        pc = self.pc
        zz = pc.z if sender is None else sender
        return remote(src, buf.at[zz, :, pc.n], self.zs.at[k, i], self.zr.at[k, zz], pc.zdev(pc.zpos(i)))

    def zsend(self, k, src, buf):
        for i in (1, 2, 3):
            self.zcopy(k, src, buf, i).start()
        self.own(k, src, buf).start()

    def own(self, k, src, buf):
        return pltpu.make_async_copy(src, buf.at[self.pc.z, :, self.pc.n], self.ls.at[k])

    def xcopy(self, k, buf, zz, src=None, col=None):
        pc = self.pc
        col = pc.n if col is None else col
        slot = buf.at[zz, :, col]
        return remote(slot if src is None else src, slot, self.xs.at[k, zz], self.xr.at[k, zz], pc.xdev)

    def ycopy(self, k, buf, zz, src=None, col=None):
        pc = self.pc
        col = pc.n if col is None else col
        slot = buf.at[zz, :, col]
        return remote(slot if src is None else src, slot, self.ys.at[k, zz], self.yr.at[k, zz], pc.ydev)

    def col(self, k, src, buf, i):
        pc = self.pc
        zz = pc.zpos(i)
        if i:
            self.zcopy(k, src, buf, i, sender=zz).wait_recv()
        s = None if i else src
        self.xcopy(k, buf, zz, s).start()
        self.ycopy(k, buf, zz, s).start()

    def dcopy(self, k, buf, zz):
        pc = self.pc
        if zz < 2:
            slot, dev = buf.at[zz, :, pc.nx], pc.ydev
        else:
            slot, dev = buf.at[zz, :, pc.ny], pc.xdev
        return remote(slot, slot, self.ds.at[k, zz], self.dr.at[k, zz], dev)

    def diag(self, k, buf, zz):
        pc = self.pc
        self.xcopy(k, buf, zz, col=pc.nx).wait_recv()
        self.ycopy(k, buf, zz, col=pc.ny).wait_recv()
        self.dcopy(k, buf, zz).start()

    def fin(self, k, src, buf, each=None):
        self.own(k, src, buf).wait()
        for zz in range(4):
            remote(
                buf.at[zz, :, self.pc.nd],
                buf.at[zz, :, self.pc.nd],
                self.ds.at[k, zz],
                self.dr.at[k, zz],
                self.pc.xdev,
            ).wait_recv()
            if each is not None:
                each(zz)

    def sent(self, k, src, buf):
        for i in (1, 2, 3):
            self.zcopy(k, src, buf, i).wait_send()
        for zz in range(4):
            self.xcopy(k, buf, zz).wait_send()
            self.ycopy(k, buf, zz).wait_send()
            self.dcopy(k, buf, zz).wait_send()


class LayerFirst:
    def __init__(self, pc, src, buf, cs, cr, us, ur, vs, vr, ls, ps, pr):
        self.pc, self.src, self.buf = pc, src, buf
        self.cs, self.cr, self.us, self.ur, self.vs, self.vr, self.ls = cs, cr, us, ur, vs, vr, ls
        self.ps, self.pr = ps, pr

    def side(self, i, src, slot):
        dev = self.pc.xdev if i in (0, 3) else self.pc.ydev
        return remote(src, slot, self.cs.at[i], self.cr.at[i], dev)

    def local(self):
        return pltpu.make_async_copy(self.src, self.buf.at[self.pc.z, :, self.pc.n], self.ls)

    def first(self):
        pc = self.pc
        self.local().start()
        for i in (0, 1):
            self.side(i, self.src, self.buf.at[pc.z, :, pc.n]).start()

    def halves(self):
        pc = self.pc
        a, b = self.buf.at[pc.z, 0, pc.nx], self.buf.at[pc.z, 1, pc.ny]
        return self.side(2, a, a), self.side(3, b, b)

    def second(self):
        for i in (0, 1):
            self.side(i, self.src, self.buf.at[self.pc.z, :, self.pc.n]).wait_recv()
        for cp in self.halves():
            cp.start()

    def up(self, r):
        return remote(self.buf.at[r], self.buf.at[r], self.us.at[r], self.ur.at[r], self.pc.zdev((self.pc.z + 1) % 4))

    def down(self, r):
        return remote(self.buf.at[r], self.buf.at[r], self.vs.at[r], self.vr.at[r], self.pc.zdev((self.pc.z + 3) % 4))

    def swap(self, r):
        return remote(self.buf.at[r], self.buf.at[r], self.ps.at[r], self.pr.at[r], self.pc.sib)

    def third(self):
        z = self.pc.z
        for cp in self.halves():
            cp.wait_recv()
        self.local().wait()

        @pl.when(z < 3)
        def _():
            self.up(z).start()

        @pl.when(z > 0)
        def _():
            self.down(z).start()

        self.swap(z).start()

    def level(self, k):
        z = self.pc.z

        @pl.when(z >= k)
        def _():
            self.up(z - k).wait_recv()

            @pl.when(z < 3)
            def _():
                self.up(z - k).start()

            self.swap(z - k).start()

        @pl.when(z + k <= 3)
        def _():
            self.down(z + k).wait_recv()

            @pl.when(z > 0)
            def _():
                self.down(z + k).start()

            self.swap(z + k).start()

    def finish(self):
        z = self.pc.z
        for i in (0, 1):
            self.side(i, self.src, self.buf.at[self.pc.z, :, self.pc.n]).wait_send()
        for cp in self.halves():
            cp.wait_send()
        for r in range(4):

            @pl.when((z < 3) & (z >= r))
            def _():
                self.up(r).wait_send()

            @pl.when((z > 0) & (z <= r))
            def _():
                self.down(r).wait_send()

            self.swap(r).wait()


def gather_sems(k):
    dma = pltpu.SemaphoreType.DMA
    return [dma((k, 4))] * 8 + [dma((k,))]


def join_pair(stage, dst_of, rows_of):
    @pl.loop(0, 4)
    def _(zz):
        for cc in range(2):
            for nn in (0, 2):
                one = stage[zz, cc, nn].astype(f32)
                two = stage[zz, cc, nn + 1].astype(f32)
                row = pl.multiple_of(zz * 192 + cc * 96 + nn * 24, 16)
                for e in rows_of:
                    both = jnp.concatenate(
                        [one[24 * e : 24 * e + 24], two[24 * e : 24 * e + 24]], axis=0
                    )
                    dst_of(e, pl.ds(row, 48), both.astype(bf16))


def k1_kernel(
    s_in, tok, dense, logit, vo, ff,
    ovo, gd, gl, ef, nrm_o, val_o, hid_o, slo_o, atl_o, atm_o, ats_o, wa_o, la_o, mix_o, vv_o, vec, eb,
    s_all, db, lb, vb, mvo, md, ml, mf, tokv, nrm, val, vst, vv, wst, lst, wv, lv, hidv, slov, atlv, atmv, atsv, mixv,
    zs, zr, xs, xr, ys, yr, ds, dr, ls, tsem, osem, wsem, lsem, ssem, rsem, msem,
    cs, cr, us, ur, vs, vr, cls, ps, pr, vss, vsr, es, er,
):
    pc = Place()
    c = pc.c
    g = Gather(pc, (zs, zr, xs, xr, ys, yr, ds, dr, ls))
    o = 1 - c
    me = pc.w * 4 + pc.n
    tcopies = []
    trows = [pl.ds(pl.multiple_of(to + c * 512, 512), 512) for to in (0, 1024)]
    for i, at in enumerate((512, 0)):
        tcopies.append(pltpu.make_async_copy(tok.at[pl.ds(at, 512)], tokv.at[trows[i]], tsem.at[i]))
    for cp in tcopies:
        cp.start()
    bar = pltpu.get_barrier_semaphore()
    everyone(me, lambda t, f, dev: pl.semaphore_signal(bar, inc=1, device_id=dev, device_id_type=MESH))
    pl.semaphore_wait(bar, 31)
    gives = [
        (vo.at[o], mvo.at[c]),
        (dense.at[pl.ds(3 * o, 3)], md.at[:, c]),
        (ff.at[o], mf.at[:, c]),
        (logit.at[pl.ds(3 * o, 3)], ml.at[:, c]),
    ]
    for i, at in enumerate((512, 0)):
        gives.append((tok.at[pl.ds(at, 512)], tokv.at[trows[i]]))
    rems = [remote(give, slot, es.at[i], er.at[i], pc.sib) for i, (give, slot) in enumerate(gives)]
    for cp in rems[0:4]:
        cp.start()
    everyone(me, lambda t, f, dev: remote(s_in, s_all.at[me], vss.at[t], vsr.at[me], dev).start())
    mvo[c] = vo[c]
    md[:, c] = dense[pl.ds(3 * c, 3)]
    mf[:, c] = ff[c]
    ml[:, c] = logit[pl.ds(3 * c, 3)]
    small = lambda t, f, dev: remote(s_in, s_all.at[f], vss.at[t], vsr.at[f], dev)
    for cp in rems[4:6]:
        cp.start()
    for cp in rems[0:4]:
        cp.wait()

    vo_args = (0, mvo, ovo.at[c])
    dd = lambda p: (1 + 2 * p, md.at[p], gd.at[p])
    ll = lambda p: (2 + 2 * p, ml.at[p], gl.at[p])
    fb = (7, mf.at[1], ef.at[c, 1])
    fa = LayerFirst(pc, mf.at[0], ef.at[c, 0], cs, cr, us, ur, vs, vr, cls, ps, pr)

    g.zsend(*vo_args)
    g.zsend(*dd(0))
    g.col(*vo_args, 0)
    g.col(*dd(0), 0)
    fa.first()
    g.col(*ll(0), 0)
    s_all[me] = s_in[...]

    for i in (1, 2, 3):
        g.col(*vo_args, i)
    g.zsend(*ll(0))
    fa.second()
    g.col(*dd(1), 0)

    def arrived(t, f, dev):
        small(t, f, dev).wait_send()
        small(t, f, dev).wait_recv()

    everyone(me, arrived)
    spread_narrow(s_all, vec)
    db[0:6] = spread(s_all, (11, 12, 13), 96, 6, 6 * c)
    lb[0:6] = spread(s_all, (8, 9, 10), 64, 6, 6 * c)
    eb[...] = spread(s_all, (7,), 96, 4, 0)
    vb[0:1] = jnp.where(c == 0, vec[2:3, 0:HALF], vec[2:3, HALF:D])

    for cp in tcopies + rems[4:6]:
        cp.wait()

    @pl.loop(0, 8)
    def _(b):
        rows = pl.ds(pl.multiple_of(b * 256, 256), 256)
        unit, _ = norm_rows(tokv[rows].astype(f32))
        nrm[rows] = (unit * vec[0:1] + vec[1:2]).astype(bf16)

    nrm_copy = pltpu.make_async_copy(nrm, nrm_o, tsem.at[4])
    nrm_copy.start()
    for i in (1, 2, 3):
        g.col(*dd(0), i)
    g.zsend(*dd(1))
    fa.third()
    for zz in range(4):
        g.diag(vo_args[0], vo_args[2], zz)
    g.col(*ll(1), 0)
    for i in (1, 2, 3):
        g.col(*ll(0), i)
    g.zsend(*ll(1))
    for zz in (0, 2, 1, 3):
        g.diag(dd(0)[0], dd(0)[2], zz)
    g.fin(*vo_args)
    vo_load = pltpu.make_async_copy(ovo.at[c], vst, tsem.at[5])
    vo_load.start()
    vo_swap = remote(ovo.at[c], ovo.at[c], ssem.at[0], rsem.at[0], pc.sib)
    vo_swap.start()
    vo_load.wait()

    def put_v(e, rows, x):
        vv[rows] = x

    join_pair(vst, put_v, (0,))

    @pl.loop(0, 4)
    def _(b):
        rows = pl.ds(pl.multiple_of(b * 512, 512), 512)
        val[rows] = (dot(nrm[rows], vv[...]) + vb[0:1]).astype(bf16)

    val_copy = pltpu.make_async_copy(val, val_o, tsem.at[6])
    val_copy.start()
    vv_copy = pltpu.make_async_copy(vv, vv_o, tsem.at[5])
    vv_copy.start()
    g.col(*dd(1), 1)
    for zz in (0, 2, 1, 3):
        g.diag(ll(0)[0], ll(0)[2], zz)
    g.fin(*dd(0))
    g.fin(*ll(0))

    lane = lax.broadcasted_iota(jnp.int32, (1, 128), 1)
    keeps = [(lane < HEAD_DIM).astype(bf16), (lane >= HEAD_DIM).astype(bf16)]

    def softmax(s):
        m = jnp.max(s, axis=-1, keepdims=True)
        ex = jnp.exp(s - m)
        return (ex / jnp.sum(ex, axis=-1, keepdims=True)).astype(bf16)

    @pl.loop(0, 3)
    def _(p):
        q = p + 1
        more = p < 2
        ka, kb = 1 + 2 * q, 2 + 2 * q

        def on_a(fn):
            @pl.when(more)
            def _():
                fn(ka, md.at[q % 3], gd.at[q % 3])

            @pl.when(jnp.logical_not(more))
            def _():
                fn(*fb)

        def on_b(fn):
            @pl.when(more)
            def _():
                fn(kb, ml.at[q % 3], gl.at[q % 3])

        def on_next(fn):
            @pl.when(p == 0)
            def _():
                fn(5, md.at[2], gd.at[2])

            @pl.when(p == 1)
            def _():
                fn(*fb)

        def on_next_b(fn):
            @pl.when(p == 0)
            def _():
                fn(6, ml.at[2], gl.at[2])

        def tick(pos):
            if pos == 0:
                on_next(lambda k, s, b: g.col(k, s, b, 0))
                on_a(lambda k, s, b: g.col(k, s, b, 2))
                on_a(lambda k, s, b: g.col(k, s, b, 3))
                on_next(g.zsend)
            elif pos == 1:
                on_b(lambda k, s, b: g.col(k, s, b, 1))
                on_b(lambda k, s, b: g.col(k, s, b, 2))
            elif pos == 2:
                on_b(lambda k, s, b: g.col(k, s, b, 3))
                on_next_b(lambda k, s, b: g.col(k, s, b, 0))
            elif pos == 3:
                on_a(lambda k, s, b: g.diag(k, b, 0))
                on_a(lambda k, s, b: g.diag(k, b, 2))
                for r in range(3):

                    @pl.when(p == r)
                    def _():
                        fa.level(r + 1)
            elif pos == 4:
                on_a(lambda k, s, b: g.diag(k, b, 1))
                on_a(lambda k, s, b: g.diag(k, b, 3))
                on_next_b(g.zsend)
            elif pos == 5:
                on_next(lambda k, s, b: g.col(k, s, b, 1))
                on_b(lambda k, s, b: g.diag(k, b, 0))
            elif pos == 6:
                on_b(lambda k, s, b: g.diag(k, b, 2))
            elif pos == 7:
                on_b(lambda k, s, b: g.diag(k, b, 1))
                on_b(lambda k, s, b: g.diag(k, b, 3))

        wload = pltpu.make_async_copy(gd.at[p], wst, tsem.at[7])
        lload = pltpu.make_async_copy(gl.at[p], lst, tsem.at[8])
        wload.start()
        lload.start()
        wcopy = lambda r: pltpu.make_async_copy(wv, wa_o.at[pl.ds(2 * r, 2)], wsem)
        lcopy = lambda r: pltpu.make_async_copy(lv, la_o.at[pl.ds(2 * r, 2)], lsem)

        @pl.when(p > 0)
        def _():
            wcopy(p - 1).wait()
            lcopy(p - 1).wait()

        wload.wait()

        def put_w(e, rows, x):
            wv[e, rows] = x

        def put_l(e, rows, x):
            lv[e, rows] = x

        join_pair(wst, put_w, (0, 1))
        lload.wait()
        join_pair(lst, put_l, (0, 1))
        wcopy(p).start()
        lcopy(p).start()
        lanes = pl.ds(pl.multiple_of(p * 128, 128), 128)

        def out_copies(e, d, long, h):
            row = d * 512 if long else 1024 + d * 512
            rows = pl.ds(row, 512)
            cps = [
                pltpu.make_async_copy(hidv.at[e], hid_o.at[h, rows], osem.at[e, 0]),
                pltpu.make_async_copy(slov.at[e], slo_o.at[h, rows], osem.at[e, 1]),
            ]
            if long:
                cps.append(pltpu.make_async_copy(atlv.at[e], atl_o.at[h, pl.ds(d * 512, 512)], osem.at[e, 2]))
            else:
                part = pl.ds(d * 256, 256)
                cps.append(pltpu.make_async_copy(atmv.at[e], atm_o.at[h, part], osem.at[e, 3]))
                cps.append(pltpu.make_async_copy(atsv.at[e], ats_o.at[h, part], osem.at[e, 4]))
            return cps

        pos = 0
        for d in range(2):
            for long in (True, False):
                row = d * 512 if long else 1024 + d * 512
                rows = slice(row, row + 512)
                mixed = None
                for e in range(2):
                    h = 2 * p + e
                    pre = dot(nrm[rows], wv[e]) + db[pl.ds(h, 1)]
                    hid, slo = gelu_both(pre)
                    if d == 0 and long:

                        @pl.when(p > 0)
                        def _():
                            for cp in out_copies(e, 1, False, h):
                                cp.wait()
                    else:
                        for cp in out_copies(e, d if not long else d - 1, not long, h):
                            cp.wait()
                    hidv[e] = hid.astype(bf16)
                    slov[e] = slo.astype(bf16)
                    lbias = lb[pl.ds(h, 1)]
                    vpair = val[rows, lanes] * keeps[e]
                    if long:
                        att = softmax(dot(hidv[e], lv[e]) + lbias)
                        atlv[e] = att
                        m = dot(att, vpair)
                    else:
                        short = softmax(dot(hidv[e, 0:256], lv[e, :, 0:128]) + lbias[:, 0:128])
                        mid = softmax(dot(hidv[e, 256:512], lv[e, :, 0:256]) + lbias[:, 0:256])
                        atsv[e] = short
                        atmv[e] = mid
                        m = jnp.concatenate(
                            [
                                dot(short[0:128], vpair[0:128]),
                                dot(short[128:256], vpair[128:256]),
                                dot(mid, vpair[256:512]),
                            ],
                            axis=0,
                        )
                    mixed = m if mixed is None else mixed + m
                    for cp in out_copies(e, d, long, h):
                        cp.start()
                    tick(pos)
                    pos += 1
                mixv[rows, lanes] = mixed.astype(bf16)

        @pl.when(more)
        def _():
            g.fin(ka, md.at[q % 3], gd.at[q % 3])

        on_b(g.fin)

        @pl.when(p == 2)
        def _():
            for e in range(2):
                for cp in out_copies(e, 1, False, 2 * p + e):
                    cp.wait()
            wcopy(p).wait()
            lcopy(p).wait()

    fb_swap = lambda r: remote(ef.at[c, 1, r], ef.at[c, 1, r], ssem.at[4 + r], rsem.at[4 + r], pc.sib)
    swaps = [vo_swap]
    for i, (start, to) in enumerate(((0, 512), (1024, 0))):
        mine = pltpu.make_async_copy(
            mixv.at[pl.ds(start + c * 512, 512)], mix_o.at[c, pl.ds(to, 512)], msem.at[i]
        )
        mine.start()
        other = remote(
            mixv.at[pl.ds(start + o * 512, 512)], mix_o.at[c, pl.ds(to, 512)], ssem.at[2 + i], rsem.at[2 + i], pc.sib
        )
        other.start()
        swaps += [mine, other]
    g.fin(*fb, each=lambda r: fb_swap(r).start())
    for cp in swaps + [nrm_copy, val_copy, vv_copy] + [fb_swap(r) for r in range(4)]:
        cp.wait()
    fa.finish()
    g.sent(*vo_args)
    for p in range(3):
        g.sent(*dd(p))
        g.sent(*ll(p))
    g.sent(*fb)


def k1_call(s_in, tok, dense, logit, vo, ff):
    sds = jax.ShapeDtypeStruct
    dma = pltpu.SemaphoreType.DMA
    return pl.pallas_call(
        k1_kernel,
        out_shape=(
            sds((2, 4, 2, 4, 48, HALF), bf16),
            sds((3, 4, 2, 4, 48, D), bf16),
            sds((3, 4, 2, 4, 48, L3), bf16),
            sds((2, 2, 4, 2, 4, 48, D), bf16),
            sds((CHIP_ROWS, D), bf16),
            sds((CHIP_ROWS, HALF), bf16),
            sds((6, CHIP_ROWS, HIDDEN_SIZE), bf16),
            sds((6, CHIP_ROWS, HIDDEN_SIZE), bf16),
            sds((6, 1024, L3), bf16),
            sds((6, 512, L2), bf16),
            sds((6, 512, L1), bf16),
            sds((6, D, HIDDEN_SIZE), bf16),
            sds((6, HIDDEN_SIZE, L3), bf16),
            sds((2, ROWS_DEV, HALF), bf16),
            sds((D, HALF), bf16),
            sds((8, D), f32),
            sds((4, D), f32),
        ),
        in_specs=[VMEM, HBM] + [VMEM] * 4,
        out_specs=(HBM,) * 15 + (VMEM,) * 2,
        scratch_shapes=[
            pltpu.VMEM((32, 16, 128), f32),
            pltpu.VMEM((8, HIDDEN_SIZE), f32),
            pltpu.VMEM((8, L3), f32),
            pltpu.VMEM((8, HALF), f32),
            pltpu.VMEM((2, 48, HALF), bf16),
            pltpu.VMEM((3, 2, 48, D), bf16),
            pltpu.VMEM((3, 2, 48, L3), bf16),
            pltpu.VMEM((2, 2, 48, D), bf16),
            pltpu.VMEM((CHIP_ROWS, D), bf16),
            pltpu.VMEM((CHIP_ROWS, D), bf16),
            pltpu.VMEM((CHIP_ROWS, HALF), bf16),
            pltpu.VMEM((4, 2, 4, 48, HALF), bf16),
            pltpu.VMEM((D, HALF), bf16),
            pltpu.VMEM((4, 2, 4, 48, D), bf16),
            pltpu.VMEM((4, 2, 4, 48, L3), bf16),
            pltpu.VMEM((2, D, HIDDEN_SIZE), bf16),
            pltpu.VMEM((2, HIDDEN_SIZE, L3), bf16),
            pltpu.VMEM((2, 512, HIDDEN_SIZE), bf16),
            pltpu.VMEM((2, 512, HIDDEN_SIZE), bf16),
            pltpu.VMEM((2, 512, L3), bf16),
            pltpu.VMEM((2, 256, L2), bf16),
            pltpu.VMEM((2, 256, L1), bf16),
            pltpu.VMEM((CHIP_ROWS, HALF), bf16),
        ]
        + gather_sems(8)
        + [dma((9,)), dma((2, 5)), dma, dma, dma((8,)), dma((8,)), dma((2,))]
        + [dma((4,))] * 6
        + [dma, dma((4,)), dma((4,)), dma((32,)), dma((32,)), dma((6,)), dma((6,))],
        compiler_params=pltpu.CompilerParams(
            collective_id=1, has_side_effects=True, vmem_limit_bytes=VMEM_LIMIT
        ),
        name="k1_attention",
    )(s_in, tok, dense, logit, vo, ff)


def prepare(tokens, attn_gain, attn_shift, dense_weight, dense_bias, logit_weight, logit_bias, value_weight,
            value_bias, output_weight, output_bias, feed_gain, feed_shift, expand_weight, expand_bias,
            reduce_weight, reduce_bias):
    narrow_rows = jnp.stack([attn_gain, attn_shift, value_bias, output_bias, feed_gain, feed_shift, reduce_bias])
    wide_rows = [(expand_bias.reshape(1, 96), 32), (logit_bias.reshape(3, 64), 64), (dense_bias.reshape(3, 96), 32)]
    small = jnp.concatenate(
        [jnp.pad(narrow_rows, ((0, 0), (0, 104)))] + [jnp.pad(v, ((0, 0), (0, pad))) for v, pad in wide_rows]
    )
    small = jnp.pad(small, ((0, 2), (0, 0))).astype(f32)
    dense = dense_weight.reshape(6, 48, D)
    logit = logit_weight.reshape(6, 48, L3)
    vo = jnp.stack([value_weight.reshape(24, 2, HALF), output_weight.reshape(24, 2, HALF)]).transpose(2, 0, 1, 3)
    vo = vo.reshape(2, 48, HALF)
    ff = jnp.stack(
        [expand_weight.reshape(24, 4, D).transpose(1, 0, 2).reshape(2, 48, D), reduce_weight.reshape(2, 48, D)]
    )
    return small, tokens, dense, logit, vo, ff


def k2_kernel(
    x, cot, counts, mix, ovo, ef, vec, eb,
    lay_o, gres_o, gmix_o, def_o, do_o, sums_o,
    ev, rv, ow, inner, ge, n2, gf, ga, acc, dst, rsem, dsem, osem,
):
    oloads = []
    for half in range(2):
        lanes = pl.ds(half * HALF, HALF)
        oloads.append(pltpu.make_async_copy(ovo.at[half], dst.at[0, :, :, :, :, lanes], osem.at[half]))
    loads = [pltpu.make_async_copy(ef.at[0, f], dst.at[1 - f], dsem.at[1 - f]) for f in range(2)]
    for cp in oloads:
        cp.start()
    loads[0].start()
    rloads = []
    for f in range(2):
        for j in range(4):
            rloads.append(
                pltpu.make_async_copy(ef.at[1, f, j], rv.at[j, :, :, pl.ds(48 * f, 48)], rsem.at[f, j])
            )
    for cp in rloads:
        cp.start()

    def put_o(e, rows, v):
        ow[rows] = v

    for cp in oloads:
        cp.wait()
    join_pair(dst.at[0], put_o, (1,))
    loads[1].start()
    for f in range(2):

        def put_e(e, rows, v):
            ev[2 * f + e, rows] = v

        loads[f].wait()
        join_pair(dst.at[1 - f], put_e, (0, 1))
    for cp in rloads:
        cp.wait()
    fg, fs = vec[4:5], vec[5:6]
    sums_o[...] = jnp.zeros_like(sums_o)

    @pl.loop(0, 4)
    def _(b):
        rows = pl.ds(pl.multiple_of(b * 256, 256), 256)
        mixed = jnp.concatenate([mix[0, rows], mix[1, rows]], axis=1)
        res = x[rows].astype(f32) + (dot(mixed, ow[...]) + vec[3:4])
        unit, inv = norm_rows(res)
        n2v = (unit * fg + fs).astype(bf16)
        n2[rows] = n2v
        later = jnp.where(b == 1, counts[0, 1], counts[0, 2])
        low = jnp.where(b == 0, counts[0, 0], later) >= 1
        high = jnp.where(b == 0, counts[0, 0] - 1, later) >= 1
        top = lax.broadcasted_iota(jnp.int32, (256, 1), 0) < L1
        alive = jnp.where(top, jnp.where(low, 1.0, 0.0), jnp.where(high, 1.0, 0.0))
        gout = cot[rows].astype(f32) * alive
        gfb = gout.astype(bf16)
        gf[rows] = gfb
        feed = None
        gn2 = None
        for j in range(4):
            cols = slice(j * D, j * D + D)
            rj = rv[j].reshape(D, D)
            hid, slo = gelu_both(dot(n2v, ev[j]) + eb[j : j + 1])
            hb = hid.astype(bf16)
            inner[rows, cols] = hb
            f_j = dot(hb, rj)
            feed = f_j if feed is None else feed + f_j
            geb = (dot(gfb, rj, NT) * slo).astype(bf16)
            ge[rows, cols] = geb
            g_j = dot(geb, ev[j], NT)
            gn2 = g_j if gn2 is None else gn2 + g_j
        lay_o[rows] = alive * (res + (feed + vec[6:7]))
        q = gn2 * fg
        gres = gout + inv * (
            q - jnp.mean(q, axis=-1, keepdims=True) - unit * jnp.mean(q * unit, axis=-1, keepdims=True)
        )
        gres_o[rows] = gres
        gab = gres.astype(bf16)
        ga[rows] = gab
        gm = dot(gab, ow[...], NT).astype(bf16)
        gmix_o[0, rows] = gm[:, :HALF]
        gmix_o[1, rows] = gm[:, HALF:]
        sums_o[0:1] += jnp.sum(gn2 * unit, axis=0, keepdims=True)
        sums_o[1:2] += jnp.sum(gn2, axis=0, keepdims=True)

    ones = jnp.ones((8, ROWS_DEV), bf16)
    sums_o[2:3] = dot(ones, gf[...])[0:1]
    sums_o[3:4] = dot(ones, ga[...])[0:1]

    def out_copy(t, f):
        return pltpu.make_async_copy(dst.at[f], def_o.at[t, f], dsem.at[f])

    for f in range(2):
        for e in range(2):
            j = 2 * f + e
            sums_o[4 + j : 5 + j] = dot(ones, ge[:, j * D : j * D + D])[0:1]
            acc[e] = dot(n2[...], ge[:, j * D : j * D + D], TN)

        @pl.loop(0, 4)
        def _(zz):
            for i in range(8):
                row = pl.ds(pl.multiple_of(zz * 192 + i * 24, 8), 24)
                both = jnp.concatenate([acc[0, row], acc[1, row]], axis=0)
                dst[f, zz, i // 4, i % 4] = both.astype(bf16)

        out_copy(0, f).start()
    for j in range(4):
        acc[j % 2] = dot(inner[:, j * D : j * D + D], gf[...], TN)
        if j == 0:
            out_copy(0, 0).wait()
            out_copy(0, 1).wait()
        for i in range(8):
            for f in range(2):
                at = i * 96 + f * 48
                dst[f, j, i // 4, i % 4] = acc[j % 2, at : at + 48].astype(bf16)
    for f in range(2):
        out_copy(1, f).start()
    zero = jnp.zeros((24, 128), f32)
    for hh in range(2):
        acc[0, 0:HALF] = dot(mix[hh], ga[...], TN)
        for i in range(16):
            for half in range(2):
                for r in range(3):
                    at = half * HALF + r * 128
                    part = acc[0, i * 24 : i * 24 + 24, at : at + 128]
                    both = jnp.concatenate([zero, part], axis=0).astype(bf16)
                    do_o[half, r, 2 * hh + i // 8, (i // 4) % 2, i % 4] = both
    for f in range(2):
        out_copy(1, f).wait()


def k2_call(x, cot, counts, mix, ovo, ef, vec, eb):
    sds = jax.ShapeDtypeStruct
    dma = pltpu.SemaphoreType.DMA
    return pl.pallas_call(
        k2_kernel,
        out_shape=(
            sds((ROWS_DEV, D), f32),
            sds((ROWS_DEV, D), f32),
            sds((2, ROWS_DEV, HALF), bf16),
            sds((2, 2, 4, 2, 4, 48, D), bf16),
            sds((2, 3, 4, 2, 4, 48, 128), bf16),
            sds((8, D), f32),
        ),
        in_specs=[VMEM, VMEM, pl.BlockSpec(memory_space=pltpu.SMEM), VMEM] + [HBM] * 2 + [VMEM] * 2,
        out_specs=(VMEM, VMEM, VMEM, HBM, VMEM, VMEM),
        scratch_shapes=[
            pltpu.VMEM((4, D, D), bf16),
            pltpu.VMEM((4, 2, 4, 96, D), bf16),
            pltpu.VMEM((D, D), bf16),
            pltpu.VMEM((ROWS_DEV, 4 * D), bf16),
            pltpu.VMEM((ROWS_DEV, 4 * D), bf16),
            pltpu.VMEM((ROWS_DEV, D), bf16),
            pltpu.VMEM((ROWS_DEV, D), bf16),
            pltpu.VMEM((ROWS_DEV, D), bf16),
            pltpu.VMEM((2, D, D), f32),
            pltpu.VMEM((2, 4, 2, 4, 48, D), bf16),
            dma((2, 4)),
            dma((2,)),
            dma((2,)),
        ],
        compiler_params=pltpu.CompilerParams(vmem_limit_bytes=VMEM_LIMIT),
        name="k2_feed",
    )(x, cot, counts, mix, ovo, ef, vec, eb)


class Scatter:
    def __init__(self, pc, sems):
        self.pc = pc
        self.as_, self.ar, self.xs, self.xr, self.ys, self.yr, self.zs, self.zr, self.os, self.or_ = sems

    def acopy(self, k, p5, bufs, zz):
        dev = self.pc.xdev if zz < 2 else self.pc.ydev
        return remote(p5.at[zz, :, self.pc.nd], bufs[0].at[zz], self.as_.at[k, zz], self.ar.at[k, zz], dev)

    def xcopy(self, k, p5, bufs, zz):
        return remote(p5.at[zz, :, self.pc.nx], bufs[1].at[zz], self.xs.at[k, zz], self.xr.at[k, zz], self.pc.xdev)

    def ycopy(self, k, p5, bufs, zz):
        return remote(p5.at[zz, :, self.pc.ny], bufs[2].at[zz], self.ys.at[k, zz], self.yr.at[k, zz], self.pc.ydev)

    def zcopy(self, k, p5, bufs, i):
        zz = self.pc.zpos(i)
        return remote(
            p5.at[zz, :, self.pc.n], bufs[3].at[i - 1], self.zs.at[k, i], self.zr.at[k, i], self.pc.zdev(zz)
        )

    def row(self, k, p5, bufs, zz):
        self.acopy(k, p5, bufs, zz).start()
        (self.xcopy if zz < 2 else self.ycopy)(k, p5, bufs, zz).start()

    def one(self, k, p5, bufs):
        for zz in (0, 2, 1, 3):
            self.acopy(k, p5, bufs, zz).start()
        for zz in (0, 2, 1, 3):
            (self.xcopy if zz < 2 else self.ycopy)(k, p5, bufs, zz).start()

    def twos(self, k, p5, bufs):
        for zz in (0, 2, 1, 3):
            self.two(k, p5, bufs, zz)

    def threes(self, k, p5, bufs):
        for i in (1, 2, 3):
            self.three(k, p5, bufs, i)

    def two(self, k, p5, bufs, zz):
        col = self.pc.ny if zz < 2 else self.pc.nx
        self.acopy(k, p5, bufs, zz).wait_recv()
        p5[zz, :, col] = (p5[zz, :, col].astype(f32) + bufs[0][zz].astype(f32)).astype(bf16)
        (self.ycopy if zz < 2 else self.xcopy)(k, p5, bufs, zz).start()

    def column(self, k, p5, bufs, zz):
        self.xcopy(k, p5, bufs, zz).wait_recv()
        self.ycopy(k, p5, bufs, zz).wait_recv()
        return p5[zz, :, self.pc.n].astype(f32) + bufs[1][zz].astype(f32) + bufs[2][zz].astype(f32)

    def three(self, k, p5, bufs, i):
        zz = self.pc.zpos(i)
        p5[zz, :, self.pc.n] = self.column(k, p5, bufs, zz).astype(bf16)
        self.zcopy(k, p5, bufs, i).start()

    def outs(self, k, st, out):
        c = self.pc.c
        return (
            pltpu.make_async_copy(st.at[c], out, self.os.at[k, 1]),
            remote(st.at[1 - c], out, self.os.at[k, 0], self.or_.at[k], self.pc.sib),
        )

    def four(self, k, p5, bufs, st, out):
        total = self.column(k, p5, bufs, self.pc.z)
        for i in (1, 2, 3):
            self.zcopy(k, p5, bufs, i).wait_recv()
            total = total + bufs[3][i - 1].astype(f32)
        st[...] = total
        for cp in self.outs(k, st, out):
            cp.start()

    def sent(self, k, p5, bufs):
        for zz in range(4):
            self.acopy(k, p5, bufs, zz).wait_send()
            self.xcopy(k, p5, bufs, zz).wait_send()
            self.ycopy(k, p5, bufs, zz).wait_send()
        for i in (1, 2, 3):
            self.zcopy(k, p5, bufs, i).wait_send()


def k3_kernel(
    def_in, do_in, nrm_i, val_i, gmix, hid_i, slo_i, atl_i, atm_i, ats_i, wa_i, la_i, vv_i, tok, gres, vec, sums,
    tg_o, od, ol, ofe, ovo, va,
    db_o, lb_o, vb_o, ag_o, vg, vr, vt,
    nrm, val, gm, gn, hid, slo, atl, atm, ats, gsl, gsm, gd, wv, lv, dwf, vsb, vv, own,
    pd, pll, pv, ad, xd, yd, zd, al, xl, yl, zl, av, xv, yv, zv, std, stl, stv,
    as_, ar, xs, xr, ys, yr, zs, zr, os_, or_, lsem, ssem, rsem, gs_, gr_, free, hsem, fsem, dsem,
    fss, fsr, v1s, v1r, v2s, v2r,
):
    pc = Place()
    c = pc.c
    o = 1 - c
    s = Scatter(pc, (as_, ar, xs, xr, ys, yr, zs, zr, os_, or_))
    copy = pltpu.make_async_copy
    first = [copy(nrm_i, nrm, lsem.at[0]), copy(val_i, val, lsem.at[1]), copy(vv_i, vv, lsem.at[2])]
    for i, (at, to) in enumerate(((512, 0), (0, 1024))):
        first.append(copy(gmix.at[c, pl.ds(at, 512)], gm.at[pl.ds(pl.multiple_of(to + c * 512, 512), 512)], lsem.at[4 + i]))
    for cp in first:
        cp.start()

    def att_loads(h):
        return [copy(atl_i.at[h], atl, hsem.at[0]), copy(atm_i.at[h], atm, hsem.at[1]), copy(ats_i.at[h], ats, hsem.at[2])]

    hid_load = lambda h: copy(hid_i.at[h], hid, hsem.at[3])
    w_load = lambda h: copy(wa_i.at[h], wv, hsem.at[4])
    l_load = lambda h: copy(la_i.at[h], lv, hsem.at[5])
    slo_load = lambda h, b: copy(slo_i.at[h, pl.ds(b * 512, 512)], slo.at[b % 2], hsem.at[6 + b % 2])
    for cp in att_loads(0) + [hid_load(0), l_load(0), slo_load(0, 0), slo_load(0, 1), w_load(0)]:
        cp.start()
    order = [(f, zz) for f in (1, 0) for zz in (0, 2, 1, 3)]
    own_load = lambda i: copy(def_in.at[(c,) + order[i]], own.at[i % 2], fsem.at[i % 2])
    own_load(0).start()
    own_load(1).start()

    me = pc.w * 4 + pc.n
    bar = pltpu.get_barrier_semaphore()
    everyone(me, lambda t, f, dev: pl.semaphore_signal(bar, inc=1, device_id=dev, device_id_type=MESH))
    pl.semaphore_wait(bar, 31)
    fswaps = []
    for i, (f, zz) in enumerate(order):
        fswaps.append(remote(def_in.at[o, f, zz], pd.at[f, zz], fss.at[i], fsr.at[i], pc.sib))
    swaps = [None, None]
    swaps.append(remote(do_in.at[o], pv, ssem.at[2], rsem.at[2], pc.sib))
    for i, (at, to) in enumerate(((512, 0), (0, 1024))):
        swaps.append(
            remote(
                gmix.at[o, pl.ds(at, 512)],
                gm.at[pl.ds(pl.multiple_of(to + c * 512, 512), 512)],
                ssem.at[3 + i],
                rsem.at[3 + i],
                pc.sib,
            )
        )
    for cp in fswaps[0:4] + swaps[3:5] + fswaps[4:8] + swaps[2:3]:
        cp.start()

    def d_args(k):
        slot = k % 3
        return pd.at[slot], (ad.at[k], xd.at[k], yd.at[k], zd.at[k])

    def l_args(p):
        return pll.at[p % 2], (al.at[p], xl.at[p], yl.at[p], zl.at[p])

    def v_args(p):
        return pv.at[p], (av.at[p], xv.at[p], yv.at[p], zv.at[p])

    gn[...] = jnp.zeros_like(gn)
    gsm[...] = jnp.zeros_like(gsm)


    def core_sum(i):
        f, zz = order[i]
        fswaps[i].wait()
        own_load(i).wait()
        pd[f, zz] = (pd[f, zz].astype(f32) + own[i % 2].astype(f32)).astype(bf16)
        if i < 6:
            own_load(i + 2).start()
        s.row(f, *d_args(f), zz)

    dloads = []
    for r in range(3):
        for zz in range(4):
            to = pl.ds(HALF * (zz % 2) + 128 * r, 128)
            dloads.append(copy(do_in.at[c, r, zz], own.at[zz // 2, :, :, :, to], dsem.at[r, zz]))

    def other_half():
        for i in range(4, 8):
            core_sum(i)
        for cp in dloads:
            cp.start()

    def dloads_done():
        for cp in swaps[2:3] + dloads:
            cp.wait()

    for i in range(4):
        core_sum(i)
    swaps[3].wait()
    swaps[4].wait()
    for cp in first:
        cp.wait()

    lane = lax.broadcasted_iota(jnp.int32, (1, 128), 1)
    keeps = [(lane < HEAD_DIM).astype(bf16), (lane >= HEAD_DIM).astype(bf16)]
    ones = jnp.ones((8, 1024), bf16)

    def score_grad(att, g):
        a = att.astype(f32)
        t = a * g
        return (t - a * jnp.sum(t, axis=-1, keepdims=True)).astype(bf16)

    def put_pair(p5, half, e, width):
        @pl.loop(0, 2)
        def _(zi):
            for i in range(8):
                row = pl.ds(pl.multiple_of(zi * 192 + i * 24, 8), 24)
                part = dwf[row, 0:width]
                if e == 0:
                    both = jnp.concatenate([part, part], axis=0)
                else:
                    old = p5[2 * half + zi, i // 4, i % 4].astype(f32)
                    both = jnp.concatenate([old[0:24], part], axis=0)
                p5[2 * half + zi, i // 4, i % 4] = both.astype(bf16)

    @pl.loop(0, 3)
    def _(p):
        lanes = pl.ds(pl.multiple_of(p * 128, 128), 128)
        begin = p == 0
        later = p > 0
        kd = p + 2
        dslot = kd % 3

        def on_a(fn):
            fn(kd - 1, *d_args(kd - 1))

        def on_b(fn):
            @pl.when(begin)
            def _():
                fn(0, *d_args(0))

            @pl.when(later)
            def _():
                fn(5 + (p + 2) % 3, *l_args((p + 2) % 3))

        def on_first(*fns):
            for r, fn in enumerate(fns):
                if fn is not None:
                    pl.when(p == r)(fn)

        def on_v(fn):
            @pl.when(later)
            def _():
                fn(8 + (p + 2) % 3, *v_args((p + 2) % 3))

        def four_a():
            @pl.when(begin)
            def _():
                s.four(1, *d_args(1), std.at[1], ofe.at[c, 1])

            @pl.when(p == 2)
            def _():
                for cp in s.outs(0, std.at[0], ofe.at[c, 0]):
                    cp.wait()

            @pl.when(later)
            def _():
                s.four(kd - 1, *d_args(kd - 1), std.at[(kd - 1) % 3], od.at[3 * c + (p + 2) % 3])

        def four_b():
            @pl.when(begin)
            def _():
                s.four(0, *d_args(0), std.at[0], ofe.at[c, 0])

            @pl.when(later)
            def _():
                r = (p + 2) % 3
                s.four(5 + r, *l_args(r), stl.at[r], ol.at[3 * c + r])

        def four_v():
            @pl.when(later)
            def _():
                r = (p + 2) % 3
                s.four(8 + r, *v_args(r), stv.at[r], ovo.at[r, c])

        def value_part():
            for half in range(2):
                cols = slice(half * HALF, half * HALF + HALF)
                dwf[:, 0:128] = dot(nrm[:, cols], gm[:, lanes], TN)

                @pl.loop(0, 8)
                def _(i):
                    for zi in range(2):
                        row = pl.ds(pl.multiple_of(zi * 192 + i * 24, 8), 24)
                        at = (2 * half + zi, i // 4, i % 4)
                        to = pl.ds(pl.multiple_of(HALF * zi + 128 * p, 128), 128)
                        both = pv[(p,) + at].astype(f32) + own[half, i // 4, i % 4, :, to].astype(f32)
                        pv[(p,) + at] = jnp.concatenate([dwf[row, 0:128], both[24:48]], axis=0).astype(bf16)

        def tick(e, what):
            if what == "gs" and e == 0:
                on_first(lambda: s.twos(1, *d_args(1)))
                on_v(s.threes)
            elif what == "gd" and e == 0:
                on_first(other_half)
                four_v()
            elif what == "dw" and e == 0:
                on_b(s.twos)
            elif what == "gs":
                on_first(dloads_done)
                value_part()
                s.one(8 + p, *v_args(p))
                on_a(s.threes)
            elif what == "gd":
                on_b(s.threes)
            elif what == "dw":
                s.twos(8 + p, *v_args(p))
                s.one(kd, *d_args(kd))
            elif what == "dl" and e == 1:
                s.one(5 + p, *l_args(p))
                four_a()
            elif what == "gn" and e == 1:
                s.twos(kd, *d_args(kd))
                four_b()

        def logit_part(e):
            h = 2 * p + e
            if e == 0:

                @pl.when(p == 2)
                def _():
                    s.sent(5, *l_args(0))

            hid_load(h).wait()
            for half in range(2):
                cols = slice(half * HALF, half * HALF + HALF)
                dwf[:, 0:512] = dot(hid[0:1024, cols], gsl[e], TN)
                dwf[:, 0:256] += dot(hid[1024:2048, cols], gsm[e], TN)
                put_pair(pll.at[p % 2], half, e, 512)

            @pl.when(h < 5)
            def _():
                hid_load(h + 1).start()

            tick(e, "dl")

        for e in range(2):
            h = 2 * p + e
            more = h < 5

            def ahead(*cps):
                @pl.when(more)
                def _():
                    for cp in cps:
                        cp.start()

            for cp in att_loads(h):
                cp.wait()
            for b in range(4):
                at = b * 512
                rows = slice(at, at + 512)
                gpair = gm[rows, lanes]
                vpair = val[rows, lanes] * keeps[e]
                gkeep = gpair * keeps[e]
                if b < 2:
                    att = atl[rows]
                    gsl[e, rows] = score_grad(att, dot(gpair, vpair, NT))
                    vs = dot(att, gkeep, TN)
                else:
                    part = slice((b - 2) * 256, (b - 2) * 256 + 256)
                    sh, mi = ats[part], atm[part]
                    g_sh = jnp.concatenate(
                        [dot(gpair[0:128], vpair[0:128], NT), dot(gpair[128:256], vpair[128:256], NT)], axis=0
                    )
                    at2 = (b - 2) * 512
                    gsm[e, at2 : at2 + 256, 0:128] = score_grad(sh, g_sh)
                    gsm[e, at2 + 256 : at2 + 512] = score_grad(mi, dot(gpair[256:512], vpair[256:512], NT))
                    vs = jnp.concatenate(
                        [
                            dot(sh[0:128], gkeep[0:128], TN),
                            dot(sh[128:256], gkeep[128:256], TN),
                            dot(mi, gkeep[256:512], TN),
                        ],
                        axis=0,
                    )
                if e == 0:
                    vsb[rows] = vs.astype(bf16)
                else:
                    gm[rows, lanes] = vsb[rows] + vs.astype(bf16)
            ahead(*att_loads(h + 1))
            lsum = dot(ones, gsl[e])
            lb_o[pl.ds(h, 1)] = lsum[0:1]
            lb_o[pl.ds(h, 1), 0:256] += dot(ones, gsm[e])[0:1]
            tick(e, "gs")
            l_load(h).wait()
            for b in range(4):
                rows = slice(b * 512, b * 512 + 512)
                slo_load(h, b).wait()
                if b < 2:
                    gh = dot(gsl[e, rows], lv[...], NT)
                else:
                    gh = dot(gsm[e, (b - 2) * 512 : (b - 2) * 512 + 512], lv[:, 0:256], NT)
                gd[rows] = (gh * slo[b % 2].astype(f32)).astype(bf16)
                if b < 2:
                    slo_load(h, b + 2).start()
                else:
                    ahead(slo_load(h + 1, b - 2))
            ahead(l_load(h + 1))
            db_o[pl.ds(h, 1)] = (dot(ones, gd[0:1024]) + dot(ones, gd[1024:2048]))[0:1]
            tick(e, "gd")
            if e == 0:

                @pl.when(later)
                def _():
                    s.sent(kd - 3, *d_args(kd - 3))

            for half in range(2):
                cols = slice(half * HALF, half * HALF + HALF)
                dwf[...] = dot(nrm[:, cols], gd[...], TN)
                put_pair(pd.at[dslot], half, e, D)
            tick(e, "dw")
            if e == 1:
                logit_part(0)
                logit_part(1)
            w_load(h).wait()

            @pl.loop(0, 4)
            def _(b):
                rows = pl.ds(pl.multiple_of(b * 512, 512), 512)
                gn[rows] += dot(gd[rows], wv[...], NT)

            ahead(w_load(h + 1))
            tick(e, "gn")

    pl.semaphore_signal(free, inc=1, device_id=pc.sib, device_id_type=MESH)
    vb_o[...] = dot(ones, gm[0:1024]) + dot(ones, gm[1024:2048])

    @pl.loop(0, 4)
    def _(b):
        rows = pl.ds(pl.multiple_of(b * 512, 512), 512)
        gn[rows] += dot(gm[rows], vv[...], NT)

    s.threes(10, *v_args(2))
    other = lambda to: pl.ds(pl.multiple_of(to + o * 512, 512), 512)
    mine = lambda to: pl.ds(pl.multiple_of(to + c * 512, 512), 512)
    hid[0:512] = gn[other(1024)].astype(bf16)
    hid[512:1024] = gn[other(0)].astype(bf16)
    pl.semaphore_wait(free, 1)
    gswap = remote(hid.at[pl.ds(0, 1024)], gd.at[pl.ds(0, 1024)], gs_, gr_, pc.sib)
    gswap.start()
    tloads = [copy(tok.at[pl.ds(i * 512, 512)], slo.at[i], hsem.at[6 + i]) for i in range(2)]
    for cp in tloads:
        cp.start()
    s.twos(7, *l_args(2))
    for cp in tloads:
        cp.wait()
    gswap.wait()
    ag_o[...] = jnp.zeros_like(ag_o)

    @pl.loop(0, 4)
    def _(b):
        nat = pl.ds(pl.multiple_of(b * 256, 256), 256)
        trow = pl.ds(pl.multiple_of(jnp.where(b < 2, 1024 + b * 256, b * 256 - 512) + c * 512, 256), 256)
        load = copy(gres.at[nat], dwf.at[pl.ds(0, 256)], lsem.at[6])
        load.start()
        unit, inv = norm_rows(slo[b // 2, pl.ds(pl.multiple_of((b % 2) * 256, 256), 256)].astype(f32))
        g = gn[trow] + gd[nat].astype(f32)
        q = g * vec[0:1]
        back = inv * (q - jnp.mean(q, axis=-1, keepdims=True) - unit * jnp.mean(q * unit, axis=-1, keepdims=True))
        load.wait()
        dwf[0:256] = dwf[0:256] + back
        ag_o[0:1] += jnp.sum(g * unit, axis=0, keepdims=True)
        ag_o[1:2] += jnp.sum(g, axis=0, keepdims=True)
        store = copy(dwf.at[pl.ds(0, 256)], tg_o.at[nat], lsem.at[7])
        store.start()
        store.wait()

    vg[...] = jnp.zeros_like(vg)
    whole = [ag_o[0:1], ag_o[1:2], None, sums[3:4], sums[0:1], sums[1:2], sums[2:3]]
    whole += [sums[4 + j : 5 + j] for j in range(4)]
    for i, row in enumerate(whole):
        if row is not None:
            for b in range(6):
                vg[i, b : b + 1] = row[:, 128 * b : 128 * b + 128]
    for b in range(3):
        vg[2, pl.ds(3 * c + b, 1)] = vb_o[0:1, 128 * b : 128 * b + 128]
    for h in range(6):
        for b in range(6):
            vg[11 + 6 * c + h, b : b + 1] = db_o[h : h + 1, 128 * b : 128 * b + 128]
        for b in range(4):
            k = 4 * h + b
            vg[23 + 4 * c + k // 6, k % 6 : k % 6 + 1] = lb_o[h : h + 1, 128 * b : 128 * b + 128]
    everyone(me, lambda t, f, dev: remote(vg.at[t], vr.at[me], v1s.at[t], v1r.at[me], dev).start())
    vr[me] = vg[me]
    s.threes(4, *d_args(4))
    s.threes(7, *l_args(2))

    def part_done(t, f, dev):
        cp = remote(vg.at[t], vr.at[f], v1s.at[t], v1r.at[f], dev)
        cp.wait_send()
        cp.wait_recv()

    everyone(me, part_done)
    vt[...] = jnp.sum(vr[...], axis=0)
    everyone(me, lambda t, f, dev: remote(vt, va.at[me], v2s.at[t], v2r.at[me], dev).start())
    va[me] = vt[...]
    s.four(10, *v_args(2), stv.at[2], ovo.at[2, c])
    for cp in s.outs(1, std.at[1], ofe.at[c, 1]):
        cp.wait()
    s.four(4, *d_args(4), std.at[1], od.at[3 * c + 2])
    s.four(7, *l_args(2), stl.at[2], ol.at[3 * c + 2])

    def whole_done(t, f, dev):
        cp = remote(vt, va.at[f], v2s.at[t], v2r.at[f], dev)
        cp.wait_send()
        cp.wait_recv()

    everyone(me, whole_done)
    ends = []
    for p in range(3):
        ends.append(s.outs(2 + p, std.at[(2 + p) % 3], od.at[3 * c + p]))
        ends.append(s.outs(5 + p, stl.at[p], ol.at[3 * c + p]))
        ends.append(s.outs(8 + p, stv.at[p], ovo.at[p, c]))
    for pair in ends:
        for cp in pair:
            cp.wait()
    for k in (2, 3, 4):
        s.sent(k, *d_args(k))
    for p in (1, 2):
        s.sent(5 + p, *l_args(p))
    for p in range(3):
        s.sent(8 + p, *v_args(p))


def k3_call(*args):
    sds = jax.ShapeDtypeStruct
    dma = pltpu.SemaphoreType.DMA
    V = pltpu.VMEM

    def bufs(shape, width):
        return [V(shape + (4, 2, 48, width), bf16)] * 3 + [V(shape + (3, 2, 48, width), bf16)]

    return pl.pallas_call(
        k3_kernel,
        out_shape=(
            sds((ROWS_DEV, D), f32),
            sds((6, 48, D), f32),
            sds((6, 48, L3), f32),
            sds((2, 2, 48, D), f32),
            sds((3, 2, 48, 128), f32),
            sds((32, 8, 128), f32),
        ),
        in_specs=[HBM] * 15 + [VMEM] * 2,
        out_specs=(HBM,) * 5 + (VMEM,),
        scratch_shapes=[
            V((8, D), f32),
            V((8, L3), f32),
            V((8, HALF), f32),
            V((8, D), f32),
            V((32, 8, 128), f32),
            V((32, 8, 128), f32),
            V((8, 128), f32),
            V((CHIP_ROWS, D), bf16),
            V((CHIP_ROWS, HALF), bf16),
            V((CHIP_ROWS, HALF), bf16),
            V((CHIP_ROWS, D), f32),
            V((CHIP_ROWS, HIDDEN_SIZE), bf16),
            V((2, 512, HIDDEN_SIZE), bf16),
            V((1024, L3), bf16),
            V((512, L2), bf16),
            V((512, L1), bf16),
            V((2, 1024, L3), bf16),
            V((2, 1024, L2), bf16),
            V((CHIP_ROWS, HIDDEN_SIZE), bf16),
            V((D, HIDDEN_SIZE), bf16),
            V((HIDDEN_SIZE, L3), bf16),
            V((HALF, D), f32),
            V((CHIP_ROWS, 128), bf16),
            V((D, HALF), bf16),
            V((2, 2, 4, 48, D), bf16),
            V((3, 4, 2, 4, 48, D), bf16),
            V((2, 4, 2, 4, 48, L3), bf16),
            V((3, 4, 2, 4, 48, 128), bf16),
        ]
        + bufs((5,), D)
        + bufs((3,), L3)
        + bufs((3,), 128)
        + [V((3, 2, 48, D), f32), V((3, 2, 48, L3), f32), V((3, 2, 48, 128), f32)]
        + [dma((11, 4))] * 8
        + [dma((11, 2)), dma((11,)), dma((8,)), dma((5,)), dma((5,)), dma, dma, pltpu.SemaphoreType.REGULAR]
        + [dma((8,)), dma((2,)), dma((3, 4))]
        + [dma((8,))] * 2
        + [dma((32,))] * 4,
        compiler_params=pltpu.CompilerParams(
            collective_id=2, has_side_effects=True, vmem_limit_bytes=VMEM_LIMIT
        ),
        name="k3_backward",
    )(*args)


def chip_body(tokens, cotangent, bucket_counts, *params):
    ovo, _, _, ef, nrm, val, hid, slo, atl, atm, ats, wa, la, mix, vv, vec, eb = k1_call(*prepare(tokens, *params))
    lay, gres, gmix, dff, dout, sums = k2_call(tokens, cotangent, bucket_counts, mix, ovo, ef, vec, eb)
    tg, od, ol, ofe, dvo, every = k3_call(
        dff, dout, nrm, val, gmix, hid, slo, atl, atm, ats, wa, la, vv, tokens, gres, vec, sums
    )
    me = lax.axis_index(AXES[0]) * 4 + lax.axis_index(AXES[1])
    every = every[:, :6]
    v7 = lax.dynamic_slice(every[0:7].reshape(7, D), (0, 24 * me), (7, 24))
    own = lambda i, j, size: lax.dynamic_slice(every[i:j].reshape(-1), (size * me,), (size,))
    vo_shard = lambda r: dvo[:, :, r : r + 24].transpose(2, 1, 0, 3).reshape(24, D)
    small = lambda i: v7[i]
    return (
        lay,
        tg,
        small(0),
        small(1),
        od.reshape(HEADS, 24, HIDDEN_SIZE),
        own(11, 23, 288),
        ol.reshape(HEADS, 24, L3),
        own(23, 31, 192),
        vo_shard(0),
        small(2),
        vo_shard(24),
        small(3),
        small(4),
        small(5),
        ofe[0].reshape(4, 24, D).transpose(1, 0, 2).reshape(24, 4 * D),
        own(7, 11, 96),
        ofe[1].reshape(96, D),
        small(6),
    )


def smooth_gate(values_in):
    return (
        0.5
        * values_in
        * (1.0 + jnp.tanh(gelu_root * (values_in + gelu_cube * values_in * values_in * values_in)))
    )


def gate_slope(values_in):
    squared = values_in * values_in
    tangent = jnp.tanh(gelu_root * (values_in + gelu_cube * squared * values_in))
    return 0.5 * (1.0 + tangent) + 0.5 * values_in * (1.0 - tangent * tangent) * gelu_root * (
        1.0 + 3.0 * gelu_cube * squared
    )


def bucket_layout():
    return ((S1, L1), (S2, L2), (S3, L3))


def live_rows(counts):
    pieces = []
    for bucket_index, (slot_count, seq_length) in enumerate(bucket_layout()):
        slot_of_row = jnp.arange(slot_count * seq_length, dtype=jnp.int32) // seq_length
        pieces.append(jnp.where(slot_of_row < counts[bucket_index], 1.0, 0.0).astype(jnp.float32))
    return jnp.concatenate(pieces)


def product(left_side, right_side):
    return jnp.dot(left_side, right_side, preferred_element_type=jnp.float32)


def column_sums(matrix_rows):
    return jnp.sum(matrix_rows.astype(jnp.float32), axis=0)


def norm_forward(inputs_float, norm_gain, norm_shift):
    row_mean = jnp.mean(inputs_float, axis=-1, keepdims=True)
    centred = inputs_float - row_mean
    inverse_scale = lax.rsqrt(jnp.mean(centred * centred, axis=-1, keepdims=True) + norm_eps)
    unit_rows = centred * inverse_scale
    return (unit_rows * norm_gain + norm_shift, unit_rows, inverse_scale)


def norm_backward(grad_normed, unit_rows, inverse_scale, norm_gain):
    grad_unit = grad_normed * norm_gain
    grad_inputs = inverse_scale * (
        grad_unit
        - jnp.mean(grad_unit, axis=-1, keepdims=True)
        - unit_rows * jnp.mean(grad_unit * unit_rows, axis=-1, keepdims=True)
    )
    return (grad_inputs, jnp.sum(grad_normed * unit_rows, axis=0), jnp.sum(grad_normed, axis=0))


def forward_pass(tokens, live_mask, gathered):
    (
        attn_gain,
        attn_shift,
        dense_weight,
        dense_bias,
        logit_weight,
        logit_bias,
        value_weight,
        value_bias,
        output_weight,
        output_bias,
        feed_gain,
        feed_shift,
        expand_weight,
        expand_bias,
        reduce_weight,
        reduce_bias,
    ) = gathered
    inputs_float = tokens.astype(jnp.float32)
    normed_float, unit_one, scale_one = norm_forward(
        inputs_float, attn_gain.astype(jnp.float32), attn_shift.astype(jnp.float32)
    )
    normed = normed_float.astype(jnp.bfloat16)
    values = (product(normed, value_weight) + value_bias.astype(jnp.float32)).astype(jnp.bfloat16)
    dense_heads = dense_bias.astype(jnp.float32).reshape(HEADS, 1, HIDDEN_SIZE)
    logit_heads = logit_bias.astype(jnp.float32).reshape(HEADS, 1, L3)
    pre_list, hidden_list, attention_list, mixed_list = ([], [], [], [])
    start_row = 0
    for slot_count, seq_length in bucket_layout():
        stop_row = start_row + slot_count * seq_length
        pre_act = (
            jnp.einsum(
                "rd,hde->hre",
                normed[start_row:stop_row],
                dense_weight,
                preferred_element_type=jnp.float32,
            )
            + dense_heads
        )
        hidden = smooth_gate(pre_act).astype(jnp.bfloat16)
        scores = (
            jnp.einsum(
                "hre,hel->hrl",
                hidden,
                logit_weight[:, :, :seq_length],
                preferred_element_type=jnp.float32,
            )
            + logit_heads[:, :, :seq_length]
        )
        attention = jax.nn.softmax(scores, axis=-1)
        attention_low = attention.astype(jnp.bfloat16).reshape(
            HEADS, slot_count, seq_length, seq_length
        )
        block_values = values[start_row:stop_row].reshape(slot_count, seq_length, HEADS, HEAD_DIM)
        mixed_heads = jnp.einsum(
            "hsql,slhc->sqhc", attention_low, block_values, preferred_element_type=jnp.float32
        )
        mixed_list.append(mixed_heads.reshape(slot_count * seq_length, D))
        pre_list.append(pre_act)
        hidden_list.append(hidden)
        attention_list.append(attention)
        start_row = stop_row
    mixed_all = jnp.concatenate(mixed_list, axis=0).astype(jnp.bfloat16)
    attended = product(mixed_all, output_weight) + output_bias.astype(jnp.float32)
    residual = inputs_float + attended
    normed_two_float, unit_two, scale_two = norm_forward(
        residual, feed_gain.astype(jnp.float32), feed_shift.astype(jnp.float32)
    )
    normed_two = normed_two_float.astype(jnp.bfloat16)
    expand_pre = product(normed_two, expand_weight) + expand_bias.astype(jnp.float32)
    inner_act = smooth_gate(expand_pre).astype(jnp.bfloat16)
    feed_out = product(inner_act, reduce_weight) + reduce_bias.astype(jnp.float32)
    layer_out = live_mask[:, None] * (residual + feed_out)
    stored = (
        normed,
        unit_one,
        scale_one,
        values,
        pre_list,
        hidden_list,
        attention_list,
        mixed_all,
        unit_two,
        scale_two,
        normed_two,
        expand_pre,
        inner_act,
    )
    return (layer_out, stored)


def backward_pass(cotangent, live_mask, gathered, stored):
    (
        attn_gain,
        attn_shift,
        dense_weight,
        dense_bias,
        logit_weight,
        logit_bias,
        value_weight,
        value_bias,
        output_weight,
        output_bias,
        feed_gain,
        feed_shift,
        expand_weight,
        expand_bias,
        reduce_weight,
        reduce_bias,
    ) = gathered
    (
        normed,
        unit_one,
        scale_one,
        values,
        pre_list,
        hidden_list,
        attention_list,
        mixed_all,
        unit_two,
        scale_two,
        normed_two,
        expand_pre,
        inner_act,
    ) = stored
    grad_out = cotangent.astype(jnp.float32) * live_mask[:, None]
    grad_feed = grad_out.astype(jnp.bfloat16)
    reduce_weight_grad = jnp.einsum(
        "rf,rd->fd", inner_act, grad_feed, preferred_element_type=jnp.float32
    )
    reduce_bias_grad = column_sums(grad_feed)
    grad_inner = jnp.einsum(
        "rd,fd->rf", grad_feed, reduce_weight, preferred_element_type=jnp.float32
    )
    grad_expand = (grad_inner * gate_slope(expand_pre)).astype(jnp.bfloat16)
    expand_weight_grad = jnp.einsum(
        "rd,rf->df", normed_two, grad_expand, preferred_element_type=jnp.float32
    )
    expand_bias_grad = column_sums(grad_expand)
    grad_normed_two = jnp.einsum(
        "rf,df->rd", grad_expand, expand_weight, preferred_element_type=jnp.float32
    )
    grad_residual_norm, feed_gain_grad, feed_shift_grad = norm_backward(
        grad_normed_two, unit_two, scale_two, feed_gain.astype(jnp.float32)
    )
    grad_residual = grad_out + grad_residual_norm
    grad_attended = grad_residual.astype(jnp.bfloat16)
    output_weight_grad = jnp.einsum(
        "rd,re->de", mixed_all, grad_attended, preferred_element_type=jnp.float32
    )
    output_bias_grad = column_sums(grad_attended)
    grad_mixed = jnp.einsum(
        "re,de->rd", grad_attended, output_weight, preferred_element_type=jnp.float32
    ).astype(jnp.bfloat16)
    dense_weight_grad = jnp.zeros((HEADS, D, HIDDEN_SIZE), jnp.float32)
    dense_bias_grad = jnp.zeros((HEADS, HIDDEN_SIZE), jnp.float32)
    logit_weight_grad = jnp.zeros((HEADS, HIDDEN_SIZE, L3), jnp.float32)
    logit_bias_grad = jnp.zeros((HEADS, L3), jnp.float32)
    grad_normed_list, value_sum_list = ([], [])
    start_row = 0
    for bucket_index, (slot_count, seq_length) in enumerate(bucket_layout()):
        row_count = slot_count * seq_length
        stop_row = start_row + row_count
        attention = attention_list[bucket_index]
        hidden = hidden_list[bucket_index]
        pre_act = pre_list[bucket_index]
        attention_low = attention.astype(jnp.bfloat16).reshape(
            HEADS, slot_count, seq_length, seq_length
        )
        block_values = values[start_row:stop_row].reshape(slot_count, seq_length, HEADS, HEAD_DIM)
        block_grad = grad_mixed[start_row:stop_row].reshape(slot_count, seq_length, HEADS, HEAD_DIM)
        grad_attention = jnp.einsum(
            "sqhc,slhc->hsql", block_grad, block_values, preferred_element_type=jnp.float32
        ).reshape(HEADS, row_count, seq_length)
        value_sum_list.append(
            jnp.einsum(
                "hsql,sqhc->slhc", attention_low, block_grad, preferred_element_type=jnp.float32
            ).reshape(row_count, D)
        )
        grad_scores = (
            attention
            * (grad_attention - jnp.sum(attention * grad_attention, axis=-1, keepdims=True))
        ).astype(jnp.bfloat16)
        logit_weight_grad = logit_weight_grad.at[:, :, :seq_length].add(
            jnp.einsum("hre,hrl->hel", hidden, grad_scores, preferred_element_type=jnp.float32)
        )
        logit_bias_grad = logit_bias_grad.at[:, :seq_length].add(
            jnp.sum(grad_scores.astype(jnp.float32), axis=1)
        )
        grad_hidden = jnp.einsum(
            "hrl,hel->hre",
            grad_scores,
            logit_weight[:, :, :seq_length],
            preferred_element_type=jnp.float32,
        )
        grad_dense = (grad_hidden * gate_slope(pre_act)).astype(jnp.bfloat16)
        dense_weight_grad = dense_weight_grad + jnp.einsum(
            "rd,hre->hde",
            normed[start_row:stop_row],
            grad_dense,
            preferred_element_type=jnp.float32,
        )
        dense_bias_grad = dense_bias_grad + jnp.sum(grad_dense.astype(jnp.float32), axis=1)
        grad_normed_list.append(
            jnp.einsum("hre,hde->rd", grad_dense, dense_weight, preferred_element_type=jnp.float32)
        )
        start_row = stop_row
    grad_values = jnp.concatenate(value_sum_list, axis=0).astype(jnp.bfloat16)
    value_weight_grad = jnp.einsum(
        "rd,re->de", normed, grad_values, preferred_element_type=jnp.float32
    )
    value_bias_grad = column_sums(grad_values)
    grad_normed = jnp.concatenate(grad_normed_list, axis=0) + jnp.einsum(
        "re,de->rd", grad_values, value_weight, preferred_element_type=jnp.float32
    )
    grad_inputs_norm, attn_gain_grad, attn_shift_grad = norm_backward(
        grad_normed, unit_one, scale_one, attn_gain.astype(jnp.float32)
    )
    tokens_grad = grad_residual + grad_inputs_norm
    return (
        tokens_grad,
        (
            attn_gain_grad,
            attn_shift_grad,
            dense_weight_grad,
            dense_bias_grad.reshape(-1),
            logit_weight_grad,
            logit_bias_grad.reshape(-1),
            value_weight_grad,
            value_bias_grad,
            output_weight_grad,
            output_bias_grad,
            feed_gain_grad,
            feed_shift_grad,
            expand_weight_grad,
            expand_bias_grad,
            reduce_weight_grad,
            reduce_bias_grad,
        ),
    )


def body(
    tokens,
    cotangent,
    bucket_counts,
    attn_gain,
    attn_shift,
    dense_weight,
    dense_bias,
    logit_weight,
    logit_bias,
    value_weight,
    value_bias,
    output_weight,
    output_bias,
    feed_gain,
    feed_shift,
    expand_weight,
    expand_bias,
    reduce_weight,
    reduce_bias,
):
    gathered = (
        lax.all_gather(attn_gain, AXES, axis=0, tiled=True),
        lax.all_gather(attn_shift, AXES, axis=0, tiled=True),
        lax.all_gather(dense_weight, AXES, axis=1, tiled=True),
        lax.all_gather(dense_bias, AXES, axis=0, tiled=True),
        lax.all_gather(logit_weight, AXES, axis=1, tiled=True),
        lax.all_gather(logit_bias, AXES, axis=0, tiled=True),
        lax.all_gather(value_weight, AXES, axis=0, tiled=True),
        lax.all_gather(value_bias, AXES, axis=0, tiled=True),
        lax.all_gather(output_weight, AXES, axis=0, tiled=True),
        lax.all_gather(output_bias, AXES, axis=0, tiled=True),
        lax.all_gather(feed_gain, AXES, axis=0, tiled=True),
        lax.all_gather(feed_shift, AXES, axis=0, tiled=True),
        lax.all_gather(expand_weight, AXES, axis=0, tiled=True),
        lax.all_gather(expand_bias, AXES, axis=0, tiled=True),
        lax.all_gather(reduce_weight, AXES, axis=0, tiled=True),
        lax.all_gather(reduce_bias, AXES, axis=0, tiled=True),
    )
    live_mask = live_rows(bucket_counts[0])
    layer_out, stored = forward_pass(tokens, live_mask, gathered)
    gathered = (
        lax.all_gather(attn_gain, AXES, axis=0, tiled=True),
        lax.all_gather(attn_shift, AXES, axis=0, tiled=True),
        lax.all_gather(dense_weight, AXES, axis=1, tiled=True),
        lax.all_gather(dense_bias, AXES, axis=0, tiled=True),
        lax.all_gather(logit_weight, AXES, axis=1, tiled=True),
        lax.all_gather(logit_bias, AXES, axis=0, tiled=True),
        lax.all_gather(value_weight, AXES, axis=0, tiled=True),
        lax.all_gather(value_bias, AXES, axis=0, tiled=True),
        lax.all_gather(output_weight, AXES, axis=0, tiled=True),
        lax.all_gather(output_bias, AXES, axis=0, tiled=True),
        lax.all_gather(feed_gain, AXES, axis=0, tiled=True),
        lax.all_gather(feed_shift, AXES, axis=0, tiled=True),
        lax.all_gather(expand_weight, AXES, axis=0, tiled=True),
        lax.all_gather(expand_bias, AXES, axis=0, tiled=True),
        lax.all_gather(reduce_weight, AXES, axis=0, tiled=True),
        lax.all_gather(reduce_bias, AXES, axis=0, tiled=True),
    )
    tokens_grad, grads = backward_pass(cotangent, live_mask, gathered, stored)
    shards = (
        lax.psum_scatter(grads[0], AXES, scatter_dimension=0, tiled=True),
        lax.psum_scatter(grads[1], AXES, scatter_dimension=0, tiled=True),
        lax.psum_scatter(grads[2], AXES, scatter_dimension=1, tiled=True),
        lax.psum_scatter(grads[3], AXES, scatter_dimension=0, tiled=True),
        lax.psum_scatter(grads[4], AXES, scatter_dimension=1, tiled=True),
        lax.psum_scatter(grads[5], AXES, scatter_dimension=0, tiled=True),
        lax.psum_scatter(grads[6], AXES, scatter_dimension=0, tiled=True),
        lax.psum_scatter(grads[7], AXES, scatter_dimension=0, tiled=True),
        lax.psum_scatter(grads[8], AXES, scatter_dimension=0, tiled=True),
        lax.psum_scatter(grads[9], AXES, scatter_dimension=0, tiled=True),
        lax.psum_scatter(grads[10], AXES, scatter_dimension=0, tiled=True),
        lax.psum_scatter(grads[11], AXES, scatter_dimension=0, tiled=True),
        lax.psum_scatter(grads[12], AXES, scatter_dimension=0, tiled=True),
        lax.psum_scatter(grads[13], AXES, scatter_dimension=0, tiled=True),
        lax.psum_scatter(grads[14], AXES, scatter_dimension=0, tiled=True),
        lax.psum_scatter(grads[15], AXES, scatter_dimension=0, tiled=True),
    )
    return (layer_out, tokens_grad) + tuple(shards)


def solution(mesh):
    in_specs = (
        P(AXES, None),
        P(AXES, None),
        P(AXES, None),
        P(AXES),
        P(AXES),
        P(None, AXES, None),
        P(AXES),
        P(None, AXES, None),
        P(AXES),
        P(AXES, None),
        P(AXES),
        P(AXES, None),
        P(AXES),
        P(AXES),
        P(AXES),
        P(AXES, None),
        P(AXES),
        P(AXES, None),
        P(AXES),
    )
    out_specs = (
        P(AXES, None),
        P(AXES, None),
        P(AXES),
        P(AXES),
        P(None, AXES, None),
        P(AXES),
        P(None, AXES, None),
        P(AXES),
        P(AXES, None),
        P(AXES),
        P(AXES, None),
        P(AXES),
        P(AXES),
        P(AXES),
        P(AXES, None),
        P(AXES),
        P(AXES, None),
        P(AXES),
    )
    shape = tuple(mesh.shape[a] for a in AXES)
    chosen = chip_body if shape == (8, 4) else body
    return jax.shard_map(chosen, mesh=mesh, in_specs=in_specs, out_specs=out_specs, check_vma=False)
```

```python
import functools

import jax
import jax.numpy as jnp
import numpy as np
from jax import lax
from jax.experimental import pallas as pl
from jax.experimental.pallas import tpu as pltpu
from jax.sharding import PartitionSpec as P

D = 768
HEADS = 12
HEAD_DIM = 64
HIDDEN_SIZE = 768
L3 = 512
AXES = ("wide", "narrow")
L1 = 128
L2 = 256
S1 = 2
S2 = 1
S3 = 1

norm_eps = 1e-05
gelu_root = 0.7978845608028654
gelu_cube = 0.044715

MESH = pl.DeviceIdType.MESH
HBM = pl.BlockSpec(memory_space=pltpu.HBM)
VMEM = pl.BlockSpec(memory_space=pltpu.VMEM)
VMEM_LIMIT = 63 * 1024 * 1024
f32 = jnp.float32
bf16 = jnp.bfloat16

ROWS_DEV = 1024
CHIP_ROWS = 2048
HALF = 384
NN = (((1,), (0,)), ((), ()))
NT = (((1,), (1,)), ((), ()))
TN = (((0,), (0,)), ((), ()))


def dot(a, b, dims=NN):
    return lax.dot_general(a, b, dims, preferred_element_type=f32)


def gelu_both(v):
    sq = v * v
    t = jnp.tanh(v * (gelu_root + gelu_root * gelu_cube * sq))
    up = 0.5 + 0.5 * t
    slope = up + 0.5 * v * (1.0 - t * t) * (gelu_root + 3.0 * gelu_root * gelu_cube * sq)
    return v * up, slope


def norm_rows(x):
    mean = jnp.mean(x, axis=-1, keepdims=True)
    cen = x - mean
    inv = lax.rsqrt(jnp.mean(cen * cen, axis=-1, keepdims=True) + norm_eps)
    return cen * inv, inv


class Place:
    def __init__(self):
        w = lax.axis_index(AXES[0])
        n = lax.axis_index(AXES[1])
        self.w, self.n = w, n
        self.z, self.c = w // 2, w % 2
        self.nx = n + 1 - 2 * (n % 2)
        self.ny = (n + 2) % 4
        self.nd = 3 - n
        self.xdev = (w, self.nx)
        self.ydev = (w, self.ny)
        self.sib = (self.z * 2 + 1 - self.c, n)

    def zpos(self, i):
        return (self.z + i) % 4

    def zdev(self, zz):
        return (zz * 2 + self.c, self.n)

    def near(self):
        return [self.xdev, self.ydev, self.sib] + [self.zdev(self.zpos(i)) for i in (1, 2, 3)]


def greet(devs):
    bar = pltpu.get_barrier_semaphore()
    for dev in devs:
        pl.semaphore_signal(bar, inc=1, device_id=dev, device_id_type=MESH)
    pl.semaphore_wait(bar, len(devs))


def remote(src, dst, ssem, rsem, dev):
    return pltpu.make_async_remote_copy(
        src_ref=src, dst_ref=dst, send_sem=ssem, recv_sem=rsem, device_id=dev, device_id_type=MESH
    )


def everyone(me, fn):
    @pl.loop(1, 32)
    def _(j):
        t = (me + j) % 32
        fn(t, (me + 32 - j) % 32, (t // 4, t % 4))


def spread(s_all, rows, width, count, base):
    n = len(rows)
    parts = jnp.concatenate([s_all[:, r, :] for r in rows], axis=0).astype(bf16)
    q = lax.broadcasted_iota(jnp.int32, (8, 32 * n), 1)
    h = lax.broadcasted_iota(jnp.int32, (8, 32 * n), 0) + base
    piece = n * (q & 31) + (q >> 5)
    lane = lax.broadcasted_iota(jnp.int32, (128, 8 * width), 0)
    to = lax.broadcasted_iota(jnp.int32, (128, 8 * width), 1)
    out = jnp.zeros((8, 8 * width), f32)
    for pos in range(8):
        pick = jnp.where(piece == 8 * h + pos, 1.0, 0.0).astype(bf16)
        move = jnp.where((to == width * pos + lane) & (lane < width), 1.0, 0.0).astype(bf16)
        out = out + dot(dot(pick, parts).astype(bf16), move)
    return out[0:count]


def spread_narrow(s_all, vec):
    dev = lax.broadcasted_iota(jnp.int32, (32, D), 0)
    owner = (lax.broadcasted_iota(jnp.int32, (32, D), 1) * 2731) >> 16
    lane = lax.broadcasted_iota(jnp.int32, (128, D), 0)
    to = lax.broadcasted_iota(jnp.int32, (128, D), 1)
    move = jnp.where(to - 24 * ((to * 2731) >> 16) == lane, 1.0, 0.0).astype(bf16)
    for i in range(7):
        wide = dot(s_all[:, i, :].astype(bf16), move)
        vec[i : i + 1] = jnp.sum(jnp.where(owner == dev, wide, 0.0), axis=0, keepdims=True)
    vec[7:8] = jnp.zeros((1, D), f32)


class Gather:
    def __init__(self, pc, sems):
        self.pc = pc
        self.zs, self.zr, self.xs, self.xr, self.ys, self.yr, self.ds, self.dr, self.ls = sems

    def zcopy(self, k, src, buf, i, sender=None):
        pc = self.pc
        zz = pc.z if sender is None else sender
        return remote(src, buf.at[zz, :, pc.n], self.zs.at[k, i], self.zr.at[k, zz], pc.zdev(pc.zpos(i)))

    def zsend(self, k, src, buf):
        for i in (1, 2, 3):
            self.zcopy(k, src, buf, i).start()
        self.own(k, src, buf).start()

    def own(self, k, src, buf):
        return pltpu.make_async_copy(src, buf.at[self.pc.z, :, self.pc.n], self.ls.at[k])

    def xcopy(self, k, buf, zz, src=None, col=None):
        pc = self.pc
        col = pc.n if col is None else col
        slot = buf.at[zz, :, col]
        return remote(slot if src is None else src, slot, self.xs.at[k, zz], self.xr.at[k, zz], pc.xdev)

    def ycopy(self, k, buf, zz, src=None, col=None):
        pc = self.pc
        col = pc.n if col is None else col
        slot = buf.at[zz, :, col]
        return remote(slot if src is None else src, slot, self.ys.at[k, zz], self.yr.at[k, zz], pc.ydev)

    def col(self, k, src, buf, i):
        pc = self.pc
        zz = pc.zpos(i)
        if i:
            self.zcopy(k, src, buf, i, sender=zz).wait_recv()
        s = None if i else src
        self.xcopy(k, buf, zz, s).start()
        self.ycopy(k, buf, zz, s).start()

    def dcopy(self, k, buf, zz):
        pc = self.pc
        if zz < 2:
            slot, dev = buf.at[zz, :, pc.nx], pc.ydev
        else:
            slot, dev = buf.at[zz, :, pc.ny], pc.xdev
        return remote(slot, slot, self.ds.at[k, zz], self.dr.at[k, zz], dev)

    def diag(self, k, buf, zz):
        pc = self.pc
        self.xcopy(k, buf, zz, col=pc.nx).wait_recv()
        self.ycopy(k, buf, zz, col=pc.ny).wait_recv()
        self.dcopy(k, buf, zz).start()

    def fin(self, k, src, buf, each=None):
        self.own(k, src, buf).wait()
        for zz in range(4):
            remote(
                buf.at[zz, :, self.pc.nd],
                buf.at[zz, :, self.pc.nd],
                self.ds.at[k, zz],
                self.dr.at[k, zz],
                self.pc.xdev,
            ).wait_recv()
            if each is not None:
                each(zz)

    def sent(self, k, src, buf):
        for i in (1, 2, 3):
            self.zcopy(k, src, buf, i).wait_send()
        for zz in range(4):
            self.xcopy(k, buf, zz).wait_send()
            self.ycopy(k, buf, zz).wait_send()
            self.dcopy(k, buf, zz).wait_send()


class LayerFirst:
    def __init__(self, pc, src, buf, cs, cr, us, ur, vs, vr, ls, ps, pr):
        self.pc, self.src, self.buf = pc, src, buf
        self.cs, self.cr, self.us, self.ur, self.vs, self.vr, self.ls = cs, cr, us, ur, vs, vr, ls
        self.ps, self.pr = ps, pr

    def side(self, i, src, slot):
        dev = self.pc.xdev if i in (0, 3) else self.pc.ydev
        return remote(src, slot, self.cs.at[i], self.cr.at[i], dev)

    def local(self):
        return pltpu.make_async_copy(self.src, self.buf.at[self.pc.z, :, self.pc.n], self.ls)

    def first(self):
        pc = self.pc
        self.local().start()
        for i in (0, 1):
            self.side(i, self.src, self.buf.at[pc.z, :, pc.n]).start()

    def halves(self):
        pc = self.pc
        a, b = self.buf.at[pc.z, 0, pc.nx], self.buf.at[pc.z, 1, pc.ny]
        return self.side(2, a, a), self.side(3, b, b)

    def second(self):
        for i in (0, 1):
            self.side(i, self.src, self.buf.at[self.pc.z, :, self.pc.n]).wait_recv()
        for cp in self.halves():
            cp.start()

    def up(self, r):
        return remote(self.buf.at[r], self.buf.at[r], self.us.at[r], self.ur.at[r], self.pc.zdev((self.pc.z + 1) % 4))

    def down(self, r):
        return remote(self.buf.at[r], self.buf.at[r], self.vs.at[r], self.vr.at[r], self.pc.zdev((self.pc.z + 3) % 4))

    def swap(self, r):
        return remote(self.buf.at[r], self.buf.at[r], self.ps.at[r], self.pr.at[r], self.pc.sib)

    def third(self):
        z = self.pc.z
        for cp in self.halves():
            cp.wait_recv()
        self.local().wait()

        @pl.when(z < 3)
        def _():
            self.up(z).start()

        @pl.when(z > 0)
        def _():
            self.down(z).start()

        self.swap(z).start()

    def level(self, k):
        z = self.pc.z

        @pl.when(z >= k)
        def _():
            self.up(z - k).wait_recv()

            @pl.when(z < 3)
            def _():
                self.up(z - k).start()

            self.swap(z - k).start()

        @pl.when(z + k <= 3)
        def _():
            self.down(z + k).wait_recv()

            @pl.when(z > 0)
            def _():
                self.down(z + k).start()

            self.swap(z + k).start()

    def finish(self):
        z = self.pc.z
        for i in (0, 1):
            self.side(i, self.src, self.buf.at[self.pc.z, :, self.pc.n]).wait_send()
        for cp in self.halves():
            cp.wait_send()
        for r in range(4):

            @pl.when((z < 3) & (z >= r))
            def _():
                self.up(r).wait_send()

            @pl.when((z > 0) & (z <= r))
            def _():
                self.down(r).wait_send()

            self.swap(r).wait()


def gather_sems(k):
    dma = pltpu.SemaphoreType.DMA
    return [dma((k, 4))] * 8 + [dma((k,))]


def join_pair(stage, dst_of, rows_of):
    @pl.loop(0, 4)
    def _(zz):
        for cc in range(2):
            for nn in (0, 2):
                one = stage[zz, cc, nn].astype(f32)
                two = stage[zz, cc, nn + 1].astype(f32)
                row = pl.multiple_of(zz * 192 + cc * 96 + nn * 24, 16)
                for e in rows_of:
                    both = jnp.concatenate(
                        [one[24 * e : 24 * e + 24], two[24 * e : 24 * e + 24]], axis=0
                    )
                    dst_of(e, pl.ds(row, 48), both.astype(bf16))


def k1_kernel(
    s_in, tok, dense, logit, vo, ff,
    ovo, gd, gl, ef, nrm_o, val_o, hid_o, slo_o, atl_o, atm_o, ats_o, wa_o, la_o, mix_o, vv_o, vec, eb,
    s_all, db, lb, vb, mvo, md, ml, mf, tokv, nrm, val, vst, vv, wst, lst, wv, lv, hidv, slov, atlv, atmv, atsv, mixv,
    zs, zr, xs, xr, ys, yr, ds, dr, ls, tsem, osem, wsem, lsem, ssem, rsem, msem,
    cs, cr, us, ur, vs, vr, cls, ps, pr, vss, vsr, es, er,
):
    pc = Place()
    c = pc.c
    g = Gather(pc, (zs, zr, xs, xr, ys, yr, ds, dr, ls))
    o = 1 - c
    me = pc.w * 4 + pc.n
    tcopies = []
    trows = [pl.ds(pl.multiple_of(to + c * 512, 512), 512) for to in (0, 1024)]
    for i, at in enumerate((512, 0)):
        tcopies.append(pltpu.make_async_copy(tok.at[pl.ds(at, 512)], tokv.at[trows[i]], tsem.at[i]))
    for cp in tcopies:
        cp.start()
    bar = pltpu.get_barrier_semaphore()
    everyone(me, lambda t, f, dev: pl.semaphore_signal(bar, inc=1, device_id=dev, device_id_type=MESH))
    pl.semaphore_wait(bar, 31)
    gives = [
        (vo.at[o], mvo.at[c]),
        (dense.at[pl.ds(3 * o, 3)], md.at[:, c]),
        (ff.at[o], mf.at[:, c]),
        (logit.at[pl.ds(3 * o, 3)], ml.at[:, c]),
    ]
    for i, at in enumerate((512, 0)):
        gives.append((tok.at[pl.ds(at, 512)], tokv.at[trows[i]]))
    rems = [remote(give, slot, es.at[i], er.at[i], pc.sib) for i, (give, slot) in enumerate(gives)]
    for cp in rems[0:4]:
        cp.start()
    everyone(me, lambda t, f, dev: remote(s_in, s_all.at[me], vss.at[t], vsr.at[me], dev).start())
    mvo[c] = vo[c]
    md[:, c] = dense[pl.ds(3 * c, 3)]
    mf[:, c] = ff[c]
    ml[:, c] = logit[pl.ds(3 * c, 3)]
    small = lambda t, f, dev: remote(s_in, s_all.at[f], vss.at[t], vsr.at[f], dev)
    for cp in rems[4:6]:
        cp.start()
    for cp in rems[0:4]:
        cp.wait()

    vo_args = (0, mvo, ovo.at[c])
    dd = lambda p: (1 + 2 * p, md.at[p], gd.at[p])
    ll = lambda p: (2 + 2 * p, ml.at[p], gl.at[p])
    fb = (7, mf.at[1], ef.at[c, 1])
    fa = LayerFirst(pc, mf.at[0], ef.at[c, 0], cs, cr, us, ur, vs, vr, cls, ps, pr)

    g.zsend(*vo_args)
    g.zsend(*dd(0))
    g.col(*vo_args, 0)
    g.col(*dd(0), 0)
    fa.first()
    g.col(*ll(0), 0)
    s_all[me] = s_in[...]

    for i in (1, 2, 3):
        g.col(*vo_args, i)
    g.zsend(*ll(0))
    fa.second()
    g.col(*dd(1), 0)

    for i in (1, 2, 3):
        g.col(*dd(0), i)
    g.zsend(*dd(1))
    fa.third()

    def arrived(t, f, dev):
        small(t, f, dev).wait_send()
        small(t, f, dev).wait_recv()

    everyone(me, arrived)
    spread_narrow(s_all, vec)
    db[0:6] = spread(s_all, (11, 12, 13), 96, 6, 6 * c)
    lb[0:6] = spread(s_all, (8, 9, 10), 64, 6, 6 * c)
    eb[...] = spread(s_all, (7,), 96, 4, 0)
    vb[0:1] = jnp.where(c == 0, vec[2:3, 0:HALF], vec[2:3, HALF:D])

    for cp in tcopies + rems[4:6]:
        cp.wait()

    @pl.loop(0, 8)
    def _(b):
        rows = pl.ds(pl.multiple_of(b * 256, 256), 256)
        unit, _ = norm_rows(tokv[rows].astype(f32))
        nrm[rows] = (unit * vec[0:1] + vec[1:2]).astype(bf16)

    nrm_copy = pltpu.make_async_copy(nrm, nrm_o, tsem.at[4])
    nrm_copy.start()
    for zz in range(4):
        g.diag(vo_args[0], vo_args[2], zz)
    g.col(*ll(1), 0)
    for i in (1, 2, 3):
        g.col(*ll(0), i)
    g.zsend(*ll(1))
    for zz in (0, 2, 1, 3):
        g.diag(dd(0)[0], dd(0)[2], zz)
    g.fin(*vo_args)
    vo_load = pltpu.make_async_copy(ovo.at[c], vst, tsem.at[5])
    vo_load.start()
    vo_swap = remote(ovo.at[c], ovo.at[c], ssem.at[0], rsem.at[0], pc.sib)
    vo_swap.start()
    vo_load.wait()

    def put_v(e, rows, x):
        vv[rows] = x

    join_pair(vst, put_v, (0,))

    @pl.loop(0, 4)
    def _(b):
        rows = pl.ds(pl.multiple_of(b * 512, 512), 512)
        val[rows] = (dot(nrm[rows], vv[...]) + vb[0:1]).astype(bf16)

    val_copy = pltpu.make_async_copy(val, val_o, tsem.at[6])
    val_copy.start()
    vv_copy = pltpu.make_async_copy(vv, vv_o, tsem.at[5])
    vv_copy.start()
    g.col(*dd(1), 1)
    for zz in (0, 2, 1, 3):
        g.diag(ll(0)[0], ll(0)[2], zz)
    g.fin(*dd(0))
    g.fin(*ll(0))

    lane = lax.broadcasted_iota(jnp.int32, (1, 128), 1)
    keeps = [(lane < HEAD_DIM).astype(bf16), (lane >= HEAD_DIM).astype(bf16)]

    def softmax(s):
        m = jnp.max(s, axis=-1, keepdims=True)
        ex = jnp.exp(s - m)
        return (ex / jnp.sum(ex, axis=-1, keepdims=True)).astype(bf16)

    @pl.loop(0, 3)
    def _(p):
        q = p + 1
        more = p < 2
        ka, kb = 1 + 2 * q, 2 + 2 * q

        def on_a(fn):
            @pl.when(more)
            def _():
                fn(ka, md.at[q % 3], gd.at[q % 3])

            @pl.when(jnp.logical_not(more))
            def _():
                fn(*fb)

        def on_b(fn):
            @pl.when(more)
            def _():
                fn(kb, ml.at[q % 3], gl.at[q % 3])

        def on_next(fn):
            @pl.when(p == 0)
            def _():
                fn(5, md.at[2], gd.at[2])

            @pl.when(p == 1)
            def _():
                fn(*fb)

        def on_next_b(fn):
            @pl.when(p == 0)
            def _():
                fn(6, ml.at[2], gl.at[2])

        def tick(pos):
            if pos == 0:
                on_next(lambda k, s, b: g.col(k, s, b, 0))
                on_a(lambda k, s, b: g.col(k, s, b, 2))
                on_a(lambda k, s, b: g.col(k, s, b, 3))
                on_next(g.zsend)
            elif pos == 1:
                on_b(lambda k, s, b: g.col(k, s, b, 1))
                on_b(lambda k, s, b: g.col(k, s, b, 2))
            elif pos == 2:
                on_b(lambda k, s, b: g.col(k, s, b, 3))
                on_next_b(lambda k, s, b: g.col(k, s, b, 0))
            elif pos == 3:
                on_a(lambda k, s, b: g.diag(k, b, 0))
                on_a(lambda k, s, b: g.diag(k, b, 2))
                for r in range(3):

                    @pl.when(p == r)
                    def _():
                        fa.level(r + 1)
            elif pos == 4:
                on_a(lambda k, s, b: g.diag(k, b, 1))
                on_a(lambda k, s, b: g.diag(k, b, 3))
                on_next_b(g.zsend)
            elif pos == 5:
                on_next(lambda k, s, b: g.col(k, s, b, 1))
                on_b(lambda k, s, b: g.diag(k, b, 0))
            elif pos == 6:
                on_b(lambda k, s, b: g.diag(k, b, 2))
            elif pos == 7:
                on_b(lambda k, s, b: g.diag(k, b, 1))
                on_b(lambda k, s, b: g.diag(k, b, 3))

        wload = pltpu.make_async_copy(gd.at[p], wst, tsem.at[7])
        lload = pltpu.make_async_copy(gl.at[p], lst, tsem.at[8])
        wload.start()
        lload.start()
        wcopy = lambda r: pltpu.make_async_copy(wv, wa_o.at[pl.ds(2 * r, 2)], wsem)
        lcopy = lambda r: pltpu.make_async_copy(lv, la_o.at[pl.ds(2 * r, 2)], lsem)

        @pl.when(p > 0)
        def _():
            wcopy(p - 1).wait()
            lcopy(p - 1).wait()

        wload.wait()

        def put_w(e, rows, x):
            wv[e, rows] = x

        def put_l(e, rows, x):
            lv[e, rows] = x

        join_pair(wst, put_w, (0, 1))
        lload.wait()
        join_pair(lst, put_l, (0, 1))
        wcopy(p).start()
        lcopy(p).start()
        lanes = pl.ds(pl.multiple_of(p * 128, 128), 128)

        def out_copies(e, d, long, h):
            row = d * 512 if long else 1024 + d * 512
            rows = pl.ds(row, 512)
            cps = [
                pltpu.make_async_copy(hidv.at[e], hid_o.at[h, rows], osem.at[e, 0]),
                pltpu.make_async_copy(slov.at[e], slo_o.at[h, rows], osem.at[e, 1]),
            ]
            if long:
                cps.append(pltpu.make_async_copy(atlv.at[e], atl_o.at[h, pl.ds(d * 512, 512)], osem.at[e, 2]))
            else:
                part = pl.ds(d * 256, 256)
                cps.append(pltpu.make_async_copy(atmv.at[e], atm_o.at[h, part], osem.at[e, 3]))
                cps.append(pltpu.make_async_copy(atsv.at[e], ats_o.at[h, part], osem.at[e, 4]))
            return cps

        pos = 0
        for d in range(2):
            for long in (True, False):
                row = d * 512 if long else 1024 + d * 512
                rows = slice(row, row + 512)
                mixed = None
                for e in range(2):
                    h = 2 * p + e
                    pre = dot(nrm[rows], wv[e]) + db[pl.ds(h, 1)]
                    hid, slo = gelu_both(pre)
                    if d == 0 and long:

                        @pl.when(p > 0)
                        def _():
                            for cp in out_copies(e, 1, False, h):
                                cp.wait()
                    else:
                        for cp in out_copies(e, d if not long else d - 1, not long, h):
                            cp.wait()
                    hidv[e] = hid.astype(bf16)
                    slov[e] = slo.astype(bf16)
                    lbias = lb[pl.ds(h, 1)]
                    vpair = val[rows, lanes] * keeps[e]
                    if long:
                        att = softmax(dot(hidv[e], lv[e]) + lbias)
                        atlv[e] = att
                        m = dot(att, vpair)
                    else:
                        short = softmax(dot(hidv[e, 0:256], lv[e, :, 0:128]) + lbias[:, 0:128])
                        mid = softmax(dot(hidv[e, 256:512], lv[e, :, 0:256]) + lbias[:, 0:256])
                        atsv[e] = short
                        atmv[e] = mid
                        m = jnp.concatenate(
                            [
                                dot(short[0:128], vpair[0:128]),
                                dot(short[128:256], vpair[128:256]),
                                dot(mid, vpair[256:512]),
                            ],
                            axis=0,
                        )
                    mixed = m if mixed is None else mixed + m
                    for cp in out_copies(e, d, long, h):
                        cp.start()
                    tick(pos)
                    pos += 1
                mixv[rows, lanes] = mixed.astype(bf16)

        @pl.when(more)
        def _():
            g.fin(ka, md.at[q % 3], gd.at[q % 3])

        on_b(g.fin)

        @pl.when(p == 2)
        def _():
            for e in range(2):
                for cp in out_copies(e, 1, False, 2 * p + e):
                    cp.wait()
            wcopy(p).wait()
            lcopy(p).wait()

    fb_swap = lambda r: remote(ef.at[c, 1, r], ef.at[c, 1, r], ssem.at[4 + r], rsem.at[4 + r], pc.sib)
    swaps = [vo_swap]
    for i, (start, to) in enumerate(((0, 512), (1024, 0))):
        mine = pltpu.make_async_copy(
            mixv.at[pl.ds(start + c * 512, 512)], mix_o.at[c, pl.ds(to, 512)], msem.at[i]
        )
        mine.start()
        other = remote(
            mixv.at[pl.ds(start + o * 512, 512)], mix_o.at[c, pl.ds(to, 512)], ssem.at[2 + i], rsem.at[2 + i], pc.sib
        )
        other.start()
        swaps += [mine, other]
    g.fin(*fb, each=lambda r: fb_swap(r).start())
    for cp in swaps + [nrm_copy, val_copy, vv_copy] + [fb_swap(r) for r in range(4)]:
        cp.wait()
    fa.finish()
    g.sent(*vo_args)
    for p in range(3):
        g.sent(*dd(p))
        g.sent(*ll(p))
    g.sent(*fb)


def k1_call(s_in, tok, dense, logit, vo, ff):
    sds = jax.ShapeDtypeStruct
    dma = pltpu.SemaphoreType.DMA
    return pl.pallas_call(
        k1_kernel,
        out_shape=(
            sds((2, 4, 2, 4, 48, HALF), bf16),
            sds((3, 4, 2, 4, 48, D), bf16),
            sds((3, 4, 2, 4, 48, L3), bf16),
            sds((2, 2, 4, 2, 4, 48, D), bf16),
            sds((CHIP_ROWS, D), bf16),
            sds((CHIP_ROWS, HALF), bf16),
            sds((6, CHIP_ROWS, HIDDEN_SIZE), bf16),
            sds((6, CHIP_ROWS, HIDDEN_SIZE), bf16),
            sds((6, 1024, L3), bf16),
            sds((6, 512, L2), bf16),
            sds((6, 512, L1), bf16),
            sds((6, D, HIDDEN_SIZE), bf16),
            sds((6, HIDDEN_SIZE, L3), bf16),
            sds((2, ROWS_DEV, HALF), bf16),
            sds((D, HALF), bf16),
            sds((8, D), f32),
            sds((4, D), f32),
        ),
        in_specs=[VMEM, HBM] + [VMEM] * 4,
        out_specs=(HBM,) * 15 + (VMEM,) * 2,
        scratch_shapes=[
            pltpu.VMEM((32, 16, 128), f32),
            pltpu.VMEM((8, HIDDEN_SIZE), f32),
            pltpu.VMEM((8, L3), f32),
            pltpu.VMEM((8, HALF), f32),
            pltpu.VMEM((2, 48, HALF), bf16),
            pltpu.VMEM((3, 2, 48, D), bf16),
            pltpu.VMEM((3, 2, 48, L3), bf16),
            pltpu.VMEM((2, 2, 48, D), bf16),
            pltpu.VMEM((CHIP_ROWS, D), bf16),
            pltpu.VMEM((CHIP_ROWS, D), bf16),
            pltpu.VMEM((CHIP_ROWS, HALF), bf16),
            pltpu.VMEM((4, 2, 4, 48, HALF), bf16),
            pltpu.VMEM((D, HALF), bf16),
            pltpu.VMEM((4, 2, 4, 48, D), bf16),
            pltpu.VMEM((4, 2, 4, 48, L3), bf16),
            pltpu.VMEM((2, D, HIDDEN_SIZE), bf16),
            pltpu.VMEM((2, HIDDEN_SIZE, L3), bf16),
            pltpu.VMEM((2, 512, HIDDEN_SIZE), bf16),
            pltpu.VMEM((2, 512, HIDDEN_SIZE), bf16),
            pltpu.VMEM((2, 512, L3), bf16),
            pltpu.VMEM((2, 256, L2), bf16),
            pltpu.VMEM((2, 256, L1), bf16),
            pltpu.VMEM((CHIP_ROWS, HALF), bf16),
        ]
        + gather_sems(8)
        + [dma((9,)), dma((2, 5)), dma, dma, dma((8,)), dma((8,)), dma((2,))]
        + [dma((4,))] * 6
        + [dma, dma((4,)), dma((4,)), dma((32,)), dma((32,)), dma((6,)), dma((6,))],
        compiler_params=pltpu.CompilerParams(
            collective_id=1, has_side_effects=True, vmem_limit_bytes=VMEM_LIMIT
        ),
        name="k1_attention",
    )(s_in, tok, dense, logit, vo, ff)


def prepare(tokens, attn_gain, attn_shift, dense_weight, dense_bias, logit_weight, logit_bias, value_weight,
            value_bias, output_weight, output_bias, feed_gain, feed_shift, expand_weight, expand_bias,
            reduce_weight, reduce_bias):
    narrow_rows = jnp.stack([attn_gain, attn_shift, value_bias, output_bias, feed_gain, feed_shift, reduce_bias])
    wide_rows = [(expand_bias.reshape(1, 96), 32), (logit_bias.reshape(3, 64), 64), (dense_bias.reshape(3, 96), 32)]
    small = jnp.concatenate(
        [jnp.pad(narrow_rows, ((0, 0), (0, 104)))] + [jnp.pad(v, ((0, 0), (0, pad))) for v, pad in wide_rows]
    )
    small = jnp.pad(small, ((0, 2), (0, 0))).astype(f32)
    dense = dense_weight.reshape(6, 48, D)
    logit = logit_weight.reshape(6, 48, L3)
    vo = jnp.stack([value_weight.reshape(24, 2, HALF), output_weight.reshape(24, 2, HALF)]).transpose(2, 0, 1, 3)
    vo = vo.reshape(2, 48, HALF)
    ff = jnp.stack(
        [expand_weight.reshape(24, 4, D).transpose(1, 0, 2).reshape(2, 48, D), reduce_weight.reshape(2, 48, D)]
    )
    return small, tokens, dense, logit, vo, ff


def k2_kernel(
    x, cot, counts, mix, ovo, ef, vec, eb,
    lay_o, gres_o, gmix_o, def_o, do_o, sums_o,
    ev, rv, ow, inner, ge, n2, gf, ga, acc, dst, rsem, dsem, osem,
):
    oloads = []
    for half in range(2):
        lanes = pl.ds(half * HALF, HALF)
        oloads.append(pltpu.make_async_copy(ovo.at[half], dst.at[0, :, :, :, :, lanes], osem.at[half]))
    loads = [pltpu.make_async_copy(ef.at[0, f], dst.at[1 - f], dsem.at[1 - f]) for f in range(2)]
    for cp in oloads:
        cp.start()
    loads[0].start()
    rloads = []
    for f in range(2):
        for j in range(4):
            rloads.append(
                pltpu.make_async_copy(ef.at[1, f, j], rv.at[j, :, :, pl.ds(48 * f, 48)], rsem.at[f, j])
            )
    for cp in rloads:
        cp.start()

    def put_o(e, rows, v):
        ow[rows] = v

    for cp in oloads:
        cp.wait()
    join_pair(dst.at[0], put_o, (1,))
    loads[1].start()
    for f in range(2):

        def put_e(e, rows, v):
            ev[2 * f + e, rows] = v

        loads[f].wait()
        join_pair(dst.at[1 - f], put_e, (0, 1))
    for cp in rloads:
        cp.wait()
    fg, fs = vec[4:5], vec[5:6]
    sums_o[...] = jnp.zeros_like(sums_o)

    @pl.loop(0, 4)
    def _(b):
        rows = pl.ds(pl.multiple_of(b * 256, 256), 256)
        mixed = jnp.concatenate([mix[0, rows], mix[1, rows]], axis=1)
        res = x[rows].astype(f32) + (dot(mixed, ow[...]) + vec[3:4])
        unit, inv = norm_rows(res)
        n2v = (unit * fg + fs).astype(bf16)
        n2[rows] = n2v
        later = jnp.where(b == 1, counts[0, 1], counts[0, 2])
        low = jnp.where(b == 0, counts[0, 0], later) >= 1
        high = jnp.where(b == 0, counts[0, 0] - 1, later) >= 1
        top = lax.broadcasted_iota(jnp.int32, (256, 1), 0) < L1
        alive = jnp.where(top, jnp.where(low, 1.0, 0.0), jnp.where(high, 1.0, 0.0))
        gout = cot[rows].astype(f32) * alive
        gfb = gout.astype(bf16)
        gf[rows] = gfb
        feed = None
        gn2 = None
        for j in range(4):
            cols = slice(j * D, j * D + D)
            rj = rv[j].reshape(D, D)
            hid, slo = gelu_both(dot(n2v, ev[j]) + eb[j : j + 1])
            hb = hid.astype(bf16)
            inner[rows, cols] = hb
            f_j = dot(hb, rj)
            feed = f_j if feed is None else feed + f_j
            geb = (dot(gfb, rj, NT) * slo).astype(bf16)
            ge[rows, cols] = geb
            g_j = dot(geb, ev[j], NT)
            gn2 = g_j if gn2 is None else gn2 + g_j
        lay_o[rows] = alive * (res + (feed + vec[6:7]))
        q = gn2 * fg
        gres = gout + inv * (
            q - jnp.mean(q, axis=-1, keepdims=True) - unit * jnp.mean(q * unit, axis=-1, keepdims=True)
        )
        gres_o[rows] = gres
        gab = gres.astype(bf16)
        ga[rows] = gab
        gm = dot(gab, ow[...], NT).astype(bf16)
        gmix_o[0, rows] = gm[:, :HALF]
        gmix_o[1, rows] = gm[:, HALF:]
        sums_o[0:1] += jnp.sum(gn2 * unit, axis=0, keepdims=True)
        sums_o[1:2] += jnp.sum(gn2, axis=0, keepdims=True)

    ones = jnp.ones((8, ROWS_DEV), bf16)
    sums_o[2:3] = dot(ones, gf[...])[0:1]
    sums_o[3:4] = dot(ones, ga[...])[0:1]

    def out_copy(t, f):
        return pltpu.make_async_copy(dst.at[f], def_o.at[t, f], dsem.at[f])

    for f in range(2):
        for e in range(2):
            j = 2 * f + e
            sums_o[4 + j : 5 + j] = dot(ones, ge[:, j * D : j * D + D])[0:1]
            acc[e] = dot(n2[...], ge[:, j * D : j * D + D], TN)

        @pl.loop(0, 4)
        def _(zz):
            for i in range(8):
                row = pl.ds(pl.multiple_of(zz * 192 + i * 24, 8), 24)
                both = jnp.concatenate([acc[0, row], acc[1, row]], axis=0)
                dst[f, zz, i // 4, i % 4] = both.astype(bf16)

        out_copy(0, f).start()
    for j in range(4):
        acc[j % 2] = dot(inner[:, j * D : j * D + D], gf[...], TN)
        if j == 0:
            out_copy(0, 0).wait()
            out_copy(0, 1).wait()
        for i in range(8):
            for f in range(2):
                at = i * 96 + f * 48
                dst[f, j, i // 4, i % 4] = acc[j % 2, at : at + 48].astype(bf16)
    for f in range(2):
        out_copy(1, f).start()
    zero = jnp.zeros((24, 128), f32)
    for hh in range(2):
        acc[0, 0:HALF] = dot(mix[hh], ga[...], TN)
        for i in range(16):
            for half in range(2):
                for r in range(3):
                    at = half * HALF + r * 128
                    part = acc[0, i * 24 : i * 24 + 24, at : at + 128]
                    both = jnp.concatenate([zero, part], axis=0).astype(bf16)
                    do_o[half, r, 2 * hh + i // 8, (i // 4) % 2, i % 4] = both
    for f in range(2):
        out_copy(1, f).wait()


def k2_call(x, cot, counts, mix, ovo, ef, vec, eb):
    sds = jax.ShapeDtypeStruct
    dma = pltpu.SemaphoreType.DMA
    return pl.pallas_call(
        k2_kernel,
        out_shape=(
            sds((ROWS_DEV, D), f32),
            sds((ROWS_DEV, D), f32),
            sds((2, ROWS_DEV, HALF), bf16),
            sds((2, 2, 4, 2, 4, 48, D), bf16),
            sds((2, 3, 4, 2, 4, 48, 128), bf16),
            sds((8, D), f32),
        ),
        in_specs=[VMEM, VMEM, pl.BlockSpec(memory_space=pltpu.SMEM), VMEM] + [HBM] * 2 + [VMEM] * 2,
        out_specs=(VMEM, VMEM, VMEM, HBM, VMEM, VMEM),
        scratch_shapes=[
            pltpu.VMEM((4, D, D), bf16),
            pltpu.VMEM((4, 2, 4, 96, D), bf16),
            pltpu.VMEM((D, D), bf16),
            pltpu.VMEM((ROWS_DEV, 4 * D), bf16),
            pltpu.VMEM((ROWS_DEV, 4 * D), bf16),
            pltpu.VMEM((ROWS_DEV, D), bf16),
            pltpu.VMEM((ROWS_DEV, D), bf16),
            pltpu.VMEM((ROWS_DEV, D), bf16),
            pltpu.VMEM((2, D, D), f32),
            pltpu.VMEM((2, 4, 2, 4, 48, D), bf16),
            dma((2, 4)),
            dma((2,)),
            dma((2,)),
        ],
        compiler_params=pltpu.CompilerParams(vmem_limit_bytes=VMEM_LIMIT),
        name="k2_feed",
    )(x, cot, counts, mix, ovo, ef, vec, eb)


class Scatter:
    def __init__(self, pc, sems):
        self.pc = pc
        self.as_, self.ar, self.xs, self.xr, self.ys, self.yr, self.zs, self.zr, self.os, self.or_ = sems

    def acopy(self, k, p5, bufs, zz):
        dev = self.pc.xdev if zz < 2 else self.pc.ydev
        return remote(p5.at[zz, :, self.pc.nd], bufs[0].at[zz], self.as_.at[k, zz], self.ar.at[k, zz], dev)

    def xcopy(self, k, p5, bufs, zz):
        return remote(p5.at[zz, :, self.pc.nx], bufs[1].at[zz], self.xs.at[k, zz], self.xr.at[k, zz], self.pc.xdev)

    def ycopy(self, k, p5, bufs, zz):
        return remote(p5.at[zz, :, self.pc.ny], bufs[2].at[zz], self.ys.at[k, zz], self.yr.at[k, zz], self.pc.ydev)

    def zcopy(self, k, p5, bufs, i):
        zz = self.pc.zpos(i)
        return remote(
            p5.at[zz, :, self.pc.n], bufs[3].at[i - 1], self.zs.at[k, i], self.zr.at[k, i], self.pc.zdev(zz)
        )

    def row(self, k, p5, bufs, zz):
        self.acopy(k, p5, bufs, zz).start()
        (self.xcopy if zz < 2 else self.ycopy)(k, p5, bufs, zz).start()

    def one(self, k, p5, bufs):
        for zz in (0, 2, 1, 3):
            self.acopy(k, p5, bufs, zz).start()
        for zz in (0, 2, 1, 3):
            (self.xcopy if zz < 2 else self.ycopy)(k, p5, bufs, zz).start()

    def twos(self, k, p5, bufs):
        for zz in (0, 2, 1, 3):
            self.two(k, p5, bufs, zz)

    def threes(self, k, p5, bufs):
        for i in (1, 2, 3):
            self.three(k, p5, bufs, i)

    def two(self, k, p5, bufs, zz):
        col = self.pc.ny if zz < 2 else self.pc.nx
        self.acopy(k, p5, bufs, zz).wait_recv()
        p5[zz, :, col] = (p5[zz, :, col].astype(f32) + bufs[0][zz].astype(f32)).astype(bf16)
        (self.ycopy if zz < 2 else self.xcopy)(k, p5, bufs, zz).start()

    def column(self, k, p5, bufs, zz):
        self.xcopy(k, p5, bufs, zz).wait_recv()
        self.ycopy(k, p5, bufs, zz).wait_recv()
        return p5[zz, :, self.pc.n].astype(f32) + bufs[1][zz].astype(f32) + bufs[2][zz].astype(f32)

    def three(self, k, p5, bufs, i):
        zz = self.pc.zpos(i)
        p5[zz, :, self.pc.n] = self.column(k, p5, bufs, zz).astype(bf16)
        self.zcopy(k, p5, bufs, i).start()

    def outs(self, k, st, out):
        c = self.pc.c
        return (
            pltpu.make_async_copy(st.at[c], out, self.os.at[k, 1]),
            remote(st.at[1 - c], out, self.os.at[k, 0], self.or_.at[k], self.pc.sib),
        )

    def four(self, k, p5, bufs, st, out):
        total = self.column(k, p5, bufs, self.pc.z)
        for i in (1, 2, 3):
            self.zcopy(k, p5, bufs, i).wait_recv()
            total = total + bufs[3][i - 1].astype(f32)
        st[...] = total
        for cp in self.outs(k, st, out):
            cp.start()

    def sent(self, k, p5, bufs):
        for zz in range(4):
            self.acopy(k, p5, bufs, zz).wait_send()
            self.xcopy(k, p5, bufs, zz).wait_send()
            self.ycopy(k, p5, bufs, zz).wait_send()
        for i in (1, 2, 3):
            self.zcopy(k, p5, bufs, i).wait_send()


def k3_kernel(
    def_in, do_in, nrm_i, val_i, gmix, hid_i, slo_i, atl_i, atm_i, ats_i, wa_i, la_i, vv_i, tok, gres, vec, sums,
    tg_o, od, ol, ofe, ovo, va,
    db_o, lb_o, vb_o, ag_o, vg, vr, vt,
    nrm, val, gm, gn, hid, slo, atl, atm, ats, gsl, gsm, gd, wv, lv, dwf, vsb, vv, own,
    pd, pll, pv, ad, xd, yd, zd, al, xl, yl, zl, av, xv, yv, zv, std, stl, stv,
    as_, ar, xs, xr, ys, yr, zs, zr, os_, or_, lsem, ssem, rsem, gs_, gr_, free, hsem, fsem, dsem,
    fss, fsr, v1s, v1r, v2s, v2r,
):
    pc = Place()
    c = pc.c
    o = 1 - c
    s = Scatter(pc, (as_, ar, xs, xr, ys, yr, zs, zr, os_, or_))
    copy = pltpu.make_async_copy
    first = [copy(nrm_i, nrm, lsem.at[0]), copy(val_i, val, lsem.at[1]), copy(vv_i, vv, lsem.at[2])]
    for i, (at, to) in enumerate(((512, 0), (0, 1024))):
        first.append(copy(gmix.at[c, pl.ds(at, 512)], gm.at[pl.ds(pl.multiple_of(to + c * 512, 512), 512)], lsem.at[4 + i]))
    for cp in first:
        cp.start()

    def att_loads(h):
        return [copy(atl_i.at[h], atl, hsem.at[0]), copy(atm_i.at[h], atm, hsem.at[1]), copy(ats_i.at[h], ats, hsem.at[2])]

    hid_load = lambda h: copy(hid_i.at[h], hid, hsem.at[3])
    w_load = lambda h: copy(wa_i.at[h], wv, hsem.at[4])
    l_load = lambda h: copy(la_i.at[h], lv, hsem.at[5])
    slo_load = lambda h, b: copy(slo_i.at[h, pl.ds(b * 512, 512)], slo.at[b % 2], hsem.at[6 + b % 2])
    for cp in att_loads(0) + [hid_load(0), l_load(0), slo_load(0, 0), slo_load(0, 1), w_load(0)]:
        cp.start()
    order = [(f, zz) for f in (1, 0) for zz in (0, 2, 1, 3)]
    own_load = lambda i: copy(def_in.at[(c,) + order[i]], own.at[i % 2], fsem.at[i % 2])
    own_load(0).start()
    own_load(1).start()

    me = pc.w * 4 + pc.n
    bar = pltpu.get_barrier_semaphore()
    everyone(me, lambda t, f, dev: pl.semaphore_signal(bar, inc=1, device_id=dev, device_id_type=MESH))
    pl.semaphore_wait(bar, 31)
    fswaps = []
    for i, (f, zz) in enumerate(order):
        fswaps.append(remote(def_in.at[o, f, zz], pd.at[f, zz], fss.at[i], fsr.at[i], pc.sib))
    swaps = [None, None]
    swaps.append(remote(do_in.at[o], pv, ssem.at[2], rsem.at[2], pc.sib))
    for i, (at, to) in enumerate(((512, 0), (0, 1024))):
        swaps.append(
            remote(
                gmix.at[o, pl.ds(at, 512)],
                gm.at[pl.ds(pl.multiple_of(to + c * 512, 512), 512)],
                ssem.at[3 + i],
                rsem.at[3 + i],
                pc.sib,
            )
        )
    for cp in fswaps[0:4] + swaps[3:5] + fswaps[4:8] + swaps[2:3]:
        cp.start()

    def d_args(k):
        slot = k % 3
        return pd.at[slot], (ad.at[k], xd.at[k], yd.at[k], zd.at[k])

    def l_args(p):
        return pll.at[p % 2], (al.at[p], xl.at[p], yl.at[p], zl.at[p])

    def v_args(p):
        return pv.at[p], (av.at[p], xv.at[p], yv.at[p], zv.at[p])

    gn[...] = jnp.zeros_like(gn)
    gsm[...] = jnp.zeros_like(gsm)


    def core_sum(i):
        f, zz = order[i]
        fswaps[i].wait()
        own_load(i).wait()
        pd[f, zz] = (pd[f, zz].astype(f32) + own[i % 2].astype(f32)).astype(bf16)
        if i < 6:
            own_load(i + 2).start()
        s.row(f, *d_args(f), zz)

    dloads = []
    for r in range(3):
        for zz in range(4):
            to = pl.ds(HALF * (zz % 2) + 128 * r, 128)
            dloads.append(copy(do_in.at[c, r, zz], own.at[zz // 2, :, :, :, to], dsem.at[r, zz]))

    def other_half():
        for i in range(4, 8):
            core_sum(i)
        for cp in dloads:
            cp.start()

    def dloads_done():
        for cp in swaps[2:3] + dloads:
            cp.wait()

    for i in range(4):
        core_sum(i)
    swaps[3].wait()
    swaps[4].wait()
    for cp in first:
        cp.wait()

    lane = lax.broadcasted_iota(jnp.int32, (1, 128), 1)
    keeps = [(lane < HEAD_DIM).astype(bf16), (lane >= HEAD_DIM).astype(bf16)]
    ones = jnp.ones((8, 1024), bf16)

    def score_grad(att, g):
        a = att.astype(f32)
        t = a * g
        return (t - a * jnp.sum(t, axis=-1, keepdims=True)).astype(bf16)

    def put_pair(p5, half, e, width):
        @pl.loop(0, 2)
        def _(zi):
            for i in range(8):
                row = pl.ds(pl.multiple_of(zi * 192 + i * 24, 8), 24)
                part = dwf[row, 0:width]
                if e == 0:
                    both = jnp.concatenate([part, part], axis=0)
                else:
                    old = p5[2 * half + zi, i // 4, i % 4].astype(f32)
                    both = jnp.concatenate([old[0:24], part], axis=0)
                p5[2 * half + zi, i // 4, i % 4] = both.astype(bf16)

    @pl.loop(0, 3)
    def _(p):
        lanes = pl.ds(pl.multiple_of(p * 128, 128), 128)
        begin = p == 0
        later = p > 0
        kd = p + 2
        dslot = kd % 3

        def on_a(fn):
            fn(kd - 1, *d_args(kd - 1))

        def on_b(fn):
            @pl.when(begin)
            def _():
                fn(0, *d_args(0))

            @pl.when(later)
            def _():
                fn(5 + (p + 2) % 3, *l_args((p + 2) % 3))

        def on_first(*fns):
            for r, fn in enumerate(fns):
                if fn is not None:
                    pl.when(p == r)(fn)

        def on_v(fn):
            @pl.when(later)
            def _():
                fn(8 + (p + 2) % 3, *v_args((p + 2) % 3))

        def four_a():
            @pl.when(begin)
            def _():
                s.four(1, *d_args(1), std.at[1], ofe.at[c, 1])

            @pl.when(p == 2)
            def _():
                for cp in s.outs(0, std.at[0], ofe.at[c, 0]):
                    cp.wait()

            @pl.when(later)
            def _():
                s.four(kd - 1, *d_args(kd - 1), std.at[(kd - 1) % 3], od.at[3 * c + (p + 2) % 3])

        def four_b():
            @pl.when(begin)
            def _():
                s.four(0, *d_args(0), std.at[0], ofe.at[c, 0])

            @pl.when(later)
            def _():
                r = (p + 2) % 3
                s.four(5 + r, *l_args(r), stl.at[r], ol.at[3 * c + r])

        def four_v():
            @pl.when(later)
            def _():
                r = (p + 2) % 3
                s.four(8 + r, *v_args(r), stv.at[r], ovo.at[r, c])

        def value_part():
            for half in range(2):
                cols = slice(half * HALF, half * HALF + HALF)
                dwf[:, 0:128] = dot(nrm[:, cols], gm[:, lanes], TN)

                @pl.loop(0, 8)
                def _(i):
                    for zi in range(2):
                        row = pl.ds(pl.multiple_of(zi * 192 + i * 24, 8), 24)
                        at = (2 * half + zi, i // 4, i % 4)
                        to = pl.ds(pl.multiple_of(HALF * zi + 128 * p, 128), 128)
                        both = pv[(p,) + at].astype(f32) + own[half, i // 4, i % 4, :, to].astype(f32)
                        pv[(p,) + at] = jnp.concatenate([dwf[row, 0:128], both[24:48]], axis=0).astype(bf16)

        def tick(e, what):
            if what == "gs" and e == 0:
                on_first(lambda: s.twos(1, *d_args(1)))
                on_v(s.threes)
            elif what == "gd" and e == 0:
                on_first(other_half)
                four_v()
            elif what == "dw" and e == 0:
                on_b(s.twos)
            elif what == "gs":
                on_first(dloads_done)
                value_part()
                s.one(8 + p, *v_args(p))
                on_a(s.threes)
            elif what == "gd":
                on_b(s.threes)
            elif what == "dw":
                s.twos(8 + p, *v_args(p))
                s.one(kd, *d_args(kd))
            elif what == "dl" and e == 1:
                s.one(5 + p, *l_args(p))
                four_a()
            elif what == "gn" and e == 1:
                s.twos(kd, *d_args(kd))
                four_b()

        def logit_part(e):
            h = 2 * p + e
            if e == 0:

                @pl.when(p == 2)
                def _():
                    s.sent(5, *l_args(0))

            hid_load(h).wait()
            for half in range(2):
                cols = slice(half * HALF, half * HALF + HALF)
                dwf[:, 0:512] = dot(hid[0:1024, cols], gsl[e], TN)
                dwf[:, 0:256] += dot(hid[1024:2048, cols], gsm[e], TN)
                put_pair(pll.at[p % 2], half, e, 512)

            @pl.when(h < 5)
            def _():
                hid_load(h + 1).start()

            tick(e, "dl")

        for e in range(2):
            h = 2 * p + e
            more = h < 5

            def ahead(*cps):
                @pl.when(more)
                def _():
                    for cp in cps:
                        cp.start()

            for cp in att_loads(h):
                cp.wait()
            for b in range(4):
                at = b * 512
                rows = slice(at, at + 512)
                gpair = gm[rows, lanes]
                vpair = val[rows, lanes] * keeps[e]
                gkeep = gpair * keeps[e]
                if b < 2:
                    att = atl[rows]
                    gsl[e, rows] = score_grad(att, dot(gpair, vpair, NT))
                    vs = dot(att, gkeep, TN)
                else:
                    part = slice((b - 2) * 256, (b - 2) * 256 + 256)
                    sh, mi = ats[part], atm[part]
                    g_sh = jnp.concatenate(
                        [dot(gpair[0:128], vpair[0:128], NT), dot(gpair[128:256], vpair[128:256], NT)], axis=0
                    )
                    at2 = (b - 2) * 512
                    gsm[e, at2 : at2 + 256, 0:128] = score_grad(sh, g_sh)
                    gsm[e, at2 + 256 : at2 + 512] = score_grad(mi, dot(gpair[256:512], vpair[256:512], NT))
                    vs = jnp.concatenate(
                        [
                            dot(sh[0:128], gkeep[0:128], TN),
                            dot(sh[128:256], gkeep[128:256], TN),
                            dot(mi, gkeep[256:512], TN),
                        ],
                        axis=0,
                    )
                if e == 0:
                    vsb[rows] = vs.astype(bf16)
                else:
                    gm[rows, lanes] = vsb[rows] + vs.astype(bf16)
            ahead(*att_loads(h + 1))
            lsum = dot(ones, gsl[e])
            lb_o[pl.ds(h, 1)] = lsum[0:1]
            lb_o[pl.ds(h, 1), 0:256] += dot(ones, gsm[e])[0:1]
            tick(e, "gs")
            l_load(h).wait()
            for b in range(4):
                rows = slice(b * 512, b * 512 + 512)
                slo_load(h, b).wait()
                if b < 2:
                    gh = dot(gsl[e, rows], lv[...], NT)
                else:
                    gh = dot(gsm[e, (b - 2) * 512 : (b - 2) * 512 + 512], lv[:, 0:256], NT)
                gd[rows] = (gh * slo[b % 2].astype(f32)).astype(bf16)
                if b < 2:
                    slo_load(h, b + 2).start()
                else:
                    ahead(slo_load(h + 1, b - 2))
            ahead(l_load(h + 1))
            db_o[pl.ds(h, 1)] = (dot(ones, gd[0:1024]) + dot(ones, gd[1024:2048]))[0:1]
            tick(e, "gd")
            if e == 0:

                @pl.when(later)
                def _():
                    s.sent(kd - 3, *d_args(kd - 3))

            for half in range(2):
                cols = slice(half * HALF, half * HALF + HALF)
                dwf[...] = dot(nrm[:, cols], gd[...], TN)
                put_pair(pd.at[dslot], half, e, D)
            tick(e, "dw")
            if e == 1:
                logit_part(0)
                logit_part(1)
            w_load(h).wait()

            @pl.loop(0, 4)
            def _(b):
                rows = pl.ds(pl.multiple_of(b * 512, 512), 512)
                gn[rows] += dot(gd[rows], wv[...], NT)

            ahead(w_load(h + 1))
            tick(e, "gn")

    pl.semaphore_signal(free, inc=1, device_id=pc.sib, device_id_type=MESH)
    vb_o[...] = dot(ones, gm[0:1024]) + dot(ones, gm[1024:2048])

    @pl.loop(0, 4)
    def _(b):
        rows = pl.ds(pl.multiple_of(b * 512, 512), 512)
        gn[rows] += dot(gm[rows], vv[...], NT)

    s.threes(10, *v_args(2))
    other = lambda to: pl.ds(pl.multiple_of(to + o * 512, 512), 512)
    mine = lambda to: pl.ds(pl.multiple_of(to + c * 512, 512), 512)
    hid[0:512] = gn[other(1024)].astype(bf16)
    hid[512:1024] = gn[other(0)].astype(bf16)
    pl.semaphore_wait(free, 1)
    gswap = remote(hid.at[pl.ds(0, 1024)], gd.at[pl.ds(0, 1024)], gs_, gr_, pc.sib)
    gswap.start()
    tloads = [copy(tok.at[pl.ds(i * 512, 512)], slo.at[i], hsem.at[6 + i]) for i in range(2)]
    for cp in tloads:
        cp.start()
    s.twos(7, *l_args(2))
    for cp in tloads:
        cp.wait()
    gswap.wait()
    ag_o[...] = jnp.zeros_like(ag_o)

    @pl.loop(0, 4)
    def _(b):
        nat = pl.ds(pl.multiple_of(b * 256, 256), 256)
        trow = pl.ds(pl.multiple_of(jnp.where(b < 2, 1024 + b * 256, b * 256 - 512) + c * 512, 256), 256)
        load = copy(gres.at[nat], dwf.at[pl.ds(0, 256)], lsem.at[6])
        load.start()
        unit, inv = norm_rows(slo[b // 2, pl.ds(pl.multiple_of((b % 2) * 256, 256), 256)].astype(f32))
        g = gn[trow] + gd[nat].astype(f32)
        q = g * vec[0:1]
        back = inv * (q - jnp.mean(q, axis=-1, keepdims=True) - unit * jnp.mean(q * unit, axis=-1, keepdims=True))
        load.wait()
        dwf[0:256] = dwf[0:256] + back
        ag_o[0:1] += jnp.sum(g * unit, axis=0, keepdims=True)
        ag_o[1:2] += jnp.sum(g, axis=0, keepdims=True)
        store = copy(dwf.at[pl.ds(0, 256)], tg_o.at[nat], lsem.at[7])
        store.start()
        store.wait()

    vg[...] = jnp.zeros_like(vg)
    whole = [ag_o[0:1], ag_o[1:2], None, sums[3:4], sums[0:1], sums[1:2], sums[2:3]]
    whole += [sums[4 + j : 5 + j] for j in range(4)]
    for i, row in enumerate(whole):
        if row is not None:
            for b in range(6):
                vg[i, b : b + 1] = row[:, 128 * b : 128 * b + 128]
    for b in range(3):
        vg[2, pl.ds(3 * c + b, 1)] = vb_o[0:1, 128 * b : 128 * b + 128]
    for h in range(6):
        for b in range(6):
            vg[11 + 6 * c + h, b : b + 1] = db_o[h : h + 1, 128 * b : 128 * b + 128]
        for b in range(4):
            k = 4 * h + b
            vg[23 + 4 * c + k // 6, k % 6 : k % 6 + 1] = lb_o[h : h + 1, 128 * b : 128 * b + 128]
    everyone(me, lambda t, f, dev: remote(vg.at[t], vr.at[me], v1s.at[t], v1r.at[me], dev).start())
    vr[me] = vg[me]
    s.threes(4, *d_args(4))
    s.threes(7, *l_args(2))

    def part_done(t, f, dev):
        cp = remote(vg.at[t], vr.at[f], v1s.at[t], v1r.at[f], dev)
        cp.wait_send()
        cp.wait_recv()

    everyone(me, part_done)
    vt[...] = jnp.sum(vr[...], axis=0)
    everyone(me, lambda t, f, dev: remote(vt, va.at[me], v2s.at[t], v2r.at[me], dev).start())
    va[me] = vt[...]
    s.four(10, *v_args(2), stv.at[2], ovo.at[2, c])
    for cp in s.outs(1, std.at[1], ofe.at[c, 1]):
        cp.wait()
    s.four(4, *d_args(4), std.at[1], od.at[3 * c + 2])
    s.four(7, *l_args(2), stl.at[2], ol.at[3 * c + 2])

    def whole_done(t, f, dev):
        cp = remote(vt, va.at[f], v2s.at[t], v2r.at[f], dev)
        cp.wait_send()
        cp.wait_recv()

    everyone(me, whole_done)
    ends = []
    for p in range(3):
        ends.append(s.outs(2 + p, std.at[(2 + p) % 3], od.at[3 * c + p]))
        ends.append(s.outs(5 + p, stl.at[p], ol.at[3 * c + p]))
        ends.append(s.outs(8 + p, stv.at[p], ovo.at[p, c]))
    for pair in ends:
        for cp in pair:
            cp.wait()
    for k in (2, 3, 4):
        s.sent(k, *d_args(k))
    for p in (1, 2):
        s.sent(5 + p, *l_args(p))
    for p in range(3):
        s.sent(8 + p, *v_args(p))


def k3_call(*args):
    sds = jax.ShapeDtypeStruct
    dma = pltpu.SemaphoreType.DMA
    V = pltpu.VMEM

    def bufs(shape, width):
        return [V(shape + (4, 2, 48, width), bf16)] * 3 + [V(shape + (3, 2, 48, width), bf16)]

    return pl.pallas_call(
        k3_kernel,
        out_shape=(
            sds((ROWS_DEV, D), f32),
            sds((6, 48, D), f32),
            sds((6, 48, L3), f32),
            sds((2, 2, 48, D), f32),
            sds((3, 2, 48, 128), f32),
            sds((32, 8, 128), f32),
        ),
        in_specs=[HBM] * 15 + [VMEM] * 2,
        out_specs=(HBM,) * 5 + (VMEM,),
        scratch_shapes=[
            V((8, D), f32),
            V((8, L3), f32),
            V((8, HALF), f32),
            V((8, D), f32),
            V((32, 8, 128), f32),
            V((32, 8, 128), f32),
            V((8, 128), f32),
            V((CHIP_ROWS, D), bf16),
            V((CHIP_ROWS, HALF), bf16),
            V((CHIP_ROWS, HALF), bf16),
            V((CHIP_ROWS, D), f32),
            V((CHIP_ROWS, HIDDEN_SIZE), bf16),
            V((2, 512, HIDDEN_SIZE), bf16),
            V((1024, L3), bf16),
            V((512, L2), bf16),
            V((512, L1), bf16),
            V((2, 1024, L3), bf16),
            V((2, 1024, L2), bf16),
            V((CHIP_ROWS, HIDDEN_SIZE), bf16),
            V((D, HIDDEN_SIZE), bf16),
            V((HIDDEN_SIZE, L3), bf16),
            V((HALF, D), f32),
            V((CHIP_ROWS, 128), bf16),
            V((D, HALF), bf16),
            V((2, 2, 4, 48, D), bf16),
            V((3, 4, 2, 4, 48, D), bf16),
            V((2, 4, 2, 4, 48, L3), bf16),
            V((3, 4, 2, 4, 48, 128), bf16),
        ]
        + bufs((5,), D)
        + bufs((3,), L3)
        + bufs((3,), 128)
        + [V((3, 2, 48, D), f32), V((3, 2, 48, L3), f32), V((3, 2, 48, 128), f32)]
        + [dma((11, 4))] * 8
        + [dma((11, 2)), dma((11,)), dma((8,)), dma((5,)), dma((5,)), dma, dma, pltpu.SemaphoreType.REGULAR]
        + [dma((8,)), dma((2,)), dma((3, 4))]
        + [dma((8,))] * 2
        + [dma((32,))] * 4,
        compiler_params=pltpu.CompilerParams(
            collective_id=2, has_side_effects=True, vmem_limit_bytes=VMEM_LIMIT
        ),
        name="k3_backward",
    )(*args)


def chip_body(tokens, cotangent, bucket_counts, *params):
    ovo, _, _, ef, nrm, val, hid, slo, atl, atm, ats, wa, la, mix, vv, vec, eb = k1_call(*prepare(tokens, *params))
    lay, gres, gmix, dff, dout, sums = k2_call(tokens, cotangent, bucket_counts, mix, ovo, ef, vec, eb)
    tg, od, ol, ofe, dvo, every = k3_call(
        dff, dout, nrm, val, gmix, hid, slo, atl, atm, ats, wa, la, vv, tokens, gres, vec, sums
    )
    me = lax.axis_index(AXES[0]) * 4 + lax.axis_index(AXES[1])
    every = every[:, :6]
    v7 = lax.dynamic_slice(every[0:7].reshape(7, D), (0, 24 * me), (7, 24))
    own = lambda i, j, size: lax.dynamic_slice(every[i:j].reshape(-1), (size * me,), (size,))
    vo_shard = lambda r: dvo[:, :, r : r + 24].transpose(2, 1, 0, 3).reshape(24, D)
    small = lambda i: v7[i]
    return (
        lay,
        tg,
        small(0),
        small(1),
        od.reshape(HEADS, 24, HIDDEN_SIZE),
        own(11, 23, 288),
        ol.reshape(HEADS, 24, L3),
        own(23, 31, 192),
        vo_shard(0),
        small(2),
        vo_shard(24),
        small(3),
        small(4),
        small(5),
        ofe[0].reshape(4, 24, D).transpose(1, 0, 2).reshape(24, 4 * D),
        own(7, 11, 96),
        ofe[1].reshape(96, D),
        small(6),
    )


def smooth_gate(values_in):
    return (
        0.5
        * values_in
        * (1.0 + jnp.tanh(gelu_root * (values_in + gelu_cube * values_in * values_in * values_in)))
    )


def gate_slope(values_in):
    squared = values_in * values_in
    tangent = jnp.tanh(gelu_root * (values_in + gelu_cube * squared * values_in))
    return 0.5 * (1.0 + tangent) + 0.5 * values_in * (1.0 - tangent * tangent) * gelu_root * (
        1.0 + 3.0 * gelu_cube * squared
    )


def bucket_layout():
    return ((S1, L1), (S2, L2), (S3, L3))


def live_rows(counts):
    pieces = []
    for bucket_index, (slot_count, seq_length) in enumerate(bucket_layout()):
        slot_of_row = jnp.arange(slot_count * seq_length, dtype=jnp.int32) // seq_length
        pieces.append(jnp.where(slot_of_row < counts[bucket_index], 1.0, 0.0).astype(jnp.float32))
    return jnp.concatenate(pieces)


def product(left_side, right_side):
    return jnp.dot(left_side, right_side, preferred_element_type=jnp.float32)


def column_sums(matrix_rows):
    return jnp.sum(matrix_rows.astype(jnp.float32), axis=0)


def norm_forward(inputs_float, norm_gain, norm_shift):
    row_mean = jnp.mean(inputs_float, axis=-1, keepdims=True)
    centred = inputs_float - row_mean
    inverse_scale = lax.rsqrt(jnp.mean(centred * centred, axis=-1, keepdims=True) + norm_eps)
    unit_rows = centred * inverse_scale
    return (unit_rows * norm_gain + norm_shift, unit_rows, inverse_scale)


def norm_backward(grad_normed, unit_rows, inverse_scale, norm_gain):
    grad_unit = grad_normed * norm_gain
    grad_inputs = inverse_scale * (
        grad_unit
        - jnp.mean(grad_unit, axis=-1, keepdims=True)
        - unit_rows * jnp.mean(grad_unit * unit_rows, axis=-1, keepdims=True)
    )
    return (grad_inputs, jnp.sum(grad_normed * unit_rows, axis=0), jnp.sum(grad_normed, axis=0))


def forward_pass(tokens, live_mask, gathered):
    (
        attn_gain,
        attn_shift,
        dense_weight,
        dense_bias,
        logit_weight,
        logit_bias,
        value_weight,
        value_bias,
        output_weight,
        output_bias,
        feed_gain,
        feed_shift,
        expand_weight,
        expand_bias,
        reduce_weight,
        reduce_bias,
    ) = gathered
    inputs_float = tokens.astype(jnp.float32)
    normed_float, unit_one, scale_one = norm_forward(
        inputs_float, attn_gain.astype(jnp.float32), attn_shift.astype(jnp.float32)
    )
    normed = normed_float.astype(jnp.bfloat16)
    values = (product(normed, value_weight) + value_bias.astype(jnp.float32)).astype(jnp.bfloat16)
    dense_heads = dense_bias.astype(jnp.float32).reshape(HEADS, 1, HIDDEN_SIZE)
    logit_heads = logit_bias.astype(jnp.float32).reshape(HEADS, 1, L3)
    pre_list, hidden_list, attention_list, mixed_list = ([], [], [], [])
    start_row = 0
    for slot_count, seq_length in bucket_layout():
        stop_row = start_row + slot_count * seq_length
        pre_act = (
            jnp.einsum(
                "rd,hde->hre",
                normed[start_row:stop_row],
                dense_weight,
                preferred_element_type=jnp.float32,
            )
            + dense_heads
        )
        hidden = smooth_gate(pre_act).astype(jnp.bfloat16)
        scores = (
            jnp.einsum(
                "hre,hel->hrl",
                hidden,
                logit_weight[:, :, :seq_length],
                preferred_element_type=jnp.float32,
            )
            + logit_heads[:, :, :seq_length]
        )
        attention = jax.nn.softmax(scores, axis=-1)
        attention_low = attention.astype(jnp.bfloat16).reshape(
            HEADS, slot_count, seq_length, seq_length
        )
        block_values = values[start_row:stop_row].reshape(slot_count, seq_length, HEADS, HEAD_DIM)
        mixed_heads = jnp.einsum(
            "hsql,slhc->sqhc", attention_low, block_values, preferred_element_type=jnp.float32
        )
        mixed_list.append(mixed_heads.reshape(slot_count * seq_length, D))
        pre_list.append(pre_act)
        hidden_list.append(hidden)
        attention_list.append(attention)
        start_row = stop_row
    mixed_all = jnp.concatenate(mixed_list, axis=0).astype(jnp.bfloat16)
    attended = product(mixed_all, output_weight) + output_bias.astype(jnp.float32)
    residual = inputs_float + attended
    normed_two_float, unit_two, scale_two = norm_forward(
        residual, feed_gain.astype(jnp.float32), feed_shift.astype(jnp.float32)
    )
    normed_two = normed_two_float.astype(jnp.bfloat16)
    expand_pre = product(normed_two, expand_weight) + expand_bias.astype(jnp.float32)
    inner_act = smooth_gate(expand_pre).astype(jnp.bfloat16)
    feed_out = product(inner_act, reduce_weight) + reduce_bias.astype(jnp.float32)
    layer_out = live_mask[:, None] * (residual + feed_out)
    stored = (
        normed,
        unit_one,
        scale_one,
        values,
        pre_list,
        hidden_list,
        attention_list,
        mixed_all,
        unit_two,
        scale_two,
        normed_two,
        expand_pre,
        inner_act,
    )
    return (layer_out, stored)


def backward_pass(cotangent, live_mask, gathered, stored):
    (
        attn_gain,
        attn_shift,
        dense_weight,
        dense_bias,
        logit_weight,
        logit_bias,
        value_weight,
        value_bias,
        output_weight,
        output_bias,
        feed_gain,
        feed_shift,
        expand_weight,
        expand_bias,
        reduce_weight,
        reduce_bias,
    ) = gathered
    (
        normed,
        unit_one,
        scale_one,
        values,
        pre_list,
        hidden_list,
        attention_list,
        mixed_all,
        unit_two,
        scale_two,
        normed_two,
        expand_pre,
        inner_act,
    ) = stored
    grad_out = cotangent.astype(jnp.float32) * live_mask[:, None]
    grad_feed = grad_out.astype(jnp.bfloat16)
    reduce_weight_grad = jnp.einsum(
        "rf,rd->fd", inner_act, grad_feed, preferred_element_type=jnp.float32
    )
    reduce_bias_grad = column_sums(grad_feed)
    grad_inner = jnp.einsum(
        "rd,fd->rf", grad_feed, reduce_weight, preferred_element_type=jnp.float32
    )
    grad_expand = (grad_inner * gate_slope(expand_pre)).astype(jnp.bfloat16)
    expand_weight_grad = jnp.einsum(
        "rd,rf->df", normed_two, grad_expand, preferred_element_type=jnp.float32
    )
    expand_bias_grad = column_sums(grad_expand)
    grad_normed_two = jnp.einsum(
        "rf,df->rd", grad_expand, expand_weight, preferred_element_type=jnp.float32
    )
    grad_residual_norm, feed_gain_grad, feed_shift_grad = norm_backward(
        grad_normed_two, unit_two, scale_two, feed_gain.astype(jnp.float32)
    )
    grad_residual = grad_out + grad_residual_norm
    grad_attended = grad_residual.astype(jnp.bfloat16)
    output_weight_grad = jnp.einsum(
        "rd,re->de", mixed_all, grad_attended, preferred_element_type=jnp.float32
    )
    output_bias_grad = column_sums(grad_attended)
    grad_mixed = jnp.einsum(
        "re,de->rd", grad_attended, output_weight, preferred_element_type=jnp.float32
    ).astype(jnp.bfloat16)
    dense_weight_grad = jnp.zeros((HEADS, D, HIDDEN_SIZE), jnp.float32)
    dense_bias_grad = jnp.zeros((HEADS, HIDDEN_SIZE), jnp.float32)
    logit_weight_grad = jnp.zeros((HEADS, HIDDEN_SIZE, L3), jnp.float32)
    logit_bias_grad = jnp.zeros((HEADS, L3), jnp.float32)
    grad_normed_list, value_sum_list = ([], [])
    start_row = 0
    for bucket_index, (slot_count, seq_length) in enumerate(bucket_layout()):
        row_count = slot_count * seq_length
        stop_row = start_row + row_count
        attention = attention_list[bucket_index]
        hidden = hidden_list[bucket_index]
        pre_act = pre_list[bucket_index]
        attention_low = attention.astype(jnp.bfloat16).reshape(
            HEADS, slot_count, seq_length, seq_length
        )
        block_values = values[start_row:stop_row].reshape(slot_count, seq_length, HEADS, HEAD_DIM)
        block_grad = grad_mixed[start_row:stop_row].reshape(slot_count, seq_length, HEADS, HEAD_DIM)
        grad_attention = jnp.einsum(
            "sqhc,slhc->hsql", block_grad, block_values, preferred_element_type=jnp.float32
        ).reshape(HEADS, row_count, seq_length)
        value_sum_list.append(
            jnp.einsum(
                "hsql,sqhc->slhc", attention_low, block_grad, preferred_element_type=jnp.float32
            ).reshape(row_count, D)
        )
        grad_scores = (
            attention
            * (grad_attention - jnp.sum(attention * grad_attention, axis=-1, keepdims=True))
        ).astype(jnp.bfloat16)
        logit_weight_grad = logit_weight_grad.at[:, :, :seq_length].add(
            jnp.einsum("hre,hrl->hel", hidden, grad_scores, preferred_element_type=jnp.float32)
        )
        logit_bias_grad = logit_bias_grad.at[:, :seq_length].add(
            jnp.sum(grad_scores.astype(jnp.float32), axis=1)
        )
        grad_hidden = jnp.einsum(
            "hrl,hel->hre",
            grad_scores,
            logit_weight[:, :, :seq_length],
            preferred_element_type=jnp.float32,
        )
        grad_dense = (grad_hidden * gate_slope(pre_act)).astype(jnp.bfloat16)
        dense_weight_grad = dense_weight_grad + jnp.einsum(
            "rd,hre->hde",
            normed[start_row:stop_row],
            grad_dense,
            preferred_element_type=jnp.float32,
        )
        dense_bias_grad = dense_bias_grad + jnp.sum(grad_dense.astype(jnp.float32), axis=1)
        grad_normed_list.append(
            jnp.einsum("hre,hde->rd", grad_dense, dense_weight, preferred_element_type=jnp.float32)
        )
        start_row = stop_row
    grad_values = jnp.concatenate(value_sum_list, axis=0).astype(jnp.bfloat16)
    value_weight_grad = jnp.einsum(
        "rd,re->de", normed, grad_values, preferred_element_type=jnp.float32
    )
    value_bias_grad = column_sums(grad_values)
    grad_normed = jnp.concatenate(grad_normed_list, axis=0) + jnp.einsum(
        "re,de->rd", grad_values, value_weight, preferred_element_type=jnp.float32
    )
    grad_inputs_norm, attn_gain_grad, attn_shift_grad = norm_backward(
        grad_normed, unit_one, scale_one, attn_gain.astype(jnp.float32)
    )
    tokens_grad = grad_residual + grad_inputs_norm
    return (
        tokens_grad,
        (
            attn_gain_grad,
            attn_shift_grad,
            dense_weight_grad,
            dense_bias_grad.reshape(-1),
            logit_weight_grad,
            logit_bias_grad.reshape(-1),
            value_weight_grad,
            value_bias_grad,
            output_weight_grad,
            output_bias_grad,
            feed_gain_grad,
            feed_shift_grad,
            expand_weight_grad,
            expand_bias_grad,
            reduce_weight_grad,
            reduce_bias_grad,
        ),
    )


def body(
    tokens,
    cotangent,
    bucket_counts,
    attn_gain,
    attn_shift,
    dense_weight,
    dense_bias,
    logit_weight,
    logit_bias,
    value_weight,
    value_bias,
    output_weight,
    output_bias,
    feed_gain,
    feed_shift,
    expand_weight,
    expand_bias,
    reduce_weight,
    reduce_bias,
):
    gathered = (
        lax.all_gather(attn_gain, AXES, axis=0, tiled=True),
        lax.all_gather(attn_shift, AXES, axis=0, tiled=True),
        lax.all_gather(dense_weight, AXES, axis=1, tiled=True),
        lax.all_gather(dense_bias, AXES, axis=0, tiled=True),
        lax.all_gather(logit_weight, AXES, axis=1, tiled=True),
        lax.all_gather(logit_bias, AXES, axis=0, tiled=True),
        lax.all_gather(value_weight, AXES, axis=0, tiled=True),
        lax.all_gather(value_bias, AXES, axis=0, tiled=True),
        lax.all_gather(output_weight, AXES, axis=0, tiled=True),
        lax.all_gather(output_bias, AXES, axis=0, tiled=True),
        lax.all_gather(feed_gain, AXES, axis=0, tiled=True),
        lax.all_gather(feed_shift, AXES, axis=0, tiled=True),
        lax.all_gather(expand_weight, AXES, axis=0, tiled=True),
        lax.all_gather(expand_bias, AXES, axis=0, tiled=True),
        lax.all_gather(reduce_weight, AXES, axis=0, tiled=True),
        lax.all_gather(reduce_bias, AXES, axis=0, tiled=True),
    )
    live_mask = live_rows(bucket_counts[0])
    layer_out, stored = forward_pass(tokens, live_mask, gathered)
    gathered = (
        lax.all_gather(attn_gain, AXES, axis=0, tiled=True),
        lax.all_gather(attn_shift, AXES, axis=0, tiled=True),
        lax.all_gather(dense_weight, AXES, axis=1, tiled=True),
        lax.all_gather(dense_bias, AXES, axis=0, tiled=True),
        lax.all_gather(logit_weight, AXES, axis=1, tiled=True),
        lax.all_gather(logit_bias, AXES, axis=0, tiled=True),
        lax.all_gather(value_weight, AXES, axis=0, tiled=True),
        lax.all_gather(value_bias, AXES, axis=0, tiled=True),
        lax.all_gather(output_weight, AXES, axis=0, tiled=True),
        lax.all_gather(output_bias, AXES, axis=0, tiled=True),
        lax.all_gather(feed_gain, AXES, axis=0, tiled=True),
        lax.all_gather(feed_shift, AXES, axis=0, tiled=True),
        lax.all_gather(expand_weight, AXES, axis=0, tiled=True),
        lax.all_gather(expand_bias, AXES, axis=0, tiled=True),
        lax.all_gather(reduce_weight, AXES, axis=0, tiled=True),
        lax.all_gather(reduce_bias, AXES, axis=0, tiled=True),
    )
    tokens_grad, grads = backward_pass(cotangent, live_mask, gathered, stored)
    shards = (
        lax.psum_scatter(grads[0], AXES, scatter_dimension=0, tiled=True),
        lax.psum_scatter(grads[1], AXES, scatter_dimension=0, tiled=True),
        lax.psum_scatter(grads[2], AXES, scatter_dimension=1, tiled=True),
        lax.psum_scatter(grads[3], AXES, scatter_dimension=0, tiled=True),
        lax.psum_scatter(grads[4], AXES, scatter_dimension=1, tiled=True),
        lax.psum_scatter(grads[5], AXES, scatter_dimension=0, tiled=True),
        lax.psum_scatter(grads[6], AXES, scatter_dimension=0, tiled=True),
        lax.psum_scatter(grads[7], AXES, scatter_dimension=0, tiled=True),
        lax.psum_scatter(grads[8], AXES, scatter_dimension=0, tiled=True),
        lax.psum_scatter(grads[9], AXES, scatter_dimension=0, tiled=True),
        lax.psum_scatter(grads[10], AXES, scatter_dimension=0, tiled=True),
        lax.psum_scatter(grads[11], AXES, scatter_dimension=0, tiled=True),
        lax.psum_scatter(grads[12], AXES, scatter_dimension=0, tiled=True),
        lax.psum_scatter(grads[13], AXES, scatter_dimension=0, tiled=True),
        lax.psum_scatter(grads[14], AXES, scatter_dimension=0, tiled=True),
        lax.psum_scatter(grads[15], AXES, scatter_dimension=0, tiled=True),
    )
    return (layer_out, tokens_grad) + tuple(shards)


def solution(mesh):
    in_specs = (
        P(AXES, None),
        P(AXES, None),
        P(AXES, None),
        P(AXES),
        P(AXES),
        P(None, AXES, None),
        P(AXES),
        P(None, AXES, None),
        P(AXES),
        P(AXES, None),
        P(AXES),
        P(AXES, None),
        P(AXES),
        P(AXES),
        P(AXES),
        P(AXES, None),
        P(AXES),
        P(AXES, None),
        P(AXES),
    )
    out_specs = (
        P(AXES, None),
        P(AXES, None),
        P(AXES),
        P(AXES),
        P(None, AXES, None),
        P(AXES),
        P(None, AXES, None),
        P(AXES),
        P(AXES, None),
        P(AXES),
        P(AXES, None),
        P(AXES),
        P(AXES),
        P(AXES),
        P(AXES, None),
        P(AXES),
        P(AXES, None),
        P(AXES),
    )
    shape = tuple(mesh.shape[a] for a in AXES)
    chosen = chip_body if shape == (8, 4) else body
    return jax.shard_map(chosen, mesh=mesh, in_specs=in_specs, out_specs=out_specs, check_vma=False)
```
